32 devices in a mesh: dp: 16 (over z, x, core), blk: 2 (over y).
Axes of the slice: x: 2, y: 2, z: 4, core: 2. Of those that a mesh axis runs over, the one named last changes fastest.
Arguments:
- hidden: bfloat16 [8192, 768], P(('dp', 'blk')), may hold values from -6 to 6
- doc_lengths: int32 [16, 4], P('dp'), may hold values from 1 to 384, 512 in all within a row
- student_first_gain: float32 [768], replicated, may hold values from 0.5 to 1.5
- student_first_shift: float32 [768], replicated, may hold values from -1.25 to 1.25
- student_project_in: bfloat16 [768, 2304], replicated, may hold values from -0.21875 to 0.21875
- student_query_value_bias: float32 [1536], replicated, may hold values from -1.25 to 1.25
- student_attend_out: bfloat16 [768, 768], replicated, may hold values from -1.25 to 1.25
- student_attend_bias: float32 [768], replicated, may hold values from -1.25 to 1.25
- student_second_gain: float32 [768], replicated, may hold values from 0.5 to 1.5
- student_second_shift: float32 [768], replicated, may hold values from -1.25 to 1.25
- student_expand_weight: bfloat16 [768, 3072], replicated, may hold values from -0.21875 to 0.21875
- student_expand_bias: float32 [3072], replicated, may hold values from -1.25 to 1.25
- student_contract_weight: bfloat16 [3072, 768], replicated, may hold values from -0.109375 to 0.109375
- student_contract_bias: float32 [768], replicated, may hold values from -1.25 to 1.25
- teacher_first_gain: float32 [768], replicated, may hold values from 0.5 to 1.5
- teacher_first_shift: float32 [768], replicated, may hold values from -1.25 to 1.25
- teacher_project_in: bfloat16 [768, 2304], replicated, may hold values from -0.21875 to 0.21875
- teacher_query_value_bias: float32 [1536], replicated, may hold values from -1.25 to 1.25
- teacher_attend_out: bfloat16 [768, 768], replicated, may hold values from -1.25 to 1.25
- teacher_attend_bias: float32 [768], replicated, may hold values from -1.25 to 1.25
- teacher_second_gain: float32 [768], replicated, may hold values from 0.5 to 1.5
- teacher_second_shift: float32 [768], replicated, may hold values from -1.25 to 1.25
- teacher_expand_weight: bfloat16 [768, 3072], replicated, may hold values from -0.21875 to 0.21875
- teacher_expand_bias: float32 [3072], replicated, may hold values from -1.25 to 1.25
- teacher_contract_weight: bfloat16 [3072, 768], replicated, may hold values from -0.109375 to 0.109375
- teacher_contract_bias: float32 [768], replicated, may hold values from -1.25 to 1.25
- final_gain: float32 [768], replicated, may hold values from 0.5 to 1.5
- final_shift: float32 [768], replicated, may hold values from -1.25 to 1.25
- embedding: bfloat16 [32768, 768], P('blk'), may hold values from -0.8984375 to 0.8984375
Outputs:
- kl_rows: float32 [8192], P(('dp', 'blk'))
- input_grad: float32 [8192, 768], P(('dp', 'blk'))
- grad_first_gain: float32 [768], P('dp')
- grad_first_shift: float32 [768], P('dp')
- grad_project_in: float32 [768, 2304], P('dp')
- grad_query_value_bias: float32 [1536], P('dp')
- grad_attend_out: float32 [768, 768], P('dp')
- grad_attend_bias: float32 [768], P('dp')
- grad_second_gain: float32 [768], P('dp')
- grad_second_shift: float32 [768], P('dp')
- grad_expand_weight: float32 [768, 3072], P('dp')
- grad_expand_bias: float32 [3072], P('dp')
- grad_contract_weight: float32 [3072, 768], P('dp')
- grad_contract_bias: float32 [768], P('dp')
The draws below stay inside these ranges and needn't reach their ends.
Inputs may be any that keep to these rules, and one draw needn't show every extreme that they name: `doc_lengths`: each stream's lengths sum to 512; one document of each stream has exactly 384 positions.
All inputs are finite; a program needn't handle non-finite values.
Results may differ from the reference program's by a relative error of at most 0.015.
Values may be sent and summed in bfloat16 or wider, within the bound.
No kernel may reach another device: no remote copies, remote signals or barrier semaphores. Data moves between devices by JAX's collectives and lax.ppermute only.
A program may use at most 320 MiB of HBM per device.

```python
import math
import jax
import jax.numpy as jnp
import numpy as np
from jax import lax

D = 768
HEADS = 12
HEAD_DIM = 64
FF = 3072
VOCAB = 32768
TOK_DEV = 256
DOCS = 4
STREAM = 512
SEQS = 16
TOKENS = 8192


def with_spikes(entries, stream_key, source, target, blocks, factor):
    def block_of(position):
        return (jnp.arange(entries.shape[position]) // (entries.shape[position] // blocks)).reshape((-1,) + (1,) * (entries.ndim - 1 - position))

    near = jax.random.permutation(stream_key, blocks)[block_of(target)]
    second = (block_of(target) + blocks // 2) % blocks
    return jnp.where((block_of(source) == near) | (block_of(source) == second), factor * entries, entries)


def block_scale(key, shape, pieces, least, top_value):
    loudness, own = 1.0, jax.random.fold_in(key, 6)
    for position, blocks in pieces:
        draws = jnp.exp(jax.random.uniform(jax.random.fold_in(own, position), (blocks,), jnp.float32, least / len(pieces), top_value / len(pieces)))
        loudness = loudness * jnp.repeat(draws, shape[position] // blocks).reshape([-1 if axis == position else 1 for axis in range(len(shape))])
    return loudness


def length_profile(number_of, total, most, skew):
    portions = [(1 << 20) // math.isqrt(standing ** skew) + 1 for standing in range(2, number_of + 1)]
    rest, given = total - most - (number_of - 1), [1] * (number_of - 1)
    while rest > 0:
        movable = [i for i in range(number_of - 1) if given[i] < most]
        pool, left = sum([portions[i] for i in movable]), rest
        for i in movable:
            more = min(most - given[i], max(1, left * portions[i] // pool), rest)
            given[i] = given[i] + more
            rest = rest - more
    return np.array([most] + given)


def ragged_sizes(key, count, total, most, lean):
    if count == 2:
        one = jax.random.randint(key, (), max(1, total - most), min(most, total - 1) + 1)
        return jnp.stack([one, total - one])
    sizes = jnp.asarray(length_profile(count, total, most, lean), jnp.int32)
    twos = (count - 1) // 2
    donor, sink = sizes[1:1 + 2 * twos:2], sizes[2:2 + 2 * twos:2]
    margin = jnp.minimum(donor - 1, most - sink)
    shifted = jax.random.randint(jax.random.fold_in(key, 1), (twos,), 0, 1 << 20) % (margin + 1)
    sizes = sizes.at[1:1 + 2 * twos:2].set(donor - shifted).at[2:2 + 2 * twos:2].set(sink + shifted)
    return sizes[jax.random.permutation(jax.random.fold_in(key, 2), count)]


def normal_values(rng, extent, spread, reach, split=(), kind=jnp.bfloat16):
    entries = jax.random.normal(rng, extent, jnp.float32) * spread
    if len(split) > 0:
        entries = block_scale(rng, extent, split, -0.22, 0.18) * entries
    return jnp.clip(entries, min=-reach, max=reach).astype(kind)


def bell_draw_with(key, dims, deviation, bound, split, heavy, kind=jnp.bfloat16):
    drawn = deviation * jax.random.normal(key, dims, jnp.float32)
    if split:
        drawn = drawn * block_scale(key, dims, split, -0.22, 0.18)
    return jnp.clip(with_spikes(drawn, jax.random.fold_in(key, 3), *heavy), -bound, bound).astype(kind)


def setup_inputs(seed: int = 0) -> dict:
    splits = jax.random.split(jax.random.key(seed), 30)
    hidden = bell_draw_with(splits[0], (TOKENS, D), 1.0, 6.0, ((0, 32),), (0, 1, 32, 2.75))
    doc_lengths = jax.vmap(lambda own: ragged_sizes(own, DOCS, STREAM, STREAM - TOK_DEV // 2, 2))(jax.random.split(splits[1], SEQS)).reshape((SEQS, DOCS)).astype(jnp.int32)
    student_first_gain = jnp.clip(1.0 + 0.1 * jax.random.normal(splits[2], (D,), jnp.float32), 0.5, 1.5)
    student_first_shift = normal_values(splits[3], (D,), 0.2, 1.25, (), jnp.float32)
    student_project_in = normal_values(splits[4], (D, 3 * D), D ** -0.5, 0.21875)
    student_query_value_bias = normal_values(splits[5], (2 * D,), 0.2, 1.25, (), jnp.float32)
    student_attend_out = normal_values(splits[6], (D, D), (D // 32) ** -0.5, 1.25)
    student_attend_bias = normal_values(splits[7], (D,), 0.2, 1.25, (), jnp.float32)
    student_second_gain = jnp.clip(1.0 + 0.1 * jax.random.normal(splits[8], (D,), jnp.float32), 0.5, 1.5)
    student_second_shift = normal_values(splits[9], (D,), 0.2, 1.25, (), jnp.float32)
    student_expand_weight = normal_values(splits[10], (D, FF), D ** -0.5, 0.21875)
    student_expand_bias = normal_values(splits[11], (FF,), 0.2, 1.25, (), jnp.float32)
    student_contract_weight = normal_values(splits[12], (FF, D), FF ** -0.5, 0.109375)
    student_contract_bias = normal_values(splits[13], (D,), 0.2, 1.25, (), jnp.float32)
    teacher_first_gain = jnp.clip(1.0 + 0.1 * jax.random.normal(splits[14], (D,), jnp.float32), 0.5, 1.5)
    teacher_first_shift = normal_values(splits[15], (D,), 0.2, 1.25, (), jnp.float32)
    teacher_project_in = normal_values(splits[16], (D, 3 * D), D ** -0.5, 0.21875)
    teacher_query_value_bias = normal_values(splits[17], (2 * D,), 0.2, 1.25, (), jnp.float32)
    teacher_attend_out = normal_values(splits[18], (D, D), (D // 32) ** -0.5, 1.25)
    teacher_attend_bias = normal_values(splits[19], (D,), 0.2, 1.25, (), jnp.float32)
    teacher_second_gain = jnp.clip(jax.random.uniform(splits[20], (D,), jnp.float32, 0.5, 1.5), 0.5, 1.5)
    teacher_second_shift = normal_values(splits[21], (D,), 0.2, 1.25, (), jnp.float32)
    teacher_expand_weight = normal_values(splits[22], (D, FF), D ** -0.5, 0.21875)
    teacher_expand_bias = normal_values(splits[23], (FF,), 0.2, 1.25, (), jnp.float32)
    teacher_contract_weight = normal_values(splits[24], (FF, D), FF ** -0.5, 0.109375)
    teacher_contract_bias = normal_values(splits[25], (D,), 0.2, 1.25, (), jnp.float32)
    final_gain = jnp.clip(1.0 + 0.1 * jax.random.normal(splits[26], (D,), jnp.float32), 0.5, 1.5)
    final_shift = normal_values(splits[27], (D,), 0.2, 1.25, (), jnp.float32)
    embedding = normal_values(splits[28], (VOCAB, D), 0.15, 0.8984375, ((0, 2),))
    return dict(hidden=hidden, doc_lengths=doc_lengths, student_first_gain=student_first_gain, student_first_shift=student_first_shift, student_project_in=student_project_in, student_query_value_bias=student_query_value_bias, student_attend_out=student_attend_out, student_attend_bias=student_attend_bias, student_second_gain=student_second_gain, student_second_shift=student_second_shift, student_expand_weight=student_expand_weight, student_expand_bias=student_expand_bias, student_contract_weight=student_contract_weight, student_contract_bias=student_contract_bias, teacher_first_gain=teacher_first_gain, teacher_first_shift=teacher_first_shift, teacher_project_in=teacher_project_in, teacher_query_value_bias=teacher_query_value_bias, teacher_attend_out=teacher_attend_out, teacher_attend_bias=teacher_attend_bias, teacher_second_gain=teacher_second_gain, teacher_second_shift=teacher_second_shift, teacher_expand_weight=teacher_expand_weight, teacher_expand_bias=teacher_expand_bias, teacher_contract_weight=teacher_contract_weight, teacher_contract_bias=teacher_contract_bias, final_gain=final_gain, final_shift=final_shift, embedding=embedding)


@jax.custom_vjp
def low(v):
    return lax.optimization_barrier(v.astype(jnp.bfloat16)).astype(jnp.float32)

@jax.custom_vjp
def low_back(v):
    return v

def low_keep(v):
    return (low(v), None)

def low_pass(kept, grad):
    return (grad,)

def back_keep(v):
    return (v, None)

def back_low(kept, grad):
    return (low(grad),)
low.defvjp(low_keep, low_pass)
low_back.defvjp(back_keep, back_low)
exact = lax.Precision.HIGHEST

def product(left, right):
    return jnp.dot(left, right, precision=exact, preferred_element_type=jnp.float32)

def layer_norm(value, gain, shift):
    centre = value - lax.optimization_barrier(jnp.mean(value, axis=-1, keepdims=True))
    return centre * lax.rsqrt(lax.optimization_barrier(jnp.mean(centre * centre, axis=-1, keepdims=True)) + 1e-05) * gain + shift

def doc_numbers(lengths, count):
    ends = jnp.cumsum(lengths)
    places = jnp.arange(count, dtype=jnp.int32)
    return lax.optimization_barrier(jnp.sum((places[:, None] >= ends[None, :]).astype(jnp.int32), axis=1))

def attention(query, keys, values, docs):
    count = query.shape[0]
    block = math.gcd(count, 512)
    query_heads = query.reshape(count, HEADS, HEAD_DIM)
    key_heads = keys.reshape(count, HEADS, HEAD_DIM)
    value_heads = values.reshape(count, HEADS, HEAD_DIM)
    places = jnp.arange(count, dtype=jnp.int32)

    def one_block(begin):
        rows_query = lax.dynamic_slice_in_dim(query_heads, begin, block, 0)
        row_places = lax.dynamic_slice_in_dim(places, begin, block, 0)
        row_docs = lax.dynamic_slice_in_dim(docs, begin, block, 0)
        scores = jnp.einsum('qhd,khd->hqk', rows_query, key_heads, precision=exact) * 0.125
        scores = low_back(scores)
        allowed = (places[None, :] <= row_places[:, None]) & (docs[None, :] == row_docs[:, None])
        weights = jax.nn.softmax(jnp.where(allowed[None], scores, -1e+30), axis=-1)
        weights = low(weights)
        return jnp.einsum('hqk,khd->qhd', weights, value_heads, precision=exact)
    starts = jnp.arange(count // block, dtype=jnp.int32) * block
    result = lax.map(jax.checkpoint(one_block), starts)
    return result.reshape(count, HEADS * HEAD_DIM)

def block_forward(x, weights, docs):
    first_gain, first_shift, project_in, qv_bias, attend_out, attend_bias, second_gain, second_shift, expand_weight, expand_bias, contract_weight, contract_bias = weights
    width = x.shape[1]
    normed = low(layer_norm(x, first_gain, first_shift))
    bias = jnp.concatenate([qv_bias[:width], jnp.zeros((width,), jnp.float32), qv_bias[width:]])
    joined = low_back(low(product(normed, project_in) + bias))
    mixed = attention(joined[:, :width], joined[:, width:2 * width], joined[:, 2 * width:], docs)
    mixed = low_back(low(mixed))
    after = x + low_back(product(mixed, attend_out) + attend_bias)
    normed_two = low(layer_norm(after, second_gain, second_shift))
    inner = low_back(product(normed_two, expand_weight) + expand_bias)
    active = low(jax.nn.gelu(inner, approximate=True))
    return after + low_back(product(active, contract_weight) + contract_bias)

def divergence(teacher_rows, student_rows, table):
    count = student_rows.shape[0]
    block = math.gcd(count, 512)

    def one_block(begin):
        rows_teacher = lax.dynamic_slice_in_dim(teacher_rows, begin, block, 0)
        rows_student = lax.dynamic_slice_in_dim(student_rows, begin, block, 0)
        half_t = product(rows_teacher, table.T) * 0.5
        half_s = low_back(product(rows_student, table.T)) * 0.5
        norm_t = jax.nn.logsumexp(half_t, axis=-1)
        norm_s = jax.nn.logsumexp(half_s, axis=-1)
        probs_t = jnp.exp(half_t - norm_t[:, None])
        return lax.optimization_barrier(jnp.sum(probs_t * (half_t - half_s), axis=-1)) - norm_t + norm_s
    starts = jnp.arange(count // block, dtype=jnp.int32) * block
    return lax.map(jax.checkpoint(one_block), starts).reshape(count)

def reference(hidden, doc_lengths, student_first_gain, student_first_shift, student_project_in, student_query_value_bias, student_attend_out, student_attend_bias, student_second_gain, student_second_shift, student_expand_weight, student_expand_bias, student_contract_weight, student_contract_bias, teacher_first_gain, teacher_first_shift, teacher_project_in, teacher_query_value_bias, teacher_attend_out, teacher_attend_bias, teacher_second_gain, teacher_second_shift, teacher_expand_weight, teacher_expand_bias, teacher_contract_weight, teacher_contract_bias, final_gain, final_shift, embedding):
    student = tuple((member.astype(jnp.float32) for member in (student_first_gain, student_first_shift, student_project_in, student_query_value_bias, student_attend_out, student_attend_bias, student_second_gain, student_second_shift, student_expand_weight, student_expand_bias, student_contract_weight, student_contract_bias)))
    teacher = tuple((member.astype(jnp.float32) for member in (teacher_first_gain, teacher_first_shift, teacher_project_in, teacher_query_value_bias, teacher_attend_out, teacher_attend_bias, teacher_second_gain, teacher_second_shift, teacher_expand_weight, teacher_expand_bias, teacher_contract_weight, teacher_contract_bias)))
    gain_final = final_gain.astype(jnp.float32)
    shift_final = final_shift.astype(jnp.float32)
    table = embedding.astype(jnp.float32)
    streams = hidden.astype(jnp.float32).reshape(SEQS, STREAM, D)

    def one_stream(totals, item):
        inputs, lengths = item
        docs = doc_numbers(lengths, STREAM)
        target = low(layer_norm(block_forward(inputs, teacher, docs), gain_final, shift_final))

        def loss(params, values):
            rows_out = low(layer_norm(block_forward(values, params, docs), gain_final, shift_final))
            per_row = divergence(target, rows_out, table)
            return (jnp.sum(per_row), per_row)
        _, back, per_row = jax.vjp(loss, student, inputs, has_aux=True)
        grads, grad_inputs = back(jnp.ones((), jnp.float32))
        totals = jax.tree.map(lambda left, right: left + right, totals, grads)
        return (totals, (per_row, grad_inputs))
    zeros = jax.tree.map(jnp.zeros_like, student)
    totals, (divergences, grad_rows) = lax.scan(one_stream, zeros, (streams, doc_lengths))
    return (divergences.reshape(TOKENS), grad_rows.reshape(TOKENS, D), totals[0], totals[1], totals[2], totals[3], totals[4], totals[5], totals[6], totals[7], totals[8], totals[9], totals[10], totals[11])
```

```python
import functools

import jax
import jax.numpy as jnp
from jax import lax
from jax.experimental import pallas as pl
from jax.experimental.pallas import tpu as pltpu
from jax.sharding import PartitionSpec as P

HEADS = 12
HEAD_DIM = 64
VMEM_LIMIT = 60 << 20
TABLE_SPAN = 2048
MASKS_A = (1, 4, 12, 2)
MASKS_B = (1, 12, 4, 2)


negative = -1e30


def layer_norm(value, gain, shift):
    centre = value - jnp.mean(value, axis=-1, keepdims=True)
    return (
        centre * lax.rsqrt(jnp.mean(centre * centre, axis=-1, keepdims=True) + 1e-05) * gain + shift
    )


def doc_numbers(lengths, count):
    ends = jnp.cumsum(lengths)
    places = jnp.arange(count, dtype=jnp.int32)
    return jnp.sum((places[:, None] >= ends[None, :]).astype(jnp.int32), axis=1)


def dense(left, right):
    return jnp.dot(left, right, preferred_element_type=jnp.float32)


def split_heads(value):
    return value.reshape(value.shape[0], HEADS, HEAD_DIM)


def input_side(inputs, gain, shift, project_in, qv_bias):
    width = inputs.shape[1]
    normed = layer_norm(inputs, gain, shift).astype(jnp.bfloat16)
    bias = jnp.concatenate([qv_bias[:width], jnp.zeros((width,), jnp.float32), qv_bias[width:]])
    joined = (dense(normed, project_in) + bias).astype(jnp.bfloat16)
    return (normed, joined[:, :width], joined[:, width : 2 * width], joined[:, 2 * width :])


def output_side(
    inputs,
    mixed_low,
    attend_out,
    attend_bias,
    second_gain,
    second_shift,
    expand_weight,
    expand_bias,
    contract_weight,
    contract_bias,
):
    after = inputs + dense(mixed_low, attend_out) + attend_bias
    normed = layer_norm(after, second_gain, second_shift).astype(jnp.bfloat16)
    inner = dense(normed, expand_weight) + expand_bias
    active = jax.nn.gelu(inner, approximate=True).astype(jnp.bfloat16)
    final = after + dense(active, contract_weight) + contract_bias
    return (after, normed, inner, active, final)


def online(state, query, keys, values, allowed):
    top, mass, summed = state
    scores = (
        jnp.einsum(
            "qhd,khd->hqk",
            split_heads(query),
            split_heads(keys),
            preferred_element_type=jnp.float32,
        )
        * 0.125
    )
    scores = jnp.where(allowed[None], scores, negative)
    new_top = jnp.maximum(top, jnp.max(scores, axis=-1))
    factor = jnp.exp(top - new_top)
    weights = jnp.where(allowed[None], jnp.exp(scores - new_top[..., None]), 0.0)
    mass = mass * factor + jnp.sum(weights, axis=-1)
    summed = summed * factor[..., None] + jnp.einsum(
        "hqk,khd->hqd",
        weights.astype(jnp.bfloat16),
        split_heads(values),
        preferred_element_type=jnp.float32,
    )
    return (new_top, mass, summed)


def score_grads(query_heads, grad_heads, log_norm, balance, key_block, value_block, allowed):
    scores = (
        jnp.einsum("qhd,khd->hqk", query_heads, key_block, preferred_element_type=jnp.float32)
        * 0.125
    )
    probs = jnp.where(allowed[None], jnp.exp(scores - log_norm[..., None]), 0.0)
    grad_probs = jnp.einsum(
        "qhd,khd->hqk", grad_heads, value_block, preferred_element_type=jnp.float32
    )
    grad_scores = (probs * (grad_probs - balance[..., None])).astype(jnp.bfloat16)
    return (probs, grad_scores)


def partial_stats(rows_teacher, rows_student, table):
    half_t = jnp.einsum("rd,vd->rv", rows_teacher, table, preferred_element_type=jnp.float32) * 0.5
    half_s = jnp.einsum("rd,vd->rv", rows_student, table, preferred_element_type=jnp.float32) * 0.5
    top_t = jnp.max(half_t, axis=-1)
    expo_t = jnp.exp(half_t - top_t[:, None])
    top_s = jnp.max(half_s, axis=-1)
    return (
        top_t,
        jnp.sum(expo_t, axis=-1),
        jnp.sum(expo_t * (half_t - half_s), axis=-1),
        top_s,
        jnp.sum(jnp.exp(half_s - top_s[:, None]), axis=-1),
    )


def combine(first_stats, second_stats):
    top_t = jnp.maximum(first_stats[0], second_stats[0])
    right_weight = jnp.exp(second_stats[0] - top_t)
    top_s = jnp.maximum(first_stats[3], second_stats[3])
    return (
        top_t,
        second_stats[1] * right_weight,
        second_stats[2] * right_weight,
        top_s,
        second_stats[4] * jnp.exp(second_stats[3] - top_s),
    )


def row_gradient(rows_teacher, rows_student, table, norm_t, norm_s):
    half_t = jnp.einsum("rd,vd->rv", rows_teacher, table, preferred_element_type=jnp.float32) * 0.5
    half_s = jnp.einsum("rd,vd->rv", rows_student, table, preferred_element_type=jnp.float32) * 0.5
    change = ((jnp.exp(half_s - norm_s[:, None]) - jnp.exp(half_t - norm_t[:, None])) * 0.5).astype(
        jnp.bfloat16
    )
    return dense(change, table)


def local_general(
    hidden,
    doc_lengths,
    student_first_gain,
    student_first_shift,
    student_project_in,
    student_query_value_bias,
    student_attend_out,
    student_attend_bias,
    student_second_gain,
    student_second_shift,
    student_expand_weight,
    student_expand_bias,
    student_contract_weight,
    student_contract_bias,
    teacher_first_gain,
    teacher_first_shift,
    teacher_project_in,
    teacher_query_value_bias,
    teacher_attend_out,
    teacher_attend_bias,
    teacher_second_gain,
    teacher_second_shift,
    teacher_expand_weight,
    teacher_expand_bias,
    teacher_contract_weight,
    teacher_contract_bias,
    final_gain,
    final_shift,
    embedding,
):
    rows, width = hidden.shape
    blocks = lax.axis_size("blk")
    stream = rows * blocks
    first = lax.axis_index("blk") * rows
    last_place = first + rows - 1
    docs = doc_numbers(doc_lengths[0], stream)
    own_places = first + jnp.arange(rows, dtype=jnp.int32)
    own_docs = lax.dynamic_slice_in_dim(docs, first, rows)
    inputs = hidden.astype(jnp.float32)
    normed_s, query_s, keys_s, values_s = input_side(
        inputs,
        student_first_gain,
        student_first_shift,
        student_project_in,
        student_query_value_bias,
    )
    normed_t, query_t, keys_t, values_t = input_side(
        inputs,
        teacher_first_gain,
        teacher_first_shift,
        teacher_project_in,
        teacher_query_value_bias,
    )

    def allowed_for(begin):
        key_places = begin + jnp.arange(rows, dtype=jnp.int32)
        key_docs = lax.dynamic_slice_in_dim(docs, begin, rows)
        return (key_places[None, :] <= own_places[:, None]) & (
            key_docs[None, :] == own_docs[:, None]
        )

    start_state = (
        jnp.full((HEADS, rows), negative, jnp.float32),
        jnp.zeros((HEADS, rows), jnp.float32),
        jnp.zeros((HEADS, rows, HEAD_DIM), jnp.float32),
    )
    carry = (start_state, start_state)
    pieces = (
        lax.all_gather(keys_s, "blk", axis=0, tiled=True),
        lax.all_gather(values_s, "blk", axis=0, tiled=True),
        lax.all_gather(keys_t, "blk", axis=0, tiled=True),
        lax.all_gather(values_t, "blk", axis=0, tiled=True),
    )
    count = pieces[0].shape[0]
    stacked = tuple((member.reshape(count // rows, rows, width) for member in pieces))
    begins = rows * jnp.arange(count // rows, dtype=jnp.int32)

    def step(state, item):
        piece_keys_s, piece_values_s, piece_keys_t, piece_values_t, begin = item

        def step_compute(inner_state):
            allowed = allowed_for(begin)
            return (
                online(inner_state[0], query_s, piece_keys_s, piece_values_s, allowed),
                online(inner_state[1], query_t, piece_keys_t, piece_values_t, allowed),
            )

        return (
            lax.cond(begin <= last_place, step_compute, lambda inner_state: inner_state, state),
            None,
        )

    carry, _ = lax.scan(step, carry, stacked + (begins,))
    state_s, state_t = carry
    out_heads_s = state_s[2] / state_s[1][..., None]
    attn_norm = state_s[0] + jnp.log(state_s[1])
    mixed_low_s = out_heads_s.transpose(1, 0, 2).reshape(rows, width).astype(jnp.bfloat16)
    mixed_low_t = (
        (state_t[2] / state_t[1][..., None])
        .transpose(1, 0, 2)
        .reshape(rows, width)
        .astype(jnp.bfloat16)
    )
    after_s, normed_two_s, inner_s, active_s, final_s = output_side(
        inputs,
        mixed_low_s,
        student_attend_out,
        student_attend_bias,
        student_second_gain,
        student_second_shift,
        student_expand_weight,
        student_expand_bias,
        student_contract_weight,
        student_contract_bias,
    )
    after_t, normed_two_t, inner_t, active_t, final_t = output_side(
        inputs,
        mixed_low_t,
        teacher_attend_out,
        teacher_attend_bias,
        teacher_second_gain,
        teacher_second_shift,
        teacher_expand_weight,
        teacher_expand_bias,
        teacher_contract_weight,
        teacher_contract_bias,
    )
    rows_s = layer_norm(final_s, final_gain, final_shift).astype(jnp.bfloat16)
    rows_t = layer_norm(final_t, final_gain, final_shift).astype(jnp.bfloat16)
    identity = (
        jnp.full((rows,), negative, jnp.float32),
        jnp.zeros((rows,), jnp.float32),
        jnp.zeros((rows,), jnp.float32),
        jnp.full((rows,), negative, jnp.float32),
        jnp.zeros((rows,), jnp.float32),
    )
    merged = combine(
        identity,
        partial_stats(rows_t, rows_s, lax.all_gather(embedding, "blk", axis=0, tiled=True)),
    )
    norm_t = merged[0] + jnp.log(merged[1])
    norm_s = merged[3] + jnp.log(merged[4])
    kl_rows = merged[2] / merged[1] - norm_t + norm_s
    grad_final = row_gradient(
        rows_t, rows_s, lax.all_gather(embedding, "blk", axis=0, tiled=True), norm_t, norm_s
    )
    _, final_back = jax.vjp(layer_norm, final_s, final_gain, final_shift)
    grad_y = final_back(grad_final)[0]
    grad_m = grad_y.astype(jnp.bfloat16)
    grad_contract_weight = jnp.einsum(
        "rf,rd->fd", active_s, grad_m, preferred_element_type=jnp.float32
    )
    grad_contract_bias = jnp.sum(grad_m.astype(jnp.float32), axis=0)
    grad_active = jnp.einsum(
        "rd,fd->rf", grad_m, student_contract_weight, preferred_element_type=jnp.float32
    )
    _, gelu_back = jax.vjp(lambda value: jax.nn.gelu(value, approximate=True), inner_s)
    grad_inner = gelu_back(grad_active)[0].astype(jnp.bfloat16)
    grad_expand_weight = jnp.einsum(
        "rd,rf->df", normed_two_s, grad_inner, preferred_element_type=jnp.float32
    )
    grad_expand_bias = jnp.sum(grad_inner.astype(jnp.float32), axis=0)
    grad_normed_two = jnp.einsum(
        "rf,df->rd", grad_inner, student_expand_weight, preferred_element_type=jnp.float32
    )
    _, second_back = jax.vjp(layer_norm, after_s, student_second_gain, student_second_shift)
    grad_after_norm, grad_second_gain, grad_second_shift = second_back(grad_normed_two)
    grad_after = grad_y + grad_after_norm
    grad_branch = grad_after.astype(jnp.bfloat16)
    grad_attend_out = jnp.einsum(
        "rc,rd->cd", mixed_low_s, grad_branch, preferred_element_type=jnp.float32
    )
    grad_attend_bias = jnp.sum(grad_branch.astype(jnp.float32), axis=0)
    grad_mixed = jnp.einsum(
        "rd,cd->rc", grad_branch, student_attend_out, preferred_element_type=jnp.float32
    ).astype(jnp.bfloat16)
    keys_all, values_all = (
        lax.all_gather(keys_s, "blk", axis=0, tiled=True),
        lax.all_gather(values_s, "blk", axis=0, tiled=True),
    )
    grad_heads = split_heads(grad_mixed)
    query_heads = split_heads(query_s)
    balance = jnp.sum(grad_heads.astype(jnp.float32).transpose(1, 0, 2) * out_heads_s, axis=-1)
    begins = rows * jnp.arange(blocks, dtype=jnp.int32)
    zero_query = jnp.zeros((rows, HEADS, HEAD_DIM), jnp.float32)

    def back_step(grad_query, begin):
        key_block = split_heads(lax.dynamic_slice_in_dim(keys_all, begin, rows, 0))
        value_block = split_heads(lax.dynamic_slice_in_dim(values_all, begin, rows, 0))

        def back_compute(total):
            probs, grad_scores = score_grads(
                query_heads,
                grad_heads,
                attn_norm,
                balance,
                key_block,
                value_block,
                allowed_for(begin),
            )
            total = (
                total
                + jnp.einsum(
                    "hqk,khd->qhd", grad_scores, key_block, preferred_element_type=jnp.float32
                )
                * 0.125
            )
            grad_keys = (
                jnp.einsum(
                    "hqk,qhd->khd", grad_scores, query_heads, preferred_element_type=jnp.float32
                )
                * 0.125
            )
            grad_values = jnp.einsum(
                "hqk,qhd->khd",
                probs.astype(jnp.bfloat16),
                grad_heads,
                preferred_element_type=jnp.float32,
            )
            return (
                total,
                jnp.concatenate(
                    [grad_keys.reshape(rows, width), grad_values.reshape(rows, width)], axis=1
                ),
            )

        def skip(total):
            return (total, jnp.zeros((rows, 2 * width), jnp.float32))

        return lax.cond(begin <= last_place, back_compute, skip, grad_query)

    grad_query, key_terms = lax.scan(back_step, zero_query, begins)
    key_value_grad = lax.psum_scatter(
        key_terms.reshape(stream, 2 * width).astype(jnp.bfloat16),
        "blk",
        scatter_dimension=0,
        tiled=True,
    ).astype(jnp.float32)
    grad_keys_low = key_value_grad[:, :width].astype(jnp.bfloat16)
    grad_values_low = key_value_grad[:, width:].astype(jnp.bfloat16)
    grad_query_low = grad_query.reshape(rows, width).astype(jnp.bfloat16)
    grad_joined = jnp.concatenate([grad_query_low, grad_keys_low, grad_values_low], axis=1)
    grad_project_in = jnp.einsum(
        "rd,rc->dc", normed_s, grad_joined, preferred_element_type=jnp.float32
    )
    grad_query_value_bias = jnp.concatenate(
        [
            jnp.sum(grad_query_low.astype(jnp.float32), axis=0),
            jnp.sum(grad_values_low.astype(jnp.float32), axis=0),
        ]
    )
    grad_normed = jnp.einsum(
        "rc,dc->rd", grad_joined, student_project_in, preferred_element_type=jnp.float32
    )
    _, first_back = jax.vjp(layer_norm, inputs, student_first_gain, student_first_shift)
    grad_inputs_norm, grad_first_gain, grad_first_shift = first_back(grad_normed)
    input_grad = grad_after + grad_inputs_norm
    shares = (
        lax.psum_scatter(
            grad_first_gain.astype(jnp.bfloat16), "dp", scatter_dimension=0, tiled=True
        ).astype(jnp.float32),
        lax.psum_scatter(
            grad_first_shift.astype(jnp.bfloat16), "dp", scatter_dimension=0, tiled=True
        ).astype(jnp.float32),
        lax.psum_scatter(
            grad_project_in.astype(jnp.bfloat16), "dp", scatter_dimension=0, tiled=True
        ).astype(jnp.float32),
        lax.psum_scatter(
            grad_query_value_bias.astype(jnp.bfloat16), "dp", scatter_dimension=0, tiled=True
        ).astype(jnp.float32),
        lax.psum_scatter(
            grad_attend_out.astype(jnp.bfloat16), "dp", scatter_dimension=0, tiled=True
        ).astype(jnp.float32),
        lax.psum_scatter(
            grad_attend_bias.astype(jnp.bfloat16), "dp", scatter_dimension=0, tiled=True
        ).astype(jnp.float32),
        lax.psum_scatter(
            grad_second_gain.astype(jnp.bfloat16), "dp", scatter_dimension=0, tiled=True
        ).astype(jnp.float32),
        lax.psum_scatter(
            grad_second_shift.astype(jnp.bfloat16), "dp", scatter_dimension=0, tiled=True
        ).astype(jnp.float32),
        lax.psum_scatter(
            grad_expand_weight.astype(jnp.bfloat16), "dp", scatter_dimension=0, tiled=True
        ).astype(jnp.float32),
        lax.psum_scatter(
            grad_expand_bias.astype(jnp.bfloat16), "dp", scatter_dimension=0, tiled=True
        ).astype(jnp.float32),
        lax.psum_scatter(
            grad_contract_weight.astype(jnp.bfloat16), "dp", scatter_dimension=0, tiled=True
        ).astype(jnp.float32),
        lax.psum_scatter(
            grad_contract_bias.astype(jnp.bfloat16), "dp", scatter_dimension=0, tiled=True
        ).astype(jnp.float32),
    )
    summed = (
        lax.psum(shares[0].astype(jnp.bfloat16), "blk").astype(jnp.float32),
        lax.psum(shares[1].astype(jnp.bfloat16), "blk").astype(jnp.float32),
        lax.psum(shares[2].astype(jnp.bfloat16), "blk").astype(jnp.float32),
        lax.psum(shares[3].astype(jnp.bfloat16), "blk").astype(jnp.float32),
        lax.psum(shares[4].astype(jnp.bfloat16), "blk").astype(jnp.float32),
        lax.psum(shares[5].astype(jnp.bfloat16), "blk").astype(jnp.float32),
        lax.psum(shares[6].astype(jnp.bfloat16), "blk").astype(jnp.float32),
        lax.psum(shares[7].astype(jnp.bfloat16), "blk").astype(jnp.float32),
        lax.psum(shares[8].astype(jnp.bfloat16), "blk").astype(jnp.float32),
        lax.psum(shares[9].astype(jnp.bfloat16), "blk").astype(jnp.float32),
        lax.psum(shares[10].astype(jnp.bfloat16), "blk").astype(jnp.float32),
        lax.psum(shares[11].astype(jnp.bfloat16), "blk").astype(jnp.float32),
    )
    return (
        kl_rows,
        input_grad,
        summed[0],
        summed[1],
        summed[2],
        summed[3],
        summed[4],
        summed[5],
        summed[6],
        summed[7],
        summed[8],
        summed[9],
        summed[10],
        summed[11],
    )


def nt(left, right):
    return lax.dot_general(
        left, right, (((1,), (1,)), ((), ())), preferred_element_type=jnp.float32
    )


def tn(left, right):
    return lax.dot_general(
        left, right, (((0,), (0,)), ((), ())), preferred_element_type=jnp.float32
    )


def normalise(value):
    centre = value - jnp.mean(value, axis=-1, keepdims=True)
    scale = lax.rsqrt(jnp.mean(centre * centre, axis=-1, keepdims=True) + 1e-05)
    return (centre * scale, scale)


def norm_back(normed, scale, gain, grad):
    weighted = grad * gain
    return scale * (
        weighted
        - jnp.mean(weighted, axis=-1, keepdims=True)
        - normed * jnp.mean(weighted * normed, axis=-1, keepdims=True)
    )


def starts_of(lengths_ref, count):
    places = lax.broadcasted_iota(jnp.int32, (1, count), 1)
    start = jnp.zeros((1, count), jnp.int32)
    end = jnp.int32(0)
    for index in range(lengths_ref.shape[1]):
        end = end + lengths_ref[0, index]
        start = jnp.where(places >= end, jnp.maximum(start, end), start)
    return start


def in_stream_order(target, own_ref, other_ref, blk):
    rows = own_ref.shape[0]
    target[pl.ds(pl.multiple_of(blk * rows, rows), rows), :] = own_ref[...].astype(target.dtype)
    target[pl.ds(pl.multiple_of((1 - blk) * rows, rows), rows), :] = other_ref[...].astype(
        target.dtype
    )


def head_mask(shape, which):
    lanes = lax.broadcasted_iota(jnp.int32, shape, 1)
    return (lanes >= HEAD_DIM) if which else (lanes < HEAD_DIM)


def forward_kernel(train, *refs):
    (
        place_ref,
        lengths_ref,
        own_ref,
        other_ref,
        first_gain,
        first_shift,
        qv_bias,
        attend_bias,
        second_gain,
        second_shift,
        expand_bias,
        contract_bias,
        final_gain,
        final_shift,
    ) = refs[:14]
    weights_hbm = refs[14:18]
    rest = refs[18:]
    if train:
        rows_out, kept_hbm, rest = rest[0], rest[1:10], rest[10:]
    else:
        rows_out, kept_hbm, rest = rest[0], (), rest[1:]
    wpi, wao, we, wc = rest[:4]
    normed_v, joined_v, probs_v, mixed_v, after_v, normed_two_v, slope_v, active_v, y_v = rest[4:13]
    x_v, bias_v, weight_sem, out_sem = rest[13:]
    kept = (normed_v, joined_v, probs_v, mixed_v, after_v, normed_two_v, slope_v, active_v, y_v)
    loads = [
        pltpu.make_async_copy(source, target, weight_sem.at[index])
        for index, (source, target) in enumerate(zip(weights_hbm, (wpi, wao, we, wc)))
    ]
    stores = [
        pltpu.make_async_copy(source, target, out_sem.at[index])
        for index, (source, target) in enumerate(zip(kept, kept_hbm))
    ]

    def send(index):
        if train:
            stores[index].start()

    for load in loads:
        load.start()
    blk = place_ref[1]
    in_stream_order(x_v, own_ref, other_ref, blk)
    count, width = x_v.shape
    block = own_ref.shape[0]
    normed, _ = normalise(x_v[...])
    normed_v[...] = (normed * first_gain[...] + first_shift[...]).astype(jnp.bfloat16)
    send(0)
    start = starts_of(lengths_ref, count)
    keys_at = lax.broadcasted_iota(jnp.int32, (count, count), 0)
    queries_at = lax.broadcasted_iota(jnp.int32, (count, count), 1)
    bias_v[...] = jnp.where((keys_at <= queries_at) & (keys_at >= start), 0.0, negative)
    loads[0].wait()
    for part in range(3):
        span = slice(part * width, (part + 1) * width)
        value = dense(normed_v[...], wpi[:, span])
        if part == 0:
            value = value + qv_bias[:, :width]
        if part == 2:
            value = value + qv_bias[:, width:]
        joined_v[:, span] = value.astype(jnp.bfloat16)
    send(1)
    pair = 2 * HEAD_DIM
    for index in range(width // pair):
        query = joined_v[:, index * pair : (index + 1) * pair] * jnp.bfloat16(0.125)
        keys = joined_v[:, width + index * pair : width + (index + 1) * pair]
        values = joined_v[:, 2 * width + index * pair : 2 * width + (index + 1) * pair]
        for piece in range(count // block):
            span = slice(piece * block, (piece + 1) * block)
            reach = (piece + 1) * block
            both = []
            for which in range(2):
                mine = jnp.where(
                    head_mask((block, pair), which), query[span], jnp.bfloat16(0.0)
                )
                scores = nt(keys[:reach], mine) + bias_v[:reach, span]
                expo = jnp.exp(scores - jnp.max(scores, axis=0, keepdims=True))
                probs = expo * (1.0 / jnp.sum(expo, axis=0, keepdims=True))
                probs = probs.astype(jnp.bfloat16)
                if train:
                    probs_v[2 * index + which, :reach, span] = probs
                both.append(tn(probs, values[:reach]))
            mixed_v[span, index * pair : (index + 1) * pair] = jnp.where(
                head_mask((block, pair), 0), both[0], both[1]
            ).astype(jnp.bfloat16)
    send(2)
    send(3)
    loads[1].wait()
    after_v[...] = x_v[...] + dense(mixed_v[...], wao[...]) + attend_bias[...]
    send(4)
    normed, _ = normalise(after_v[...])
    normed_two_v[...] = (normed * second_gain[...] + second_shift[...]).astype(jnp.bfloat16)
    send(5)
    loads[2].wait()
    loads[3].wait()
    hidden_width = we.shape[1]
    total = after_v[...] + contract_bias[...]
    root = 0.7978845608028654
    for part in range(hidden_width // width):
        span = slice(part * width, (part + 1) * width)
        inner = dense(normed_two_v[...], we[:, span]) + expand_bias[:, span]
        square = inner * inner
        bent = jnp.tanh(root * (inner + 0.044715 * (square * inner)))
        upper = 0.5 * (1.0 + bent)
        active = (inner * upper).astype(jnp.bfloat16)
        if train:
            active_v[:, span] = active
            slope_v[:, span] = (
                upper
                + (0.5 * root) * inner * (1.0 - bent * bent) * (1.0 + (3 * 0.044715) * square)
            ).astype(jnp.bfloat16)
        total = total + dense(active, wc[span, :])
    send(6)
    send(7)
    if train:
        y_v[...] = total
    send(8)
    normed, _ = normalise(total)
    rows_out[...] = (normed * final_gain[...] + final_shift[...]).astype(jnp.bfloat16) * jnp.bfloat16(0.5)
    if train:
        for store in stores:
            store.wait()


def whole_vmem():
    return pl.BlockSpec(memory_space=pltpu.VMEM)


def in_place():
    return pl.BlockSpec(memory_space=pl.ANY)


def scalars():
    return pl.BlockSpec(memory_space=pltpu.SMEM)


def forward(train, place, lengths, own, other, vectors, weights):
    rows, width = own.shape
    count = 2 * rows
    hidden_width = weights[2].shape[1]
    low, full = jnp.bfloat16, jnp.float32
    kept = [
        ((count, width), low),
        ((count, 3 * width), low),
        ((HEADS, count, count), low),
        ((count, width), low),
        ((count, width), full),
        ((count, width), low),
        ((count, hidden_width), low),
        ((count, hidden_width), low),
        ((count, width), full),
    ]
    small = ((8, 128), low)
    scratch = [kept[0], kept[1], kept[2] if train else ((1, 8, 128), low), kept[3], kept[4], kept[5]]
    scratch += [kept[6], kept[7], kept[8]] if train else [small, small, ((8, 128), full)]
    out_shape = [jax.ShapeDtypeStruct((count, width), low)]
    out_specs = [whole_vmem()]
    if train:
        out_shape += [jax.ShapeDtypeStruct(*item) for item in kept]
        out_specs += [in_place()] * len(kept)
    return pl.pallas_call(
        functools.partial(forward_kernel, train),
        in_specs=[scalars(), scalars()] + [whole_vmem()] * 12 + [in_place()] * 4,
        out_specs=out_specs,
        out_shape=out_shape,
        scratch_shapes=[pltpu.VMEM(item.shape, low) for item in weights]
        + [pltpu.VMEM(*item) for item in scratch]
        + [
            pltpu.VMEM((count, width), full),
            pltpu.VMEM((count, count), full),
            pltpu.SemaphoreType.DMA((4,)),
            pltpu.SemaphoreType.DMA((9,)),
        ],
        compiler_params=pltpu.CompilerParams(vmem_limit_bytes=VMEM_LIMIT),
        cost_estimate=pl.CostEstimate(
            flops=8_000_000_000, bytes_accessed=20_000_000, transcendentals=0
        ),
        name="forward_student" if train else "forward_teacher",
    )(place, lengths, own, other, *vectors, *weights)


def logits_kernel(student_ref, teacher_ref, table_ref, diff_ref, expo_ref, stats_ref, sums_ref):
    count = student_ref.shape[0]
    span = table_ref.shape[0] // 8
    lanes = lax.broadcasted_iota(jnp.int32, (count, 128), 1)
    packed = jnp.zeros((count, 128), jnp.float32)
    for part in range(8):
        where = slice(part * span, (part + 1) * span)
        table = table_ref[where, :]
        half_s = nt(student_ref[...], table)
        top_s = jnp.max(half_s, axis=1, keepdims=True)
        expo_s = jnp.exp(half_s - top_s)
        mass_s = jnp.sum(expo_s, axis=1, keepdims=True)
        half_t = nt(teacher_ref[...], table)
        top_t = jnp.max(half_t, axis=1, keepdims=True)
        expo_t = jnp.exp(half_t - top_t)
        mass_t = jnp.sum(expo_t, axis=1, keepdims=True)
        cross = jnp.sum(expo_t * (half_t - half_s), axis=1, keepdims=True)
        diff_ref[:, where] = (expo_s * (mass_t / mass_s) - expo_t).astype(jnp.bfloat16)
        expo_ref[:, where] = expo_t.astype(jnp.bfloat16)
        for index, column in enumerate((top_s, mass_s, top_t, mass_t, cross)):
            packed = jnp.where(lanes == 8 * index + part, column, packed)
    stats = packed.T
    stats_ref[0] = stats[:40]
    top_s, mass_s, top_t, mass_t, cross = (stats[8 * i : 8 * i + 8] for i in range(5))

    @pl.when(pl.program_id(0) == 0)
    def _():
        row = lax.broadcasted_iota(jnp.int32, sums_ref.shape, 0)
        sums_ref[...] = jnp.where((row == 0) | (row == 2), negative, 0.0)

    old = sums_ref[...]
    new_s = jnp.maximum(old[0:1], jnp.max(top_s, axis=0, keepdims=True))
    new_t = jnp.maximum(old[2:3], jnp.max(top_t, axis=0, keepdims=True))
    keep_s = jnp.exp(old[0:1] - new_s)
    keep_t = jnp.exp(old[2:3] - new_t)
    scale_s = jnp.exp(top_s - new_s)
    scale_t = jnp.exp(top_t - new_t)
    sums_ref[0:1] = new_s
    sums_ref[1:2] = old[1:2] * keep_s + jnp.sum(mass_s * scale_s, axis=0, keepdims=True)
    sums_ref[2:3] = new_t
    sums_ref[3:4] = old[3:4] * keep_t + jnp.sum(mass_t * scale_t, axis=0, keepdims=True)
    sums_ref[4:5] = old[4:5] * keep_t + jnp.sum(cross * scale_t, axis=0, keepdims=True)


def logits_phase(student, teacher, table):
    count, width = student.shape
    entries = table.shape[0]
    span = TABLE_SPAN
    steps = entries // span
    rows = pl.BlockSpec((count, width), lambda j: (0, 0))
    wide = pl.BlockSpec((count, span), lambda j: (0, j))
    return pl.pallas_call(
        logits_kernel,
        grid=(steps,),
        in_specs=[rows, rows, pl.BlockSpec((span, width), lambda j: (j, 0))],
        out_specs=[
            wide,
            wide,
            pl.BlockSpec((1, 40, count), lambda j: (j, 0, 0)),
            pl.BlockSpec((8, count), lambda j: (0, 0)),
        ],
        out_shape=[
            jax.ShapeDtypeStruct((count, entries), jnp.bfloat16),
            jax.ShapeDtypeStruct((count, entries), jnp.bfloat16),
            jax.ShapeDtypeStruct((steps, 40, count), jnp.float32),
            jax.ShapeDtypeStruct((8, count), jnp.float32),
        ],
        compiler_params=pltpu.CompilerParams(vmem_limit_bytes=VMEM_LIMIT),
        cost_estimate=pl.CostEstimate(
            flops=4 * count * width * entries, bytes_accessed=60_000_000, transcendentals=0
        ),
        name="logits_phase",
    )(student, teacher, table)


def joined_norms(own, other):
    top_s = jnp.maximum(own[0:1], other[0:1])
    top_t = jnp.maximum(own[2:3], other[2:3])
    own_t, other_t = jnp.exp(own[2:3] - top_t), jnp.exp(other[2:3] - top_t)
    mass_s = own[1:2] * jnp.exp(own[0:1] - top_s) + other[1:2] * jnp.exp(other[0:1] - top_s)
    mass_t = own[3:4] * own_t + other[3:4] * other_t
    cross = own[4:5] * own_t + other[4:5] * other_t
    norm_s = top_s + jnp.log(mass_s)
    norm_t = top_t + jnp.log(mass_t)
    return (norm_s, norm_t, cross / mass_t - norm_t + norm_s)


def gradient_kernel(
    place_ref,
    diff_ref,
    expo_ref,
    table_ref,
    stats_ref,
    own_ref,
    other_ref,
    total_ref,
    low_ref,
    kl_ref,
    norms,
):
    step = pl.program_id(0)
    count = diff_ref.shape[0]

    @pl.when(step == 0)
    def _():
        norm_s, norm_t, divergence = joined_norms(own_ref[...], other_ref[...])
        norms[0:1] = norm_s
        norms[1:2] = norm_t
        norms[2:3] = divergence
        rows = kl_ref.shape[1]
        kl_ref[0:1] = norms[2:3, pl.ds(pl.multiple_of(place_ref[1] * rows, rows), rows)]
        total_ref[...] = jnp.zeros_like(total_ref)

    top_s, mass_s, top_t, mass_t = (stats_ref[0, 8 * i : 8 * i + 8] for i in range(4))
    first = 0.5 * jnp.exp(top_s - norms[0:1]) * mass_s / mass_t
    second = first - 0.5 * jnp.exp(top_t - norms[1:2])
    factors = jnp.concatenate([first, second, jnp.zeros((112, count), jnp.float32)], axis=0).T
    span = table_ref.shape[0] // 8
    total = total_ref[...]
    for group in range(2):
        pieces = []
        for part in range(4 * group, 4 * group + 4):
            where = slice(part * span, (part + 1) * span)
            pieces.append(
                (
                    diff_ref[:, where].astype(jnp.float32) * factors[:, part : part + 1]
                    + expo_ref[:, where].astype(jnp.float32) * factors[:, 8 + part : 9 + part]
                ).astype(jnp.bfloat16)
            )
        where = slice(4 * group * span, 4 * (group + 1) * span)
        total = total + dense(jnp.concatenate(pieces, axis=1), table_ref[where, :])
    total_ref[...] = total

    @pl.when(step == pl.num_programs(0) - 1)
    def _():
        low_ref[...] = total_ref[...].astype(jnp.bfloat16)


def gradient_phase(place, diff, expo, table, stats, own, other):
    count, entries = diff.shape
    width = table.shape[1]
    span = TABLE_SPAN
    wide = pl.BlockSpec((count, span), lambda j: (0, j))
    sums = pl.BlockSpec((8, count), lambda j: (0, 0))
    fixed = pl.BlockSpec((count, width), lambda j: (0, 0))
    return pl.pallas_call(
        gradient_kernel,
        grid=(entries // span,),
        in_specs=[
            scalars(),
            wide,
            wide,
            pl.BlockSpec((span, width), lambda j: (j, 0)),
            pl.BlockSpec((1, 40, count), lambda j: (j, 0, 0)),
            sums,
            sums,
        ],
        out_specs=[fixed, fixed, pl.BlockSpec((1, count // 2), lambda j: (0, 0))],
        out_shape=[
            jax.ShapeDtypeStruct((count, width), jnp.float32),
            jax.ShapeDtypeStruct((count, width), jnp.bfloat16),
            jax.ShapeDtypeStruct((1, count // 2), jnp.float32),
        ],
        scratch_shapes=[pltpu.VMEM((8, count), jnp.float32)],
        compiler_params=pltpu.CompilerParams(vmem_limit_bytes=VMEM_LIMIT),
        cost_estimate=pl.CostEstimate(
            flops=2 * count * width * entries, bytes_accessed=60_000_000, transcendentals=0
        ),
        name="gradient_phase",
    )(place, diff, expo, table, stats, own, other)


def spans_of(masks):
    size = 1 << len(masks)
    table = []
    for index in range(size):
        value = 0
        for bit, mask in enumerate(masks):
            if index >> (len(masks) - 1 - bit) & 1:
                value ^= mask
        table.append(value)
    return table


def shard_copies(me, natural, keep, send, sems, masks):
    half = keep.shape[0]
    return [
        pltpu.make_async_copy(
            natural.at[lax.bitwise_xor(me, jnp.int32(offset))],
            (keep if index < half else send).at[index % half],
            sems.at[index],
        )
        for index, offset in enumerate(spans_of(masks))
    ]


def feed_kernel(
    place_ref,
    own_ref,
    other_ref,
    y_ref,
    normed_two_ref,
    final_gain,
    wc_hbm,
    active_hbm,
    slope_hbm,
    cw_keep,
    cw_send,
    ew_keep,
    ew_send,
    dy_out,
    dinner_hbm,
    contract_bias_out,
    expand_bias_out,
    wc,
    active_v,
    slope_v,
    dm_v,
    dinner_v,
    cw_v,
    ew_v,
    load_sem,
    cw_sem,
    ew_sem,
    out_sem,
):
    me, blk = place_ref[0], place_ref[1]
    loads = [
        pltpu.make_async_copy(source, target, load_sem.at[index])
        for index, (source, target) in enumerate(
            ((active_hbm, active_v), (wc_hbm, wc), (slope_hbm, slope_v))
        )
    ]
    for load in loads:
        load.start()
    width = y_ref.shape[1]
    part_width = width // 2
    hidden_width = wc.shape[0]
    shards = cw_v.shape[0]
    normed, scale = normalise(y_ref[...])
    grad = own_ref[...] + other_ref[...].astype(jnp.float32)
    dy = norm_back(normed, scale, final_gain[...], grad)
    dy_out[...] = dy
    dm = dy.astype(jnp.bfloat16)
    dm_v[...] = dm
    contract_bias_out[...] = jnp.sum(dm.astype(jnp.float32), axis=0, keepdims=True)
    dm_half = dm_v[:, pl.ds(pl.multiple_of(blk * part_width, part_width), part_width)]
    loads[0].wait()
    group = shards * width // hidden_width
    for part in range(hidden_width // width):
        span = slice(part * width, (part + 1) * width)
        value = tn(active_v[:, span], dm_half).astype(jnp.bfloat16)
        cw_v[part * group : (part + 1) * group] = value.reshape(group, width // group, part_width)
    cw_copies = shard_copies(me, cw_v, cw_keep, cw_send, cw_sem, MASKS_A)
    for copy in cw_copies:
        copy.start()
    loads[1].wait()
    loads[2].wait()
    for part in range(hidden_width // width):
        span = slice(part * width, (part + 1) * width)
        dact = nt(dm_v[...], wc[span, :])
        dinner = (dact * slope_v[:, span].astype(jnp.float32)).astype(jnp.bfloat16)
        dinner_v[:, span] = dinner
        expand_bias_out[:, span] = jnp.sum(dinner.astype(jnp.float32), axis=0, keepdims=True)
    save = pltpu.make_async_copy(dinner_v, dinner_hbm, out_sem.at[0])
    save.start()
    chunk = width // shards
    for part in range(hidden_width // 2 // width):
        offset = pl.multiple_of(blk * (hidden_width // 2), width) + part * width
        value = tn(normed_two_ref[...], dinner_v[:, pl.ds(pl.multiple_of(offset, width), width)])
        value = value.astype(jnp.bfloat16)
        for half in range(2):
            row = (2 * part + half) * chunk
            ew_v[:, row : row + chunk, :] = value[
                :, half * part_width : (half + 1) * part_width
            ].reshape(shards, chunk, part_width)
    ew_copies = shard_copies(me, ew_v, ew_keep, ew_send, ew_sem, MASKS_B)
    for copy in ew_copies:
        copy.start()
    for copy in cw_copies + ew_copies + [save]:
        copy.wait()


def feed_back(place, own, other, y, normed_two, final_gain, wc, active, slope, shards):
    count, width = y.shape
    hidden_width = wc.shape[0]
    low, full = jnp.bfloat16, jnp.float32
    rows = hidden_width // shards
    half = jax.ShapeDtypeStruct((shards // 2, rows, width // 2), low)
    return pl.pallas_call(
        feed_kernel,
        in_specs=[scalars()] + [whole_vmem()] * 5 + [in_place()] * 3,
        out_specs=[in_place()] * 4 + [whole_vmem(), in_place(), whole_vmem(), whole_vmem()],
        out_shape=[
            half,
            half,
            half,
            half,
            jax.ShapeDtypeStruct((count, width), full),
            jax.ShapeDtypeStruct((count, hidden_width), low),
            jax.ShapeDtypeStruct((1, width), full),
            jax.ShapeDtypeStruct((1, hidden_width), full),
        ],
        scratch_shapes=[
            pltpu.VMEM(wc.shape, low),
            pltpu.VMEM((count, hidden_width), low),
            pltpu.VMEM((count, hidden_width), low),
            pltpu.VMEM((count, width), low),
            pltpu.VMEM((count, hidden_width), low),
            pltpu.VMEM((shards, rows, width // 2), low),
            pltpu.VMEM((shards, rows, width // 2), low),
            pltpu.SemaphoreType.DMA((3,)),
            pltpu.SemaphoreType.DMA((shards,)),
            pltpu.SemaphoreType.DMA((shards,)),
            pltpu.SemaphoreType.DMA((1,)),
        ],
        compiler_params=pltpu.CompilerParams(vmem_limit_bytes=VMEM_LIMIT),
        cost_estimate=pl.CostEstimate(
            flops=6_000_000_000, bytes_accessed=30_000_000, transcendentals=0
        ),
        name="feed_back",
    )(place, own, other, y, normed_two, final_gain, wc, active, slope)


def branch_kernel(
    place_ref,
    dy_ref,
    after_ref,
    mixed_ref,
    second_gain,
    dinner_hbm,
    we_hbm,
    wao_hbm,
    dafter_out,
    dmixed_out,
    attend_out,
    second_gain_out,
    second_shift_out,
    attend_bias_out,
    dinner_v,
    we,
    wao,
    dbranch_v,
    load_sem,
):
    blk = place_ref[1]
    loads = [
        pltpu.make_async_copy(source, target, load_sem.at[index])
        for index, (source, target) in enumerate(
            ((dinner_hbm, dinner_v), (we_hbm, we), (wao_hbm, wao))
        )
    ]
    for load in loads:
        load.start()
    width = after_ref.shape[1]
    part_width = width // 2
    loads[0].wait()
    loads[1].wait()
    dh2 = nt(dinner_v[...], we[...])
    normed, scale = normalise(after_ref[...])
    second_gain_out[...] = jnp.sum(dh2 * normed, axis=0, keepdims=True)
    second_shift_out[...] = jnp.sum(dh2, axis=0, keepdims=True)
    dafter = dy_ref[...] + norm_back(normed, scale, second_gain[...], dh2)
    dafter_out[...] = dafter
    dbranch = dafter.astype(jnp.bfloat16)
    dbranch_v[...] = dbranch
    attend_bias_out[...] = jnp.sum(dbranch.astype(jnp.float32), axis=0, keepdims=True)
    loads[2].wait()
    dmixed_out[...] = nt(dbranch, wao[...]).astype(jnp.bfloat16)
    part = dbranch_v[:, pl.ds(pl.multiple_of(blk * part_width, part_width), part_width)]
    attend_out[...] = tn(mixed_ref[...], part).astype(jnp.bfloat16).reshape(attend_out.shape)


def branch_back(place, dy, after, mixed, second_gain, dinner, we, wao, shards):
    count, width = after.shape
    low, full = jnp.bfloat16, jnp.float32
    vector = jax.ShapeDtypeStruct((1, width), full)
    return pl.pallas_call(
        branch_kernel,
        in_specs=[scalars()] + [whole_vmem()] * 4 + [in_place()] * 3,
        out_specs=[whole_vmem()] * 6,
        out_shape=[
            jax.ShapeDtypeStruct((count, width), full),
            jax.ShapeDtypeStruct((count, width), low),
            jax.ShapeDtypeStruct((shards, width // shards, width // 2), low),
            vector,
            vector,
            vector,
        ],
        scratch_shapes=[
            pltpu.VMEM(dinner.shape, low),
            pltpu.VMEM(we.shape, low),
            pltpu.VMEM(wao.shape, low),
            pltpu.VMEM((count, width), low),
            pltpu.SemaphoreType.DMA((3,)),
        ],
        compiler_params=pltpu.CompilerParams(vmem_limit_bytes=VMEM_LIMIT),
        cost_estimate=pl.CostEstimate(
            flops=3_500_000_000, bytes_accessed=15_000_000, transcendentals=0
        ),
        name="branch_back",
    )(place, dy, after, mixed, second_gain, dinner, we, wao)


def attend_kernel(
    block, query_ref, keys_ref, values_ref, probs_ref, dmixed_ref, dq_ref, dk_ref, dv_ref
):
    count, pair = query_ref.shape
    query = query_ref[...] * jnp.bfloat16(0.125)
    zero = jnp.bfloat16(0.0)
    dkeys = jnp.zeros((count, pair), jnp.float32)
    dvalues = jnp.zeros((count, pair), jnp.float32)
    keys = keys_ref[...] * jnp.bfloat16(0.125)
    for piece in reversed(range(count // block)):
        span = slice(piece * block, (piece + 1) * block)
        reach = (piece + 1) * block
        dquery = jnp.zeros((block, pair), jnp.float32)
        add_keys = jnp.zeros((reach, pair), jnp.float32)
        add_values = jnp.zeros((reach, pair), jnp.float32)
        for which in range(2):
            mask = head_mask((block, pair), which)
            grad = jnp.where(mask, dmixed_ref[span], zero)
            mine = jnp.where(mask, query[span], zero)
            probs = probs_ref[which, :reach, span]
            dprobs = nt(values_ref[:reach], grad)
            wide = probs.astype(jnp.float32)
            product = wide * dprobs
            balance = jnp.sum(product, axis=0, keepdims=True)
            dscores = (product - wide * balance).astype(jnp.bfloat16)
            add_values = add_values + dense(probs, grad)
            add_keys = add_keys + dense(dscores, mine)
            dquery = dquery + tn(
                dscores, jnp.where(head_mask((reach, pair), which), keys[:reach], zero)
            )
        dq_ref[span] = dquery.astype(jnp.bfloat16)
        if reach < count:
            pad = jnp.zeros((count - reach, pair), jnp.float32)
            add_keys = jnp.concatenate([add_keys, pad], axis=0)
            add_values = jnp.concatenate([add_values, pad], axis=0)
        dkeys = dkeys + add_keys
        dvalues = dvalues + add_values
    dk_ref[...] = dkeys.astype(jnp.bfloat16)
    dv_ref[...] = dvalues.astype(jnp.bfloat16)


def attend_back(joined, probs, dmixed, block):
    count, width = dmixed.shape
    pair = 2 * HEAD_DIM
    pairs = width // pair
    column = pl.BlockSpec((count, pair), lambda p: (0, p))
    return pl.pallas_call(
        functools.partial(attend_kernel, block),
        grid=(pairs,),
        in_specs=[
            column,
            pl.BlockSpec((count, pair), lambda p: (0, pairs + p)),
            pl.BlockSpec((count, pair), lambda p: (0, 2 * pairs + p)),
            pl.BlockSpec((2, count, count), lambda p: (p, 0, 0)),
            column,
        ],
        out_specs=[column] * 3,
        out_shape=[jax.ShapeDtypeStruct((count, width), jnp.bfloat16)] * 3,
        compiler_params=pltpu.CompilerParams(vmem_limit_bytes=VMEM_LIMIT),
        cost_estimate=pl.CostEstimate(
            flops=6_000_000_000, bytes_accessed=15_000_000, transcendentals=0
        ),
        name="attend_back",
    )(joined, joined, joined, probs, dmixed)


def project_kernel(
    place_ref,
    own_ref,
    other_ref,
    dq_ref,
    dk_ref,
    dv_ref,
    normed_ref,
    dafter_ref,
    first_gain,
    attend_ref,
    attend_bias_grad,
    second_gain_grad,
    second_shift_grad,
    expand_bias_grad,
    contract_bias_grad,
    wpi_hbm,
    a_keep,
    a_send,
    b_keep,
    b_send,
    grad_out,
    wpi,
    joined_v,
    x_v,
    grad_v,
    a_v,
    b_v,
    load_sem,
    a_sem,
    b_sem,
):
    me, blk = place_ref[0], place_ref[1]
    load = pltpu.make_async_copy(wpi_hbm, wpi, load_sem.at[0])
    load.start()
    count, width = x_v.shape
    part_width = width // 2
    shards = a_v.shape[0]
    chunk = width // shards
    in_stream_order(x_v, own_ref, other_ref, blk)
    joined_v[:, :width] = dq_ref[...]
    joined_v[:, width : 2 * width] = dk_ref[...]
    joined_v[:, 2 * width :] = dv_ref[...]
    pieces = []
    for part in range(3):
        offset = blk * (3 * part_width) + part * part_width
        value = tn(
            normed_ref[...],
            joined_v[:, pl.ds(pl.multiple_of(offset, part_width), part_width)],
        )
        pieces.append(value.astype(jnp.bfloat16).reshape(shards, chunk, part_width))
    b_v[:, :chunk, :] = pieces[1]
    b_v[:, chunk:, :] = pieces[2]
    b_copies = shard_copies(me, b_v, b_keep, b_send, b_sem, MASKS_B)
    for copy in b_copies:
        copy.start()
    a_v[:, :chunk, :] = attend_ref[...]
    a_v[:, chunk : 2 * chunk, :] = pieces[0]
    load.wait()
    dh1 = nt(joined_v[...], wpi[...])
    normed, scale = normalise(x_v[...])
    sums = jnp.sum(joined_v[...].astype(jnp.float32), axis=0, keepdims=True)
    vectors = [
        jnp.sum(dh1 * normed, axis=0, keepdims=True),
        jnp.sum(dh1, axis=0, keepdims=True),
        jnp.concatenate([sums[:, :width], sums[:, 2 * width :]], axis=1),
        attend_bias_grad[...],
        second_gain_grad[...],
        second_shift_grad[...],
        expand_bias_grad[...],
        contract_bias_grad[...],
    ]
    a_v[:, 2 * chunk :, :] = jnp.zeros((shards, a_v.shape[1] - 2 * chunk, part_width), jnp.bfloat16)
    for shard in range(shards):
        rows = []
        for vector in vectors:
            size = vector.shape[1] // shards
            piece = vector[:, shard * size : (shard + 1) * size]
            rows.append(jnp.concatenate([piece, jnp.zeros((1, 256 - size), jnp.float32)], axis=1))
        rows.append(jnp.zeros((8, 256), jnp.float32))
        a_v[shard, 2 * chunk :, :256] = jnp.concatenate(rows, axis=0).astype(jnp.bfloat16)
    a_copies = shard_copies(me, a_v, a_keep, a_send, a_sem, MASKS_A)
    for copy in a_copies:
        copy.start()
    grad_v[...] = dafter_ref[...] + norm_back(normed, scale, first_gain[...], dh1)
    rows = own_ref.shape[0]
    grad_out[...] = grad_v[pl.ds(pl.multiple_of(blk * rows, rows), rows), :]
    for copy in a_copies + b_copies:
        copy.wait()


def project_back(place, own, other, dq, dk, dv, normed, dafter, gain, attend, vectors, wpi, shards):
    count, width = normed.shape
    rows = own.shape[0]
    chunk = width // shards
    low, full = jnp.bfloat16, jnp.float32
    a_half = jax.ShapeDtypeStruct((shards // 2, 2 * chunk + 16, width // 2), low)
    b_half = jax.ShapeDtypeStruct((shards // 2, 2 * chunk, width // 2), low)
    return pl.pallas_call(
        project_kernel,
        in_specs=[scalars()] + [whole_vmem()] * 14 + [in_place()],
        out_specs=[in_place()] * 4 + [whole_vmem()],
        out_shape=[a_half, a_half, b_half, b_half, jax.ShapeDtypeStruct((rows, width), full)],
        scratch_shapes=[
            pltpu.VMEM(wpi.shape, low),
            pltpu.VMEM((count, 3 * width), low),
            pltpu.VMEM((count, width), full),
            pltpu.VMEM((count, width), full),
            pltpu.VMEM((shards, 2 * chunk + 16, width // 2), low),
            pltpu.VMEM((shards, 2 * chunk, width // 2), low),
            pltpu.SemaphoreType.DMA((1,)),
            pltpu.SemaphoreType.DMA((shards,)),
            pltpu.SemaphoreType.DMA((shards,)),
        ],
        compiler_params=pltpu.CompilerParams(vmem_limit_bytes=VMEM_LIMIT),
        cost_estimate=pl.CostEstimate(
            flops=3_000_000_000, bytes_accessed=15_000_000, transcendentals=0
        ),
        name="project_back",
    )(place, own, other, dq, dk, dv, normed, dafter, gain, attend, *vectors, wpi)


def halving(keep, send, masks):
    devices = lax.axis_size("dp")
    for index, mask in enumerate(masks):
        received = lax.ppermute(send, "dp", [(i, i ^ mask) for i in range(devices)])
        half = keep.shape[0] // 2
        if half == 0:
            return (keep + received)[0]
        send = keep[half:] + received[half:]
        keep = keep[:half] + received[:half]
    return keep[0]


def swap(value):
    return lax.ppermute(value, "blk", [(0, 1), (1, 0)])


def both_halves(own, other, blk):
    return jnp.where(
        blk == 0,
        jnp.concatenate([own, other], axis=-1),
        jnp.concatenate([other, own], axis=-1),
    ).astype(jnp.float32)


def local_pair(hidden, doc_lengths, *arrays):
    student, teacher = arrays[:12], arrays[12:24]
    final_gain, final_shift, table = arrays[24:]
    rows, width = hidden.shape
    shards = lax.axis_size("dp")
    blk = lax.axis_index("blk")
    place = jnp.stack([lax.axis_index("dp"), blk]).astype(jnp.int32)
    other = swap(hidden)
    row = lambda vector: vector.reshape(1, -1)

    def block(train, params):
        gain, shift, wpi, qvb, wao, bao, gain_two, shift_two, we, be, wc, bc = params
        vectors = (gain, shift, qvb, bao, gain_two, shift_two, be, bc, final_gain, final_shift)
        return forward(
            train,
            place,
            doc_lengths,
            hidden,
            other,
            tuple(row(vector) for vector in vectors),
            (wpi, wao, we, wc),
        )

    (rows_t,) = block(False, teacher)
    rows_s, normed, joined, probs, mixed, after, normed_two, slope, active, y = block(True, student)
    diff, expo, stats, sums = logits_phase(rows_s, rows_t, table)
    grad_own, grad_low, divergence = gradient_phase(
        place, diff, expo, table, stats, sums, swap(sums)
    )
    grad_other = swap(grad_low)
    gain, shift, wpi, qvb, wao, bao, gain_two, shift_two, we, be, wc, bc = student
    cw_keep, cw_send, ew_keep, ew_send, dy, dinner, dbc, dbe = feed_back(
        place, grad_own, grad_other, y, normed_two, row(final_gain), wc, active, slope, shards
    )
    dafter, dmixed, attend, dgain_two, dshift_two, dbao = branch_back(
        place, dy, after, mixed, row(gain_two), dinner, we, wao, shards
    )
    dq, dk, dv = attend_back(joined, probs, dmixed, rows)
    a_keep, a_send, b_keep, b_send, input_grad = project_back(
        place,
        hidden,
        other,
        dq,
        dk,
        dv,
        normed,
        dafter,
        row(gain),
        attend,
        (dbao, dgain_two, dshift_two, dbe, dbc),
        wpi,
        shards,
    )
    cw = halving(cw_keep, cw_send, MASKS_A)
    ew = halving(ew_keep, ew_send, MASKS_B)
    a_sum = halving(a_keep, a_send, MASKS_A)
    b_sum = halving(b_keep, b_send, MASKS_B)
    chunk = width // shards
    first = jnp.concatenate([cw, ew], axis=0)
    second = jnp.concatenate([a_sum[: 2 * chunk], b_sum], axis=0)
    first_other, second_other = swap(first), swap(second)

    def wide(part):
        parts = part.reshape(-1, chunk, part.shape[1])
        return jnp.concatenate([parts[i] for i in range(parts.shape[0])], axis=1)

    tall = cw.shape[0]
    grad_cw = both_halves(cw, first_other[:tall], blk)
    grad_ew = both_halves(wide(ew), wide(first_other[tall:]), blk)
    grad_ao = both_halves(second[:chunk], second_other[:chunk], blk)
    grad_pi = both_halves(wide(second[chunk:]), wide(second_other[chunk:]), blk)
    vectors = a_sum[2 * chunk :].astype(jnp.float32)
    sizes = (chunk, chunk, 2 * chunk, chunk, chunk, chunk, be.shape[0] // shards, chunk)
    dgain, dshift, dqvb, dbao, dgain_two, dshift_two, dbe, dbc = (
        vectors[index, :size] for index, size in enumerate(sizes)
    )
    return (
        divergence[0],
        input_grad,
        dgain,
        dshift,
        grad_pi,
        dqvb,
        grad_ao,
        dbao,
        dgain_two,
        dshift_two,
        grad_ew,
        dbe,
        grad_cw,
        dbc,
    )


def solution(mesh):
    pair = mesh.shape["dp"] == 16 and mesh.shape["blk"] == 2
    return jax.shard_map(
        local_pair if pair else local_general,
        mesh=mesh,
        in_specs=(
            P(("dp", "blk"), None),
            P("dp", None),
            P(),
            P(),
            P(),
            P(),
            P(),
            P(),
            P(),
            P(),
            P(),
            P(),
            P(),
            P(),
            P(),
            P(),
            P(),
            P(),
            P(),
            P(),
            P(),
            P(),
            P(),
            P(),
            P(),
            P(),
            P(),
            P(),
            P("blk", None),
        ),
        out_specs=(
            P(("dp", "blk")),
            P(("dp", "blk"), None),
            P("dp"),
            P("dp"),
            P("dp", None),
            P("dp"),
            P("dp", None),
            P("dp"),
            P("dp"),
            P("dp"),
            P("dp", None),
            P("dp"),
            P("dp", None),
            P("dp"),
        ),
        check_vma=False,
    )
```

```python
import functools

import jax
import jax.numpy as jnp
from jax import lax
from jax.experimental import pallas as pl
from jax.experimental.pallas import tpu as pltpu
from jax.sharding import PartitionSpec as P

HEADS = 12
HEAD_DIM = 64
TABLE_SPAN = 2048
MASKS = (1, 2, 4, 8)
MASKS_B = (1, 4, 2, 8)


negative = -1e30


def layer_norm(value, gain, shift):
    centre = value - jnp.mean(value, axis=-1, keepdims=True)
    return (
        centre * lax.rsqrt(jnp.mean(centre * centre, axis=-1, keepdims=True) + 1e-05) * gain + shift
    )


def doc_numbers(lengths, count):
    ends = jnp.cumsum(lengths)
    places = jnp.arange(count, dtype=jnp.int32)
    return jnp.sum((places[:, None] >= ends[None, :]).astype(jnp.int32), axis=1)


def dense(left, right):
    return jnp.dot(left, right, preferred_element_type=jnp.float32)


def split_heads(value):
    return value.reshape(value.shape[0], HEADS, HEAD_DIM)


def input_side(inputs, gain, shift, project_in, qv_bias):
    width = inputs.shape[1]
    normed = layer_norm(inputs, gain, shift).astype(jnp.bfloat16)
    bias = jnp.concatenate([qv_bias[:width], jnp.zeros((width,), jnp.float32), qv_bias[width:]])
    joined = (dense(normed, project_in) + bias).astype(jnp.bfloat16)
    return (normed, joined[:, :width], joined[:, width : 2 * width], joined[:, 2 * width :])


def output_side(
    inputs,
    mixed_low,
    attend_out,
    attend_bias,
    second_gain,
    second_shift,
    expand_weight,
    expand_bias,
    contract_weight,
    contract_bias,
):
    after = inputs + dense(mixed_low, attend_out) + attend_bias
    normed = layer_norm(after, second_gain, second_shift).astype(jnp.bfloat16)
    inner = dense(normed, expand_weight) + expand_bias
    active = jax.nn.gelu(inner, approximate=True).astype(jnp.bfloat16)
    final = after + dense(active, contract_weight) + contract_bias
    return (after, normed, inner, active, final)


def online(state, query, keys, values, allowed):
    top, mass, summed = state
    scores = (
        jnp.einsum(
            "qhd,khd->hqk",
            split_heads(query),
            split_heads(keys),
            preferred_element_type=jnp.float32,
        )
        * 0.125
    )
    scores = jnp.where(allowed[None], scores, negative)
    new_top = jnp.maximum(top, jnp.max(scores, axis=-1))
    factor = jnp.exp(top - new_top)
    weights = jnp.where(allowed[None], jnp.exp(scores - new_top[..., None]), 0.0)
    mass = mass * factor + jnp.sum(weights, axis=-1)
    summed = summed * factor[..., None] + jnp.einsum(
        "hqk,khd->hqd",
        weights.astype(jnp.bfloat16),
        split_heads(values),
        preferred_element_type=jnp.float32,
    )
    return (new_top, mass, summed)


def score_grads(query_heads, grad_heads, log_norm, balance, key_block, value_block, allowed):
    scores = (
        jnp.einsum("qhd,khd->hqk", query_heads, key_block, preferred_element_type=jnp.float32)
        * 0.125
    )
    probs = jnp.where(allowed[None], jnp.exp(scores - log_norm[..., None]), 0.0)
    grad_probs = jnp.einsum(
        "qhd,khd->hqk", grad_heads, value_block, preferred_element_type=jnp.float32
    )
    grad_scores = (probs * (grad_probs - balance[..., None])).astype(jnp.bfloat16)
    return (probs, grad_scores)


def partial_stats(rows_teacher, rows_student, table):
    half_t = jnp.einsum("rd,vd->rv", rows_teacher, table, preferred_element_type=jnp.float32) * 0.5
    half_s = jnp.einsum("rd,vd->rv", rows_student, table, preferred_element_type=jnp.float32) * 0.5
    top_t = jnp.max(half_t, axis=-1)
    expo_t = jnp.exp(half_t - top_t[:, None])
    top_s = jnp.max(half_s, axis=-1)
    return (
        top_t,
        jnp.sum(expo_t, axis=-1),
        jnp.sum(expo_t * (half_t - half_s), axis=-1),
        top_s,
        jnp.sum(jnp.exp(half_s - top_s[:, None]), axis=-1),
    )


def combine(first_stats, second_stats):
    top_t = jnp.maximum(first_stats[0], second_stats[0])
    right_weight = jnp.exp(second_stats[0] - top_t)
    top_s = jnp.maximum(first_stats[3], second_stats[3])
    return (
        top_t,
        second_stats[1] * right_weight,
        second_stats[2] * right_weight,
        top_s,
        second_stats[4] * jnp.exp(second_stats[3] - top_s),
    )


def row_gradient(rows_teacher, rows_student, table, norm_t, norm_s):
    half_t = jnp.einsum("rd,vd->rv", rows_teacher, table, preferred_element_type=jnp.float32) * 0.5
    half_s = jnp.einsum("rd,vd->rv", rows_student, table, preferred_element_type=jnp.float32) * 0.5
    change = ((jnp.exp(half_s - norm_s[:, None]) - jnp.exp(half_t - norm_t[:, None])) * 0.5).astype(
        jnp.bfloat16
    )
    return dense(change, table)


def local_general(
    hidden,
    doc_lengths,
    student_first_gain,
    student_first_shift,
    student_project_in,
    student_query_value_bias,
    student_attend_out,
    student_attend_bias,
    student_second_gain,
    student_second_shift,
    student_expand_weight,
    student_expand_bias,
    student_contract_weight,
    student_contract_bias,
    teacher_first_gain,
    teacher_first_shift,
    teacher_project_in,
    teacher_query_value_bias,
    teacher_attend_out,
    teacher_attend_bias,
    teacher_second_gain,
    teacher_second_shift,
    teacher_expand_weight,
    teacher_expand_bias,
    teacher_contract_weight,
    teacher_contract_bias,
    final_gain,
    final_shift,
    embedding,
):
    rows, width = hidden.shape
    blocks = lax.axis_size("blk")
    stream = rows * blocks
    first = lax.axis_index("blk") * rows
    last_place = first + rows - 1
    docs = doc_numbers(doc_lengths[0], stream)
    own_places = first + jnp.arange(rows, dtype=jnp.int32)
    own_docs = lax.dynamic_slice_in_dim(docs, first, rows)
    inputs = hidden.astype(jnp.float32)
    normed_s, query_s, keys_s, values_s = input_side(
        inputs,
        student_first_gain,
        student_first_shift,
        student_project_in,
        student_query_value_bias,
    )
    normed_t, query_t, keys_t, values_t = input_side(
        inputs,
        teacher_first_gain,
        teacher_first_shift,
        teacher_project_in,
        teacher_query_value_bias,
    )

    def allowed_for(begin):
        key_places = begin + jnp.arange(rows, dtype=jnp.int32)
        key_docs = lax.dynamic_slice_in_dim(docs, begin, rows)
        return (key_places[None, :] <= own_places[:, None]) & (
            key_docs[None, :] == own_docs[:, None]
        )

    start_state = (
        jnp.full((HEADS, rows), negative, jnp.float32),
        jnp.zeros((HEADS, rows), jnp.float32),
        jnp.zeros((HEADS, rows, HEAD_DIM), jnp.float32),
    )
    carry = (start_state, start_state)
    pieces = (
        lax.all_gather(keys_s, "blk", axis=0, tiled=True),
        lax.all_gather(values_s, "blk", axis=0, tiled=True),
        lax.all_gather(keys_t, "blk", axis=0, tiled=True),
        lax.all_gather(values_t, "blk", axis=0, tiled=True),
    )
    count = pieces[0].shape[0]
    stacked = tuple((member.reshape(count // rows, rows, width) for member in pieces))
    begins = rows * jnp.arange(count // rows, dtype=jnp.int32)

    def step(state, item):
        piece_keys_s, piece_values_s, piece_keys_t, piece_values_t, begin = item

        def step_compute(inner_state):
            allowed = allowed_for(begin)
            return (
                online(inner_state[0], query_s, piece_keys_s, piece_values_s, allowed),
                online(inner_state[1], query_t, piece_keys_t, piece_values_t, allowed),
            )

        return (
            lax.cond(begin <= last_place, step_compute, lambda inner_state: inner_state, state),
            None,
        )

    carry, _ = lax.scan(step, carry, stacked + (begins,))
    state_s, state_t = carry
    out_heads_s = state_s[2] / state_s[1][..., None]
    attn_norm = state_s[0] + jnp.log(state_s[1])
    mixed_low_s = out_heads_s.transpose(1, 0, 2).reshape(rows, width).astype(jnp.bfloat16)
    mixed_low_t = (
        (state_t[2] / state_t[1][..., None])
        .transpose(1, 0, 2)
        .reshape(rows, width)
        .astype(jnp.bfloat16)
    )
    after_s, normed_two_s, inner_s, active_s, final_s = output_side(
        inputs,
        mixed_low_s,
        student_attend_out,
        student_attend_bias,
        student_second_gain,
        student_second_shift,
        student_expand_weight,
        student_expand_bias,
        student_contract_weight,
        student_contract_bias,
    )
    after_t, normed_two_t, inner_t, active_t, final_t = output_side(
        inputs,
        mixed_low_t,
        teacher_attend_out,
        teacher_attend_bias,
        teacher_second_gain,
        teacher_second_shift,
        teacher_expand_weight,
        teacher_expand_bias,
        teacher_contract_weight,
        teacher_contract_bias,
    )
    rows_s = layer_norm(final_s, final_gain, final_shift).astype(jnp.bfloat16)
    rows_t = layer_norm(final_t, final_gain, final_shift).astype(jnp.bfloat16)
    identity = (
        jnp.full((rows,), negative, jnp.float32),
        jnp.zeros((rows,), jnp.float32),
        jnp.zeros((rows,), jnp.float32),
        jnp.full((rows,), negative, jnp.float32),
        jnp.zeros((rows,), jnp.float32),
    )
    merged = combine(
        identity,
        partial_stats(rows_t, rows_s, lax.all_gather(embedding, "blk", axis=0, tiled=True)),
    )
    norm_t = merged[0] + jnp.log(merged[1])
    norm_s = merged[3] + jnp.log(merged[4])
    kl_rows = merged[2] / merged[1] - norm_t + norm_s
    grad_final = row_gradient(
        rows_t, rows_s, lax.all_gather(embedding, "blk", axis=0, tiled=True), norm_t, norm_s
    )
    _, final_back = jax.vjp(layer_norm, final_s, final_gain, final_shift)
    grad_y = final_back(grad_final)[0]
    grad_m = grad_y.astype(jnp.bfloat16)
    grad_contract_weight = jnp.einsum(
        "rf,rd->fd", active_s, grad_m, preferred_element_type=jnp.float32
    )
    grad_contract_bias = jnp.sum(grad_m.astype(jnp.float32), axis=0)
    grad_active = jnp.einsum(
        "rd,fd->rf", grad_m, student_contract_weight, preferred_element_type=jnp.float32
    )
    _, gelu_back = jax.vjp(lambda value: jax.nn.gelu(value, approximate=True), inner_s)
    grad_inner = gelu_back(grad_active)[0].astype(jnp.bfloat16)
    grad_expand_weight = jnp.einsum(
        "rd,rf->df", normed_two_s, grad_inner, preferred_element_type=jnp.float32
    )
    grad_expand_bias = jnp.sum(grad_inner.astype(jnp.float32), axis=0)
    grad_normed_two = jnp.einsum(
        "rf,df->rd", grad_inner, student_expand_weight, preferred_element_type=jnp.float32
    )
    _, second_back = jax.vjp(layer_norm, after_s, student_second_gain, student_second_shift)
    grad_after_norm, grad_second_gain, grad_second_shift = second_back(grad_normed_two)
    grad_after = grad_y + grad_after_norm
    grad_branch = grad_after.astype(jnp.bfloat16)
    grad_attend_out = jnp.einsum(
        "rc,rd->cd", mixed_low_s, grad_branch, preferred_element_type=jnp.float32
    )
    grad_attend_bias = jnp.sum(grad_branch.astype(jnp.float32), axis=0)
    grad_mixed = jnp.einsum(
        "rd,cd->rc", grad_branch, student_attend_out, preferred_element_type=jnp.float32
    ).astype(jnp.bfloat16)
    keys_all, values_all = (
        lax.all_gather(keys_s, "blk", axis=0, tiled=True),
        lax.all_gather(values_s, "blk", axis=0, tiled=True),
    )
    grad_heads = split_heads(grad_mixed)
    query_heads = split_heads(query_s)
    balance = jnp.sum(grad_heads.astype(jnp.float32).transpose(1, 0, 2) * out_heads_s, axis=-1)
    begins = rows * jnp.arange(blocks, dtype=jnp.int32)
    zero_query = jnp.zeros((rows, HEADS, HEAD_DIM), jnp.float32)

    def back_step(grad_query, begin):
        key_block = split_heads(lax.dynamic_slice_in_dim(keys_all, begin, rows, 0))
        value_block = split_heads(lax.dynamic_slice_in_dim(values_all, begin, rows, 0))

        def back_compute(total):
            probs, grad_scores = score_grads(
                query_heads,
                grad_heads,
                attn_norm,
                balance,
                key_block,
                value_block,
                allowed_for(begin),
            )
            total = (
                total
                + jnp.einsum(
                    "hqk,khd->qhd", grad_scores, key_block, preferred_element_type=jnp.float32
                )
                * 0.125
            )
            grad_keys = (
                jnp.einsum(
                    "hqk,qhd->khd", grad_scores, query_heads, preferred_element_type=jnp.float32
                )
                * 0.125
            )
            grad_values = jnp.einsum(
                "hqk,qhd->khd",
                probs.astype(jnp.bfloat16),
                grad_heads,
                preferred_element_type=jnp.float32,
            )
            return (
                total,
                jnp.concatenate(
                    [grad_keys.reshape(rows, width), grad_values.reshape(rows, width)], axis=1
                ),
            )

        def skip(total):
            return (total, jnp.zeros((rows, 2 * width), jnp.float32))

        return lax.cond(begin <= last_place, back_compute, skip, grad_query)

    grad_query, key_terms = lax.scan(back_step, zero_query, begins)
    key_value_grad = lax.psum_scatter(
        key_terms.reshape(stream, 2 * width).astype(jnp.bfloat16),
        "blk",
        scatter_dimension=0,
        tiled=True,
    ).astype(jnp.float32)
    grad_keys_low = key_value_grad[:, :width].astype(jnp.bfloat16)
    grad_values_low = key_value_grad[:, width:].astype(jnp.bfloat16)
    grad_query_low = grad_query.reshape(rows, width).astype(jnp.bfloat16)
    grad_joined = jnp.concatenate([grad_query_low, grad_keys_low, grad_values_low], axis=1)
    grad_project_in = jnp.einsum(
        "rd,rc->dc", normed_s, grad_joined, preferred_element_type=jnp.float32
    )
    grad_query_value_bias = jnp.concatenate(
        [
            jnp.sum(grad_query_low.astype(jnp.float32), axis=0),
            jnp.sum(grad_values_low.astype(jnp.float32), axis=0),
        ]
    )
    grad_normed = jnp.einsum(
        "rc,dc->rd", grad_joined, student_project_in, preferred_element_type=jnp.float32
    )
    _, first_back = jax.vjp(layer_norm, inputs, student_first_gain, student_first_shift)
    grad_inputs_norm, grad_first_gain, grad_first_shift = first_back(grad_normed)
    input_grad = grad_after + grad_inputs_norm
    shares = (
        lax.psum_scatter(
            grad_first_gain.astype(jnp.bfloat16), "dp", scatter_dimension=0, tiled=True
        ).astype(jnp.float32),
        lax.psum_scatter(
            grad_first_shift.astype(jnp.bfloat16), "dp", scatter_dimension=0, tiled=True
        ).astype(jnp.float32),
        lax.psum_scatter(
            grad_project_in.astype(jnp.bfloat16), "dp", scatter_dimension=0, tiled=True
        ).astype(jnp.float32),
        lax.psum_scatter(
            grad_query_value_bias.astype(jnp.bfloat16), "dp", scatter_dimension=0, tiled=True
        ).astype(jnp.float32),
        lax.psum_scatter(
            grad_attend_out.astype(jnp.bfloat16), "dp", scatter_dimension=0, tiled=True
        ).astype(jnp.float32),
        lax.psum_scatter(
            grad_attend_bias.astype(jnp.bfloat16), "dp", scatter_dimension=0, tiled=True
        ).astype(jnp.float32),
        lax.psum_scatter(
            grad_second_gain.astype(jnp.bfloat16), "dp", scatter_dimension=0, tiled=True
        ).astype(jnp.float32),
        lax.psum_scatter(
            grad_second_shift.astype(jnp.bfloat16), "dp", scatter_dimension=0, tiled=True
        ).astype(jnp.float32),
        lax.psum_scatter(
            grad_expand_weight.astype(jnp.bfloat16), "dp", scatter_dimension=0, tiled=True
        ).astype(jnp.float32),
        lax.psum_scatter(
            grad_expand_bias.astype(jnp.bfloat16), "dp", scatter_dimension=0, tiled=True
        ).astype(jnp.float32),
        lax.psum_scatter(
            grad_contract_weight.astype(jnp.bfloat16), "dp", scatter_dimension=0, tiled=True
        ).astype(jnp.float32),
        lax.psum_scatter(
            grad_contract_bias.astype(jnp.bfloat16), "dp", scatter_dimension=0, tiled=True
        ).astype(jnp.float32),
    )
    summed = (
        lax.psum(shares[0].astype(jnp.bfloat16), "blk").astype(jnp.float32),
        lax.psum(shares[1].astype(jnp.bfloat16), "blk").astype(jnp.float32),
        lax.psum(shares[2].astype(jnp.bfloat16), "blk").astype(jnp.float32),
        lax.psum(shares[3].astype(jnp.bfloat16), "blk").astype(jnp.float32),
        lax.psum(shares[4].astype(jnp.bfloat16), "blk").astype(jnp.float32),
        lax.psum(shares[5].astype(jnp.bfloat16), "blk").astype(jnp.float32),
        lax.psum(shares[6].astype(jnp.bfloat16), "blk").astype(jnp.float32),
        lax.psum(shares[7].astype(jnp.bfloat16), "blk").astype(jnp.float32),
        lax.psum(shares[8].astype(jnp.bfloat16), "blk").astype(jnp.float32),
        lax.psum(shares[9].astype(jnp.bfloat16), "blk").astype(jnp.float32),
        lax.psum(shares[10].astype(jnp.bfloat16), "blk").astype(jnp.float32),
        lax.psum(shares[11].astype(jnp.bfloat16), "blk").astype(jnp.float32),
    )
    return (
        kl_rows,
        input_grad,
        summed[0],
        summed[1],
        summed[2],
        summed[3],
        summed[4],
        summed[5],
        summed[6],
        summed[7],
        summed[8],
        summed[9],
        summed[10],
        summed[11],
    )


def nt(left, right):
    return lax.dot_general(
        left, right, (((1,), (1,)), ((), ())), preferred_element_type=jnp.float32
    )


def tn(left, right):
    return lax.dot_general(
        left, right, (((0,), (0,)), ((), ())), preferred_element_type=jnp.float32
    )


def normalise(value):
    centre = value - jnp.mean(value, axis=-1, keepdims=True)
    scale = lax.rsqrt(jnp.mean(centre * centre, axis=-1, keepdims=True) + 1e-05)
    return (centre * scale, scale)


def norm_back(normed, scale, gain, grad):
    weighted = grad * gain
    return scale * (
        weighted
        - jnp.mean(weighted, axis=-1, keepdims=True)
        - normed * jnp.mean(weighted * normed, axis=-1, keepdims=True)
    )


def starts_of(lengths_ref, count):
    places = lax.broadcasted_iota(jnp.int32, (1, count), 1)
    start = jnp.zeros((1, count), jnp.int32)
    end = jnp.int32(0)
    for index in range(lengths_ref.shape[1]):
        end = end + lengths_ref[0, index]
        start = jnp.where(places >= end, jnp.maximum(start, end), start)
    return start


def in_stream_order(target, own_ref, other_ref, blk):
    rows = own_ref.shape[0]
    target[pl.ds(pl.multiple_of(blk * rows, rows), rows), :] = own_ref[...].astype(target.dtype)
    target[pl.ds(pl.multiple_of((1 - blk) * rows, rows), rows), :] = other_ref[...].astype(
        target.dtype
    )


def head_mask(shape, which):
    lanes = lax.broadcasted_iota(jnp.int32, shape, 1)
    return (lanes >= HEAD_DIM) if which else (lanes < HEAD_DIM)


def forward_kernel(train, *refs):
    (
        place_ref,
        lengths_ref,
        own_ref,
        other_ref,
    ) = refs[:4]
    (
        first_gain,
        first_shift,
        qv_bias,
        attend_bias,
        second_gain,
        second_shift,
        expand_bias,
        contract_bias,
        final_gain,
        final_shift,
    ) = (as_row(ref) for ref in refs[4:14])
    weights_hbm = refs[14:18]
    rest = refs[18:]
    if train:
        rows_out, kept_hbm, rest = rest[0], rest[1:10], rest[10:]
    else:
        rows_out, kept_hbm, rest = rest[0], (), rest[1:]
    wpi, wao, we, wc = rest[:4]
    normed_v, joined_v, probs_v, mixed_v, after_v, normed_two_v, slope_v, active_v, y_v = rest[4:13]
    x_v, bias_v, weight_sem, out_sem, probs_sem = rest[13:]
    kept = (normed_v, joined_v, probs_v, mixed_v, after_v, normed_two_v, slope_v, active_v, y_v)
    loads = [
        pltpu.make_async_copy(source, target, weight_sem.at[index])
        for index, (source, target) in enumerate(zip(weights_hbm, (wpi, wao, we, wc)))
    ]
    stores = []

    def save(index, *at):
        if train:
            source, target = kept[index], kept_hbm[index]
            if at:
                source, target = source.at[at], target.at[at]
            store = pltpu.make_async_copy(source, target, out_sem.at[len(stores)])
            store.start()
            stores.append(store)

    for load in loads:
        load.start()
    blk = place_ref[1]
    in_stream_order(x_v, own_ref, other_ref, blk)
    count, width = x_v.shape
    block = own_ref.shape[0]
    normed, _ = normalise(x_v[...])
    normed_v[...] = (normed * first_gain + first_shift).astype(jnp.bfloat16)
    save(0)
    start = starts_of(lengths_ref, count)
    keys_at = lax.broadcasted_iota(jnp.int32, (count, count), 0)
    queries_at = lax.broadcasted_iota(jnp.int32, (count, count), 1)
    bias_v[...] = jnp.where((keys_at <= queries_at) & (keys_at >= start), 0.0, negative)
    loads[0].wait()
    for part in range(3):
        span = slice(part * width, (part + 1) * width)
        value = dense(normed_v[...], wpi[:, span])
        if part == 0:
            value = value + qv_bias[:, :width]
        if part == 2:
            value = value + qv_bias[:, width:]
        joined_v[:, span] = value.astype(jnp.bfloat16)
    save(1)
    pair = 2 * HEAD_DIM
    pairs = width // pair

    def attend(index, _):
        column = pl.ds(pl.multiple_of(index * pair, pair), pair)
        query = joined_v[:, column] * jnp.bfloat16(0.125)
        keys = joined_v[:, pl.ds(pl.multiple_of(width + index * pair, pair), pair)]
        values = joined_v[:, pl.ds(pl.multiple_of(2 * width + index * pair, pair), pair)]
        for piece in range(count // block):
            span = slice(piece * block, (piece + 1) * block)
            reach = (piece + 1) * block
            both = []
            for which in range(2):
                mine = jnp.where(
                    head_mask((block, pair), which), query[span], jnp.bfloat16(0.0)
                )
                scores = nt(keys[:reach], mine) + bias_v[:reach, span]
                expo = jnp.exp(scores - jnp.max(scores, axis=0, keepdims=True))
                probs = expo * (1.0 / jnp.sum(expo, axis=0, keepdims=True))
                probs = probs.astype(jnp.bfloat16)
                if train:
                    probs_v[2 * index + which, :reach, span] = probs
                both.append(tn(probs, values[:reach]))
            mixed_v[span, column] = jnp.where(
                head_mask((block, pair), 0), both[0], both[1]
            ).astype(jnp.bfloat16)
        if train:
            heads = pl.ds(2 * index, 2)
            pltpu.make_async_copy(
                probs_v.at[heads], kept_hbm[2].at[heads], probs_sem.at[index]
            ).start()
        return 0

    lax.fori_loop(0, pairs, attend, 0, unroll=3)
    if train:
        for index in range(pairs):
            heads = pl.ds(2 * index, 2)
            stores.append(
                pltpu.make_async_copy(
                    probs_v.at[heads], kept_hbm[2].at[heads], probs_sem.at[index]
                )
            )
    save(3)
    loads[1].wait()
    after_v[...] = x_v[...] + dense(mixed_v[...], wao[...]) + attend_bias
    save(4)
    normed, _ = normalise(after_v[...])
    normed_two_v[...] = (normed * second_gain + second_shift).astype(jnp.bfloat16)
    save(5)
    loads[2].wait()
    loads[3].wait()
    hidden_width = we.shape[1]
    total = after_v[...] + contract_bias
    root = 0.7978845608028654
    for part in range(hidden_width // width):
        span = slice(part * width, (part + 1) * width)
        inner = dense(normed_two_v[...], we[:, span]) + expand_bias[:, span]
        square = inner * inner
        bent = jnp.tanh(root * (inner + 0.044715 * (square * inner)))
        upper = 0.5 * (1.0 + bent)
        active = (inner * upper).astype(jnp.bfloat16)
        if train:
            active_v[:, span] = active
            slope_v[:, span] = (
                upper
                + (0.5 * root) * inner * (1.0 - bent * bent) * (1.0 + (3 * 0.044715) * square)
            ).astype(jnp.bfloat16)
            save(6, slice(None), pl.ds(part * width, width))
            save(7, slice(None), pl.ds(part * width, width))
        total = total + dense(active, wc[span, :])
    if train:
        y_v[...] = total
    save(8)
    normed, _ = normalise(total)
    rows_out[...] = (normed * final_gain + final_shift).astype(jnp.bfloat16) * jnp.bfloat16(0.5)
    if train:
        for store in stores:
            store.wait()


def carrying(kernel, inputs, outputs, carried):
    def body(*refs):
        rest = refs[inputs + carried :]
        kernel(*refs[:inputs], *rest[:outputs], *rest[outputs + carried :])

    return body


def shapes_of(carry):
    return [jax.ShapeDtypeStruct(item.shape, item.dtype) for item in carry]


def aliases(inputs, outputs, carry):
    return {inputs + index: outputs + index for index in range(len(carry))}


def as_row(ref):
    return ref[...].reshape(1, ref.shape[0])


def whole_vmem():
    return pl.BlockSpec(memory_space=pltpu.VMEM)


def in_place():
    return pl.BlockSpec(memory_space=pl.ANY)


def scalars():
    return pl.BlockSpec(memory_space=pltpu.SMEM)


def forward(train, place, lengths, own, other, vectors, weights):
    rows, width = own.shape
    count = 2 * rows
    hidden_width = weights[2].shape[1]
    low, full = jnp.bfloat16, jnp.float32
    kept = [
        ((count, width), low),
        ((count, 3 * width), low),
        ((HEADS, count, count), low),
        ((count, width), low),
        ((count, width), full),
        ((count, width), low),
        ((count, hidden_width), low),
        ((count, hidden_width), low),
        ((count, width), full),
    ]
    small = ((8, 128), low)
    scratch = [kept[0], kept[1], kept[2] if train else ((1, 8, 128), low), kept[3], kept[4], kept[5]]
    scratch += [kept[6], kept[7], kept[8]] if train else [small, small, ((8, 128), full)]
    out_shape = [jax.ShapeDtypeStruct((count, width), low)]
    out_specs = [whole_vmem()]
    if train:
        out_shape += [jax.ShapeDtypeStruct(*item) for item in kept]
        out_specs += [in_place()] * len(kept)
    return pl.pallas_call(
        functools.partial(forward_kernel, train),
        in_specs=[scalars(), scalars()] + [whole_vmem()] * 12 + [in_place()] * 4,
        out_specs=out_specs,
        out_shape=out_shape,
        scratch_shapes=[pltpu.VMEM(item.shape, low) for item in weights]
        + [pltpu.VMEM(*item) for item in scratch]
        + [
            pltpu.VMEM((count, width), full),
            pltpu.VMEM((count, count), full),
            pltpu.SemaphoreType.DMA((4,)),
            pltpu.SemaphoreType.DMA((32,)),
            pltpu.SemaphoreType.DMA((HEADS // 2,)),
        ],
        compiler_params=pltpu.CompilerParams(vmem_limit_bytes=(58 if train else 60) << 20),
        cost_estimate=pl.CostEstimate(
            flops=8_000_000_000, bytes_accessed=20_000_000, transcendentals=0
        ),
        name="forward_student" if train else "forward_teacher",
    )(place, lengths, own, other, *vectors, *weights)


def logits_kernel(student_ref, teacher_ref, table_ref, diff_ref, expo_ref, stats_ref, sums_ref):
    count = student_ref.shape[0]
    span = table_ref.shape[0] // 8
    lanes = lax.broadcasted_iota(jnp.int32, (count, 128), 1)
    packed = jnp.zeros((count, 128), jnp.float32)
    for part in range(8):
        where = slice(part * span, (part + 1) * span)
        table = table_ref[where, :]
        half_s = nt(student_ref[...], table)
        top_s = jnp.max(half_s, axis=1, keepdims=True)
        expo_s = jnp.exp(half_s - top_s)
        mass_s = jnp.sum(expo_s, axis=1, keepdims=True)
        half_t = nt(teacher_ref[...], table)
        top_t = jnp.max(half_t, axis=1, keepdims=True)
        expo_t = jnp.exp(half_t - top_t)
        mass_t = jnp.sum(expo_t, axis=1, keepdims=True)
        cross = jnp.sum(expo_t * (half_t - half_s), axis=1, keepdims=True)
        diff_ref[:, where] = (expo_s * (mass_t / mass_s) - expo_t).astype(jnp.bfloat16)
        expo_ref[:, where] = expo_t.astype(jnp.bfloat16)
        for index, column in enumerate((top_s, mass_s, top_t, mass_t, cross)):
            packed = jnp.where(lanes == 8 * index + part, column, packed)
    stats = packed.T
    stats_ref[0] = stats[:40]
    top_s, mass_s, top_t, mass_t, cross = (stats[8 * i : 8 * i + 8] for i in range(5))

    @pl.when(pl.program_id(0) == 0)
    def _():
        row = lax.broadcasted_iota(jnp.int32, sums_ref.shape, 0)
        sums_ref[...] = jnp.where((row == 0) | (row == 2), negative, 0.0)

    old = sums_ref[...]
    new_s = jnp.maximum(old[0:1], jnp.max(top_s, axis=0, keepdims=True))
    new_t = jnp.maximum(old[2:3], jnp.max(top_t, axis=0, keepdims=True))
    keep_s = jnp.exp(old[0:1] - new_s)
    keep_t = jnp.exp(old[2:3] - new_t)
    scale_s = jnp.exp(top_s - new_s)
    scale_t = jnp.exp(top_t - new_t)
    sums_ref[0:1] = new_s
    sums_ref[1:2] = old[1:2] * keep_s + jnp.sum(mass_s * scale_s, axis=0, keepdims=True)
    sums_ref[2:3] = new_t
    sums_ref[3:4] = old[3:4] * keep_t + jnp.sum(mass_t * scale_t, axis=0, keepdims=True)
    sums_ref[4:5] = old[4:5] * keep_t + jnp.sum(cross * scale_t, axis=0, keepdims=True)


def logits_phase(student, teacher, table):
    count, width = student.shape
    entries = table.shape[0]
    span = TABLE_SPAN
    steps = entries // span
    rows = pl.BlockSpec((count, width), lambda j: (0, 0))
    wide = pl.BlockSpec((count, span), lambda j: (0, j))
    return pl.pallas_call(
        logits_kernel,
        grid=(steps,),
        in_specs=[rows, rows, pl.BlockSpec((span, width), lambda j: (j, 0))],
        out_specs=[
            wide,
            wide,
            pl.BlockSpec((1, 40, count), lambda j: (j, 0, 0)),
            pl.BlockSpec((8, count), lambda j: (0, 0)),
        ],
        out_shape=[
            jax.ShapeDtypeStruct((count, entries), jnp.bfloat16),
            jax.ShapeDtypeStruct((count, entries), jnp.bfloat16),
            jax.ShapeDtypeStruct((steps, 40, count), jnp.float32),
            jax.ShapeDtypeStruct((8, count), jnp.float32),
        ],
        compiler_params=pltpu.CompilerParams(vmem_limit_bytes=40 << 20),
        cost_estimate=pl.CostEstimate(
            flops=4 * count * width * entries, bytes_accessed=60_000_000, transcendentals=0
        ),
        name="logits_phase",
    )(student, teacher, table)


def joined_norms(own, other):
    top_s = jnp.maximum(own[0:1], other[0:1])
    top_t = jnp.maximum(own[2:3], other[2:3])
    own_t, other_t = jnp.exp(own[2:3] - top_t), jnp.exp(other[2:3] - top_t)
    mass_s = own[1:2] * jnp.exp(own[0:1] - top_s) + other[1:2] * jnp.exp(other[0:1] - top_s)
    mass_t = own[3:4] * own_t + other[3:4] * other_t
    cross = own[4:5] * own_t + other[4:5] * other_t
    norm_s = top_s + jnp.log(mass_s)
    norm_t = top_t + jnp.log(mass_t)
    return (norm_s, norm_t, cross / mass_t - norm_t + norm_s)


def gradient_kernel(
    place_ref,
    diff_ref,
    expo_ref,
    table_ref,
    stats_ref,
    own_ref,
    other_ref,
    total_ref,
    low_ref,
    kl_ref,
    norms,
):
    step = pl.program_id(0)
    count = diff_ref.shape[0]

    @pl.when(step == 0)
    def _():
        norm_s, norm_t, divergence = joined_norms(own_ref[...], other_ref[...])
        norms[0:1] = norm_s
        norms[1:2] = norm_t
        norms[2:3] = divergence
        rows = kl_ref.shape[1]
        kl_ref[0:1] = norms[2:3, pl.ds(pl.multiple_of(place_ref[1] * rows, rows), rows)]
        total_ref[...] = jnp.zeros_like(total_ref)

    top_s, mass_s, top_t, mass_t = (stats_ref[0, 8 * i : 8 * i + 8] for i in range(4))
    first = 0.5 * jnp.exp(top_s - norms[0:1]) * mass_s / mass_t
    second = first - 0.5 * jnp.exp(top_t - norms[1:2])
    factors = jnp.concatenate([first, second, jnp.zeros((112, count), jnp.float32)], axis=0).T
    span = table_ref.shape[0] // 8
    total = total_ref[...]
    for group in range(2):
        pieces = []
        for part in range(4 * group, 4 * group + 4):
            where = slice(part * span, (part + 1) * span)
            pieces.append(
                (
                    diff_ref[:, where].astype(jnp.float32) * factors[:, part : part + 1]
                    + expo_ref[:, where].astype(jnp.float32) * factors[:, 8 + part : 9 + part]
                ).astype(jnp.bfloat16)
            )
        where = slice(4 * group * span, 4 * (group + 1) * span)
        total = total + dense(jnp.concatenate(pieces, axis=1), table_ref[where, :])
    total_ref[...] = total

    @pl.when(step == pl.num_programs(0) - 1)
    def _():
        low_ref[...] = total_ref[...].astype(jnp.bfloat16)


def gradient_phase(place, diff, expo, table, stats, own, other):
    count, entries = diff.shape
    width = table.shape[1]
    span = TABLE_SPAN
    wide = pl.BlockSpec((count, span), lambda j: (0, j))
    sums = pl.BlockSpec((8, count), lambda j: (0, 0))
    fixed = pl.BlockSpec((count, width), lambda j: (0, 0))
    return pl.pallas_call(
        gradient_kernel,
        grid=(entries // span,),
        in_specs=[
            scalars(),
            wide,
            wide,
            pl.BlockSpec((span, width), lambda j: (j, 0)),
            pl.BlockSpec((1, 40, count), lambda j: (j, 0, 0)),
            sums,
            sums,
        ],
        out_specs=[fixed, fixed, pl.BlockSpec((1, count // 2), lambda j: (0, 0))],
        out_shape=[
            jax.ShapeDtypeStruct((count, width), jnp.float32),
            jax.ShapeDtypeStruct((count, width), jnp.bfloat16),
            jax.ShapeDtypeStruct((1, count // 2), jnp.float32),
        ],
        scratch_shapes=[pltpu.VMEM((8, count), jnp.float32)],
        compiler_params=pltpu.CompilerParams(vmem_limit_bytes=36 << 20),
        cost_estimate=pl.CostEstimate(
            flops=2 * count * width * entries, bytes_accessed=60_000_000, transcendentals=0
        ),
        name="gradient_phase",
    )(place, diff, expo, table, stats, own, other)


def position(device, masks):
    rest = masks[1:]
    place = jnp.int32(0) if not isinstance(device, int) else 0
    for index, mask in enumerate(rest):
        if isinstance(device, int):
            bit = (device // mask) % 2
        else:
            bit = lax.rem(lax.div(device, mask), 2)
        place = place + (bit << (len(rest) - 1 - index))
    return place


def shard_copies(me, natural, keep, send, sems, masks, first, shards, rows=None):
    mine = lax.rem(me, 2)
    place = position(me, masks)
    copies = []
    for pair in range(first // 2, (first + shards) // 2):
        target = lax.bitwise_xor(place, jnp.int32(position(2 * pair, masks)))
        for side, array in ((mine, keep), (1 - mine, send)):
            source = natural.at[2 * pair + side]
            target_ref = array.at[target]
            if rows is not None:
                source = source.at[rows]
                target_ref = target_ref.at[rows]
            copies.append(pltpu.make_async_copy(source, target_ref, sems.at[len(copies)]))
    return copies


def contract_kernel(
    place_ref,
    own_ref,
    other_ref,
    y_ref,
    final_gain,
    active_hbm,
    keep,
    send,
    dy_out,
    dm_out,
    bias_out,
    active_v,
    natural,
    load_sem,
    copy_sem,
):
    me, blk = place_ref[0], place_ref[1]
    load = pltpu.make_async_copy(active_hbm, active_v, load_sem.at[0])
    load.start()
    width = y_ref.shape[1]
    part_width = width // 2
    hidden_width = active_v.shape[1]
    shards = natural.shape[0]
    normed, scale = normalise(y_ref[...])
    grad = own_ref[...] + other_ref[...].astype(jnp.float32)
    dy = norm_back(normed, scale, as_row(final_gain), grad)
    dy_out[...] = dy
    dm = dy.astype(jnp.bfloat16)
    dm_out[...] = dm
    bias_out[...] = jnp.sum(dm.astype(jnp.float32), axis=0, keepdims=True)
    dm_half = dm_out[:, pl.ds(pl.multiple_of(blk * part_width, part_width), part_width)]
    load.wait()
    group = shards * width // hidden_width
    copies = []
    for part in range(hidden_width // width):
        span = slice(part * width, (part + 1) * width)
        value = tn(active_v[:, span], dm_half).astype(jnp.bfloat16)
        natural[part * group : (part + 1) * group] = value.reshape(
            group, width // group, part_width
        )
        ready = shard_copies(
            me, natural, keep, send, copy_sem.at[part], MASKS, part * group, group
        )
        for copy in ready:
            copy.start()
        copies += ready
    for copy in copies:
        copy.wait()


def contract_back(place, own, other, y, final_gain, active, shards):
    count, width = y.shape
    hidden_width = active.shape[1]
    low, full = jnp.bfloat16, jnp.float32
    rows = hidden_width // shards
    half = jax.ShapeDtypeStruct((shards // 2, rows, width // 2), low)
    return pl.pallas_call(
        contract_kernel,
        in_specs=[scalars()] + [whole_vmem()] * 4 + [in_place()],
        out_specs=[in_place()] * 2 + [whole_vmem()] * 3,
        out_shape=[
            half,
            half,
            jax.ShapeDtypeStruct((count, width), full),
            jax.ShapeDtypeStruct((count, width), low),
            jax.ShapeDtypeStruct((1, width), full),
        ],
        scratch_shapes=[
            pltpu.VMEM((count, hidden_width), low),
            pltpu.VMEM((shards, rows, width // 2), low),
            pltpu.SemaphoreType.DMA((1,)),
            pltpu.SemaphoreType.DMA((hidden_width // width, shards * width // hidden_width)),
        ],
        compiler_params=pltpu.CompilerParams(vmem_limit_bytes=26 << 20),
        cost_estimate=pl.CostEstimate(
            flops=12_000_000_000, bytes_accessed=1_000_000, transcendentals=0
        ),
        name="contract_back",
    )(place, own, other, y, final_gain, active)


def expand_kernel(
    place_ref,
    dm_ref,
    normed_two_ref,
    wc_hbm,
    slope_hbm,
    keep,
    send,
    dinner_hbm,
    bias_out,
    wc,
    slope_v,
    dinner_v,
    natural,
    load_sem,
    copy_sem,
    out_sem,
):
    me, blk = place_ref[0], place_ref[1]
    hidden_width, width = wc.shape
    parts = hidden_width // width
    loads = []
    for part in range(parts):
        span = pl.ds(part * width, width)
        loads.append(
            (
                pltpu.make_async_copy(wc_hbm.at[span], wc.at[span], load_sem.at[2 * part]),
                pltpu.make_async_copy(
                    slope_hbm.at[:, span], slope_v.at[:, span], load_sem.at[2 * part + 1]
                ),
            )
        )
    for pair in loads:
        for load in pair:
            load.start()
    part_width = width // 2
    shards = natural.shape[0]
    for part in range(parts):
        span = slice(part * width, (part + 1) * width)
        for load in loads[part]:
            load.wait()
        dact = nt(dm_ref[...], wc[span, :])
        dinner = (dact * slope_v[:, span].astype(jnp.float32)).astype(jnp.bfloat16)
        dinner_v[:, span] = dinner
        bias_out[:, span] = jnp.sum(dinner.astype(jnp.float32), axis=0, keepdims=True)
    save = pltpu.make_async_copy(dinner_v, dinner_hbm, out_sem.at[0])
    save.start()
    chunk = width // shards
    copies = []
    for part in range(parts // 2):
        offset = pl.multiple_of(blk * (hidden_width // 2), width) + part * width
        value = tn(normed_two_ref[...], dinner_v[:, pl.ds(pl.multiple_of(offset, width), width)])
        value = value.astype(jnp.bfloat16)
        for half in range(2):
            row = (2 * part + half) * chunk
            natural[:, row : row + chunk, :] = value[
                :, half * part_width : (half + 1) * part_width
            ].reshape(shards, chunk, part_width)
        rows = pl.ds(2 * part * chunk, 2 * chunk)
        ready = shard_copies(me, natural, keep, send, copy_sem.at[part], MASKS_B, 0, shards, rows)
        for copy in ready:
            copy.start()
        copies += ready
    for copy in copies + [save]:
        copy.wait()


def expand_back(place, dm, normed_two, wc, slope, shards):
    count, width = dm.shape
    hidden_width = wc.shape[0]
    low, full = jnp.bfloat16, jnp.float32
    rows = hidden_width // shards
    half = jax.ShapeDtypeStruct((shards // 2, rows, width // 2), low)
    return pl.pallas_call(
        expand_kernel,
        in_specs=[scalars()] + [whole_vmem()] * 2 + [in_place()] * 2,
        out_specs=[in_place()] * 3 + [whole_vmem()],
        out_shape=[
            half,
            half,
            jax.ShapeDtypeStruct((count, hidden_width), low),
            jax.ShapeDtypeStruct((1, hidden_width), full),
        ],
        scratch_shapes=[
            pltpu.VMEM(wc.shape, low),
            pltpu.VMEM((count, hidden_width), low),
            pltpu.VMEM((count, hidden_width), low),
            pltpu.VMEM((shards, rows, width // 2), low),
            pltpu.SemaphoreType.DMA((2 * hidden_width // width,)),
            pltpu.SemaphoreType.DMA((hidden_width // width // 2, shards)),
            pltpu.SemaphoreType.DMA((1,)),
        ],
        compiler_params=pltpu.CompilerParams(vmem_limit_bytes=44 << 20),
        cost_estimate=pl.CostEstimate(
            flops=12_000_000_000, bytes_accessed=1_000_000, transcendentals=0
        ),
        name="expand_back",
    )(place, dm, normed_two, wc, slope)


def branch_kernel(
    place_ref,
    dy_ref,
    after_ref,
    mixed_ref,
    second_gain,
    dinner_hbm,
    we_hbm,
    wao_hbm,
    dafter_out,
    dmixed_out,
    attend_out,
    second_gain_out,
    second_shift_out,
    attend_bias_out,
    dinner_v,
    we,
    wao,
    dbranch_v,
    load_sem,
):
    blk = place_ref[1]
    width = after_ref.shape[1]
    part_width = width // 2
    loads = []
    for part in range(we.shape[1] // width):
        span = pl.ds(part * width, width)
        loads.append(
            [
                pltpu.make_async_copy(
                    source.at[:, span], target.at[:, span], load_sem.at[2 * part + index]
                )
                for index, (source, target) in enumerate(((dinner_hbm, dinner_v), (we_hbm, we)))
            ]
        )
    loads.append([pltpu.make_async_copy(wao_hbm, wao, load_sem.at[2 * len(loads)])])
    for group in loads:
        for load in group:
            load.start()
    dh2 = None
    for part, group in enumerate(loads[:-1]):
        span = slice(part * width, (part + 1) * width)
        for load in group:
            load.wait()
        term = nt(dinner_v[:, span], we[:, span])
        dh2 = term if dh2 is None else dh2 + term
    normed, scale = normalise(after_ref[...])
    second_gain_out[...] = jnp.sum(dh2 * normed, axis=0, keepdims=True)
    second_shift_out[...] = jnp.sum(dh2, axis=0, keepdims=True)
    dafter = dy_ref[...] + norm_back(normed, scale, as_row(second_gain), dh2)
    dafter_out[...] = dafter
    dbranch = dafter.astype(jnp.bfloat16)
    dbranch_v[...] = dbranch
    attend_bias_out[...] = jnp.sum(dbranch.astype(jnp.float32), axis=0, keepdims=True)
    loads[-1][0].wait()
    dmixed_out[...] = nt(dbranch, wao[...]).astype(jnp.bfloat16)
    part = dbranch_v[:, pl.ds(pl.multiple_of(blk * part_width, part_width), part_width)]
    attend_out[...] = tn(mixed_ref[...], part).astype(jnp.bfloat16).reshape(attend_out.shape)


def branch_back(place, dy, after, mixed, second_gain, dinner, we, wao, carry, shards):
    count, width = after.shape
    low, full = jnp.bfloat16, jnp.float32
    vector = jax.ShapeDtypeStruct((1, width), full)
    return pl.pallas_call(
        carrying(branch_kernel, 8, 6, len(carry)),
        in_specs=[scalars()] + [whole_vmem()] * 4 + [in_place()] * (3 + len(carry)),
        out_specs=[whole_vmem()] * 6 + [in_place()] * len(carry),
        input_output_aliases=aliases(8, 6, carry),
        out_shape=[
            jax.ShapeDtypeStruct((count, width), full),
            jax.ShapeDtypeStruct((count, width), low),
            jax.ShapeDtypeStruct((shards, width // shards, width // 2), low),
            vector,
            vector,
            vector,
        ]
        + shapes_of(carry),
        scratch_shapes=[
            pltpu.VMEM(dinner.shape, low),
            pltpu.VMEM(we.shape, low),
            pltpu.VMEM(wao.shape, low),
            pltpu.VMEM((count, width), low),
            pltpu.SemaphoreType.DMA((2 * (we.shape[1] // width) + 1,)),
        ],
        compiler_params=pltpu.CompilerParams(vmem_limit_bytes=30 << 20),
        cost_estimate=pl.CostEstimate(
            flops=12_000_000_000, bytes_accessed=1_000_000, transcendentals=0
        ),
        name="branch_back",
    )(place, dy, after, mixed, second_gain, dinner, we, wao, *carry)


def attend_pair(block, query_ref, keys_ref, values_ref, probs_ref, dmixed_ref):
    count, pair = query_ref.shape
    query = query_ref[...] * jnp.bfloat16(0.125)
    zero = jnp.bfloat16(0.0)
    dkeys = jnp.zeros((count, pair), jnp.float32)
    dvalues = jnp.zeros((count, pair), jnp.float32)
    keys = keys_ref[...] * jnp.bfloat16(0.125)
    dqueries = []
    for piece in reversed(range(count // block)):
        span = slice(piece * block, (piece + 1) * block)
        reach = (piece + 1) * block
        dquery = jnp.zeros((block, pair), jnp.float32)
        add_keys = jnp.zeros((reach, pair), jnp.float32)
        add_values = jnp.zeros((reach, pair), jnp.float32)
        for which in range(2):
            mask = head_mask((block, pair), which)
            grad = jnp.where(mask, dmixed_ref[span], zero)
            mine = jnp.where(mask, query[span], zero)
            probs = probs_ref[which, :reach, span]
            dprobs = nt(values_ref[:reach], grad)
            wide = probs.astype(jnp.float32)
            product = wide * dprobs
            balance = jnp.sum(product, axis=0, keepdims=True)
            dscores = (product - wide * balance).astype(jnp.bfloat16)
            add_values = add_values + dense(probs, grad)
            add_keys = add_keys + dense(dscores, mine)
            dquery = dquery + tn(
                dscores, jnp.where(head_mask((reach, pair), which), keys[:reach], zero)
            )
        dqueries.insert(0, dquery.astype(jnp.bfloat16))
        if reach < count:
            pad = jnp.zeros((count - reach, pair), jnp.float32)
            add_keys = jnp.concatenate([add_keys, pad], axis=0)
            add_values = jnp.concatenate([add_values, pad], axis=0)
        dkeys = dkeys + add_keys
        dvalues = dvalues + add_values
    return (
        jnp.concatenate(dqueries, axis=0),
        dkeys.astype(jnp.bfloat16),
        dvalues.astype(jnp.bfloat16),
    )


def attend_kernel(
    block, _, query_ref, keys_ref, values_ref, probs_ref, dmixed_ref, dq_ref, dk_ref, dv_ref
):
    grads = attend_pair(block, query_ref, keys_ref, values_ref, probs_ref, dmixed_ref)
    for ref, grad in zip((dq_ref, dk_ref, dv_ref), grads):
        ref[...] = grad


def project_kernel(
    block,
    place_ref,
    query_ref,
    keys_ref,
    values_ref,
    probs_ref,
    dmixed_ref,
    normed_ref,
    attend_ref,
    dq_ref,
    dk_ref,
    dv_ref,
    keep,
    send,
    natural,
    copy_sem,
):
    step = pl.program_id(0)
    pair = query_ref.shape[1]
    column = pl.ds(pl.multiple_of(step * pair, pair), pair)
    grads = attend_pair(block, query_ref, keys_ref, values_ref, probs_ref, dmixed_ref)
    for ref, grad in zip((dq_ref, dk_ref, dv_ref), grads):
        ref[:, column] = grad

    @pl.when(step == pl.num_programs(0) - 1)
    def _():
        me = place_ref[0]
        shards = natural.shape[0]
        width = normed_ref.shape[1]
        part_width = width // 2
        chunk = width // shards
        natural[:, :chunk, :] = attend_ref[...]
        copies = []
        for part, ref in enumerate((dq_ref, dk_ref, dv_ref)):
            value = tn(normed_ref[...], ref[...]).astype(jnp.bfloat16)
            natural[:, (part + 1) * chunk : (part + 2) * chunk, :] = value.reshape(
                shards, chunk, part_width
            )
            rows = pl.ds(0, 2 * chunk) if part == 0 else pl.ds((part + 1) * chunk, chunk)
            ready = shard_copies(
                me, natural, keep, send, copy_sem.at[part], MASKS, 0, shards, rows
            )
            for copy in ready:
                copy.start()
            copies += ready
        for copy in copies:
            copy.wait()


def attend_specs(joined, dmixed, own):
    count, width = dmixed.shape
    pair = 2 * HEAD_DIM
    pairs = width // pair
    half = pairs // 2

    def first(place_ref):
        blk = place_ref[1]
        return half * (blk if own else 1 - blk)

    def column(offset):
        return pl.BlockSpec((count, pair), lambda p, place_ref: (0, offset + first(place_ref) + p))

    return half, [
        column(0),
        column(pairs),
        column(2 * pairs),
        pl.BlockSpec((2, count, count), lambda p, place_ref: (first(place_ref) + p, 0, 0)),
        column(0),
    ]


def attend_back(place, joined, probs, dmixed, carry, block):
    count, width = dmixed.shape
    half, specs = attend_specs(joined, dmixed, False)
    result = pl.BlockSpec((count, 2 * HEAD_DIM), lambda p, place_ref: (0, p))
    return pl.pallas_call(
        carrying(functools.partial(attend_kernel, block), 6, 3, len(carry)),
        grid_spec=pltpu.PrefetchScalarGridSpec(
            num_scalar_prefetch=1,
            grid=(half,),
            in_specs=specs + [in_place()] * len(carry),
            out_specs=[result] * 3 + [in_place()] * len(carry),
        ),
        out_shape=[jax.ShapeDtypeStruct((count, width // 2), jnp.bfloat16)] * 3
        + shapes_of(carry),
        input_output_aliases=aliases(6, 3, carry),
        compiler_params=pltpu.CompilerParams(vmem_limit_bytes=16 << 20),
        cost_estimate=pl.CostEstimate(
            flops=12_000_000_000, bytes_accessed=1_000_000, transcendentals=0
        ),
        name="attend_back",
    )(place, joined, joined, joined, probs, dmixed, *carry)


def project_back(place, joined, probs, dmixed, normed, attend, carry, block, shards):
    count, width = dmixed.shape
    chunk = width // shards
    half, specs = attend_specs(joined, dmixed, True)
    result = pl.BlockSpec((count, width // 2), lambda p, place_ref: (0, 0))
    piece = jax.ShapeDtypeStruct((shards // 2, 4 * chunk, width // 2), jnp.bfloat16)
    specs = specs + [
        pl.BlockSpec(normed.shape, lambda p, place_ref: (0, 0)),
        pl.BlockSpec(attend.shape, lambda p, place_ref: (0, 0, 0)),
    ]
    return pl.pallas_call(
        carrying(functools.partial(project_kernel, block), 8, 5, len(carry)),
        grid_spec=pltpu.PrefetchScalarGridSpec(
            num_scalar_prefetch=1,
            grid=(half,),
            in_specs=specs + [in_place()] * len(carry),
            out_specs=[result] * 3 + [in_place()] * (2 + len(carry)),
            scratch_shapes=[
                pltpu.VMEM((shards, 4 * chunk, width // 2), jnp.bfloat16),
                pltpu.SemaphoreType.DMA((3, shards)),
            ],
        ),
        out_shape=[jax.ShapeDtypeStruct((count, width // 2), jnp.bfloat16)] * 3
        + [piece, piece]
        + shapes_of(carry),
        input_output_aliases=aliases(8, 5, carry),
        compiler_params=pltpu.CompilerParams(vmem_limit_bytes=20 << 20),
        cost_estimate=pl.CostEstimate(
            flops=12_000_000_000, bytes_accessed=1_000_000, transcendentals=0
        ),
        name="project_back",
    )(place, joined, joined, joined, probs, dmixed, normed, attend, *carry)


def input_kernel(
    place_ref,
    own_ref,
    other_ref,
    dq_own,
    dk_own,
    dv_own,
    dq_other,
    dk_other,
    dv_other,
    dafter_ref,
    first_gain,
    attend_bias_grad,
    second_gain_grad,
    second_shift_grad,
    expand_bias_grad,
    contract_bias_grad,
    wpi_hbm,
    grad_out,
    keep,
    send,
    wpi,
    joined_v,
    x_v,
    grad_v,
    load_sem,
):
    me, blk = place_ref[0], place_ref[1]
    load = pltpu.make_async_copy(wpi_hbm, wpi, load_sem.at[0])
    load.start()
    count, width = x_v.shape
    part_width = width // 2
    shards = 2 * keep.shape[0]
    in_stream_order(x_v, own_ref, other_ref, blk)
    for side, group in ((blk, (dq_own, dk_own, dv_own)), (1 - blk, (dq_other, dk_other, dv_other))):
        for part, ref in enumerate(group):
            offset = part * width + side * part_width
            joined_v[:, pl.ds(pl.multiple_of(offset, part_width), part_width)] = ref[...]
    normed, scale = normalise(x_v[...])
    load.wait()
    dh1 = nt(joined_v[...], wpi[...])
    sums = jnp.sum(joined_v[...].astype(jnp.float32), axis=0, keepdims=True)
    vectors = [
        jnp.sum(dh1 * normed, axis=0, keepdims=True),
        jnp.sum(dh1, axis=0, keepdims=True),
        jnp.concatenate([sums[:, :width], sums[:, 2 * width :]], axis=1),
        attend_bias_grad[...],
        second_gain_grad[...],
        second_shift_grad[...],
        expand_bias_grad[...],
        contract_bias_grad[...],
    ]
    mine = lax.rem(me, 2)
    place = position(me, MASKS)
    for shard in range(shards):
        rows = []
        for vector in vectors:
            size = vector.shape[1] // shards
            piece = vector[:, shard * size : (shard + 1) * size]
            rows.append(jnp.concatenate([piece, jnp.zeros((1, 256 - size), jnp.float32)], axis=1))
        value = jnp.concatenate(rows, axis=0)
        target = lax.bitwise_xor(place, jnp.int32(position(shard, MASKS)))

        @pl.when(mine == shard % 2)
        def _():
            keep[target] = value

        @pl.when(mine != shard % 2)
        def _():
            send[target] = value

    grad_v[...] = dafter_ref[...] + norm_back(normed, scale, as_row(first_gain), dh1)
    rows = own_ref.shape[0]
    grad_out[...] = grad_v[pl.ds(pl.multiple_of(blk * rows, rows), rows), :]


def input_back(place, own, other, parts, dafter, gain, vectors, wpi, carry, shards):
    rows, width = own.shape
    count = 2 * rows
    low, full = jnp.bfloat16, jnp.float32
    half = jax.ShapeDtypeStruct((shards // 2, len(vectors) + 3, 256), full)
    return pl.pallas_call(
        carrying(input_kernel, 17, 3, len(carry)),
        in_specs=[scalars()] + [whole_vmem()] * 15 + [in_place()] * (1 + len(carry)),
        out_specs=[whole_vmem()] * 3 + [in_place()] * len(carry),
        out_shape=[jax.ShapeDtypeStruct((rows, width), full), half, half] + shapes_of(carry),
        input_output_aliases=aliases(17, 3, carry),
        scratch_shapes=[
            pltpu.VMEM(wpi.shape, low),
            pltpu.VMEM((count, 3 * width), low),
            pltpu.VMEM((count, width), full),
            pltpu.VMEM((count, width), full),
            pltpu.SemaphoreType.DMA((1,)),
        ],
        compiler_params=pltpu.CompilerParams(vmem_limit_bytes=26 << 20),
        cost_estimate=pl.CostEstimate(
            flops=12_000_000_000, bytes_accessed=1_000_000, transcendentals=0
        ),
        name="input_back",
    )(place, own, other, *parts, dafter, gain, *vectors, wpi, *carry)


def across(value, mask):
    return lax.ppermute(value, "dp", [(i, i ^ mask) for i in range(lax.axis_size("dp"))])


def halve(keep, received):
    half = keep.shape[0] // 2
    return (keep[:half] + received[:half], keep[half:] + received[half:])


def merge_kernel(layout, *refs):
    total = sum(1 + parts for parts in layout)
    inputs, outputs = list(refs[:total]), list(refs[total:])
    done = 0
    for parts in layout:
        keep = inputs.pop(0)
        half = keep.shape[0] // 2
        if half == 0:
            targets = [(outputs[-1].at[done : done + 1], slice(0, 1))]
            done += 1
        else:
            targets = [(outputs.pop(0), slice(0, half)), (outputs.pop(0), slice(half, 2 * half))]
        row = 0
        for _ in range(parts):
            got = inputs.pop(0)
            rows = slice(row, row + got.shape[1])
            row = rows.stop
            for target, which in targets:
                target[:, rows] = keep[which, rows] + got[which]


def merge(*pairs):
    shapes, finals = [], [pair[0] for pair in pairs if pair[0].shape[0] == 1]
    for keep, *_ in pairs:
        if keep.shape[0] > 1:
            shapes += [jax.ShapeDtypeStruct((keep.shape[0] // 2, *keep.shape[1:]), keep.dtype)] * 2
    if finals:
        shapes.append(jax.ShapeDtypeStruct((len(finals), *finals[0].shape[1:]), finals[0].dtype))
    arrays = [array for pair in pairs for array in pair]
    return pl.pallas_call(
        functools.partial(merge_kernel, [len(pair) - 1 for pair in pairs]),
        in_specs=[whole_vmem()] * len(arrays),
        out_specs=[whole_vmem()] * len(shapes),
        out_shape=shapes,
        compiler_params=pltpu.CompilerParams(vmem_limit_bytes=16 << 20),
        cost_estimate=pl.CostEstimate(flops=1_000_000, bytes_accessed=1_000_000, transcendentals=0),
        name="merge",
    )(*arrays)


def swap(value):
    return lax.ppermute(value, "blk", [(0, 1), (1, 0)])


def both_halves(own, other, blk):
    return jnp.where(
        blk == 0,
        jnp.concatenate([own, other], axis=-1),
        jnp.concatenate([other, own], axis=-1),
    ).astype(jnp.float32)


def local_pair(hidden, doc_lengths, *arrays):
    student, teacher = arrays[:12], arrays[12:24]
    final_gain, final_shift, table = arrays[24:]
    rows, width = hidden.shape
    shards = lax.axis_size("dp")
    blk = lax.axis_index("blk")
    place = jnp.stack([lax.axis_index("dp"), blk]).astype(jnp.int32)
    other = swap(hidden)
    def block(train, params):
        gain, shift, wpi, qvb, wao, bao, gain_two, shift_two, we, be, wc, bc = params
        vectors = (gain, shift, qvb, bao, gain_two, shift_two, be, bc, final_gain, final_shift)
        return forward(
            train,
            place,
            doc_lengths,
            hidden,
            other,
            vectors,
            (wpi, wao, we, wc),
        )

    (rows_t,) = block(False, teacher)
    rows_s, normed, joined, probs, mixed, after, normed_two, slope, active, y = block(True, student)
    diff, expo, stats, sums = logits_phase(rows_s, rows_t, table)
    grad_own, grad_low, divergence = gradient_phase(
        place, diff, expo, table, stats, sums, swap(sums)
    )
    grad_other = swap(grad_low)
    gain, shift, wpi, qvb, wao, bao, gain_two, shift_two, we, be, wc, bc = student
    cw_keep, cw_send, dy, dm, dbc = contract_back(
        place, grad_own, grad_other, y, final_gain, active, shards
    )
    ew_keep, ew_send, dinner, dbe = expand_back(place, dm, normed_two, wc, slope, shards)
    cw_keep, cw_send = halve(cw_keep, across(cw_send, MASKS[0]))
    cw_got = across(cw_send, MASKS[1])
    ew_got = across(ew_send, MASKS_B[0])
    dafter, dmixed, attend, dgain_two, dshift_two, dbao, cw_keep, ew_keep = branch_back(
        place, dy, after, mixed, gain_two, dinner, we, wao, (cw_keep, ew_keep), shards
    )
    ew_keep, ew_send = halve(ew_keep, ew_got)
    ew_got = across(ew_send, MASKS_B[1])
    *own_grads, keep, send, cw_keep, ew_keep = project_back(
        place, joined, probs, dmixed, normed, attend, (cw_keep, ew_keep), rows, shards
    )
    got = across(send, MASKS[0])
    cw_keep, cw_send, ew_keep, ew_send = merge((cw_keep, cw_got), (ew_keep, ew_got))
    cw_got = across(cw_send, MASKS[2])
    ew_got = across(ew_send, MASKS_B[2])
    *other_grads, keep, cw_keep, ew_keep = attend_back(
        place, joined, probs, dmixed, (keep, cw_keep, ew_keep), rows
    )
    keep, send, cw_keep, cw_send, ew_keep, ew_send = merge(
        (keep, got), (cw_keep, cw_got), (ew_keep, ew_got)
    )
    got = across(send, MASKS[1])
    cw_got = across(cw_send, MASKS[3])
    ew_got = across(ew_send, MASKS_B[3])
    input_grad, vector_keep, vector_send, keep, cw_keep, ew_keep = input_back(
        place,
        hidden,
        other,
        (*own_grads, *other_grads),
        dafter,
        gain,
        (dbao, dgain_two, dshift_two, dbe, dbc),
        wpi,
        (keep, cw_keep, ew_keep),
        shards,
    )
    vector_got = across(vector_send, MASKS[0])
    keep, send, vector_keep, vector_send, both = merge(
        (keep, got), (cw_keep, cw_got), (ew_keep, ew_got), (vector_keep, vector_got)
    )
    got, both_other = across(send, MASKS[2]), swap(both)
    vector_got = across(vector_send, MASKS[1])
    keep, send, vector_keep, vector_send = merge((keep, got), (vector_keep, vector_got))
    got, vector_got = across(send, MASKS[3]), across(vector_send, MASKS[2])
    vector_keep, vector_send, last = merge((keep, got), (vector_keep, vector_got))
    last = last[0]
    last_other = swap(last)
    vectors = (vector_keep + across(vector_send, MASKS[3]))[0]
    cw, ew, cw_other, ew_other = both[0], both[1], both_other[0], both_other[1]
    chunk = width // shards

    def wide(own, other):
        own, other = (part.reshape(-1, chunk, part.shape[1]) for part in (own, other))
        order = [own[i] for i in range(own.shape[0])], [other[i] for i in range(own.shape[0])]
        return order

    grad_cw = both_halves(cw, cw_other, blk)
    own, other = wide(ew, ew_other)
    grad_ew = both_halves(jnp.concatenate(own, axis=1), jnp.concatenate(other, axis=1), blk)
    own, other = wide(last, last_other)
    grad_ao = both_halves(own[0], other[0], blk)
    grad_pi = jnp.concatenate([both_halves(own[i], other[i], blk) for i in (1, 2, 3)], axis=1)
    sizes = (chunk, chunk, 2 * chunk, chunk, chunk, chunk, be.shape[0] // shards, chunk)
    dgain, dshift, dqvb, dbao, dgain_two, dshift_two, dbe, dbc = (
        vectors[index, :size] for index, size in enumerate(sizes)
    )
    return (
        divergence[0],
        input_grad,
        dgain,
        dshift,
        grad_pi,
        dqvb,
        grad_ao,
        dbao,
        dgain_two,
        dshift_two,
        grad_ew,
        dbe,
        grad_cw,
        dbc,
    )


def solution(mesh):
    pair = mesh.shape["dp"] == 16 and mesh.shape["blk"] == 2
    return jax.shard_map(
        local_pair if pair else local_general,
        mesh=mesh,
        in_specs=(
            P(("dp", "blk"), None),
            P("dp", None),
            P(),
            P(),
            P(),
            P(),
            P(),
            P(),
            P(),
            P(),
            P(),
            P(),
            P(),
            P(),
            P(),
            P(),
            P(),
            P(),
            P(),
            P(),
            P(),
            P(),
            P(),
            P(),
            P(),
            P(),
            P(),
            P(),
            P("blk", None),
        ),
        out_specs=(
            P(("dp", "blk")),
            P(("dp", "blk"), None),
            P("dp"),
            P("dp"),
            P("dp", None),
            P("dp"),
            P("dp", None),
            P("dp"),
            P("dp"),
            P("dp"),
            P("dp", None),
            P("dp"),
            P("dp", None),
            P("dp"),
        ),
        check_vma=False,
    )
```

```python
import functools

import jax
import jax.numpy as jnp
from jax import lax
from jax.experimental import pallas as pl
from jax.experimental.pallas import tpu as pltpu
from jax.sharding import PartitionSpec as P

HEADS = 12
HEAD_DIM = 64
TABLE_SPAN = 2048
MASKS = (1, 2, 4, 8)
MASKS_B = (1, 4, 2, 8)


negative = -1e30


def layer_norm(value, gain, shift):
    centre = value - jnp.mean(value, axis=-1, keepdims=True)
    return (
        centre * lax.rsqrt(jnp.mean(centre * centre, axis=-1, keepdims=True) + 1e-05) * gain + shift
    )


def doc_numbers(lengths, count):
    ends = jnp.cumsum(lengths)
    places = jnp.arange(count, dtype=jnp.int32)
    return jnp.sum((places[:, None] >= ends[None, :]).astype(jnp.int32), axis=1)


def dense(left, right):
    return jnp.dot(left, right, preferred_element_type=jnp.float32)


def split_heads(value):
    return value.reshape(value.shape[0], HEADS, HEAD_DIM)


def input_side(inputs, gain, shift, project_in, qv_bias):
    width = inputs.shape[1]
    normed = layer_norm(inputs, gain, shift).astype(jnp.bfloat16)
    bias = jnp.concatenate([qv_bias[:width], jnp.zeros((width,), jnp.float32), qv_bias[width:]])
    joined = (dense(normed, project_in) + bias).astype(jnp.bfloat16)
    return (normed, joined[:, :width], joined[:, width : 2 * width], joined[:, 2 * width :])


def output_side(
    inputs,
    mixed_low,
    attend_out,
    attend_bias,
    second_gain,
    second_shift,
    expand_weight,
    expand_bias,
    contract_weight,
    contract_bias,
):
    after = inputs + dense(mixed_low, attend_out) + attend_bias
    normed = layer_norm(after, second_gain, second_shift).astype(jnp.bfloat16)
    inner = dense(normed, expand_weight) + expand_bias
    active = jax.nn.gelu(inner, approximate=True).astype(jnp.bfloat16)
    final = after + dense(active, contract_weight) + contract_bias
    return (after, normed, inner, active, final)


def online(state, query, keys, values, allowed):
    top, mass, summed = state
    scores = (
        jnp.einsum(
            "qhd,khd->hqk",
            split_heads(query),
            split_heads(keys),
            preferred_element_type=jnp.float32,
        )
        * 0.125
    )
    scores = jnp.where(allowed[None], scores, negative)
    new_top = jnp.maximum(top, jnp.max(scores, axis=-1))
    factor = jnp.exp(top - new_top)
    weights = jnp.where(allowed[None], jnp.exp(scores - new_top[..., None]), 0.0)
    mass = mass * factor + jnp.sum(weights, axis=-1)
    summed = summed * factor[..., None] + jnp.einsum(
        "hqk,khd->hqd",
        weights.astype(jnp.bfloat16),
        split_heads(values),
        preferred_element_type=jnp.float32,
    )
    return (new_top, mass, summed)


def score_grads(query_heads, grad_heads, log_norm, balance, key_block, value_block, allowed):
    scores = (
        jnp.einsum("qhd,khd->hqk", query_heads, key_block, preferred_element_type=jnp.float32)
        * 0.125
    )
    probs = jnp.where(allowed[None], jnp.exp(scores - log_norm[..., None]), 0.0)
    grad_probs = jnp.einsum(
        "qhd,khd->hqk", grad_heads, value_block, preferred_element_type=jnp.float32
    )
    grad_scores = (probs * (grad_probs - balance[..., None])).astype(jnp.bfloat16)
    return (probs, grad_scores)


def partial_stats(rows_teacher, rows_student, table):
    half_t = jnp.einsum("rd,vd->rv", rows_teacher, table, preferred_element_type=jnp.float32) * 0.5
    half_s = jnp.einsum("rd,vd->rv", rows_student, table, preferred_element_type=jnp.float32) * 0.5
    top_t = jnp.max(half_t, axis=-1)
    expo_t = jnp.exp(half_t - top_t[:, None])
    top_s = jnp.max(half_s, axis=-1)
    return (
        top_t,
        jnp.sum(expo_t, axis=-1),
        jnp.sum(expo_t * (half_t - half_s), axis=-1),
        top_s,
        jnp.sum(jnp.exp(half_s - top_s[:, None]), axis=-1),
    )


def combine(first_stats, second_stats):
    top_t = jnp.maximum(first_stats[0], second_stats[0])
    right_weight = jnp.exp(second_stats[0] - top_t)
    top_s = jnp.maximum(first_stats[3], second_stats[3])
    return (
        top_t,
        second_stats[1] * right_weight,
        second_stats[2] * right_weight,
        top_s,
        second_stats[4] * jnp.exp(second_stats[3] - top_s),
    )


def row_gradient(rows_teacher, rows_student, table, norm_t, norm_s):
    half_t = jnp.einsum("rd,vd->rv", rows_teacher, table, preferred_element_type=jnp.float32) * 0.5
    half_s = jnp.einsum("rd,vd->rv", rows_student, table, preferred_element_type=jnp.float32) * 0.5
    change = ((jnp.exp(half_s - norm_s[:, None]) - jnp.exp(half_t - norm_t[:, None])) * 0.5).astype(
        jnp.bfloat16
    )
    return dense(change, table)


def local_general(
    hidden,
    doc_lengths,
    student_first_gain,
    student_first_shift,
    student_project_in,
    student_query_value_bias,
    student_attend_out,
    student_attend_bias,
    student_second_gain,
    student_second_shift,
    student_expand_weight,
    student_expand_bias,
    student_contract_weight,
    student_contract_bias,
    teacher_first_gain,
    teacher_first_shift,
    teacher_project_in,
    teacher_query_value_bias,
    teacher_attend_out,
    teacher_attend_bias,
    teacher_second_gain,
    teacher_second_shift,
    teacher_expand_weight,
    teacher_expand_bias,
    teacher_contract_weight,
    teacher_contract_bias,
    final_gain,
    final_shift,
    embedding,
):
    rows, width = hidden.shape
    blocks = lax.axis_size("blk")
    stream = rows * blocks
    first = lax.axis_index("blk") * rows
    last_place = first + rows - 1
    docs = doc_numbers(doc_lengths[0], stream)
    own_places = first + jnp.arange(rows, dtype=jnp.int32)
    own_docs = lax.dynamic_slice_in_dim(docs, first, rows)
    inputs = hidden.astype(jnp.float32)
    normed_s, query_s, keys_s, values_s = input_side(
        inputs,
        student_first_gain,
        student_first_shift,
        student_project_in,
        student_query_value_bias,
    )
    normed_t, query_t, keys_t, values_t = input_side(
        inputs,
        teacher_first_gain,
        teacher_first_shift,
        teacher_project_in,
        teacher_query_value_bias,
    )

    def allowed_for(begin):
        key_places = begin + jnp.arange(rows, dtype=jnp.int32)
        key_docs = lax.dynamic_slice_in_dim(docs, begin, rows)
        return (key_places[None, :] <= own_places[:, None]) & (
            key_docs[None, :] == own_docs[:, None]
        )

    start_state = (
        jnp.full((HEADS, rows), negative, jnp.float32),
        jnp.zeros((HEADS, rows), jnp.float32),
        jnp.zeros((HEADS, rows, HEAD_DIM), jnp.float32),
    )
    carry = (start_state, start_state)
    pieces = (
        lax.all_gather(keys_s, "blk", axis=0, tiled=True),
        lax.all_gather(values_s, "blk", axis=0, tiled=True),
        lax.all_gather(keys_t, "blk", axis=0, tiled=True),
        lax.all_gather(values_t, "blk", axis=0, tiled=True),
    )
    count = pieces[0].shape[0]
    stacked = tuple((member.reshape(count // rows, rows, width) for member in pieces))
    begins = rows * jnp.arange(count // rows, dtype=jnp.int32)

    def step(state, item):
        piece_keys_s, piece_values_s, piece_keys_t, piece_values_t, begin = item

        def step_compute(inner_state):
            allowed = allowed_for(begin)
            return (
                online(inner_state[0], query_s, piece_keys_s, piece_values_s, allowed),
                online(inner_state[1], query_t, piece_keys_t, piece_values_t, allowed),
            )

        return (
            lax.cond(begin <= last_place, step_compute, lambda inner_state: inner_state, state),
            None,
        )

    carry, _ = lax.scan(step, carry, stacked + (begins,))
    state_s, state_t = carry
    out_heads_s = state_s[2] / state_s[1][..., None]
    attn_norm = state_s[0] + jnp.log(state_s[1])
    mixed_low_s = out_heads_s.transpose(1, 0, 2).reshape(rows, width).astype(jnp.bfloat16)
    mixed_low_t = (
        (state_t[2] / state_t[1][..., None])
        .transpose(1, 0, 2)
        .reshape(rows, width)
        .astype(jnp.bfloat16)
    )
    after_s, normed_two_s, inner_s, active_s, final_s = output_side(
        inputs,
        mixed_low_s,
        student_attend_out,
        student_attend_bias,
        student_second_gain,
        student_second_shift,
        student_expand_weight,
        student_expand_bias,
        student_contract_weight,
        student_contract_bias,
    )
    after_t, normed_two_t, inner_t, active_t, final_t = output_side(
        inputs,
        mixed_low_t,
        teacher_attend_out,
        teacher_attend_bias,
        teacher_second_gain,
        teacher_second_shift,
        teacher_expand_weight,
        teacher_expand_bias,
        teacher_contract_weight,
        teacher_contract_bias,
    )
    rows_s = layer_norm(final_s, final_gain, final_shift).astype(jnp.bfloat16)
    rows_t = layer_norm(final_t, final_gain, final_shift).astype(jnp.bfloat16)
    identity = (
        jnp.full((rows,), negative, jnp.float32),
        jnp.zeros((rows,), jnp.float32),
        jnp.zeros((rows,), jnp.float32),
        jnp.full((rows,), negative, jnp.float32),
        jnp.zeros((rows,), jnp.float32),
    )
    merged = combine(
        identity,
        partial_stats(rows_t, rows_s, lax.all_gather(embedding, "blk", axis=0, tiled=True)),
    )
    norm_t = merged[0] + jnp.log(merged[1])
    norm_s = merged[3] + jnp.log(merged[4])
    kl_rows = merged[2] / merged[1] - norm_t + norm_s
    grad_final = row_gradient(
        rows_t, rows_s, lax.all_gather(embedding, "blk", axis=0, tiled=True), norm_t, norm_s
    )
    _, final_back = jax.vjp(layer_norm, final_s, final_gain, final_shift)
    grad_y = final_back(grad_final)[0]
    grad_m = grad_y.astype(jnp.bfloat16)
    grad_contract_weight = jnp.einsum(
        "rf,rd->fd", active_s, grad_m, preferred_element_type=jnp.float32
    )
    grad_contract_bias = jnp.sum(grad_m.astype(jnp.float32), axis=0)
    grad_active = jnp.einsum(
        "rd,fd->rf", grad_m, student_contract_weight, preferred_element_type=jnp.float32
    )
    _, gelu_back = jax.vjp(lambda value: jax.nn.gelu(value, approximate=True), inner_s)
    grad_inner = gelu_back(grad_active)[0].astype(jnp.bfloat16)
    grad_expand_weight = jnp.einsum(
        "rd,rf->df", normed_two_s, grad_inner, preferred_element_type=jnp.float32
    )
    grad_expand_bias = jnp.sum(grad_inner.astype(jnp.float32), axis=0)
    grad_normed_two = jnp.einsum(
        "rf,df->rd", grad_inner, student_expand_weight, preferred_element_type=jnp.float32
    )
    _, second_back = jax.vjp(layer_norm, after_s, student_second_gain, student_second_shift)
    grad_after_norm, grad_second_gain, grad_second_shift = second_back(grad_normed_two)
    grad_after = grad_y + grad_after_norm
    grad_branch = grad_after.astype(jnp.bfloat16)
    grad_attend_out = jnp.einsum(
        "rc,rd->cd", mixed_low_s, grad_branch, preferred_element_type=jnp.float32
    )
    grad_attend_bias = jnp.sum(grad_branch.astype(jnp.float32), axis=0)
    grad_mixed = jnp.einsum(
        "rd,cd->rc", grad_branch, student_attend_out, preferred_element_type=jnp.float32
    ).astype(jnp.bfloat16)
    keys_all, values_all = (
        lax.all_gather(keys_s, "blk", axis=0, tiled=True),
        lax.all_gather(values_s, "blk", axis=0, tiled=True),
    )
    grad_heads = split_heads(grad_mixed)
    query_heads = split_heads(query_s)
    balance = jnp.sum(grad_heads.astype(jnp.float32).transpose(1, 0, 2) * out_heads_s, axis=-1)
    begins = rows * jnp.arange(blocks, dtype=jnp.int32)
    zero_query = jnp.zeros((rows, HEADS, HEAD_DIM), jnp.float32)

    def back_step(grad_query, begin):
        key_block = split_heads(lax.dynamic_slice_in_dim(keys_all, begin, rows, 0))
        value_block = split_heads(lax.dynamic_slice_in_dim(values_all, begin, rows, 0))

        def back_compute(total):
            probs, grad_scores = score_grads(
                query_heads,
                grad_heads,
                attn_norm,
                balance,
                key_block,
                value_block,
                allowed_for(begin),
            )
            total = (
                total
                + jnp.einsum(
                    "hqk,khd->qhd", grad_scores, key_block, preferred_element_type=jnp.float32
                )
                * 0.125
            )
            grad_keys = (
                jnp.einsum(
                    "hqk,qhd->khd", grad_scores, query_heads, preferred_element_type=jnp.float32
                )
                * 0.125
            )
            grad_values = jnp.einsum(
                "hqk,qhd->khd",
                probs.astype(jnp.bfloat16),
                grad_heads,
                preferred_element_type=jnp.float32,
            )
            return (
                total,
                jnp.concatenate(
                    [grad_keys.reshape(rows, width), grad_values.reshape(rows, width)], axis=1
                ),
            )

        def skip(total):
            return (total, jnp.zeros((rows, 2 * width), jnp.float32))

        return lax.cond(begin <= last_place, back_compute, skip, grad_query)

    grad_query, key_terms = lax.scan(back_step, zero_query, begins)
    key_value_grad = lax.psum_scatter(
        key_terms.reshape(stream, 2 * width).astype(jnp.bfloat16),
        "blk",
        scatter_dimension=0,
        tiled=True,
    ).astype(jnp.float32)
    grad_keys_low = key_value_grad[:, :width].astype(jnp.bfloat16)
    grad_values_low = key_value_grad[:, width:].astype(jnp.bfloat16)
    grad_query_low = grad_query.reshape(rows, width).astype(jnp.bfloat16)
    grad_joined = jnp.concatenate([grad_query_low, grad_keys_low, grad_values_low], axis=1)
    grad_project_in = jnp.einsum(
        "rd,rc->dc", normed_s, grad_joined, preferred_element_type=jnp.float32
    )
    grad_query_value_bias = jnp.concatenate(
        [
            jnp.sum(grad_query_low.astype(jnp.float32), axis=0),
            jnp.sum(grad_values_low.astype(jnp.float32), axis=0),
        ]
    )
    grad_normed = jnp.einsum(
        "rc,dc->rd", grad_joined, student_project_in, preferred_element_type=jnp.float32
    )
    _, first_back = jax.vjp(layer_norm, inputs, student_first_gain, student_first_shift)
    grad_inputs_norm, grad_first_gain, grad_first_shift = first_back(grad_normed)
    input_grad = grad_after + grad_inputs_norm
    shares = (
        lax.psum_scatter(
            grad_first_gain.astype(jnp.bfloat16), "dp", scatter_dimension=0, tiled=True
        ).astype(jnp.float32),
        lax.psum_scatter(
            grad_first_shift.astype(jnp.bfloat16), "dp", scatter_dimension=0, tiled=True
        ).astype(jnp.float32),
        lax.psum_scatter(
            grad_project_in.astype(jnp.bfloat16), "dp", scatter_dimension=0, tiled=True
        ).astype(jnp.float32),
        lax.psum_scatter(
            grad_query_value_bias.astype(jnp.bfloat16), "dp", scatter_dimension=0, tiled=True
        ).astype(jnp.float32),
        lax.psum_scatter(
            grad_attend_out.astype(jnp.bfloat16), "dp", scatter_dimension=0, tiled=True
        ).astype(jnp.float32),
        lax.psum_scatter(
            grad_attend_bias.astype(jnp.bfloat16), "dp", scatter_dimension=0, tiled=True
        ).astype(jnp.float32),
        lax.psum_scatter(
            grad_second_gain.astype(jnp.bfloat16), "dp", scatter_dimension=0, tiled=True
        ).astype(jnp.float32),
        lax.psum_scatter(
            grad_second_shift.astype(jnp.bfloat16), "dp", scatter_dimension=0, tiled=True
        ).astype(jnp.float32),
        lax.psum_scatter(
            grad_expand_weight.astype(jnp.bfloat16), "dp", scatter_dimension=0, tiled=True
        ).astype(jnp.float32),
        lax.psum_scatter(
            grad_expand_bias.astype(jnp.bfloat16), "dp", scatter_dimension=0, tiled=True
        ).astype(jnp.float32),
        lax.psum_scatter(
            grad_contract_weight.astype(jnp.bfloat16), "dp", scatter_dimension=0, tiled=True
        ).astype(jnp.float32),
        lax.psum_scatter(
            grad_contract_bias.astype(jnp.bfloat16), "dp", scatter_dimension=0, tiled=True
        ).astype(jnp.float32),
    )
    summed = (
        lax.psum(shares[0].astype(jnp.bfloat16), "blk").astype(jnp.float32),
        lax.psum(shares[1].astype(jnp.bfloat16), "blk").astype(jnp.float32),
        lax.psum(shares[2].astype(jnp.bfloat16), "blk").astype(jnp.float32),
        lax.psum(shares[3].astype(jnp.bfloat16), "blk").astype(jnp.float32),
        lax.psum(shares[4].astype(jnp.bfloat16), "blk").astype(jnp.float32),
        lax.psum(shares[5].astype(jnp.bfloat16), "blk").astype(jnp.float32),
        lax.psum(shares[6].astype(jnp.bfloat16), "blk").astype(jnp.float32),
        lax.psum(shares[7].astype(jnp.bfloat16), "blk").astype(jnp.float32),
        lax.psum(shares[8].astype(jnp.bfloat16), "blk").astype(jnp.float32),
        lax.psum(shares[9].astype(jnp.bfloat16), "blk").astype(jnp.float32),
        lax.psum(shares[10].astype(jnp.bfloat16), "blk").astype(jnp.float32),
        lax.psum(shares[11].astype(jnp.bfloat16), "blk").astype(jnp.float32),
    )
    return (
        kl_rows,
        input_grad,
        summed[0],
        summed[1],
        summed[2],
        summed[3],
        summed[4],
        summed[5],
        summed[6],
        summed[7],
        summed[8],
        summed[9],
        summed[10],
        summed[11],
    )


def nt(left, right):
    return lax.dot_general(
        left, right, (((1,), (1,)), ((), ())), preferred_element_type=jnp.float32
    )


def tn(left, right):
    return lax.dot_general(
        left, right, (((0,), (0,)), ((), ())), preferred_element_type=jnp.float32
    )


def normalise(value):
    centre = value - jnp.mean(value, axis=-1, keepdims=True)
    scale = lax.rsqrt(jnp.mean(centre * centre, axis=-1, keepdims=True) + 1e-05)
    return (centre * scale, scale)


def norm_back(normed, scale, gain, grad):
    weighted = grad * gain
    return scale * (
        weighted
        - jnp.mean(weighted, axis=-1, keepdims=True)
        - normed * jnp.mean(weighted * normed, axis=-1, keepdims=True)
    )


def starts_of(lengths_ref, count):
    places = lax.broadcasted_iota(jnp.int32, (1, count), 1)
    start = jnp.zeros((1, count), jnp.int32)
    end = jnp.int32(0)
    for index in range(lengths_ref.shape[1]):
        end = end + lengths_ref[0, index]
        start = jnp.where(places >= end, jnp.maximum(start, end), start)
    return start


def in_stream_order(target, own_ref, other_ref, blk):
    rows = own_ref.shape[0]
    target[pl.ds(pl.multiple_of(blk * rows, rows), rows), :] = own_ref[...].astype(target.dtype)
    target[pl.ds(pl.multiple_of((1 - blk) * rows, rows), rows), :] = other_ref[...].astype(
        target.dtype
    )


def head_mask(shape, which):
    lanes = lax.broadcasted_iota(jnp.int32, shape, 1)
    return (lanes >= HEAD_DIM) if which else (lanes < HEAD_DIM)


def forward_kernel(train, *refs):
    (
        place_ref,
        lengths_ref,
        own_ref,
        other_ref,
    ) = refs[:4]
    (
        first_gain,
        first_shift,
        qv_bias,
        attend_bias,
        second_gain,
        second_shift,
        expand_bias,
        contract_bias,
        final_gain,
        final_shift,
    ) = (as_row(ref) for ref in refs[4:14])
    weights_hbm = refs[14:18]
    rest = refs[18:]
    if train:
        rows_out, kept_hbm, rest = rest[0], rest[1:10], rest[10:]
    else:
        rows_out, kept_hbm, rest = rest[0], (), rest[1:]
    wpi, wao, we, wc = rest[:4]
    normed_v, joined_v, probs_v, mixed_v, after_v, normed_two_v, slope_v, active_v, y_v = rest[4:13]
    x_v, bias_v, weight_sem, out_sem, probs_sem = rest[13:]
    kept = (normed_v, joined_v, probs_v, mixed_v, after_v, normed_two_v, slope_v, active_v, y_v)
    loads = [
        pltpu.make_async_copy(source, target, weight_sem.at[index])
        for index, (source, target) in enumerate(zip(weights_hbm, (wpi, wao, we, wc)))
    ]
    stores = []

    def save(index, *at):
        if train:
            source, target = kept[index], kept_hbm[index]
            if at:
                source, target = source.at[at], target.at[at]
            store = pltpu.make_async_copy(source, target, out_sem.at[len(stores)])
            store.start()
            stores.append(store)

    for load in loads:
        load.start()
    blk = place_ref[1]
    in_stream_order(x_v, own_ref, other_ref, blk)
    count, width = x_v.shape
    block = own_ref.shape[0]
    normed, _ = normalise(x_v[...])
    normed_v[...] = (normed * first_gain + first_shift).astype(jnp.bfloat16)
    save(0)
    start = starts_of(lengths_ref, count)
    keys_at = lax.broadcasted_iota(jnp.int32, (count, count), 0)
    queries_at = lax.broadcasted_iota(jnp.int32, (count, count), 1)
    bias_v[...] = jnp.where((keys_at <= queries_at) & (keys_at >= start), 0.0, negative)
    loads[0].wait()
    for part in range(3):
        span = slice(part * width, (part + 1) * width)
        value = dense(normed_v[...], wpi[:, span])
        if part == 0:
            value = value + qv_bias[:, :width]
        if part == 2:
            value = value + qv_bias[:, width:]
        joined_v[:, span] = value.astype(jnp.bfloat16)
    save(1)
    pair = 2 * HEAD_DIM
    pairs = width // pair

    def attend(index, _):
        column = pl.ds(pl.multiple_of(index * pair, pair), pair)
        query = joined_v[:, column] * jnp.bfloat16(0.125)
        keys = joined_v[:, pl.ds(pl.multiple_of(width + index * pair, pair), pair)]
        values = joined_v[:, pl.ds(pl.multiple_of(2 * width + index * pair, pair), pair)]
        for piece in range(count // block):
            span = slice(piece * block, (piece + 1) * block)
            reach = (piece + 1) * block
            both = []
            for which in range(2):
                mine = jnp.where(
                    head_mask((block, pair), which), query[span], jnp.bfloat16(0.0)
                )
                scores = nt(keys[:reach], mine) + bias_v[:reach, span]
                expo = jnp.exp(scores - jnp.max(scores, axis=0, keepdims=True))
                probs = expo * (1.0 / jnp.sum(expo, axis=0, keepdims=True))
                probs = probs.astype(jnp.bfloat16)
                if train:
                    probs_v[2 * index + which, :reach, span] = probs
                both.append(tn(probs, values[:reach]))
            mixed_v[span, column] = jnp.where(
                head_mask((block, pair), 0), both[0], both[1]
            ).astype(jnp.bfloat16)
        if train:
            heads = pl.ds(2 * index, 2)
            pltpu.make_async_copy(
                probs_v.at[heads], kept_hbm[2].at[heads], probs_sem.at[index]
            ).start()
        return 0

    lax.fori_loop(0, pairs, attend, 0, unroll=3)
    if train:
        for index in range(pairs):
            heads = pl.ds(2 * index, 2)
            stores.append(
                pltpu.make_async_copy(
                    probs_v.at[heads], kept_hbm[2].at[heads], probs_sem.at[index]
                )
            )
    save(3)
    loads[1].wait()
    after_v[...] = x_v[...] + dense(mixed_v[...], wao[...]) + attend_bias
    save(4)
    normed, _ = normalise(after_v[...])
    normed_two_v[...] = (normed * second_gain + second_shift).astype(jnp.bfloat16)
    save(5)
    loads[2].wait()
    loads[3].wait()
    hidden_width = we.shape[1]
    total = after_v[...] + contract_bias
    root = 0.7978845608028654
    for part in range(hidden_width // width):
        span = slice(part * width, (part + 1) * width)
        inner = dense(normed_two_v[...], we[:, span]) + expand_bias[:, span]
        square = inner * inner
        bent = jnp.tanh(root * (inner + 0.044715 * (square * inner)))
        upper = 0.5 * (1.0 + bent)
        active = (inner * upper).astype(jnp.bfloat16)
        if train:
            active_v[:, span] = active
            slope_v[:, span] = (
                upper
                + (0.5 * root) * inner * (1.0 - bent * bent) * (1.0 + (3 * 0.044715) * square)
            ).astype(jnp.bfloat16)
            save(6, slice(None), pl.ds(part * width, width))
            save(7, slice(None), pl.ds(part * width, width))
        total = total + dense(active, wc[span, :])
    if train:
        y_v[...] = total
    save(8)
    normed, _ = normalise(total)
    rows_out[...] = (normed * final_gain + final_shift).astype(jnp.bfloat16) * jnp.bfloat16(0.5)
    if train:
        for store in stores:
            store.wait()


def carrying(kernel, inputs, outputs, carried):
    def body(*refs):
        rest = refs[inputs + carried :]
        kernel(*refs[:inputs], *rest[:outputs], *rest[outputs + carried :])

    return body


def shapes_of(carry):
    return [jax.ShapeDtypeStruct(item.shape, item.dtype) for item in carry]


def aliases(inputs, outputs, carry):
    return {inputs + index: outputs + index for index in range(len(carry))}


def as_row(ref):
    return ref[...].reshape(1, ref.shape[0])


def whole_vmem():
    return pl.BlockSpec(memory_space=pltpu.VMEM)


def in_place():
    return pl.BlockSpec(memory_space=pl.ANY)


def far(*arrays):
    return [pltpu.with_memory_space_constraint(array, pltpu.HBM) for array in arrays]


def scalars():
    return pl.BlockSpec(memory_space=pltpu.SMEM)


def forward(train, place, lengths, own, other, vectors, weights):
    rows, width = own.shape
    count = 2 * rows
    hidden_width = weights[2].shape[1]
    low, full = jnp.bfloat16, jnp.float32
    kept = [
        ((count, width), low),
        ((count, 3 * width), low),
        ((HEADS, count, count), low),
        ((count, width), low),
        ((count, width), full),
        ((count, width), low),
        ((count, hidden_width), low),
        ((count, hidden_width), low),
        ((count, width), full),
    ]
    small = ((8, 128), low)
    scratch = [kept[0], kept[1], kept[2] if train else ((1, 8, 128), low), kept[3], kept[4], kept[5]]
    scratch += [kept[6], kept[7], kept[8]] if train else [small, small, ((8, 128), full)]
    out_shape = [jax.ShapeDtypeStruct((count, width), low)]
    out_specs = [whole_vmem()]
    if train:
        out_shape += [jax.ShapeDtypeStruct(*item) for item in kept]
        out_specs += [in_place()] * len(kept)
    return pl.pallas_call(
        functools.partial(forward_kernel, train),
        in_specs=[scalars(), scalars()] + [whole_vmem()] * 12 + [in_place()] * 4,
        out_specs=out_specs,
        out_shape=out_shape,
        scratch_shapes=[pltpu.VMEM(item.shape, low) for item in weights]
        + [pltpu.VMEM(*item) for item in scratch]
        + [
            pltpu.VMEM((count, width), full),
            pltpu.VMEM((count, count), full),
            pltpu.SemaphoreType.DMA((4,)),
            pltpu.SemaphoreType.DMA((32,)),
            pltpu.SemaphoreType.DMA((HEADS // 2,)),
        ],
        compiler_params=pltpu.CompilerParams(vmem_limit_bytes=(54 if train else 44) << 20),
        cost_estimate=pl.CostEstimate(
            flops=8_000_000_000, bytes_accessed=20_000_000, transcendentals=0
        ),
        name="forward_student" if train else "forward_teacher",
    )(place, lengths, own, other, *far(*vectors, *weights))


def logits_kernel(student_ref, teacher_ref, table_ref, diff_ref, expo_ref, stats_ref, sums_ref):
    count = student_ref.shape[0]
    span = table_ref.shape[0] // 8
    lanes = lax.broadcasted_iota(jnp.int32, (count, 128), 1)
    packed = jnp.zeros((count, 128), jnp.float32)
    for part in range(8):
        where = slice(part * span, (part + 1) * span)
        table = table_ref[where, :]
        half_s = nt(student_ref[...], table)
        top_s = jnp.max(half_s, axis=1, keepdims=True)
        expo_s = jnp.exp(half_s - top_s)
        mass_s = jnp.sum(expo_s, axis=1, keepdims=True)
        half_t = nt(teacher_ref[...], table)
        top_t = jnp.max(half_t, axis=1, keepdims=True)
        expo_t = jnp.exp(half_t - top_t)
        mass_t = jnp.sum(expo_t, axis=1, keepdims=True)
        cross = jnp.sum(expo_t * (half_t - half_s), axis=1, keepdims=True)
        diff_ref[:, where] = (expo_s * (mass_t / mass_s) - expo_t).astype(jnp.bfloat16)
        expo_ref[:, where] = expo_t.astype(jnp.bfloat16)
        for index, column in enumerate((top_s, mass_s, top_t, mass_t, cross)):
            packed = jnp.where(lanes == 8 * index + part, column, packed)
    stats = packed.T
    stats_ref[0] = stats[:40]
    top_s, mass_s, top_t, mass_t, cross = (stats[8 * i : 8 * i + 8] for i in range(5))

    @pl.when(pl.program_id(0) == 0)
    def _():
        row = lax.broadcasted_iota(jnp.int32, sums_ref.shape, 0)
        sums_ref[...] = jnp.where((row == 0) | (row == 2), negative, 0.0)

    old = sums_ref[...]
    new_s = jnp.maximum(old[0:1], jnp.max(top_s, axis=0, keepdims=True))
    new_t = jnp.maximum(old[2:3], jnp.max(top_t, axis=0, keepdims=True))
    keep_s = jnp.exp(old[0:1] - new_s)
    keep_t = jnp.exp(old[2:3] - new_t)
    scale_s = jnp.exp(top_s - new_s)
    scale_t = jnp.exp(top_t - new_t)
    sums_ref[0:1] = new_s
    sums_ref[1:2] = old[1:2] * keep_s + jnp.sum(mass_s * scale_s, axis=0, keepdims=True)
    sums_ref[2:3] = new_t
    sums_ref[3:4] = old[3:4] * keep_t + jnp.sum(mass_t * scale_t, axis=0, keepdims=True)
    sums_ref[4:5] = old[4:5] * keep_t + jnp.sum(cross * scale_t, axis=0, keepdims=True)


def logits_phase(student, teacher, table):
    count, width = student.shape
    entries = table.shape[0]
    span = TABLE_SPAN
    steps = entries // span
    rows = pl.BlockSpec((count, width), lambda j: (0, 0))
    wide = pl.BlockSpec((count, span), lambda j: (0, j))
    return pl.pallas_call(
        logits_kernel,
        grid=(steps,),
        in_specs=[rows, rows, pl.BlockSpec((span, width), lambda j: (j, 0))],
        out_specs=[
            wide,
            wide,
            pl.BlockSpec((1, 40, count), lambda j: (j, 0, 0)),
            pl.BlockSpec((8, count), lambda j: (0, 0)),
        ],
        out_shape=[
            jax.ShapeDtypeStruct((count, entries), jnp.bfloat16),
            jax.ShapeDtypeStruct((count, entries), jnp.bfloat16),
            jax.ShapeDtypeStruct((steps, 40, count), jnp.float32),
            jax.ShapeDtypeStruct((8, count), jnp.float32),
        ],
        compiler_params=pltpu.CompilerParams(vmem_limit_bytes=24 << 20),
        cost_estimate=pl.CostEstimate(
            flops=4 * count * width * entries, bytes_accessed=60_000_000, transcendentals=0
        ),
        name="logits_phase",
    )(student, teacher, *far(table))


def joined_norms(own, other):
    top_s = jnp.maximum(own[0:1], other[0:1])
    top_t = jnp.maximum(own[2:3], other[2:3])
    own_t, other_t = jnp.exp(own[2:3] - top_t), jnp.exp(other[2:3] - top_t)
    mass_s = own[1:2] * jnp.exp(own[0:1] - top_s) + other[1:2] * jnp.exp(other[0:1] - top_s)
    mass_t = own[3:4] * own_t + other[3:4] * other_t
    cross = own[4:5] * own_t + other[4:5] * other_t
    norm_s = top_s + jnp.log(mass_s)
    norm_t = top_t + jnp.log(mass_t)
    return (norm_s, norm_t, cross / mass_t - norm_t + norm_s)


def gradient_kernel(
    half,
    diff_ref,
    expo_ref,
    table_ref,
    stats_ref,
    own_ref,
    other_ref,
    total_ref,
    low_ref,
    kl_ref,
    norms,
):
    step = pl.program_id(0)
    count = diff_ref.shape[0]
    mine = slice(half * count, (half + 1) * count)

    @pl.when(step == 0)
    def _():
        norm_s, norm_t, divergence = joined_norms(own_ref[:, mine], other_ref[:, mine])
        norms[0:1] = norm_s
        norms[1:2] = norm_t
        kl_ref[...] = divergence
        total_ref[...] = jnp.zeros_like(total_ref)

    top_s, mass_s, top_t, mass_t = (stats_ref[0, 8 * i : 8 * i + 8, mine] for i in range(4))
    first = 0.5 * jnp.exp(top_s - norms[0:1]) * mass_s / mass_t
    second = first - 0.5 * jnp.exp(top_t - norms[1:2])
    factors = jnp.concatenate([first, second, jnp.zeros((112, count), jnp.float32)], axis=0).T
    span = table_ref.shape[0] // 8
    total = total_ref[...]
    for group in range(2):
        pieces = []
        for part in range(4 * group, 4 * group + 4):
            where = slice(part * span, (part + 1) * span)
            pieces.append(
                (
                    diff_ref[:, where].astype(jnp.float32) * factors[:, part : part + 1]
                    + expo_ref[:, where].astype(jnp.float32) * factors[:, 8 + part : 9 + part]
                ).astype(jnp.bfloat16)
            )
        where = slice(4 * group * span, 4 * (group + 1) * span)
        total = total + dense(jnp.concatenate(pieces, axis=1), table_ref[where, :])
    total_ref[...] = total

    @pl.when(step == pl.num_programs(0) - 1)
    def _():
        low_ref[...] = total_ref[...].astype(jnp.bfloat16)


def gradient_phase(diff, expo, table, stats, own, other, half):
    count, entries = diff.shape
    rows = count // 2
    width = table.shape[1]
    span = TABLE_SPAN
    wide = pl.BlockSpec((rows, span), lambda j: (half, j))
    sums = pl.BlockSpec((8, count), lambda j: (0, 0))
    fixed = pl.BlockSpec((rows, width), lambda j: (0, 0))
    return pl.pallas_call(
        functools.partial(gradient_kernel, half),
        grid=(entries // span,),
        in_specs=[
            wide,
            wide,
            pl.BlockSpec((span, width), lambda j: (j, 0)),
            pl.BlockSpec((1, 40, count), lambda j: (j, 0, 0)),
            sums,
            sums,
        ],
        out_specs=[fixed, fixed, pl.BlockSpec((1, rows), lambda j: (0, 0))],
        out_shape=[
            jax.ShapeDtypeStruct((rows, width), jnp.float32),
            jax.ShapeDtypeStruct((rows, width), jnp.bfloat16),
            jax.ShapeDtypeStruct((1, rows), jnp.float32),
        ],
        scratch_shapes=[pltpu.VMEM((8, rows), jnp.float32)],
        compiler_params=pltpu.CompilerParams(vmem_limit_bytes=20 << 20),
        cost_estimate=pl.CostEstimate(
            flops=2 * count * width * entries, bytes_accessed=60_000_000, transcendentals=0
        ),
        name="gradient_second" if half else "gradient_first",
    )(diff, *far(expo, table), stats, own, other)


def position(device, masks):
    rest = masks[1:]
    place = jnp.int32(0) if not isinstance(device, int) else 0
    for index, mask in enumerate(rest):
        if isinstance(device, int):
            bit = (device // mask) % 2
        else:
            bit = lax.rem(lax.div(device, mask), 2)
        place = place + (bit << (len(rest) - 1 - index))
    return place


def place_shards(me, natural, keep, send, masks, first, shards, rows=slice(None)):
    mine = lax.rem(me, 2)
    place = position(me, masks)
    for pair in range(first // 2, (first + shards) // 2):
        target = lax.bitwise_xor(place, jnp.int32(position(2 * pair, masks)))
        keep[target, rows] = natural[2 * pair + mine, rows]
        send[target, rows] = natural[2 * pair + 1 - mine, rows]


def row_sums(value):
    return jnp.sum(value.astype(jnp.float32), axis=0, keepdims=True)


def back_to_norm(own_ref, other_ref, y_ref, gain):
    normed, scale = normalise(y_ref[...])
    grad = own_ref[...] + other_ref[...].astype(jnp.float32)
    return norm_back(normed, scale, as_row(gain), grad)


def feed_loads(wc_hbm, wc, slope_hbm, slope_v, rows, sems):
    hidden_width, width = wc.shape
    loads = []
    for part in range(hidden_width // width):
        span = pl.ds(part * width, width)
        loads.append(
            (
                pltpu.make_async_copy(wc_hbm.at[span], wc.at[span], sems.at[0, part]),
                pltpu.make_async_copy(
                    slope_hbm.at[rows, span], slope_v.at[:, span], sems.at[1, part]
                ),
            )
        )
    return loads


def feed_rows(dm, wc, slope_v, loads, dinner, rows, bias_out, bias_before):
    width = wc.shape[1]
    for part, pair in enumerate(loads):
        span = slice(part * width, (part + 1) * width)
        for load in pair:
            load.wait()
        value = nt(dm, wc[span, :]) * slope_v[:, span].astype(jnp.float32)
        value = value.astype(jnp.bfloat16)
        dinner[rows, span] = value
        before = 0.0 if bias_before is None else bias_before[:, span]
        bias_out[:, span] = before + row_sums(value)


def expand_loads(we_hbm, we, wao_hbm, wao, sems):
    width = we.shape[0]
    parts = we.shape[1] // width
    spans = [pl.ds(part * width, width) for part in range(parts)]
    return [
        pltpu.make_async_copy(we_hbm.at[:, span], we.at[:, span], sems.at[part])
        for part, span in enumerate(spans)
    ] + [pltpu.make_async_copy(wao_hbm, wao, sems.at[parts])]


def branch_rows(dinner, we, loads, after_ref, gain, dy):
    width = we.shape[0]
    dh2 = None
    for part, load in enumerate(loads[:-1]):
        span = slice(part * width, (part + 1) * width)
        load.wait()
        term = nt(dinner[:, span], we[:, span])
        dh2 = term if dh2 is None else dh2 + term
    normed, scale = normalise(after_ref[...])
    dafter = dy + norm_back(normed, scale, as_row(gain), dh2)
    return dafter, row_sums(dh2 * normed), row_sums(dh2)


def first_kernel(
    own_ref,
    other_ref,
    y_ref,
    after_ref,
    final_gain,
    second_gain,
    wc_hbm,
    we_hbm,
    wao_hbm,
    slope_hbm,
    dm_out,
    dinner_out,
    dafter_out,
    dbranch_out,
    dmixed_out,
    contract_bias_out,
    expand_bias_out,
    second_gain_out,
    second_shift_out,
    attend_bias_out,
    wc,
    we,
    wao,
    slope_v,
    feed_sem,
    branch_sem,
):
    count = own_ref.shape[0]
    feeding = feed_loads(wc_hbm, wc, slope_hbm, slope_v, pl.ds(0, count), feed_sem)
    branching = expand_loads(we_hbm, we, wao_hbm, wao, branch_sem)
    for pair in feeding:
        for load in pair:
            load.start()
    for load in branching:
        load.start()
    dy = back_to_norm(own_ref, other_ref, y_ref, final_gain)
    dm = dy.astype(jnp.bfloat16)
    dm_out[...] = dm
    contract_bias_out[...] = row_sums(dm)
    feed_rows(dm, wc, slope_v, feeding, dinner_out, slice(0, count), expand_bias_out, None)
    dafter, second_gain_out[...], second_shift_out[...] = branch_rows(
        dinner_out, we, branching, after_ref, second_gain, dy
    )
    dafter_out[...] = dafter
    dbranch = dafter.astype(jnp.bfloat16)
    dbranch_out[...] = dbranch
    attend_bias_out[...] = row_sums(dbranch)
    branching[-1].wait()
    dmixed_out[...] = nt(dbranch, wao[...]).astype(jnp.bfloat16)


def first_rows(own, other, y, after, final_gain, second_gain, wc, we, wao, slope):
    rows, width = own.shape
    hidden_width = wc.shape[0]
    low, full = jnp.bfloat16, jnp.float32
    parts = hidden_width // width

    def array(size, kind):
        return jax.ShapeDtypeStruct((rows, size), kind)

    def vector(size):
        return jax.ShapeDtypeStruct((1, size), full)

    top = pl.BlockSpec((rows, width), lambda i: (0, 0))
    return pl.pallas_call(
        first_kernel,
        grid=(1,),
        in_specs=[whole_vmem()] * 2 + [top] * 2 + [whole_vmem()] * 2 + [in_place()] * 4,
        out_specs=[whole_vmem()] * 10,
        out_shape=[
            array(width, low),
            array(hidden_width, low),
            array(width, full),
            array(width, low),
            array(width, low),
            vector(width),
            vector(hidden_width),
            vector(width),
            vector(width),
            vector(width),
        ],
        scratch_shapes=[
            pltpu.VMEM(wc.shape, low),
            pltpu.VMEM(we.shape, low),
            pltpu.VMEM(wao.shape, low),
            pltpu.VMEM((rows, hidden_width), low),
            pltpu.SemaphoreType.DMA((2, parts)),
            pltpu.SemaphoreType.DMA((parts + 1,)),
        ],
        compiler_params=pltpu.CompilerParams(vmem_limit_bytes=24 << 20),
        cost_estimate=pl.CostEstimate(
            flops=12_000_000_000, bytes_accessed=1_000_000, transcendentals=0
        ),
        name="first_rows",
    )(own, other, *far(y, after, final_gain, second_gain, wc, we, wao, slope))


def feed_kernel(
    place_ref,
    own_ref,
    other_ref,
    y_ref,
    final_gain,
    dm_first,
    normed_two_ref,
    contract_bias_first,
    expand_bias_first,
    wc_hbm,
    slope_hbm,
    active_hbm,
    dinner_hbm,
    cw_keep,
    cw_send,
    ew_keep,
    ew_send,
    dy_out,
    dinner_out,
    contract_bias_out,
    expand_bias_out,
    wc,
    slope_v,
    active_v,
    dinner_v,
    dm_v,
    cw_natural,
    ew_natural,
    feed_sem,
    load_sem,
    out_sem,
):
    me, blk = place_ref[0], place_ref[1]
    rows = own_ref.shape[0]
    second = slice(rows, 2 * rows)
    hidden_width, width = wc.shape
    parts = hidden_width // width
    part_width = width // 2
    shards = cw_natural.shape[0]
    chunk = width // shards
    feeding = feed_loads(wc_hbm, wc, slope_hbm, slope_v, pl.ds(rows, rows), feed_sem)
    early = pltpu.make_async_copy(dinner_hbm, dinner_v.at[pl.ds(0, rows)], load_sem.at[0])
    loads = [
        pltpu.make_async_copy(
            active_hbm.at[:, pl.ds(part * width, width)],
            active_v.at[:, pl.ds(part * width, width)],
            load_sem.at[1 + part],
        )
        for part in range(parts)
    ]
    for load in loads:
        load.start()
    for pair in feeding:
        for load in pair:
            load.start()
    early.start()
    dy = back_to_norm(own_ref, other_ref, y_ref, final_gain)
    dy_out[...] = dy
    dm = dy.astype(jnp.bfloat16)
    dm_v[:rows] = dm_first[...]
    dm_v[second] = dm
    contract_bias_out[...] = contract_bias_first[...] + row_sums(dm)
    dm_half = dm_v[:, pl.ds(pl.multiple_of(blk * part_width, part_width), part_width)]
    group = shards // parts
    for part in range(parts):
        span = slice(part * width, (part + 1) * width)
        loads[part].wait()
        value = tn(active_v[:, span], dm_half).astype(jnp.bfloat16)
        cw_natural[part * group : (part + 1) * group] = value.reshape(
            group, width // group, part_width
        )
        place_shards(me, cw_natural, cw_keep, cw_send, MASKS, part * group, group)
    feed_rows(dm, wc, slope_v, feeding, dinner_v, second, expand_bias_out, expand_bias_first)
    save = pltpu.make_async_copy(dinner_v.at[pl.ds(rows, rows)], dinner_out, out_sem.at[0])
    save.start()
    early.wait()
    for part in range(parts // 2):
        offset = pl.multiple_of(blk * (hidden_width // 2), width) + part * width
        value = tn(normed_two_ref[...], dinner_v[:, pl.ds(pl.multiple_of(offset, width), width)])
        value = value.astype(jnp.bfloat16)
        for half in range(2):
            row = (2 * part + half) * chunk
            ew_natural[:, row : row + chunk, :] = value[
                :, half * part_width : (half + 1) * part_width
            ].reshape(shards, chunk, part_width)
        rows_at = slice(2 * part * chunk, (2 * part + 2) * chunk)
        place_shards(me, ew_natural, ew_keep, ew_send, MASKS_B, 0, shards, rows_at)
    save.wait()


def feed_back(
    place, own, other, y, final_gain, dm, normed_two, biases, wc, slope, active, dinner, shards
):
    rows, width = own.shape
    count = 2 * rows
    hidden_width = wc.shape[0]
    parts = hidden_width // width
    low, full = jnp.bfloat16, jnp.float32
    height = hidden_width // shards
    half = jax.ShapeDtypeStruct((shards // 2, height, width // 2), low)
    bottom = pl.BlockSpec((rows, width), lambda i: (1, 0))
    return pl.pallas_call(
        feed_kernel,
        grid=(1,),
        in_specs=[scalars()]
        + [whole_vmem()] * 2
        + [bottom]
        + [whole_vmem()] * 5
        + [in_place()] * 4,
        out_specs=[whole_vmem()] * 5 + [in_place(), whole_vmem(), whole_vmem()],
        out_shape=[half] * 4
        + [
            jax.ShapeDtypeStruct((rows, width), full),
            jax.ShapeDtypeStruct((rows, hidden_width), low),
            jax.ShapeDtypeStruct((1, width), full),
            jax.ShapeDtypeStruct((1, hidden_width), full),
        ],
        scratch_shapes=[
            pltpu.VMEM(wc.shape, low),
            pltpu.VMEM((rows, hidden_width), low),
            pltpu.VMEM((count, hidden_width), low),
            pltpu.VMEM((count, hidden_width), low),
            pltpu.VMEM((count, width), low),
            pltpu.VMEM((shards, height, width // 2), low),
            pltpu.VMEM((shards, height, width // 2), low),
            pltpu.SemaphoreType.DMA((2, parts)),
            pltpu.SemaphoreType.DMA((1 + parts,)),
            pltpu.SemaphoreType.DMA((1,)),
        ],
        compiler_params=pltpu.CompilerParams(vmem_limit_bytes=34 << 20),
        cost_estimate=pl.CostEstimate(
            flops=12_000_000_000, bytes_accessed=1_000_000, transcendentals=0
        ),
        name="feed_back",
    )(
        place,
        own,
        other,
        *far(y, final_gain),
        dm,
        *far(normed_two),
        *biases,
        *far(wc, slope, active),
        dinner,
    )


def branch_kernel(
    place_ref,
    dy_ref,
    after_ref,
    mixed_ref,
    second_gain,
    dbranch_first,
    second_gain_first,
    second_shift_first,
    attend_bias_first,
    dinner_ref,
    we_hbm,
    wao_hbm,
    dafter_out,
    dmixed_out,
    attend_out,
    second_gain_out,
    second_shift_out,
    attend_bias_out,
    we,
    wao,
    dbranch_v,
    load_sem,
):
    blk = place_ref[1]
    loads = expand_loads(we_hbm, we, wao_hbm, wao, load_sem)
    for load in loads:
        load.start()
    rows, width = after_ref.shape
    part_width = width // 2
    dafter, gain_sum, shift_sum = branch_rows(
        dinner_ref, we, loads, after_ref, second_gain, dy_ref[...]
    )
    dafter_out[...] = dafter
    second_gain_out[...] = second_gain_first[...] + gain_sum
    second_shift_out[...] = second_shift_first[...] + shift_sum
    dbranch = dafter.astype(jnp.bfloat16)
    dbranch_v[:rows] = dbranch_first[...]
    dbranch_v[rows:] = dbranch
    attend_bias_out[...] = attend_bias_first[...] + row_sums(dbranch)
    loads[-1].wait()
    dmixed_out[...] = nt(dbranch, wao[...]).astype(jnp.bfloat16)
    part = dbranch_v[:, pl.ds(pl.multiple_of(blk * part_width, part_width), part_width)]
    attend_out[...] = tn(mixed_ref[...], part).astype(jnp.bfloat16).reshape(attend_out.shape)


def branch_back(place, dy, after, mixed, second_gain, dbranch, sums, dinner, we, wao, carry, shards):
    rows, width = dy.shape
    parts = we.shape[1] // width
    low, full = jnp.bfloat16, jnp.float32
    vector = jax.ShapeDtypeStruct((1, width), full)
    bottom = pl.BlockSpec((rows, width), lambda i: (1, 0))
    return pl.pallas_call(
        carrying(branch_kernel, 12, 6, len(carry)),
        grid=(1,),
        in_specs=[scalars(), whole_vmem(), bottom]
        + [whole_vmem()] * 7
        + [in_place()] * (2 + len(carry)),
        out_specs=[whole_vmem()] * 6 + [in_place()] * len(carry),
        input_output_aliases=aliases(12, 6, carry),
        out_shape=[
            jax.ShapeDtypeStruct((rows, width), full),
            jax.ShapeDtypeStruct((rows, width), low),
            jax.ShapeDtypeStruct((shards, width // shards, width // 2), low),
            vector,
            vector,
            vector,
        ]
        + shapes_of(carry),
        scratch_shapes=[
            pltpu.VMEM(we.shape, low),
            pltpu.VMEM(wao.shape, low),
            pltpu.VMEM((2 * rows, width), low),
            pltpu.SemaphoreType.DMA((parts + 1,)),
        ],
        compiler_params=pltpu.CompilerParams(vmem_limit_bytes=22 << 20),
        cost_estimate=pl.CostEstimate(
            flops=12_000_000_000, bytes_accessed=1_000_000, transcendentals=0
        ),
        name="branch_back",
    )(
        place,
        dy,
        *far(after, mixed, second_gain),
        dbranch,
        *sums,
        dinner,
        *far(we, wao),
        *carry,
    )


def attend_pair(block, query_ref, keys_ref, values_ref, probs_ref, dmixed_refs):
    count, pair = query_ref.shape
    query = query_ref[...] * jnp.bfloat16(0.125)
    zero = jnp.bfloat16(0.0)
    dkeys = jnp.zeros((count, pair), jnp.float32)
    dvalues = jnp.zeros((count, pair), jnp.float32)
    keys = keys_ref[...] * jnp.bfloat16(0.125)
    dqueries = []
    for piece in reversed(range(count // block)):
        span = slice(piece * block, (piece + 1) * block)
        reach = (piece + 1) * block
        dquery = jnp.zeros((block, pair), jnp.float32)
        add_keys = jnp.zeros((reach, pair), jnp.float32)
        add_values = jnp.zeros((reach, pair), jnp.float32)
        for which in range(2):
            mask = head_mask((block, pair), which)
            grad = jnp.where(mask, dmixed_refs[piece][...], zero)
            mine = jnp.where(mask, query[span], zero)
            probs = probs_ref[which, :reach, span]
            dprobs = nt(values_ref[:reach], grad)
            wide = probs.astype(jnp.float32)
            product = wide * dprobs
            balance = jnp.sum(product, axis=0, keepdims=True)
            dscores = (product - wide * balance).astype(jnp.bfloat16)
            add_values = add_values + dense(probs, grad)
            add_keys = add_keys + dense(dscores, mine)
            dquery = dquery + tn(
                dscores, jnp.where(head_mask((reach, pair), which), keys[:reach], zero)
            )
        dqueries.insert(0, dquery.astype(jnp.bfloat16))
        if reach < count:
            pad = jnp.zeros((count - reach, pair), jnp.float32)
            add_keys = jnp.concatenate([add_keys, pad], axis=0)
            add_values = jnp.concatenate([add_values, pad], axis=0)
        dkeys = dkeys + add_keys
        dvalues = dvalues + add_values
    return (
        jnp.concatenate(dqueries, axis=0),
        dkeys.astype(jnp.bfloat16),
        dvalues.astype(jnp.bfloat16),
    )


def attend_kernel(
    block,
    _,
    query_ref,
    keys_ref,
    values_ref,
    probs_ref,
    dmixed_first,
    dmixed_second,
    dq_ref,
    dk_ref,
    dv_ref,
):
    dmixed = (dmixed_first, dmixed_second)
    grads = attend_pair(block, query_ref, keys_ref, values_ref, probs_ref, dmixed)
    for ref, grad in zip((dq_ref, dk_ref, dv_ref), grads):
        ref[...] = grad


def project_kernel(
    block,
    place_ref,
    query_ref,
    keys_ref,
    values_ref,
    probs_ref,
    dmixed_first,
    dmixed_second,
    normed_ref,
    attend_ref,
    dq_ref,
    dk_ref,
    dv_ref,
    keep,
    send,
    natural,
):
    step = pl.program_id(0)
    pair = query_ref.shape[1]
    column = pl.ds(pl.multiple_of(step * pair, pair), pair)
    dmixed = (dmixed_first, dmixed_second)
    grads = attend_pair(block, query_ref, keys_ref, values_ref, probs_ref, dmixed)
    for ref, grad in zip((dq_ref, dk_ref, dv_ref), grads):
        ref[:, column] = grad

    @pl.when(step == pl.num_programs(0) - 1)
    def _():
        me = place_ref[0]
        shards = natural.shape[0]
        width = normed_ref.shape[1]
        part_width = width // 2
        chunk = width // shards
        natural[:, :chunk, :] = attend_ref[...]
        for part, ref in enumerate((dq_ref, dk_ref, dv_ref)):
            value = tn(normed_ref[...], ref[...]).astype(jnp.bfloat16)
            natural[:, (part + 1) * chunk : (part + 2) * chunk, :] = value.reshape(
                shards, chunk, part_width
            )
            rows = slice(0, 2 * chunk) if part == 0 else slice((part + 1) * chunk, (part + 2) * chunk)
            place_shards(me, natural, keep, send, MASKS, 0, shards, rows)


def attend_specs(joined, dmixed, own):
    rows, width = dmixed[0].shape
    count = 2 * rows
    pair = 2 * HEAD_DIM
    pairs = width // pair
    half = pairs // 2

    def first(place_ref):
        blk = place_ref[1]
        return half * (blk if own else 1 - blk)

    def column(height, offset):
        return pl.BlockSpec((height, pair), lambda p, place_ref: (0, offset + first(place_ref) + p))

    return half, [
        column(count, 0),
        column(count, pairs),
        column(count, 2 * pairs),
        pl.BlockSpec((2, count, count), lambda p, place_ref: (first(place_ref) + p, 0, 0)),
        column(rows, 0),
        column(rows, 0),
    ]


def attend_back(place, joined, probs, dmixed, carry, block):
    width = dmixed[0].shape[1]
    count = joined.shape[0]
    half, specs = attend_specs(joined, dmixed, False)
    result = pl.BlockSpec((count, 2 * HEAD_DIM), lambda p, place_ref: (0, p))
    return pl.pallas_call(
        carrying(functools.partial(attend_kernel, block), 7, 3, len(carry)),
        grid_spec=pltpu.PrefetchScalarGridSpec(
            num_scalar_prefetch=1,
            grid=(half,),
            in_specs=specs + [in_place()] * len(carry),
            out_specs=[result] * 3 + [in_place()] * len(carry),
        ),
        out_shape=[jax.ShapeDtypeStruct((count, width // 2), jnp.bfloat16)] * 3
        + shapes_of(carry),
        input_output_aliases=aliases(7, 3, carry),
        compiler_params=pltpu.CompilerParams(vmem_limit_bytes=16 << 20),
        cost_estimate=pl.CostEstimate(
            flops=12_000_000_000, bytes_accessed=1_000_000, transcendentals=0
        ),
        name="attend_back",
    )(place, *far(joined, joined, joined, probs), *dmixed, *carry)


def project_back(place, joined, probs, dmixed, normed, attend, carry, block, shards):
    count, width = normed.shape
    chunk = width // shards
    half, specs = attend_specs(joined, dmixed, True)
    result = pl.BlockSpec((count, width // 2), lambda p, place_ref: (0, 0))
    piece = jax.ShapeDtypeStruct((shards // 2, 4 * chunk, width // 2), jnp.bfloat16)
    specs = specs + [
        pl.BlockSpec(normed.shape, lambda p, place_ref: (0, 0)),
        pl.BlockSpec(attend.shape, lambda p, place_ref: (0, 0, 0)),
    ]
    return pl.pallas_call(
        carrying(functools.partial(project_kernel, block), 9, 5, len(carry)),
        grid_spec=pltpu.PrefetchScalarGridSpec(
            num_scalar_prefetch=1,
            grid=(half,),
            in_specs=specs + [in_place()] * len(carry),
            out_specs=[result] * 3 + [whole_vmem()] * 2 + [in_place()] * len(carry),
            scratch_shapes=[pltpu.VMEM((shards, 4 * chunk, width // 2), jnp.bfloat16)],
        ),
        out_shape=[jax.ShapeDtypeStruct((count, width // 2), jnp.bfloat16)] * 3
        + [piece, piece]
        + shapes_of(carry),
        input_output_aliases=aliases(9, 5, carry),
        compiler_params=pltpu.CompilerParams(vmem_limit_bytes=18 << 20),
        cost_estimate=pl.CostEstimate(
            flops=12_000_000_000, bytes_accessed=1_000_000, transcendentals=0
        ),
        name="project_back",
    )(place, *far(joined, joined, joined, probs), *dmixed, *far(normed), attend, *carry)


def input_kernel(
    place_ref,
    own_ref,
    other_ref,
    dq_own,
    dk_own,
    dv_own,
    dq_other,
    dk_other,
    dv_other,
    dafter_first,
    dafter_second,
    first_gain,
    attend_bias_grad,
    second_gain_grad,
    second_shift_grad,
    expand_bias_grad,
    contract_bias_grad,
    wpi_hbm,
    grad_out,
    keep,
    send,
    wpi,
    joined_v,
    x_v,
    grad_v,
    load_sem,
):
    me, blk = place_ref[0], place_ref[1]
    load = pltpu.make_async_copy(wpi_hbm, wpi, load_sem.at[0])
    load.start()
    count, width = x_v.shape
    part_width = width // 2
    shards = 2 * keep.shape[0]
    in_stream_order(x_v, own_ref, other_ref, blk)
    for side, group in ((blk, (dq_own, dk_own, dv_own)), (1 - blk, (dq_other, dk_other, dv_other))):
        for part, ref in enumerate(group):
            offset = part * width + side * part_width
            joined_v[:, pl.ds(pl.multiple_of(offset, part_width), part_width)] = ref[...]
    normed, scale = normalise(x_v[...])
    load.wait()
    dh1 = nt(joined_v[...], wpi[...])
    sums = jnp.sum(joined_v[...].astype(jnp.float32), axis=0, keepdims=True)
    vectors = [
        jnp.sum(dh1 * normed, axis=0, keepdims=True),
        jnp.sum(dh1, axis=0, keepdims=True),
        jnp.concatenate([sums[:, :width], sums[:, 2 * width :]], axis=1),
        attend_bias_grad[...],
        second_gain_grad[...],
        second_shift_grad[...],
        expand_bias_grad[...],
        contract_bias_grad[...],
    ]
    mine = lax.rem(me, 2)
    place = position(me, MASKS)
    for shard in range(shards):
        rows = []
        for vector in vectors:
            size = vector.shape[1] // shards
            piece = vector[:, shard * size : (shard + 1) * size]
            rows.append(jnp.concatenate([piece, jnp.zeros((1, 256 - size), jnp.float32)], axis=1))
        value = jnp.concatenate(rows, axis=0)
        target = lax.bitwise_xor(place, jnp.int32(position(shard, MASKS)))

        @pl.when(mine == shard % 2)
        def _():
            keep[target] = value

        @pl.when(mine != shard % 2)
        def _():
            send[target] = value

    rows = own_ref.shape[0]
    grad_v[...] = norm_back(normed, scale, as_row(first_gain), dh1)
    grad_v[:rows] += dafter_first[...]
    grad_v[rows:] += dafter_second[...]
    grad_out[...] = grad_v[pl.ds(pl.multiple_of(blk * rows, rows), rows), :]


def input_back(place, own, other, parts, dafter, gain, vectors, wpi, carry, shards):
    rows, width = own.shape
    count = 2 * rows
    low, full = jnp.bfloat16, jnp.float32
    half = jax.ShapeDtypeStruct((shards // 2, len(vectors) + 3, 256), full)
    return pl.pallas_call(
        carrying(input_kernel, 18, 3, len(carry)),
        in_specs=[scalars()] + [whole_vmem()] * 16 + [in_place()] * (1 + len(carry)),
        out_specs=[whole_vmem()] * 3 + [in_place()] * len(carry),
        out_shape=[jax.ShapeDtypeStruct((rows, width), full), half, half] + shapes_of(carry),
        input_output_aliases=aliases(18, 3, carry),
        scratch_shapes=[
            pltpu.VMEM(wpi.shape, low),
            pltpu.VMEM((count, 3 * width), low),
            pltpu.VMEM((count, width), full),
            pltpu.VMEM((count, width), full),
            pltpu.SemaphoreType.DMA((1,)),
        ],
        compiler_params=pltpu.CompilerParams(vmem_limit_bytes=24 << 20),
        cost_estimate=pl.CostEstimate(
            flops=12_000_000_000, bytes_accessed=1_000_000, transcendentals=0
        ),
        name="input_back",
    )(
        place, *far(own, other), *parts, *dafter, *far(gain), *vectors, *far(wpi), *carry
    )


def across(value, mask):
    return lax.ppermute(value, "dp", [(i, i ^ mask) for i in range(lax.axis_size("dp"))])


def halve(keep, received):
    half = keep.shape[0] // 2
    return (keep[:half] + received[:half], keep[half:] + received[half:])


def merge_kernel(layout, *refs):
    total = sum(1 + parts for parts in layout)
    inputs, outputs = list(refs[:total]), list(refs[total:])
    done = 0
    for parts in layout:
        keep = inputs.pop(0)
        half = keep.shape[0] // 2
        if half == 0:
            targets = [(outputs[-1].at[done : done + 1], slice(0, 1))]
            done += 1
        else:
            targets = [(outputs.pop(0), slice(0, half)), (outputs.pop(0), slice(half, 2 * half))]
        row = 0
        for _ in range(parts):
            got = inputs.pop(0)
            rows = slice(row, row + got.shape[1])
            row = rows.stop
            for target, which in targets:
                target[:, rows] = keep[which, rows] + got[which]


def merge(*pairs):
    shapes, finals = [], [pair[0] for pair in pairs if pair[0].shape[0] == 1]
    for keep, *_ in pairs:
        if keep.shape[0] > 1:
            shapes += [jax.ShapeDtypeStruct((keep.shape[0] // 2, *keep.shape[1:]), keep.dtype)] * 2
    if finals:
        shapes.append(jax.ShapeDtypeStruct((len(finals), *finals[0].shape[1:]), finals[0].dtype))
    arrays = [array for pair in pairs for array in pair]
    return pl.pallas_call(
        functools.partial(merge_kernel, [len(pair) - 1 for pair in pairs]),
        in_specs=[whole_vmem()] * len(arrays),
        out_specs=[whole_vmem()] * len(shapes),
        out_shape=shapes,
        compiler_params=pltpu.CompilerParams(vmem_limit_bytes=16 << 20),
        cost_estimate=pl.CostEstimate(flops=1_000_000, bytes_accessed=1_000_000, transcendentals=0),
        name="merge",
    )(*arrays)


def swap(value):
    return lax.ppermute(value, "blk", [(0, 1), (1, 0)])


def both_halves(own, other, blk):
    return jnp.where(
        blk == 0,
        jnp.concatenate([own, other], axis=-1),
        jnp.concatenate([other, own], axis=-1),
    ).astype(jnp.float32)


def local_pair(hidden, doc_lengths, *arrays):
    student, teacher = arrays[:12], arrays[12:24]
    final_gain, final_shift, table = arrays[24:]
    rows, width = hidden.shape
    shards = lax.axis_size("dp")
    blk = lax.axis_index("blk")
    place = jnp.stack([lax.axis_index("dp"), blk]).astype(jnp.int32)
    other = swap(hidden)
    def block(train, params):
        gain, shift, wpi, qvb, wao, bao, gain_two, shift_two, we, be, wc, bc = params
        vectors = (gain, shift, qvb, bao, gain_two, shift_two, be, bc, final_gain, final_shift)
        return forward(
            train,
            place,
            doc_lengths,
            hidden,
            other,
            vectors,
            (wpi, wao, we, wc),
        )

    (rows_t,) = block(False, teacher)
    rows_s, normed, joined, probs, mixed, after, normed_two, slope, active, y = block(True, student)
    diff, expo, stats, sums = logits_phase(rows_s, rows_t, table)
    gain, shift, wpi, qvb, wao, bao, gain_two, shift_two, we, be, wc, bc = student
    sums_other = swap(sums)
    own_first, low_first, kl_first = gradient_phase(diff, expo, table, stats, sums, sums_other, 0)
    got_first = swap(low_first)
    own_second, low_second, kl_second = gradient_phase(
        diff, expo, table, stats, sums, sums_other, 1
    )
    got_second = swap(low_second)
    dm, dinner, dafter_first, dbranch, dmixed_first, dbc, dbe, *branch_sums = first_rows(
        own_first, got_first, y, after, final_gain, gain_two, wc, we, wao, slope
    )
    cw_keep, cw_send, ew_keep, ew_send, dy, dinner, dbc, dbe = feed_back(
        place,
        own_second,
        got_second,
        y,
        final_gain,
        dm,
        normed_two,
        (dbc, dbe),
        wc,
        slope,
        active,
        dinner,
        shards,
    )
    cw_got = across(cw_send, MASKS[0])
    ew_got = across(ew_send, MASKS_B[0])
    dafter_second, dmixed_second, attend, dgain_two, dshift_two, dbao, cw_keep, ew_keep = (
        branch_back(
            place,
            dy,
            after,
            mixed,
            gain_two,
            dbranch,
            branch_sums,
            dinner,
            we,
            wao,
            (cw_keep, ew_keep),
            shards,
        )
    )
    dafter, dmixed = (dafter_first, dafter_second), (dmixed_first, dmixed_second)
    cw_keep, cw_send = halve(cw_keep, cw_got)
    cw_got = across(cw_send, MASKS[1])
    ew_keep, ew_send = halve(ew_keep, ew_got)
    ew_got = across(ew_send, MASKS_B[1])
    *own_grads, keep, send, cw_keep, ew_keep = project_back(
        place, joined, probs, dmixed, normed, attend, (cw_keep, ew_keep), rows, shards
    )
    got = across(send, MASKS[0])
    cw_keep, cw_send, ew_keep, ew_send = merge((cw_keep, cw_got), (ew_keep, ew_got))
    cw_got = across(cw_send, MASKS[2])
    ew_got = across(ew_send, MASKS_B[2])
    *other_grads, keep, cw_keep, ew_keep = attend_back(
        place, joined, probs, dmixed, (keep, cw_keep, ew_keep), rows
    )
    keep, send, cw_keep, cw_send, ew_keep, ew_send = merge(
        (keep, got), (cw_keep, cw_got), (ew_keep, ew_got)
    )
    got = across(send, MASKS[1])
    cw_got = across(cw_send, MASKS[3])
    ew_got = across(ew_send, MASKS_B[3])
    input_grad, vector_keep, vector_send, keep, cw_keep, ew_keep = input_back(
        place,
        hidden,
        other,
        (*own_grads, *other_grads),
        dafter,
        gain,
        (dbao, dgain_two, dshift_two, dbe, dbc),
        wpi,
        (keep, cw_keep, ew_keep),
        shards,
    )
    vector_got = across(vector_send, MASKS[0])
    keep, send, vector_keep, vector_send, both = merge(
        (keep, got), (cw_keep, cw_got), (ew_keep, ew_got), (vector_keep, vector_got)
    )
    got, both_other = across(send, MASKS[2]), swap(both)
    vector_got = across(vector_send, MASKS[1])
    keep, send, vector_keep, vector_send = merge((keep, got), (vector_keep, vector_got))
    got, vector_got = across(send, MASKS[3]), across(vector_send, MASKS[2])
    vector_keep, vector_send, last = merge((keep, got), (vector_keep, vector_got))
    last = last[0]
    last_other = swap(last)
    vectors = (vector_keep + across(vector_send, MASKS[3]))[0]
    cw, ew, cw_other, ew_other = both[0], both[1], both_other[0], both_other[1]
    chunk = width // shards

    def wide(own, other):
        own, other = (part.reshape(-1, chunk, part.shape[1]) for part in (own, other))
        order = [own[i] for i in range(own.shape[0])], [other[i] for i in range(own.shape[0])]
        return order

    grad_cw = both_halves(cw, cw_other, blk)
    own, other = wide(ew, ew_other)
    grad_ew = both_halves(jnp.concatenate(own, axis=1), jnp.concatenate(other, axis=1), blk)
    own, other = wide(last, last_other)
    grad_ao = both_halves(own[0], other[0], blk)
    grad_pi = jnp.concatenate([both_halves(own[i], other[i], blk) for i in (1, 2, 3)], axis=1)
    sizes = (chunk, chunk, 2 * chunk, chunk, chunk, chunk, be.shape[0] // shards, chunk)
    dgain, dshift, dqvb, dbao, dgain_two, dshift_two, dbe, dbc = (
        vectors[index, :size] for index, size in enumerate(sizes)
    )
    return (
        jnp.where(blk == 0, kl_first[0], kl_second[0]),
        input_grad,
        dgain,
        dshift,
        grad_pi,
        dqvb,
        grad_ao,
        dbao,
        dgain_two,
        dshift_two,
        grad_ew,
        dbe,
        grad_cw,
        dbc,
    )


def solution(mesh):
    pair = mesh.shape["dp"] == 16 and mesh.shape["blk"] == 2
    return jax.shard_map(
        local_pair if pair else local_general,
        mesh=mesh,
        in_specs=(
            P(("dp", "blk"), None),
            P("dp", None),
            P(),
            P(),
            P(),
            P(),
            P(),
            P(),
            P(),
            P(),
            P(),
            P(),
            P(),
            P(),
            P(),
            P(),
            P(),
            P(),
            P(),
            P(),
            P(),
            P(),
            P(),
            P(),
            P(),
            P(),
            P(),
            P(),
            P("blk", None),
        ),
        out_specs=(
            P(("dp", "blk")),
            P(("dp", "blk"), None),
            P("dp"),
            P("dp"),
            P("dp", None),
            P("dp"),
            P("dp", None),
            P("dp"),
            P("dp"),
            P("dp"),
            P("dp", None),
            P("dp"),
            P("dp", None),
            P("dp"),
        ),
        check_vma=False,
    )
```

```python
import functools

import jax
import jax.numpy as jnp
from jax import lax
from jax.experimental import pallas as pl
from jax.experimental.pallas import tpu as pltpu
from jax.sharding import PartitionSpec as P

HEADS = 12
HEAD_DIM = 64
TABLE_SPAN = 2048
SPLIT_STEPS = 4
MASKS = (1, 2, 4, 8)
MASKS_B = (1, 4, 2, 8)


negative = -1e30


def layer_norm(value, gain, shift):
    centre = value - jnp.mean(value, axis=-1, keepdims=True)
    return (
        centre * lax.rsqrt(jnp.mean(centre * centre, axis=-1, keepdims=True) + 1e-05) * gain + shift
    )


def doc_numbers(lengths, count):
    ends = jnp.cumsum(lengths)
    places = jnp.arange(count, dtype=jnp.int32)
    return jnp.sum((places[:, None] >= ends[None, :]).astype(jnp.int32), axis=1)


def dense(left, right):
    return jnp.dot(left, right, preferred_element_type=jnp.float32)


def split_heads(value):
    return value.reshape(value.shape[0], HEADS, HEAD_DIM)


def input_side(inputs, gain, shift, project_in, qv_bias):
    width = inputs.shape[1]
    normed = layer_norm(inputs, gain, shift).astype(jnp.bfloat16)
    bias = jnp.concatenate([qv_bias[:width], jnp.zeros((width,), jnp.float32), qv_bias[width:]])
    joined = (dense(normed, project_in) + bias).astype(jnp.bfloat16)
    return (normed, joined[:, :width], joined[:, width : 2 * width], joined[:, 2 * width :])


def output_side(
    inputs,
    mixed_low,
    attend_out,
    attend_bias,
    second_gain,
    second_shift,
    expand_weight,
    expand_bias,
    contract_weight,
    contract_bias,
):
    after = inputs + dense(mixed_low, attend_out) + attend_bias
    normed = layer_norm(after, second_gain, second_shift).astype(jnp.bfloat16)
    inner = dense(normed, expand_weight) + expand_bias
    active = jax.nn.gelu(inner, approximate=True).astype(jnp.bfloat16)
    final = after + dense(active, contract_weight) + contract_bias
    return (after, normed, inner, active, final)


def online(state, query, keys, values, allowed):
    top, mass, summed = state
    scores = (
        jnp.einsum(
            "qhd,khd->hqk",
            split_heads(query),
            split_heads(keys),
            preferred_element_type=jnp.float32,
        )
        * 0.125
    )
    scores = jnp.where(allowed[None], scores, negative)
    new_top = jnp.maximum(top, jnp.max(scores, axis=-1))
    factor = jnp.exp(top - new_top)
    weights = jnp.where(allowed[None], jnp.exp(scores - new_top[..., None]), 0.0)
    mass = mass * factor + jnp.sum(weights, axis=-1)
    summed = summed * factor[..., None] + jnp.einsum(
        "hqk,khd->hqd",
        weights.astype(jnp.bfloat16),
        split_heads(values),
        preferred_element_type=jnp.float32,
    )
    return (new_top, mass, summed)


def score_grads(query_heads, grad_heads, log_norm, balance, key_block, value_block, allowed):
    scores = (
        jnp.einsum("qhd,khd->hqk", query_heads, key_block, preferred_element_type=jnp.float32)
        * 0.125
    )
    probs = jnp.where(allowed[None], jnp.exp(scores - log_norm[..., None]), 0.0)
    grad_probs = jnp.einsum(
        "qhd,khd->hqk", grad_heads, value_block, preferred_element_type=jnp.float32
    )
    grad_scores = (probs * (grad_probs - balance[..., None])).astype(jnp.bfloat16)
    return (probs, grad_scores)


def partial_stats(rows_teacher, rows_student, table):
    half_t = jnp.einsum("rd,vd->rv", rows_teacher, table, preferred_element_type=jnp.float32) * 0.5
    half_s = jnp.einsum("rd,vd->rv", rows_student, table, preferred_element_type=jnp.float32) * 0.5
    top_t = jnp.max(half_t, axis=-1)
    expo_t = jnp.exp(half_t - top_t[:, None])
    top_s = jnp.max(half_s, axis=-1)
    return (
        top_t,
        jnp.sum(expo_t, axis=-1),
        jnp.sum(expo_t * (half_t - half_s), axis=-1),
        top_s,
        jnp.sum(jnp.exp(half_s - top_s[:, None]), axis=-1),
    )


def combine(first_stats, second_stats):
    top_t = jnp.maximum(first_stats[0], second_stats[0])
    right_weight = jnp.exp(second_stats[0] - top_t)
    top_s = jnp.maximum(first_stats[3], second_stats[3])
    return (
        top_t,
        second_stats[1] * right_weight,
        second_stats[2] * right_weight,
        top_s,
        second_stats[4] * jnp.exp(second_stats[3] - top_s),
    )


def row_gradient(rows_teacher, rows_student, table, norm_t, norm_s):
    half_t = jnp.einsum("rd,vd->rv", rows_teacher, table, preferred_element_type=jnp.float32) * 0.5
    half_s = jnp.einsum("rd,vd->rv", rows_student, table, preferred_element_type=jnp.float32) * 0.5
    change = ((jnp.exp(half_s - norm_s[:, None]) - jnp.exp(half_t - norm_t[:, None])) * 0.5).astype(
        jnp.bfloat16
    )
    return dense(change, table)


def local_general(
    hidden,
    doc_lengths,
    student_first_gain,
    student_first_shift,
    student_project_in,
    student_query_value_bias,
    student_attend_out,
    student_attend_bias,
    student_second_gain,
    student_second_shift,
    student_expand_weight,
    student_expand_bias,
    student_contract_weight,
    student_contract_bias,
    teacher_first_gain,
    teacher_first_shift,
    teacher_project_in,
    teacher_query_value_bias,
    teacher_attend_out,
    teacher_attend_bias,
    teacher_second_gain,
    teacher_second_shift,
    teacher_expand_weight,
    teacher_expand_bias,
    teacher_contract_weight,
    teacher_contract_bias,
    final_gain,
    final_shift,
    embedding,
):
    rows, width = hidden.shape
    blocks = lax.axis_size("blk")
    stream = rows * blocks
    first = lax.axis_index("blk") * rows
    last_place = first + rows - 1
    docs = doc_numbers(doc_lengths[0], stream)
    own_places = first + jnp.arange(rows, dtype=jnp.int32)
    own_docs = lax.dynamic_slice_in_dim(docs, first, rows)
    inputs = hidden.astype(jnp.float32)
    normed_s, query_s, keys_s, values_s = input_side(
        inputs,
        student_first_gain,
        student_first_shift,
        student_project_in,
        student_query_value_bias,
    )
    normed_t, query_t, keys_t, values_t = input_side(
        inputs,
        teacher_first_gain,
        teacher_first_shift,
        teacher_project_in,
        teacher_query_value_bias,
    )

    def allowed_for(begin):
        key_places = begin + jnp.arange(rows, dtype=jnp.int32)
        key_docs = lax.dynamic_slice_in_dim(docs, begin, rows)
        return (key_places[None, :] <= own_places[:, None]) & (
            key_docs[None, :] == own_docs[:, None]
        )

    start_state = (
        jnp.full((HEADS, rows), negative, jnp.float32),
        jnp.zeros((HEADS, rows), jnp.float32),
        jnp.zeros((HEADS, rows, HEAD_DIM), jnp.float32),
    )
    carry = (start_state, start_state)
    pieces = (
        lax.all_gather(keys_s, "blk", axis=0, tiled=True),
        lax.all_gather(values_s, "blk", axis=0, tiled=True),
        lax.all_gather(keys_t, "blk", axis=0, tiled=True),
        lax.all_gather(values_t, "blk", axis=0, tiled=True),
    )
    count = pieces[0].shape[0]
    stacked = tuple((member.reshape(count // rows, rows, width) for member in pieces))
    begins = rows * jnp.arange(count // rows, dtype=jnp.int32)

    def step(state, item):
        piece_keys_s, piece_values_s, piece_keys_t, piece_values_t, begin = item

        def step_compute(inner_state):
            allowed = allowed_for(begin)
            return (
                online(inner_state[0], query_s, piece_keys_s, piece_values_s, allowed),
                online(inner_state[1], query_t, piece_keys_t, piece_values_t, allowed),
            )

        return (
            lax.cond(begin <= last_place, step_compute, lambda inner_state: inner_state, state),
            None,
        )

    carry, _ = lax.scan(step, carry, stacked + (begins,))
    state_s, state_t = carry
    out_heads_s = state_s[2] / state_s[1][..., None]
    attn_norm = state_s[0] + jnp.log(state_s[1])
    mixed_low_s = out_heads_s.transpose(1, 0, 2).reshape(rows, width).astype(jnp.bfloat16)
    mixed_low_t = (
        (state_t[2] / state_t[1][..., None])
        .transpose(1, 0, 2)
        .reshape(rows, width)
        .astype(jnp.bfloat16)
    )
    after_s, normed_two_s, inner_s, active_s, final_s = output_side(
        inputs,
        mixed_low_s,
        student_attend_out,
        student_attend_bias,
        student_second_gain,
        student_second_shift,
        student_expand_weight,
        student_expand_bias,
        student_contract_weight,
        student_contract_bias,
    )
    after_t, normed_two_t, inner_t, active_t, final_t = output_side(
        inputs,
        mixed_low_t,
        teacher_attend_out,
        teacher_attend_bias,
        teacher_second_gain,
        teacher_second_shift,
        teacher_expand_weight,
        teacher_expand_bias,
        teacher_contract_weight,
        teacher_contract_bias,
    )
    rows_s = layer_norm(final_s, final_gain, final_shift).astype(jnp.bfloat16)
    rows_t = layer_norm(final_t, final_gain, final_shift).astype(jnp.bfloat16)
    identity = (
        jnp.full((rows,), negative, jnp.float32),
        jnp.zeros((rows,), jnp.float32),
        jnp.zeros((rows,), jnp.float32),
        jnp.full((rows,), negative, jnp.float32),
        jnp.zeros((rows,), jnp.float32),
    )
    merged = combine(
        identity,
        partial_stats(rows_t, rows_s, lax.all_gather(embedding, "blk", axis=0, tiled=True)),
    )
    norm_t = merged[0] + jnp.log(merged[1])
    norm_s = merged[3] + jnp.log(merged[4])
    kl_rows = merged[2] / merged[1] - norm_t + norm_s
    grad_final = row_gradient(
        rows_t, rows_s, lax.all_gather(embedding, "blk", axis=0, tiled=True), norm_t, norm_s
    )
    _, final_back = jax.vjp(layer_norm, final_s, final_gain, final_shift)
    grad_y = final_back(grad_final)[0]
    grad_m = grad_y.astype(jnp.bfloat16)
    grad_contract_weight = jnp.einsum(
        "rf,rd->fd", active_s, grad_m, preferred_element_type=jnp.float32
    )
    grad_contract_bias = jnp.sum(grad_m.astype(jnp.float32), axis=0)
    grad_active = jnp.einsum(
        "rd,fd->rf", grad_m, student_contract_weight, preferred_element_type=jnp.float32
    )
    _, gelu_back = jax.vjp(lambda value: jax.nn.gelu(value, approximate=True), inner_s)
    grad_inner = gelu_back(grad_active)[0].astype(jnp.bfloat16)
    grad_expand_weight = jnp.einsum(
        "rd,rf->df", normed_two_s, grad_inner, preferred_element_type=jnp.float32
    )
    grad_expand_bias = jnp.sum(grad_inner.astype(jnp.float32), axis=0)
    grad_normed_two = jnp.einsum(
        "rf,df->rd", grad_inner, student_expand_weight, preferred_element_type=jnp.float32
    )
    _, second_back = jax.vjp(layer_norm, after_s, student_second_gain, student_second_shift)
    grad_after_norm, grad_second_gain, grad_second_shift = second_back(grad_normed_two)
    grad_after = grad_y + grad_after_norm
    grad_branch = grad_after.astype(jnp.bfloat16)
    grad_attend_out = jnp.einsum(
        "rc,rd->cd", mixed_low_s, grad_branch, preferred_element_type=jnp.float32
    )
    grad_attend_bias = jnp.sum(grad_branch.astype(jnp.float32), axis=0)
    grad_mixed = jnp.einsum(
        "rd,cd->rc", grad_branch, student_attend_out, preferred_element_type=jnp.float32
    ).astype(jnp.bfloat16)
    keys_all, values_all = (
        lax.all_gather(keys_s, "blk", axis=0, tiled=True),
        lax.all_gather(values_s, "blk", axis=0, tiled=True),
    )
    grad_heads = split_heads(grad_mixed)
    query_heads = split_heads(query_s)
    balance = jnp.sum(grad_heads.astype(jnp.float32).transpose(1, 0, 2) * out_heads_s, axis=-1)
    begins = rows * jnp.arange(blocks, dtype=jnp.int32)
    zero_query = jnp.zeros((rows, HEADS, HEAD_DIM), jnp.float32)

    def back_step(grad_query, begin):
        key_block = split_heads(lax.dynamic_slice_in_dim(keys_all, begin, rows, 0))
        value_block = split_heads(lax.dynamic_slice_in_dim(values_all, begin, rows, 0))

        def back_compute(total):
            probs, grad_scores = score_grads(
                query_heads,
                grad_heads,
                attn_norm,
                balance,
                key_block,
                value_block,
                allowed_for(begin),
            )
            total = (
                total
                + jnp.einsum(
                    "hqk,khd->qhd", grad_scores, key_block, preferred_element_type=jnp.float32
                )
                * 0.125
            )
            grad_keys = (
                jnp.einsum(
                    "hqk,qhd->khd", grad_scores, query_heads, preferred_element_type=jnp.float32
                )
                * 0.125
            )
            grad_values = jnp.einsum(
                "hqk,qhd->khd",
                probs.astype(jnp.bfloat16),
                grad_heads,
                preferred_element_type=jnp.float32,
            )
            return (
                total,
                jnp.concatenate(
                    [grad_keys.reshape(rows, width), grad_values.reshape(rows, width)], axis=1
                ),
            )

        def skip(total):
            return (total, jnp.zeros((rows, 2 * width), jnp.float32))

        return lax.cond(begin <= last_place, back_compute, skip, grad_query)

    grad_query, key_terms = lax.scan(back_step, zero_query, begins)
    key_value_grad = lax.psum_scatter(
        key_terms.reshape(stream, 2 * width).astype(jnp.bfloat16),
        "blk",
        scatter_dimension=0,
        tiled=True,
    ).astype(jnp.float32)
    grad_keys_low = key_value_grad[:, :width].astype(jnp.bfloat16)
    grad_values_low = key_value_grad[:, width:].astype(jnp.bfloat16)
    grad_query_low = grad_query.reshape(rows, width).astype(jnp.bfloat16)
    grad_joined = jnp.concatenate([grad_query_low, grad_keys_low, grad_values_low], axis=1)
    grad_project_in = jnp.einsum(
        "rd,rc->dc", normed_s, grad_joined, preferred_element_type=jnp.float32
    )
    grad_query_value_bias = jnp.concatenate(
        [
            jnp.sum(grad_query_low.astype(jnp.float32), axis=0),
            jnp.sum(grad_values_low.astype(jnp.float32), axis=0),
        ]
    )
    grad_normed = jnp.einsum(
        "rc,dc->rd", grad_joined, student_project_in, preferred_element_type=jnp.float32
    )
    _, first_back = jax.vjp(layer_norm, inputs, student_first_gain, student_first_shift)
    grad_inputs_norm, grad_first_gain, grad_first_shift = first_back(grad_normed)
    input_grad = grad_after + grad_inputs_norm
    shares = (
        lax.psum_scatter(
            grad_first_gain.astype(jnp.bfloat16), "dp", scatter_dimension=0, tiled=True
        ).astype(jnp.float32),
        lax.psum_scatter(
            grad_first_shift.astype(jnp.bfloat16), "dp", scatter_dimension=0, tiled=True
        ).astype(jnp.float32),
        lax.psum_scatter(
            grad_project_in.astype(jnp.bfloat16), "dp", scatter_dimension=0, tiled=True
        ).astype(jnp.float32),
        lax.psum_scatter(
            grad_query_value_bias.astype(jnp.bfloat16), "dp", scatter_dimension=0, tiled=True
        ).astype(jnp.float32),
        lax.psum_scatter(
            grad_attend_out.astype(jnp.bfloat16), "dp", scatter_dimension=0, tiled=True
        ).astype(jnp.float32),
        lax.psum_scatter(
            grad_attend_bias.astype(jnp.bfloat16), "dp", scatter_dimension=0, tiled=True
        ).astype(jnp.float32),
        lax.psum_scatter(
            grad_second_gain.astype(jnp.bfloat16), "dp", scatter_dimension=0, tiled=True
        ).astype(jnp.float32),
        lax.psum_scatter(
            grad_second_shift.astype(jnp.bfloat16), "dp", scatter_dimension=0, tiled=True
        ).astype(jnp.float32),
        lax.psum_scatter(
            grad_expand_weight.astype(jnp.bfloat16), "dp", scatter_dimension=0, tiled=True
        ).astype(jnp.float32),
        lax.psum_scatter(
            grad_expand_bias.astype(jnp.bfloat16), "dp", scatter_dimension=0, tiled=True
        ).astype(jnp.float32),
        lax.psum_scatter(
            grad_contract_weight.astype(jnp.bfloat16), "dp", scatter_dimension=0, tiled=True
        ).astype(jnp.float32),
        lax.psum_scatter(
            grad_contract_bias.astype(jnp.bfloat16), "dp", scatter_dimension=0, tiled=True
        ).astype(jnp.float32),
    )
    summed = (
        lax.psum(shares[0].astype(jnp.bfloat16), "blk").astype(jnp.float32),
        lax.psum(shares[1].astype(jnp.bfloat16), "blk").astype(jnp.float32),
        lax.psum(shares[2].astype(jnp.bfloat16), "blk").astype(jnp.float32),
        lax.psum(shares[3].astype(jnp.bfloat16), "blk").astype(jnp.float32),
        lax.psum(shares[4].astype(jnp.bfloat16), "blk").astype(jnp.float32),
        lax.psum(shares[5].astype(jnp.bfloat16), "blk").astype(jnp.float32),
        lax.psum(shares[6].astype(jnp.bfloat16), "blk").astype(jnp.float32),
        lax.psum(shares[7].astype(jnp.bfloat16), "blk").astype(jnp.float32),
        lax.psum(shares[8].astype(jnp.bfloat16), "blk").astype(jnp.float32),
        lax.psum(shares[9].astype(jnp.bfloat16), "blk").astype(jnp.float32),
        lax.psum(shares[10].astype(jnp.bfloat16), "blk").astype(jnp.float32),
        lax.psum(shares[11].astype(jnp.bfloat16), "blk").astype(jnp.float32),
    )
    return (
        kl_rows,
        input_grad,
        summed[0],
        summed[1],
        summed[2],
        summed[3],
        summed[4],
        summed[5],
        summed[6],
        summed[7],
        summed[8],
        summed[9],
        summed[10],
        summed[11],
    )


def nt(left, right):
    return lax.dot_general(
        left, right, (((1,), (1,)), ((), ())), preferred_element_type=jnp.float32
    )


def tn(left, right):
    return lax.dot_general(
        left, right, (((0,), (0,)), ((), ())), preferred_element_type=jnp.float32
    )


def normalise(value):
    centre = value - jnp.mean(value, axis=-1, keepdims=True)
    scale = lax.rsqrt(jnp.mean(centre * centre, axis=-1, keepdims=True) + 1e-05)
    return (centre * scale, scale)


def norm_back(normed, scale, gain, grad):
    weighted = grad * gain
    return scale * (
        weighted
        - jnp.mean(weighted, axis=-1, keepdims=True)
        - normed * jnp.mean(weighted * normed, axis=-1, keepdims=True)
    )


def starts_of(lengths_ref, count):
    places = lax.broadcasted_iota(jnp.int32, (1, count), 1)
    start = jnp.zeros((1, count), jnp.int32)
    end = jnp.int32(0)
    for index in range(lengths_ref.shape[1]):
        end = end + lengths_ref[0, index]
        start = jnp.where(places >= end, jnp.maximum(start, end), start)
    return start


def in_stream_order(target, own_ref, other_ref, blk):
    rows = own_ref.shape[0]
    target[pl.ds(pl.multiple_of(blk * rows, rows), rows), :] = own_ref[...].astype(target.dtype)
    target[pl.ds(pl.multiple_of((1 - blk) * rows, rows), rows), :] = other_ref[...].astype(
        target.dtype
    )


def head_mask(shape, which):
    lanes = lax.broadcasted_iota(jnp.int32, shape, 1)
    return (lanes >= HEAD_DIM) if which else (lanes < HEAD_DIM)


def forward_kernel(train, *refs):
    (
        place_ref,
        lengths_ref,
        own_ref,
        other_ref,
    ) = refs[:4]
    (
        first_gain,
        first_shift,
        qv_bias,
        attend_bias,
        second_gain,
        second_shift,
        expand_bias,
        contract_bias,
        final_gain,
        final_shift,
    ) = (as_row(ref) for ref in refs[4:14])
    weights_hbm = refs[14:18]
    rest = refs[18:]
    if train:
        rows_out, kept_hbm, rest = rest[0], rest[1:10], rest[10:]
    else:
        rows_out, kept_hbm, rest = rest[0], (), rest[1:]
    wpi, wao, we, wc = rest[:4]
    normed_v, joined_v, probs_v, mixed_v, after_v, normed_two_v, slope_v, active_v, y_v = rest[4:13]
    x_v, bias_v, weight_sem, out_sem, probs_sem = rest[13:]
    kept = (normed_v, joined_v, probs_v, mixed_v, after_v, normed_two_v, slope_v, active_v, y_v)
    loads = [
        pltpu.make_async_copy(source, target, weight_sem.at[index])
        for index, (source, target) in enumerate(zip(weights_hbm, (wpi, wao, we, wc)))
    ]
    stores = []

    def save(index, *at):
        if train:
            source, target = kept[index], kept_hbm[index]
            if at:
                source, target = source.at[at], target.at[at]
            store = pltpu.make_async_copy(source, target, out_sem.at[len(stores)])
            store.start()
            stores.append(store)

    for load in loads:
        load.start()
    blk = place_ref[1]
    in_stream_order(x_v, own_ref, other_ref, blk)
    count, width = x_v.shape
    block = own_ref.shape[0]
    normed, _ = normalise(x_v[...])
    normed_v[...] = (normed * first_gain + first_shift).astype(jnp.bfloat16)
    save(0)
    start = starts_of(lengths_ref, count)
    keys_at = lax.broadcasted_iota(jnp.int32, (count, count), 0)
    queries_at = lax.broadcasted_iota(jnp.int32, (count, count), 1)
    bias_v[...] = jnp.where((keys_at <= queries_at) & (keys_at >= start), 0.0, negative)
    loads[0].wait()
    for part in range(3):
        span = slice(part * width, (part + 1) * width)
        value = dense(normed_v[...], wpi[:, span])
        if part == 0:
            value = value + qv_bias[:, :width]
        if part == 2:
            value = value + qv_bias[:, width:]
        joined_v[:, span] = value.astype(jnp.bfloat16)
    save(1)
    pair = 2 * HEAD_DIM
    pairs = width // pair

    def attend(index, _):
        column = pl.ds(pl.multiple_of(index * pair, pair), pair)
        query = joined_v[:, column] * jnp.bfloat16(0.125)
        keys = joined_v[:, pl.ds(pl.multiple_of(width + index * pair, pair), pair)]
        values = joined_v[:, pl.ds(pl.multiple_of(2 * width + index * pair, pair), pair)]
        for piece in range(count // block):
            span = slice(piece * block, (piece + 1) * block)
            reach = (piece + 1) * block
            both = []
            for which in range(2):
                mine = jnp.where(
                    head_mask((block, pair), which), query[span], jnp.bfloat16(0.0)
                )
                scores = nt(keys[:reach], mine) + bias_v[:reach, span]
                expo = jnp.exp(scores - jnp.max(scores, axis=0, keepdims=True))
                probs = expo * (1.0 / jnp.sum(expo, axis=0, keepdims=True))
                probs = probs.astype(jnp.bfloat16)
                if train:
                    probs_v[2 * index + which, :reach, span] = probs
                both.append(tn(probs, values[:reach]))
            mixed_v[span, column] = jnp.where(
                head_mask((block, pair), 0), both[0], both[1]
            ).astype(jnp.bfloat16)
        if train:
            heads = pl.ds(2 * index, 2)
            pltpu.make_async_copy(
                probs_v.at[heads], kept_hbm[2].at[heads], probs_sem.at[index]
            ).start()
        return 0

    lax.fori_loop(0, pairs, attend, 0, unroll=3)
    if train:
        for index in range(pairs):
            heads = pl.ds(2 * index, 2)
            stores.append(
                pltpu.make_async_copy(
                    probs_v.at[heads], kept_hbm[2].at[heads], probs_sem.at[index]
                )
            )
    save(3)
    loads[1].wait()
    after_v[...] = x_v[...] + dense(mixed_v[...], wao[...]) + attend_bias
    save(4)
    normed, _ = normalise(after_v[...])
    normed_two_v[...] = (normed * second_gain + second_shift).astype(jnp.bfloat16)
    save(5)
    loads[2].wait()
    loads[3].wait()
    hidden_width = we.shape[1]
    total = after_v[...] + contract_bias
    root = 0.7978845608028654
    for part in range(hidden_width // width):
        span = slice(part * width, (part + 1) * width)
        inner = dense(normed_two_v[...], we[:, span]) + expand_bias[:, span]
        square = inner * inner
        bent = jnp.tanh(root * (inner + 0.044715 * (square * inner)))
        upper = 0.5 * (1.0 + bent)
        active = (inner * upper).astype(jnp.bfloat16)
        if train:
            active_v[:, span] = active
            slope_v[:, span] = (
                upper
                + (0.5 * root) * inner * (1.0 - bent * bent) * (1.0 + (3 * 0.044715) * square)
            ).astype(jnp.bfloat16)
            save(6, slice(None), pl.ds(part * width, width))
            save(7, slice(None), pl.ds(part * width, width))
        total = total + dense(active, wc[span, :])
    if train:
        y_v[...] = total
    save(8)
    normed, _ = normalise(total)
    rows_out[...] = (normed * final_gain + final_shift).astype(jnp.bfloat16) * jnp.bfloat16(0.5)
    if train:
        for store in stores:
            store.wait()


def carrying(kernel, inputs, outputs, carried):
    def body(*refs):
        rest = refs[inputs + carried :]
        kernel(*refs[:inputs], *rest[:outputs], *rest[outputs + carried :])

    return body


def shapes_of(carry):
    return [jax.ShapeDtypeStruct(item.shape, item.dtype) for item in carry]


def aliases(inputs, outputs, carry):
    return {inputs + index: outputs + index for index in range(len(carry))}


def as_row(ref):
    return ref[...].reshape(1, ref.shape[0])


def whole_vmem():
    return pl.BlockSpec(memory_space=pltpu.VMEM)


def in_place():
    return pl.BlockSpec(memory_space=pl.ANY)


def far(*arrays):
    return [pltpu.with_memory_space_constraint(array, pltpu.HBM) for array in arrays]


def near(*arrays):
    return [pltpu.with_memory_space_constraint(array, pltpu.VMEM) for array in arrays]


def scalars():
    return pl.BlockSpec(memory_space=pltpu.SMEM)


def forward(train, place, lengths, own, other, vectors, weights):
    rows, width = own.shape
    count = 2 * rows
    hidden_width = weights[2].shape[1]
    low, full = jnp.bfloat16, jnp.float32
    kept = [
        ((count, width), low),
        ((count, 3 * width), low),
        ((HEADS, count, count), low),
        ((count, width), low),
        ((count, width), full),
        ((count, width), low),
        ((count, hidden_width), low),
        ((count, hidden_width), low),
        ((count, width), full),
    ]
    small = ((8, 128), low)
    scratch = [kept[0], kept[1], kept[2] if train else ((1, 8, 128), low), kept[3], kept[4], kept[5]]
    scratch += [kept[6], kept[7], kept[8]] if train else [small, small, ((8, 128), full)]
    out_shape = [jax.ShapeDtypeStruct((count, width), low)]
    out_specs = [whole_vmem()]
    if train:
        out_shape += [jax.ShapeDtypeStruct(*item) for item in kept]
        out_specs += [in_place()] * len(kept)
    return pl.pallas_call(
        functools.partial(forward_kernel, train),
        in_specs=[scalars(), scalars()] + [whole_vmem()] * 12 + [in_place()] * 4,
        out_specs=out_specs,
        out_shape=out_shape,
        scratch_shapes=[pltpu.VMEM(item.shape, low) for item in weights]
        + [pltpu.VMEM(*item) for item in scratch]
        + [
            pltpu.VMEM((count, width), full),
            pltpu.VMEM((count, count), full),
            pltpu.SemaphoreType.DMA((4,)),
            pltpu.SemaphoreType.DMA((32,)),
            pltpu.SemaphoreType.DMA((HEADS // 2,)),
        ],
        compiler_params=pltpu.CompilerParams(vmem_limit_bytes=(54 if train else 44) << 20),
        cost_estimate=pl.CostEstimate(
            flops=8_000_000_000, bytes_accessed=20_000_000, transcendentals=0
        ),
        name="forward_student" if train else "forward_teacher",
    )(place, lengths, own, other, *far(*vectors, *weights))


def logits_kernel(student_ref, teacher_ref, table_ref, diff_ref, expo_ref, stats_ref, sums_ref):
    count = student_ref.shape[0]
    span = table_ref.shape[0] // 8
    lanes = lax.broadcasted_iota(jnp.int32, (count, 128), 1)
    packed = jnp.zeros((count, 128), jnp.float32)
    for part in range(8):
        where = slice(part * span, (part + 1) * span)
        table = table_ref[where, :]
        half_s = nt(student_ref[...], table)
        top_s = jnp.max(half_s, axis=1, keepdims=True)
        expo_s = jnp.exp(half_s - top_s)
        mass_s = jnp.sum(expo_s, axis=1, keepdims=True)
        half_t = nt(teacher_ref[...], table)
        top_t = jnp.max(half_t, axis=1, keepdims=True)
        expo_t = jnp.exp(half_t - top_t)
        mass_t = jnp.sum(expo_t, axis=1, keepdims=True)
        cross = jnp.sum(expo_t * (half_t - half_s), axis=1, keepdims=True)
        diff_ref[:, where] = (expo_s * (mass_t / mass_s) - expo_t).astype(jnp.bfloat16)
        expo_ref[:, where] = expo_t.astype(jnp.bfloat16)
        for index, column in enumerate((top_s, mass_s, top_t, mass_t, cross)):
            packed = jnp.where(lanes == 8 * index + part, column, packed)
    stats = packed.T
    stats_ref[0] = stats[:40]
    top_s, mass_s, top_t, mass_t, cross = (stats[8 * i : 8 * i + 8] for i in range(5))

    @pl.when(pl.program_id(0) == 0)
    def _():
        row = lax.broadcasted_iota(jnp.int32, sums_ref.shape, 0)
        sums_ref[...] = jnp.where((row == 0) | (row == 2), negative, 0.0)

    old = sums_ref[...]
    new_s = jnp.maximum(old[0:1], jnp.max(top_s, axis=0, keepdims=True))
    new_t = jnp.maximum(old[2:3], jnp.max(top_t, axis=0, keepdims=True))
    keep_s = jnp.exp(old[0:1] - new_s)
    keep_t = jnp.exp(old[2:3] - new_t)
    scale_s = jnp.exp(top_s - new_s)
    scale_t = jnp.exp(top_t - new_t)
    sums_ref[0:1] = new_s
    sums_ref[1:2] = old[1:2] * keep_s + jnp.sum(mass_s * scale_s, axis=0, keepdims=True)
    sums_ref[2:3] = new_t
    sums_ref[3:4] = old[3:4] * keep_t + jnp.sum(mass_t * scale_t, axis=0, keepdims=True)
    sums_ref[4:5] = old[4:5] * keep_t + jnp.sum(cross * scale_t, axis=0, keepdims=True)


def logits_phase(student, teacher, table):
    count, width = student.shape
    entries = table.shape[0]
    span = TABLE_SPAN
    steps = entries // span
    rows = pl.BlockSpec((count, width), lambda j: (0, 0))
    wide = pl.BlockSpec((count, span), lambda j: (0, j))
    return pl.pallas_call(
        logits_kernel,
        grid=(steps,),
        in_specs=[rows, rows, pl.BlockSpec((span, width), lambda j: (j, 0))],
        out_specs=[
            wide,
            wide,
            pl.BlockSpec((1, 40, count), lambda j: (j, 0, 0)),
            pl.BlockSpec((8, count), lambda j: (0, 0)),
        ],
        out_shape=[
            jax.ShapeDtypeStruct((count, entries), jnp.bfloat16),
            jax.ShapeDtypeStruct((count, entries), jnp.bfloat16),
            jax.ShapeDtypeStruct((steps, 40, count), jnp.float32),
            jax.ShapeDtypeStruct((8, count), jnp.float32),
        ],
        compiler_params=pltpu.CompilerParams(vmem_limit_bytes=24 << 20),
        cost_estimate=pl.CostEstimate(
            flops=4 * count * width * entries, bytes_accessed=60_000_000, transcendentals=0
        ),
        name="logits_phase",
    )(student, teacher, *far(table))


def joined_norms(own, other):
    top_s = jnp.maximum(own[0:1], other[0:1])
    top_t = jnp.maximum(own[2:3], other[2:3])
    own_t, other_t = jnp.exp(own[2:3] - top_t), jnp.exp(other[2:3] - top_t)
    mass_s = own[1:2] * jnp.exp(own[0:1] - top_s) + other[1:2] * jnp.exp(other[0:1] - top_s)
    mass_t = own[3:4] * own_t + other[3:4] * other_t
    cross = own[4:5] * own_t + other[4:5] * other_t
    norm_s = top_s + jnp.log(mass_s)
    norm_t = top_t + jnp.log(mass_t)
    return (norm_s, norm_t, cross / mass_t - norm_t + norm_s)


def chunk_factors(stats_ref, norms, rows):
    top_s, mass_s, top_t, mass_t = (stats_ref[0, 8 * i : 8 * i + 8, rows] for i in range(4))
    first = 0.5 * jnp.exp(top_s - norms[0:1, rows]) * mass_s / mass_t
    second = first - 0.5 * jnp.exp(top_t - norms[1:2, rows])
    pad = jnp.zeros((112, first.shape[1]), jnp.float32)
    return jnp.concatenate([first, second, pad], axis=0).T


def chunk_product(total, diffs, expos, factors, table_ref):
    span = table_ref.shape[0] // 8
    for group in range(2):
        pieces = []
        for part in range(4 * group, 4 * group + 4):
            where = slice(part * span, (part + 1) * span)
            pieces.append(
                jnp.concatenate(
                    [
                        (
                            diff[:, where].astype(jnp.float32) * factor[:, part : part + 1]
                            + expo[:, where].astype(jnp.float32) * factor[:, 8 + part : 9 + part]
                        ).astype(jnp.bfloat16)
                        for diff, expo, factor in zip(diffs, expos, factors)
                    ],
                    axis=0,
                )
            )
        where = slice(4 * group * span, 4 * (group + 1) * span)
        total = total + dense(jnp.concatenate(pieces, axis=1), table_ref[where, :])
    return total


def gradient_kernel(
    joint,
    diff_first,
    diff_second,
    expo_first,
    expo_second,
    table_ref,
    stats_ref,
    own_ref,
    other_ref,
    we_hbm,
    first_out,
    first_low,
    second_out,
    norms_out,
    we_out,
    total_ref,
    load_sem,
):
    step = pl.program_id(0)
    rows = diff_first.shape[0]
    load = pltpu.make_async_copy(we_hbm, we_out, load_sem)
    top, bottom = slice(0, rows), slice(rows, 2 * rows)

    @pl.when(step == 0)
    def _():
        load.start()
        norm_s, norm_t, divergence = joined_norms(own_ref[...], other_ref[...])
        norms_out[0:1] = norm_s
        norms_out[1:2] = norm_t
        norms_out[2:3] = divergence
        total_ref[...] = jnp.zeros_like(total_ref)

    @pl.when(step < joint)
    def _():
        total_ref[...] = chunk_product(
            total_ref[...],
            (diff_first, diff_second),
            (expo_first, expo_second),
            (
                chunk_factors(stats_ref, norms_out, top),
                chunk_factors(stats_ref, norms_out, bottom),
            ),
            table_ref,
        )

    @pl.when(step >= joint)
    def _():
        total_ref[top] = chunk_product(
            total_ref[top],
            (diff_first,),
            (expo_first,),
            (chunk_factors(stats_ref, norms_out, top),),
            table_ref,
        )

    @pl.when(step == pl.num_programs(0) - 1)
    def _():
        first_out[...] = total_ref[top]
        second_out[...] = total_ref[bottom]
        first_low[...] = total_ref[top].astype(jnp.bfloat16)
        load.wait()


def gradient_phase(diff, expo, table, stats, own, other, we):
    count, entries = diff.shape
    rows = count // 2
    width = table.shape[1]
    span = TABLE_SPAN
    steps = entries // span
    joint = steps - SPLIT_STEPS
    top = pl.BlockSpec((rows, span), lambda j: (0, j))
    bottom = pl.BlockSpec((rows, span), lambda j: (1, jnp.minimum(j, joint - 1)))
    sums = pl.BlockSpec((8, count), lambda j: (0, 0))
    fixed = pl.BlockSpec((rows, width), lambda j: (0, 0))
    full = jnp.float32
    return pl.pallas_call(
        functools.partial(gradient_kernel, joint),
        grid=(steps,),
        in_specs=[
            top,
            bottom,
            top,
            bottom,
            pl.BlockSpec((span, width), lambda j: (j, 0)),
            pl.BlockSpec((1, 40, count), lambda j: (j, 0, 0)),
            sums,
            sums,
            in_place(),
        ],
        out_specs=[fixed] * 3 + [sums, whole_vmem()],
        out_shape=[
            jax.ShapeDtypeStruct((rows, width), full),
            jax.ShapeDtypeStruct((rows, width), jnp.bfloat16),
            jax.ShapeDtypeStruct((rows, width), full),
            jax.ShapeDtypeStruct((8, count), full),
            pltpu.VMEM(we.shape, we.dtype),
        ],
        scratch_shapes=[
            pltpu.VMEM((count, width), full),
            pltpu.SemaphoreType.DMA,
        ],
        compiler_params=pltpu.CompilerParams(vmem_limit_bytes=20 << 20),
        cost_estimate=pl.CostEstimate(
            flops=2 * count * width * entries, bytes_accessed=60_000_000, transcendentals=0
        ),
        name="gradient_phase",
    )(diff, diff, *far(expo, expo, table), stats, own, other, *far(we))


def gradient_rest_kernel(
    diff_ref, expo_ref, table_ref, stats_ref, norms_ref, partial_ref, total_ref, low_ref
):
    step = pl.program_id(0)
    rows = diff_ref.shape[0]

    @pl.when(step == 0)
    def _():
        total_ref[...] = partial_ref[...]

    total_ref[...] = chunk_product(
        total_ref[...],
        (diff_ref,),
        (expo_ref,),
        (chunk_factors(stats_ref, norms_ref, slice(rows, 2 * rows)),),
        table_ref,
    )

    @pl.when(step == pl.num_programs(0) - 1)
    def _():
        low_ref[...] = total_ref[...].astype(jnp.bfloat16)


def gradient_rest(diff, expo, table, stats, norms, partial):
    count, entries = diff.shape
    rows, width = partial.shape
    span = TABLE_SPAN
    begin = entries // span - SPLIT_STEPS
    wide = pl.BlockSpec((rows, span), lambda j: (1, begin + j))
    fixed = pl.BlockSpec((rows, width), lambda j: (0, 0))
    return pl.pallas_call(
        gradient_rest_kernel,
        grid=(SPLIT_STEPS,),
        in_specs=[
            wide,
            wide,
            pl.BlockSpec((span, width), lambda j: (begin + j, 0)),
            pl.BlockSpec((1, 40, count), lambda j: (begin + j, 0, 0)),
            pl.BlockSpec((8, count), lambda j: (0, 0)),
            fixed,
        ],
        out_specs=[fixed, fixed],
        out_shape=[
            jax.ShapeDtypeStruct((rows, width), jnp.float32),
            jax.ShapeDtypeStruct((rows, width), jnp.bfloat16),
        ],
        compiler_params=pltpu.CompilerParams(vmem_limit_bytes=18 << 20),
        cost_estimate=pl.CostEstimate(
            flops=12_000_000_000, bytes_accessed=1_000_000, transcendentals=0
        ),
        name="gradient_rest",
    )(diff, *far(expo, table), stats, norms, partial)


def position(device, masks):
    rest = masks[1:]
    place = jnp.int32(0) if not isinstance(device, int) else 0
    for index, mask in enumerate(rest):
        if isinstance(device, int):
            bit = (device // mask) % 2
        else:
            bit = lax.rem(lax.div(device, mask), 2)
        place = place + (bit << (len(rest) - 1 - index))
    return place


def place_shards(me, natural, keep, send, masks, first, shards, rows=slice(None)):
    mine = lax.rem(me, 2)
    place = position(me, masks)
    for pair in range(first // 2, (first + shards) // 2):
        target = lax.bitwise_xor(place, jnp.int32(position(2 * pair, masks)))
        keep[target, rows] = natural[2 * pair + mine, rows]
        send[target, rows] = natural[2 * pair + 1 - mine, rows]


def row_sums(value):
    return jnp.sum(value.astype(jnp.float32), axis=0, keepdims=True)


def back_to_norm(own_ref, other_ref, y_ref, gain):
    normed, scale = normalise(y_ref[...])
    grad = own_ref[...] + other_ref[...].astype(jnp.float32)
    return norm_back(normed, scale, as_row(gain), grad)


def feed_rows(dm, wc, slope, dinner, rows, bias_out, bias_before):
    hidden_width, width = wc.shape
    for part in range(hidden_width // width):
        span = slice(part * width, (part + 1) * width)
        value = nt(dm, wc[span, :]) * slope[rows, span].astype(jnp.float32)
        value = value.astype(jnp.bfloat16)
        dinner[rows, span] = value
        before = 0.0 if bias_before is None else bias_before[:, span]
        bias_out[:, span] = before + row_sums(value)


def branch_rows(dinner, we, after_ref, gain, dy):
    dh2 = nt(dinner[...], we[...])
    normed, scale = normalise(after_ref[...])
    dafter = dy + norm_back(normed, scale, as_row(gain), dh2)
    return dafter, row_sums(dh2 * normed), row_sums(dh2)


def first_kernel(
    own_ref,
    other_ref,
    y_ref,
    after_ref,
    final_gain,
    second_gain,
    wc,
    we,
    wao,
    slope,
    dm_out,
    dinner_out,
    dafter_out,
    dbranch_out,
    dmixed_out,
    contract_bias_out,
    expand_bias_out,
    second_gain_out,
    second_shift_out,
    attend_bias_out,
):
    count = own_ref.shape[0]
    dy = back_to_norm(own_ref, other_ref, y_ref, final_gain)
    dm = dy.astype(jnp.bfloat16)
    dm_out[...] = dm
    contract_bias_out[...] = row_sums(dm)
    feed_rows(dm, wc, slope, dinner_out, slice(0, count), expand_bias_out, None)
    dafter, second_gain_out[...], second_shift_out[...] = branch_rows(
        dinner_out, we, after_ref, second_gain, dy
    )
    dafter_out[...] = dafter
    dbranch = dafter.astype(jnp.bfloat16)
    dbranch_out[...] = dbranch
    attend_bias_out[...] = row_sums(dbranch)
    dmixed_out[...] = nt(dbranch, wao[...]).astype(jnp.bfloat16)


def first_rows(own, other, y, after, final_gain, second_gain, wc, we, wao, slope):
    rows, width = own.shape
    hidden_width = wc.shape[0]
    low, full = jnp.bfloat16, jnp.float32

    def array(size, kind):
        return jax.ShapeDtypeStruct((rows, size), kind)

    def vector(size):
        return jax.ShapeDtypeStruct((1, size), full)

    top = pl.BlockSpec((rows, width), lambda i: (0, 0))
    return pl.pallas_call(
        first_kernel,
        grid=(1,),
        in_specs=[whole_vmem()] * 2 + [top] * 2 + [whole_vmem()] * 6,
        out_specs=[whole_vmem()] * 10,
        out_shape=[
            array(width, low),
            array(hidden_width, low),
            array(width, full),
            array(width, low),
            array(width, low),
            vector(width),
            vector(hidden_width),
            vector(width),
            vector(width),
            vector(width),
        ],
        compiler_params=pltpu.CompilerParams(vmem_limit_bytes=14 << 20),
        cost_estimate=pl.CostEstimate(
            flops=12_000_000_000, bytes_accessed=1_000_000, transcendentals=0
        ),
        name="first_rows",
    )(own, other, *far(y, after, final_gain, second_gain), *near(wc, we, wao, slope))


def feed_kernel(
    place_ref,
    own_ref,
    other_ref,
    y_ref,
    final_gain,
    dm_first,
    normed_two_ref,
    contract_bias_first,
    expand_bias_first,
    wc_hbm,
    slope,
    active,
    dinner_first,
    cw_keep,
    cw_send,
    ew_keep,
    ew_send,
    dy_out,
    dinner_out,
    contract_bias_out,
    expand_bias_out,
    wc,
    dinner_v,
    dm_v,
    cw_natural,
    ew_natural,
    load_sem,
):
    me, blk = place_ref[0], place_ref[1]
    rows = own_ref.shape[0]
    second = slice(rows, 2 * rows)
    hidden_width, width = wc.shape
    parts = hidden_width // width
    part_width = width // 2
    shards = cw_natural.shape[0]
    chunk = width // shards
    loads = [
        pltpu.make_async_copy(
            wc_hbm.at[pl.ds(part * width, width)],
            wc.at[pl.ds(part * width, width)],
            load_sem.at[part],
        )
        for part in range(parts)
    ]
    for load in loads:
        load.start()
    dinner_v[:rows] = dinner_first[...]
    dy = back_to_norm(own_ref, other_ref, y_ref, final_gain)
    dy_out[...] = dy
    dm = dy.astype(jnp.bfloat16)
    dm_v[:rows] = dm_first[...]
    dm_v[second] = dm
    contract_bias_out[...] = contract_bias_first[...] + row_sums(dm)
    dm_half = dm_v[:, pl.ds(pl.multiple_of(blk * part_width, part_width), part_width)]
    group = shards // parts
    for part in range(parts):
        span = slice(part * width, (part + 1) * width)
        value = tn(active[:, span], dm_half).astype(jnp.bfloat16)
        cw_natural[part * group : (part + 1) * group] = value.reshape(
            group, width // group, part_width
        )
        place_shards(me, cw_natural, cw_keep, cw_send, MASKS, part * group, group)
    for load in loads:
        load.wait()
    feed_rows(dm, wc, slope, dinner_v, second, expand_bias_out, expand_bias_first)
    dinner_out[...] = dinner_v[second]
    for part in range(parts // 2):
        offset = pl.multiple_of(blk * (hidden_width // 2), width) + part * width
        value = tn(normed_two_ref[...], dinner_v[:, pl.ds(pl.multiple_of(offset, width), width)])
        value = value.astype(jnp.bfloat16)
        for half in range(2):
            row = (2 * part + half) * chunk
            ew_natural[:, row : row + chunk, :] = value[
                :, half * part_width : (half + 1) * part_width
            ].reshape(shards, chunk, part_width)
        rows_at = slice(2 * part * chunk, (2 * part + 2) * chunk)
        place_shards(me, ew_natural, ew_keep, ew_send, MASKS_B, 0, shards, rows_at)


def feed_back(
    place, own, other, y, final_gain, dm, normed_two, biases, wc, slope, active, dinner, shards
):
    rows, width = own.shape
    count = 2 * rows
    hidden_width = wc.shape[0]
    low, full = jnp.bfloat16, jnp.float32
    height = hidden_width // shards
    half = jax.ShapeDtypeStruct((shards // 2, height, width // 2), low)
    bottom = pl.BlockSpec((rows, width), lambda i: (1, 0))
    return pl.pallas_call(
        feed_kernel,
        grid=(1,),
        in_specs=[scalars()]
        + [whole_vmem()] * 2
        + [bottom]
        + [whole_vmem()] * 5
        + [in_place()]
        + [whole_vmem()] * 3,
        out_specs=[whole_vmem()] * 8,
        out_shape=[half] * 4
        + [
            jax.ShapeDtypeStruct((rows, width), full),
            jax.ShapeDtypeStruct((rows, hidden_width), low),
            jax.ShapeDtypeStruct((1, width), full),
            jax.ShapeDtypeStruct((1, hidden_width), full),
        ],
        scratch_shapes=[
            pltpu.VMEM(wc.shape, low),
            pltpu.VMEM((count, hidden_width), low),
            pltpu.VMEM((count, width), low),
            pltpu.VMEM((shards, height, width // 2), low),
            pltpu.VMEM((shards, height, width // 2), low),
            pltpu.SemaphoreType.DMA((hidden_width // width,)),
        ],
        compiler_params=pltpu.CompilerParams(vmem_limit_bytes=26 << 20),
        cost_estimate=pl.CostEstimate(
            flops=12_000_000_000, bytes_accessed=1_000_000, transcendentals=0
        ),
        name="feed_back",
    )(
        place,
        own,
        other,
        *far(y, final_gain),
        dm,
        *far(normed_two),
        *biases,
        *far(wc),
        *near(slope, active),
        dinner,
    )


def branch_kernel(
    place_ref,
    dy_ref,
    after_ref,
    mixed_ref,
    second_gain,
    dbranch_first,
    second_gain_first,
    second_shift_first,
    attend_bias_first,
    dinner_ref,
    we,
    wao,
    dafter_out,
    dmixed_out,
    attend_out,
    second_gain_out,
    second_shift_out,
    attend_bias_out,
    dbranch_v,
):
    blk = place_ref[1]
    rows, width = after_ref.shape
    part_width = width // 2
    dafter, gain_sum, shift_sum = branch_rows(
        dinner_ref, we, after_ref, second_gain, dy_ref[...]
    )
    dafter_out[...] = dafter
    second_gain_out[...] = second_gain_first[...] + gain_sum
    second_shift_out[...] = second_shift_first[...] + shift_sum
    dbranch = dafter.astype(jnp.bfloat16)
    dbranch_v[:rows] = dbranch_first[...]
    dbranch_v[rows:] = dbranch
    attend_bias_out[...] = attend_bias_first[...] + row_sums(dbranch)
    dmixed_out[...] = nt(dbranch, wao[...]).astype(jnp.bfloat16)
    part = dbranch_v[:, pl.ds(pl.multiple_of(blk * part_width, part_width), part_width)]
    attend_out[...] = tn(mixed_ref[...], part).astype(jnp.bfloat16).reshape(attend_out.shape)


def branch_back(place, dy, after, mixed, second_gain, dbranch, sums, dinner, we, wao, carry, shards):
    rows, width = dy.shape
    low, full = jnp.bfloat16, jnp.float32
    vector = jax.ShapeDtypeStruct((1, width), full)
    bottom = pl.BlockSpec((rows, width), lambda i: (1, 0))
    return pl.pallas_call(
        carrying(branch_kernel, 12, 6, len(carry)),
        grid=(1,),
        in_specs=[scalars(), whole_vmem(), bottom]
        + [whole_vmem()] * 9
        + [in_place()] * len(carry),
        out_specs=[whole_vmem()] * 6 + [in_place()] * len(carry),
        input_output_aliases=aliases(12, 6, carry),
        out_shape=[
            jax.ShapeDtypeStruct((rows, width), full),
            jax.ShapeDtypeStruct((rows, width), low),
            jax.ShapeDtypeStruct((shards, width // shards, width // 2), low),
            vector,
            vector,
            vector,
        ]
        + shapes_of(carry),
        scratch_shapes=[
            pltpu.VMEM((2 * rows, width), low),
        ],
        compiler_params=pltpu.CompilerParams(vmem_limit_bytes=12 << 20),
        cost_estimate=pl.CostEstimate(
            flops=12_000_000_000, bytes_accessed=1_000_000, transcendentals=0
        ),
        name="branch_back",
    )(
        place,
        dy,
        *far(after, mixed, second_gain),
        dbranch,
        *sums,
        dinner,
        *near(we, wao),
        *carry,
    )


def attend_pair(block, query_ref, keys_ref, values_ref, probs_ref, dmixed_refs):
    count, pair = query_ref.shape
    query = query_ref[...] * jnp.bfloat16(0.125)
    zero = jnp.bfloat16(0.0)
    dkeys = jnp.zeros((count, pair), jnp.float32)
    dvalues = jnp.zeros((count, pair), jnp.float32)
    keys = keys_ref[...] * jnp.bfloat16(0.125)
    dqueries = []
    for piece in reversed(range(count // block)):
        span = slice(piece * block, (piece + 1) * block)
        reach = (piece + 1) * block
        dquery = jnp.zeros((block, pair), jnp.float32)
        add_keys = jnp.zeros((reach, pair), jnp.float32)
        add_values = jnp.zeros((reach, pair), jnp.float32)
        for which in range(2):
            mask = head_mask((block, pair), which)
            grad = jnp.where(mask, dmixed_refs[piece][...], zero)
            mine = jnp.where(mask, query[span], zero)
            probs = probs_ref[which, :reach, span]
            dprobs = nt(values_ref[:reach], grad)
            wide = probs.astype(jnp.float32)
            product = wide * dprobs
            balance = jnp.sum(product, axis=0, keepdims=True)
            dscores = (product - wide * balance).astype(jnp.bfloat16)
            add_values = add_values + dense(probs, grad)
            add_keys = add_keys + dense(dscores, mine)
            dquery = dquery + tn(
                dscores, jnp.where(head_mask((reach, pair), which), keys[:reach], zero)
            )
        dqueries.insert(0, dquery.astype(jnp.bfloat16))
        if reach < count:
            pad = jnp.zeros((count - reach, pair), jnp.float32)
            add_keys = jnp.concatenate([add_keys, pad], axis=0)
            add_values = jnp.concatenate([add_values, pad], axis=0)
        dkeys = dkeys + add_keys
        dvalues = dvalues + add_values
    return (
        jnp.concatenate(dqueries, axis=0),
        dkeys.astype(jnp.bfloat16),
        dvalues.astype(jnp.bfloat16),
    )


def attend_kernel(
    block,
    _,
    query_ref,
    keys_ref,
    values_ref,
    probs_ref,
    dmixed_first,
    dmixed_second,
    dq_ref,
    dk_ref,
    dv_ref,
):
    dmixed = (dmixed_first, dmixed_second)
    grads = attend_pair(block, query_ref, keys_ref, values_ref, probs_ref, dmixed)
    for ref, grad in zip((dq_ref, dk_ref, dv_ref), grads):
        ref[...] = grad


def project_kernel(
    block,
    place_ref,
    query_ref,
    keys_ref,
    values_ref,
    probs_ref,
    dmixed_first,
    dmixed_second,
    normed_ref,
    attend_ref,
    dq_ref,
    dk_ref,
    dv_ref,
    keep,
    send,
    natural,
):
    step = pl.program_id(0)
    pair = query_ref.shape[1]
    column = pl.ds(pl.multiple_of(step * pair, pair), pair)
    dmixed = (dmixed_first, dmixed_second)
    grads = attend_pair(block, query_ref, keys_ref, values_ref, probs_ref, dmixed)
    for ref, grad in zip((dq_ref, dk_ref, dv_ref), grads):
        ref[:, column] = grad

    @pl.when(step == pl.num_programs(0) - 1)
    def _():
        me = place_ref[0]
        shards = natural.shape[0]
        width = normed_ref.shape[1]
        part_width = width // 2
        chunk = width // shards
        natural[:, :chunk, :] = attend_ref[...]
        for part, ref in enumerate((dq_ref, dk_ref, dv_ref)):
            value = tn(normed_ref[...], ref[...]).astype(jnp.bfloat16)
            natural[:, (part + 1) * chunk : (part + 2) * chunk, :] = value.reshape(
                shards, chunk, part_width
            )
            rows = slice(0, 2 * chunk) if part == 0 else slice((part + 1) * chunk, (part + 2) * chunk)
            place_shards(me, natural, keep, send, MASKS, 0, shards, rows)


def attend_specs(joined, dmixed, own):
    rows, width = dmixed[0].shape
    count = 2 * rows
    pair = 2 * HEAD_DIM
    pairs = width // pair
    half = pairs // 2

    def first(place_ref):
        blk = place_ref[1]
        return half * (blk if own else 1 - blk)

    def column(height, offset):
        return pl.BlockSpec((height, pair), lambda p, place_ref: (0, offset + first(place_ref) + p))

    return half, [
        column(count, 0),
        column(count, pairs),
        column(count, 2 * pairs),
        pl.BlockSpec((2, count, count), lambda p, place_ref: (first(place_ref) + p, 0, 0)),
        column(rows, 0),
        column(rows, 0),
    ]


def attend_back(place, joined, probs, dmixed, carry, block):
    width = dmixed[0].shape[1]
    count = joined.shape[0]
    half, specs = attend_specs(joined, dmixed, False)
    result = pl.BlockSpec((count, 2 * HEAD_DIM), lambda p, place_ref: (0, p))
    return pl.pallas_call(
        carrying(functools.partial(attend_kernel, block), 7, 3, len(carry)),
        grid_spec=pltpu.PrefetchScalarGridSpec(
            num_scalar_prefetch=1,
            grid=(half,),
            in_specs=specs + [in_place()] * len(carry),
            out_specs=[result] * 3 + [in_place()] * len(carry),
        ),
        out_shape=[jax.ShapeDtypeStruct((count, width // 2), jnp.bfloat16)] * 3
        + shapes_of(carry),
        input_output_aliases=aliases(7, 3, carry),
        compiler_params=pltpu.CompilerParams(vmem_limit_bytes=16 << 20),
        cost_estimate=pl.CostEstimate(
            flops=12_000_000_000, bytes_accessed=1_000_000, transcendentals=0
        ),
        name="attend_back",
    )(place, *far(joined, joined, joined, probs), *dmixed, *carry)


def project_back(place, joined, probs, dmixed, normed, attend, carry, block, shards):
    count, width = normed.shape
    chunk = width // shards
    half, specs = attend_specs(joined, dmixed, True)
    result = pl.BlockSpec((count, width // 2), lambda p, place_ref: (0, 0))
    piece = jax.ShapeDtypeStruct((shards // 2, 4 * chunk, width // 2), jnp.bfloat16)
    specs = specs + [
        pl.BlockSpec(normed.shape, lambda p, place_ref: (0, 0)),
        pl.BlockSpec(attend.shape, lambda p, place_ref: (0, 0, 0)),
    ]
    return pl.pallas_call(
        carrying(functools.partial(project_kernel, block), 9, 5, len(carry)),
        grid_spec=pltpu.PrefetchScalarGridSpec(
            num_scalar_prefetch=1,
            grid=(half,),
            in_specs=specs + [in_place()] * len(carry),
            out_specs=[result] * 3 + [whole_vmem()] * 2 + [in_place()] * len(carry),
            scratch_shapes=[pltpu.VMEM((shards, 4 * chunk, width // 2), jnp.bfloat16)],
        ),
        out_shape=[jax.ShapeDtypeStruct((count, width // 2), jnp.bfloat16)] * 3
        + [piece, piece]
        + shapes_of(carry),
        input_output_aliases=aliases(9, 5, carry),
        compiler_params=pltpu.CompilerParams(vmem_limit_bytes=18 << 20),
        cost_estimate=pl.CostEstimate(
            flops=12_000_000_000, bytes_accessed=1_000_000, transcendentals=0
        ),
        name="project_back",
    )(place, *far(joined, joined, joined, probs), *dmixed, *far(normed), attend, *carry)


def input_kernel(
    place_ref,
    own_ref,
    other_ref,
    dq_own,
    dk_own,
    dv_own,
    dq_other,
    dk_other,
    dv_other,
    dafter_first,
    dafter_second,
    first_gain,
    attend_bias_grad,
    second_gain_grad,
    second_shift_grad,
    expand_bias_grad,
    contract_bias_grad,
    wpi_hbm,
    grad_out,
    keep,
    send,
    wpi,
    joined_v,
    x_v,
    grad_v,
    load_sem,
):
    me, blk = place_ref[0], place_ref[1]
    load = pltpu.make_async_copy(wpi_hbm, wpi, load_sem.at[0])
    load.start()
    count, width = x_v.shape
    part_width = width // 2
    shards = 2 * keep.shape[0]
    in_stream_order(x_v, own_ref, other_ref, blk)
    for side, group in ((blk, (dq_own, dk_own, dv_own)), (1 - blk, (dq_other, dk_other, dv_other))):
        for part, ref in enumerate(group):
            offset = part * width + side * part_width
            joined_v[:, pl.ds(pl.multiple_of(offset, part_width), part_width)] = ref[...]
    normed, scale = normalise(x_v[...])
    load.wait()
    dh1 = nt(joined_v[...], wpi[...])
    sums = jnp.sum(joined_v[...].astype(jnp.float32), axis=0, keepdims=True)
    vectors = [
        jnp.sum(dh1 * normed, axis=0, keepdims=True),
        jnp.sum(dh1, axis=0, keepdims=True),
        jnp.concatenate([sums[:, :width], sums[:, 2 * width :]], axis=1),
        attend_bias_grad[...],
        second_gain_grad[...],
        second_shift_grad[...],
        expand_bias_grad[...],
        contract_bias_grad[...],
    ]
    mine = lax.rem(me, 2)
    place = position(me, MASKS)
    for shard in range(shards):
        rows = []
        for vector in vectors:
            size = vector.shape[1] // shards
            piece = vector[:, shard * size : (shard + 1) * size]
            rows.append(jnp.concatenate([piece, jnp.zeros((1, 256 - size), jnp.float32)], axis=1))
        value = jnp.concatenate(rows, axis=0)
        target = lax.bitwise_xor(place, jnp.int32(position(shard, MASKS)))

        @pl.when(mine == shard % 2)
        def _():
            keep[target] = value

        @pl.when(mine != shard % 2)
        def _():
            send[target] = value

    rows = own_ref.shape[0]
    grad_v[...] = norm_back(normed, scale, as_row(first_gain), dh1)
    grad_v[:rows] += dafter_first[...]
    grad_v[rows:] += dafter_second[...]
    grad_out[...] = grad_v[pl.ds(pl.multiple_of(blk * rows, rows), rows), :]


def input_back(place, own, other, parts, dafter, gain, vectors, wpi, carry, shards):
    rows, width = own.shape
    count = 2 * rows
    low, full = jnp.bfloat16, jnp.float32
    half = jax.ShapeDtypeStruct((shards // 2, len(vectors) + 3, 256), full)
    return pl.pallas_call(
        carrying(input_kernel, 18, 3, len(carry)),
        in_specs=[scalars()] + [whole_vmem()] * 16 + [in_place()] * (1 + len(carry)),
        out_specs=[whole_vmem()] * 3 + [in_place()] * len(carry),
        out_shape=[jax.ShapeDtypeStruct((rows, width), full), half, half] + shapes_of(carry),
        input_output_aliases=aliases(18, 3, carry),
        scratch_shapes=[
            pltpu.VMEM(wpi.shape, low),
            pltpu.VMEM((count, 3 * width), low),
            pltpu.VMEM((count, width), full),
            pltpu.VMEM((count, width), full),
            pltpu.SemaphoreType.DMA((1,)),
        ],
        compiler_params=pltpu.CompilerParams(vmem_limit_bytes=24 << 20),
        cost_estimate=pl.CostEstimate(
            flops=12_000_000_000, bytes_accessed=1_000_000, transcendentals=0
        ),
        name="input_back",
    )(
        place, *far(own, other), *parts, *dafter, *far(gain), *vectors, *far(wpi), *carry
    )


def across(value, mask):
    return lax.ppermute(value, "dp", [(i, i ^ mask) for i in range(lax.axis_size("dp"))])


def halve(keep, received):
    half = keep.shape[0] // 2
    return (keep[:half] + received[:half], keep[half:] + received[half:])


def merge_kernel(layout, *refs):
    inputs, outputs = list(refs[: 2 * len(layout)]), list(refs[2 * len(layout) :])
    for index, mode in enumerate(layout):
        keep, got = inputs[2 * index], inputs[2 * index + 1]
        half = keep.shape[0] // 2
        if mode == "sum":
            outputs.pop(0)[...] = keep[...] + got[...]
        elif mode == "pass":
            outputs.pop(0)[...] = keep[...]
        elif mode == "halve":
            outputs.pop(0)[...] = keep[:half] + got[:half]
            outputs.pop(0)[...] = keep[half:] + got[half:]
        else:
            place = layout[:index].count("stack")
            if place == 0:
                stacked = (outputs.pop(0), outputs.pop(0))
            stacked[0][place : place + half] = keep[:half] + got[:half]
            stacked[1][place : place + half] = keep[half:] + got[half:]


def merge(*groups):
    layout = [mode for mode, _, _ in groups]
    shapes = []
    for index, (mode, keep, _) in enumerate(groups):
        size = keep.shape[0]
        if mode in ("sum", "pass"):
            shapes.append(jax.ShapeDtypeStruct(keep.shape, keep.dtype))
        elif mode == "halve" or "stack" not in layout[:index]:
            rows = size // 2 * (layout.count("stack") if mode == "stack" else 1)
            shapes += [jax.ShapeDtypeStruct((rows, *keep.shape[1:]), keep.dtype)] * 2
    arrays = [array for _, keep, got in groups for array in (keep, got)]
    return pl.pallas_call(
        functools.partial(merge_kernel, layout),
        in_specs=[whole_vmem()] * len(arrays),
        out_specs=[whole_vmem()] * len(shapes),
        out_shape=shapes,
        compiler_params=pltpu.CompilerParams(vmem_limit_bytes=16 << 20),
        cost_estimate=pl.CostEstimate(flops=1_000_000, bytes_accessed=1_000_000, transcendentals=0),
        name="merge",
    )(*arrays)


def feed_finish_kernel(place_ref, own_ref, other_ref, contract_out, expand_out):
    blk = place_ref[1]
    part = own_ref.shape[2]
    chunk = expand_out.shape[0]
    half = expand_out.shape[1] // 2
    for side, ref in ((blk, own_ref), (1 - blk, other_ref)):
        contract_out[:, pl.ds(pl.multiple_of(side * part, part), part)] = ref[0].astype(jnp.float32)
        for index in range(half // part):
            offset = side * half + index * part
            expand_out[:, pl.ds(pl.multiple_of(offset, part), part)] = ref[
                1, index * chunk : (index + 1) * chunk
            ].astype(jnp.float32)


def feed_finish(place, own, other, chunk):
    _, rows, part = own.shape
    full = jnp.float32
    return pl.pallas_call(
        feed_finish_kernel,
        in_specs=[scalars()] + [whole_vmem()] * 2,
        out_specs=[whole_vmem()] * 2,
        out_shape=[
            jax.ShapeDtypeStruct((rows, 2 * part), full),
            jax.ShapeDtypeStruct((chunk, 2 * part * rows // chunk), full),
        ],
        compiler_params=pltpu.CompilerParams(vmem_limit_bytes=16 << 20),
        cost_estimate=pl.CostEstimate(flops=1_000_000, bytes_accessed=1_000_000, transcendentals=0),
        name="feed_finish",
    )(place, own, other)


def finish_kernel(
    place_ref, own_ref, other_ref, keep_ref, got_ref, _, attend_out, project_out, *vector_outs
):
    blk = place_ref[1]
    chunk, width = attend_out.shape
    part = width // 2
    for side, ref in ((blk, own_ref), (1 - blk, other_ref)):
        for index in range(4):
            value = ref[index * chunk : (index + 1) * chunk].astype(jnp.float32)
            if index == 0:
                target, offset = attend_out, side * part
            else:
                target, offset = project_out, (index - 1) * width + side * part
            target[:, pl.ds(pl.multiple_of(offset, part), part)] = value
    total = keep_ref[0] + got_ref[0]
    for index, out in enumerate(vector_outs):
        out[...] = total[index : index + 1, : out.shape[1]]


def finish(place, own, other, keep, got, ready, chunk, sizes):
    width = 2 * own.shape[1]
    full = jnp.float32
    return pl.pallas_call(
        finish_kernel,
        in_specs=[scalars()] + [whole_vmem()] * 4 + [in_place()],
        out_specs=[whole_vmem()] * (2 + len(sizes)),
        out_shape=[
            jax.ShapeDtypeStruct((chunk, width), full),
            jax.ShapeDtypeStruct((chunk, 3 * width), full),
        ]
        + [jax.ShapeDtypeStruct((1, size), full) for size in sizes],
        compiler_params=pltpu.CompilerParams(vmem_limit_bytes=16 << 20),
        cost_estimate=pl.CostEstimate(flops=1_000_000, bytes_accessed=1_000_000, transcendentals=0),
        name="finish",
    )(place, own, other, keep, got, ready)


def swap(value):
    return lax.ppermute(value, "blk", [(0, 1), (1, 0)])


def both_halves(own, other, blk):
    return jnp.where(
        blk == 0,
        jnp.concatenate([own, other], axis=-1),
        jnp.concatenate([other, own], axis=-1),
    ).astype(jnp.float32)


def local_pair(hidden, doc_lengths, *arrays):
    student, teacher = arrays[:12], arrays[12:24]
    final_gain, final_shift, table = arrays[24:]
    rows, width = hidden.shape
    shards = lax.axis_size("dp")
    blk = lax.axis_index("blk")
    place = jnp.stack([lax.axis_index("dp"), blk]).astype(jnp.int32)
    other = swap(hidden)
    def block(train, params):
        gain, shift, wpi, qvb, wao, bao, gain_two, shift_two, we, be, wc, bc = params
        vectors = (gain, shift, qvb, bao, gain_two, shift_two, be, bc, final_gain, final_shift)
        return forward(
            train,
            place,
            doc_lengths,
            hidden,
            other,
            vectors,
            (wpi, wao, we, wc),
        )

    (rows_t,) = block(False, teacher)
    rows_s, normed, joined, probs, mixed, after, normed_two, slope, active, y = block(True, student)
    diff, expo, stats, sums = logits_phase(rows_s, rows_t, table)
    gain, shift, wpi, qvb, wao, bao, gain_two, shift_two, we, be, wc, bc = student
    sums_other = swap(sums)
    own_first, low_first, partial, norms, we = gradient_phase(
        diff, expo, table, stats, sums, sums_other, we
    )
    got_first = swap(low_first)
    own_second, low_second = gradient_rest(diff, expo, table, stats, norms, partial)
    got_second = swap(low_second)
    dm, dinner, dafter_first, dbranch, dmixed_first, dbc, dbe, *branch_sums = first_rows(
        own_first, got_first, y, after, final_gain, gain_two, wc, we, wao, slope
    )
    cw_keep, cw_send, ew_keep, ew_send, dy, dinner, dbc, dbe = feed_back(
        place,
        own_second,
        got_second,
        y,
        final_gain,
        dm,
        normed_two,
        (dbc, dbe),
        wc,
        slope,
        active,
        dinner,
        shards,
    )
    cw_got = across(cw_send, MASKS[0])
    ew_got = across(ew_send, MASKS_B[0])
    dafter_second, dmixed_second, attend, dgain_two, dshift_two, dbao, cw_keep, ew_keep = (
        branch_back(
            place,
            dy,
            after,
            mixed,
            gain_two,
            dbranch,
            branch_sums,
            dinner,
            we,
            wao,
            (cw_keep, ew_keep),
            shards,
        )
    )
    dafter, dmixed = (dafter_first, dafter_second), (dmixed_first, dmixed_second)
    cw_keep, cw_send = halve(cw_keep, cw_got)
    cw_got = across(cw_send, MASKS[1])
    ew_keep, ew_send = halve(ew_keep, ew_got)
    ew_got = across(ew_send, MASKS_B[1])
    *own_grads, keep, send, cw_keep, ew_keep = project_back(
        place, joined, probs, dmixed, normed, attend, (cw_keep, ew_keep), rows, shards
    )
    got = across(send, MASKS[0])
    cw_keep, cw_send, ew_keep, ew_send = merge(("halve", cw_keep, cw_got), ("halve", ew_keep, ew_got))
    cw_got = across(cw_send, MASKS[2])
    ew_got = across(ew_send, MASKS_B[2])
    *other_grads, keep, cw_keep, ew_keep = attend_back(
        place, joined, probs, dmixed, (keep, cw_keep, ew_keep), rows
    )
    keep, send, both_keep, both_send = merge(
        ("halve", keep, got), ("stack", cw_keep, cw_got), ("stack", ew_keep, ew_got)
    )
    got = across(send, MASKS[1])
    both_got = across(both_send, MASKS[3])
    input_grad, vector_keep, vector_send, keep, both_keep = input_back(
        place,
        hidden,
        other,
        (*own_grads, *other_grads),
        dafter,
        gain,
        (dbao, dgain_two, dshift_two, dbe, dbc),
        wpi,
        (keep, both_keep),
        shards,
    )
    vector_got = across(vector_send, MASKS[0])
    keep, send, both, vector_keep, vector_send = merge(
        ("halve", keep, got),
        ("sum", both_keep, both_got),
        ("halve", vector_keep, vector_got),
    )
    got, vector_got = across(send, MASKS[2]), across(vector_send, MASKS[1])
    keep, send, both, vector_keep, vector_send = merge(
        ("halve", keep, got),
        ("pass", both, both),
        ("halve", vector_keep, vector_got),
    )
    got, vector_got, both_other = (
        across(send, MASKS[3]),
        across(vector_send, MASKS[2]),
        swap(both),
    )
    last, vector_keep, vector_send = merge(
        ("sum", keep, got), ("halve", vector_keep, vector_got)
    )
    last = last[0]
    last_other = swap(last)
    vector_got = across(vector_send, MASKS[3])
    chunk = width // shards
    grad_cw, grad_ew = feed_finish(place, both, both_other, chunk)
    sizes = (chunk, chunk, 2 * chunk, chunk, chunk, chunk, be.shape[0] // shards, chunk)
    grad_ao, grad_pi, *vectors = finish(
        place, last, last_other, vector_keep, vector_got, grad_cw, chunk, sizes
    )
    dgain, dshift, dqvb, dbao, dgain_two, dshift_two, dbe, dbc = (
        vector.reshape(-1) for vector in vectors
    )
    return (
        lax.dynamic_slice_in_dim(norms[2], blk * rows, rows),
        input_grad,
        dgain,
        dshift,
        grad_pi,
        dqvb,
        grad_ao,
        dbao,
        dgain_two,
        dshift_two,
        grad_ew,
        dbe,
        grad_cw,
        dbc,
    )


def solution(mesh):
    pair = mesh.shape["dp"] == 16 and mesh.shape["blk"] == 2
    return jax.shard_map(
        local_pair if pair else local_general,
        mesh=mesh,
        in_specs=(
            P(("dp", "blk"), None),
            P("dp", None),
            P(),
            P(),
            P(),
            P(),
            P(),
            P(),
            P(),
            P(),
            P(),
            P(),
            P(),
            P(),
            P(),
            P(),
            P(),
            P(),
            P(),
            P(),
            P(),
            P(),
            P(),
            P(),
            P(),
            P(),
            P(),
            P(),
            P("blk", None),
        ),
        out_specs=(
            P(("dp", "blk")),
            P(("dp", "blk"), None),
            P("dp"),
            P("dp"),
            P("dp", None),
            P("dp"),
            P("dp", None),
            P("dp"),
            P("dp"),
            P("dp"),
            P("dp", None),
            P("dp"),
            P("dp", None),
            P("dp"),
        ),
        check_vma=False,
    )
```

```python
import functools

import jax
import jax.numpy as jnp
from jax import lax
from jax.experimental import pallas as pl
from jax.experimental.pallas import tpu as pltpu
from jax.sharding import PartitionSpec as P

HEADS = 12
HEAD_DIM = 64
TABLE_SPAN = 2048
SPLIT_STEPS = 4
MASKS = (1, 2, 4, 8)
MASKS_B = (1, 4, 2, 8)


negative = -1e30


def layer_norm(value, gain, shift):
    centre = value - jnp.mean(value, axis=-1, keepdims=True)
    return (
        centre * lax.rsqrt(jnp.mean(centre * centre, axis=-1, keepdims=True) + 1e-05) * gain + shift
    )


def doc_numbers(lengths, count):
    ends = jnp.cumsum(lengths)
    places = jnp.arange(count, dtype=jnp.int32)
    return jnp.sum((places[:, None] >= ends[None, :]).astype(jnp.int32), axis=1)


def dense(left, right):
    return jnp.dot(left, right, preferred_element_type=jnp.float32)


def split_heads(value):
    return value.reshape(value.shape[0], HEADS, HEAD_DIM)


def input_side(inputs, gain, shift, project_in, qv_bias):
    width = inputs.shape[1]
    normed = layer_norm(inputs, gain, shift).astype(jnp.bfloat16)
    bias = jnp.concatenate([qv_bias[:width], jnp.zeros((width,), jnp.float32), qv_bias[width:]])
    joined = (dense(normed, project_in) + bias).astype(jnp.bfloat16)
    return (normed, joined[:, :width], joined[:, width : 2 * width], joined[:, 2 * width :])


def output_side(
    inputs,
    mixed_low,
    attend_out,
    attend_bias,
    second_gain,
    second_shift,
    expand_weight,
    expand_bias,
    contract_weight,
    contract_bias,
):
    after = inputs + dense(mixed_low, attend_out) + attend_bias
    normed = layer_norm(after, second_gain, second_shift).astype(jnp.bfloat16)
    inner = dense(normed, expand_weight) + expand_bias
    active = jax.nn.gelu(inner, approximate=True).astype(jnp.bfloat16)
    final = after + dense(active, contract_weight) + contract_bias
    return (after, normed, inner, active, final)


def online(state, query, keys, values, allowed):
    top, mass, summed = state
    scores = (
        jnp.einsum(
            "qhd,khd->hqk",
            split_heads(query),
            split_heads(keys),
            preferred_element_type=jnp.float32,
        )
        * 0.125
    )
    scores = jnp.where(allowed[None], scores, negative)
    new_top = jnp.maximum(top, jnp.max(scores, axis=-1))
    factor = jnp.exp(top - new_top)
    weights = jnp.where(allowed[None], jnp.exp(scores - new_top[..., None]), 0.0)
    mass = mass * factor + jnp.sum(weights, axis=-1)
    summed = summed * factor[..., None] + jnp.einsum(
        "hqk,khd->hqd",
        weights.astype(jnp.bfloat16),
        split_heads(values),
        preferred_element_type=jnp.float32,
    )
    return (new_top, mass, summed)


def score_grads(query_heads, grad_heads, log_norm, balance, key_block, value_block, allowed):
    scores = (
        jnp.einsum("qhd,khd->hqk", query_heads, key_block, preferred_element_type=jnp.float32)
        * 0.125
    )
    probs = jnp.where(allowed[None], jnp.exp(scores - log_norm[..., None]), 0.0)
    grad_probs = jnp.einsum(
        "qhd,khd->hqk", grad_heads, value_block, preferred_element_type=jnp.float32
    )
    grad_scores = (probs * (grad_probs - balance[..., None])).astype(jnp.bfloat16)
    return (probs, grad_scores)


def partial_stats(rows_teacher, rows_student, table):
    half_t = jnp.einsum("rd,vd->rv", rows_teacher, table, preferred_element_type=jnp.float32) * 0.5
    half_s = jnp.einsum("rd,vd->rv", rows_student, table, preferred_element_type=jnp.float32) * 0.5
    top_t = jnp.max(half_t, axis=-1)
    expo_t = jnp.exp(half_t - top_t[:, None])
    top_s = jnp.max(half_s, axis=-1)
    return (
        top_t,
        jnp.sum(expo_t, axis=-1),
        jnp.sum(expo_t * (half_t - half_s), axis=-1),
        top_s,
        jnp.sum(jnp.exp(half_s - top_s[:, None]), axis=-1),
    )


def combine(first_stats, second_stats):
    top_t = jnp.maximum(first_stats[0], second_stats[0])
    right_weight = jnp.exp(second_stats[0] - top_t)
    top_s = jnp.maximum(first_stats[3], second_stats[3])
    return (
        top_t,
        second_stats[1] * right_weight,
        second_stats[2] * right_weight,
        top_s,
        second_stats[4] * jnp.exp(second_stats[3] - top_s),
    )


def row_gradient(rows_teacher, rows_student, table, norm_t, norm_s):
    half_t = jnp.einsum("rd,vd->rv", rows_teacher, table, preferred_element_type=jnp.float32) * 0.5
    half_s = jnp.einsum("rd,vd->rv", rows_student, table, preferred_element_type=jnp.float32) * 0.5
    change = ((jnp.exp(half_s - norm_s[:, None]) - jnp.exp(half_t - norm_t[:, None])) * 0.5).astype(
        jnp.bfloat16
    )
    return dense(change, table)


def local_general(
    hidden,
    doc_lengths,
    student_first_gain,
    student_first_shift,
    student_project_in,
    student_query_value_bias,
    student_attend_out,
    student_attend_bias,
    student_second_gain,
    student_second_shift,
    student_expand_weight,
    student_expand_bias,
    student_contract_weight,
    student_contract_bias,
    teacher_first_gain,
    teacher_first_shift,
    teacher_project_in,
    teacher_query_value_bias,
    teacher_attend_out,
    teacher_attend_bias,
    teacher_second_gain,
    teacher_second_shift,
    teacher_expand_weight,
    teacher_expand_bias,
    teacher_contract_weight,
    teacher_contract_bias,
    final_gain,
    final_shift,
    embedding,
):
    rows, width = hidden.shape
    blocks = lax.axis_size("blk")
    stream = rows * blocks
    first = lax.axis_index("blk") * rows
    last_place = first + rows - 1
    docs = doc_numbers(doc_lengths[0], stream)
    own_places = first + jnp.arange(rows, dtype=jnp.int32)
    own_docs = lax.dynamic_slice_in_dim(docs, first, rows)
    inputs = hidden.astype(jnp.float32)
    normed_s, query_s, keys_s, values_s = input_side(
        inputs,
        student_first_gain,
        student_first_shift,
        student_project_in,
        student_query_value_bias,
    )
    normed_t, query_t, keys_t, values_t = input_side(
        inputs,
        teacher_first_gain,
        teacher_first_shift,
        teacher_project_in,
        teacher_query_value_bias,
    )

    def allowed_for(begin):
        key_places = begin + jnp.arange(rows, dtype=jnp.int32)
        key_docs = lax.dynamic_slice_in_dim(docs, begin, rows)
        return (key_places[None, :] <= own_places[:, None]) & (
            key_docs[None, :] == own_docs[:, None]
        )

    start_state = (
        jnp.full((HEADS, rows), negative, jnp.float32),
        jnp.zeros((HEADS, rows), jnp.float32),
        jnp.zeros((HEADS, rows, HEAD_DIM), jnp.float32),
    )
    carry = (start_state, start_state)
    pieces = (
        lax.all_gather(keys_s, "blk", axis=0, tiled=True),
        lax.all_gather(values_s, "blk", axis=0, tiled=True),
        lax.all_gather(keys_t, "blk", axis=0, tiled=True),
        lax.all_gather(values_t, "blk", axis=0, tiled=True),
    )
    count = pieces[0].shape[0]
    stacked = tuple((member.reshape(count // rows, rows, width) for member in pieces))
    begins = rows * jnp.arange(count // rows, dtype=jnp.int32)

    def step(state, item):
        piece_keys_s, piece_values_s, piece_keys_t, piece_values_t, begin = item

        def step_compute(inner_state):
            allowed = allowed_for(begin)
            return (
                online(inner_state[0], query_s, piece_keys_s, piece_values_s, allowed),
                online(inner_state[1], query_t, piece_keys_t, piece_values_t, allowed),
            )

        return (
            lax.cond(begin <= last_place, step_compute, lambda inner_state: inner_state, state),
            None,
        )

    carry, _ = lax.scan(step, carry, stacked + (begins,))
    state_s, state_t = carry
    out_heads_s = state_s[2] / state_s[1][..., None]
    attn_norm = state_s[0] + jnp.log(state_s[1])
    mixed_low_s = out_heads_s.transpose(1, 0, 2).reshape(rows, width).astype(jnp.bfloat16)
    mixed_low_t = (
        (state_t[2] / state_t[1][..., None])
        .transpose(1, 0, 2)
        .reshape(rows, width)
        .astype(jnp.bfloat16)
    )
    after_s, normed_two_s, inner_s, active_s, final_s = output_side(
        inputs,
        mixed_low_s,
        student_attend_out,
        student_attend_bias,
        student_second_gain,
        student_second_shift,
        student_expand_weight,
        student_expand_bias,
        student_contract_weight,
        student_contract_bias,
    )
    after_t, normed_two_t, inner_t, active_t, final_t = output_side(
        inputs,
        mixed_low_t,
        teacher_attend_out,
        teacher_attend_bias,
        teacher_second_gain,
        teacher_second_shift,
        teacher_expand_weight,
        teacher_expand_bias,
        teacher_contract_weight,
        teacher_contract_bias,
    )
    rows_s = layer_norm(final_s, final_gain, final_shift).astype(jnp.bfloat16)
    rows_t = layer_norm(final_t, final_gain, final_shift).astype(jnp.bfloat16)
    identity = (
        jnp.full((rows,), negative, jnp.float32),
        jnp.zeros((rows,), jnp.float32),
        jnp.zeros((rows,), jnp.float32),
        jnp.full((rows,), negative, jnp.float32),
        jnp.zeros((rows,), jnp.float32),
    )
    merged = combine(
        identity,
        partial_stats(rows_t, rows_s, lax.all_gather(embedding, "blk", axis=0, tiled=True)),
    )
    norm_t = merged[0] + jnp.log(merged[1])
    norm_s = merged[3] + jnp.log(merged[4])
    kl_rows = merged[2] / merged[1] - norm_t + norm_s
    grad_final = row_gradient(
        rows_t, rows_s, lax.all_gather(embedding, "blk", axis=0, tiled=True), norm_t, norm_s
    )
    _, final_back = jax.vjp(layer_norm, final_s, final_gain, final_shift)
    grad_y = final_back(grad_final)[0]
    grad_m = grad_y.astype(jnp.bfloat16)
    grad_contract_weight = jnp.einsum(
        "rf,rd->fd", active_s, grad_m, preferred_element_type=jnp.float32
    )
    grad_contract_bias = jnp.sum(grad_m.astype(jnp.float32), axis=0)
    grad_active = jnp.einsum(
        "rd,fd->rf", grad_m, student_contract_weight, preferred_element_type=jnp.float32
    )
    _, gelu_back = jax.vjp(lambda value: jax.nn.gelu(value, approximate=True), inner_s)
    grad_inner = gelu_back(grad_active)[0].astype(jnp.bfloat16)
    grad_expand_weight = jnp.einsum(
        "rd,rf->df", normed_two_s, grad_inner, preferred_element_type=jnp.float32
    )
    grad_expand_bias = jnp.sum(grad_inner.astype(jnp.float32), axis=0)
    grad_normed_two = jnp.einsum(
        "rf,df->rd", grad_inner, student_expand_weight, preferred_element_type=jnp.float32
    )
    _, second_back = jax.vjp(layer_norm, after_s, student_second_gain, student_second_shift)
    grad_after_norm, grad_second_gain, grad_second_shift = second_back(grad_normed_two)
    grad_after = grad_y + grad_after_norm
    grad_branch = grad_after.astype(jnp.bfloat16)
    grad_attend_out = jnp.einsum(
        "rc,rd->cd", mixed_low_s, grad_branch, preferred_element_type=jnp.float32
    )
    grad_attend_bias = jnp.sum(grad_branch.astype(jnp.float32), axis=0)
    grad_mixed = jnp.einsum(
        "rd,cd->rc", grad_branch, student_attend_out, preferred_element_type=jnp.float32
    ).astype(jnp.bfloat16)
    keys_all, values_all = (
        lax.all_gather(keys_s, "blk", axis=0, tiled=True),
        lax.all_gather(values_s, "blk", axis=0, tiled=True),
    )
    grad_heads = split_heads(grad_mixed)
    query_heads = split_heads(query_s)
    balance = jnp.sum(grad_heads.astype(jnp.float32).transpose(1, 0, 2) * out_heads_s, axis=-1)
    begins = rows * jnp.arange(blocks, dtype=jnp.int32)
    zero_query = jnp.zeros((rows, HEADS, HEAD_DIM), jnp.float32)

    def back_step(grad_query, begin):
        key_block = split_heads(lax.dynamic_slice_in_dim(keys_all, begin, rows, 0))
        value_block = split_heads(lax.dynamic_slice_in_dim(values_all, begin, rows, 0))

        def back_compute(total):
            probs, grad_scores = score_grads(
                query_heads,
                grad_heads,
                attn_norm,
                balance,
                key_block,
                value_block,
                allowed_for(begin),
            )
            total = (
                total
                + jnp.einsum(
                    "hqk,khd->qhd", grad_scores, key_block, preferred_element_type=jnp.float32
                )
                * 0.125
            )
            grad_keys = (
                jnp.einsum(
                    "hqk,qhd->khd", grad_scores, query_heads, preferred_element_type=jnp.float32
                )
                * 0.125
            )
            grad_values = jnp.einsum(
                "hqk,qhd->khd",
                probs.astype(jnp.bfloat16),
                grad_heads,
                preferred_element_type=jnp.float32,
            )
            return (
                total,
                jnp.concatenate(
                    [grad_keys.reshape(rows, width), grad_values.reshape(rows, width)], axis=1
                ),
            )

        def skip(total):
            return (total, jnp.zeros((rows, 2 * width), jnp.float32))

        return lax.cond(begin <= last_place, back_compute, skip, grad_query)

    grad_query, key_terms = lax.scan(back_step, zero_query, begins)
    key_value_grad = lax.psum_scatter(
        key_terms.reshape(stream, 2 * width).astype(jnp.bfloat16),
        "blk",
        scatter_dimension=0,
        tiled=True,
    ).astype(jnp.float32)
    grad_keys_low = key_value_grad[:, :width].astype(jnp.bfloat16)
    grad_values_low = key_value_grad[:, width:].astype(jnp.bfloat16)
    grad_query_low = grad_query.reshape(rows, width).astype(jnp.bfloat16)
    grad_joined = jnp.concatenate([grad_query_low, grad_keys_low, grad_values_low], axis=1)
    grad_project_in = jnp.einsum(
        "rd,rc->dc", normed_s, grad_joined, preferred_element_type=jnp.float32
    )
    grad_query_value_bias = jnp.concatenate(
        [
            jnp.sum(grad_query_low.astype(jnp.float32), axis=0),
            jnp.sum(grad_values_low.astype(jnp.float32), axis=0),
        ]
    )
    grad_normed = jnp.einsum(
        "rc,dc->rd", grad_joined, student_project_in, preferred_element_type=jnp.float32
    )
    _, first_back = jax.vjp(layer_norm, inputs, student_first_gain, student_first_shift)
    grad_inputs_norm, grad_first_gain, grad_first_shift = first_back(grad_normed)
    input_grad = grad_after + grad_inputs_norm
    shares = (
        lax.psum_scatter(
            grad_first_gain.astype(jnp.bfloat16), "dp", scatter_dimension=0, tiled=True
        ).astype(jnp.float32),
        lax.psum_scatter(
            grad_first_shift.astype(jnp.bfloat16), "dp", scatter_dimension=0, tiled=True
        ).astype(jnp.float32),
        lax.psum_scatter(
            grad_project_in.astype(jnp.bfloat16), "dp", scatter_dimension=0, tiled=True
        ).astype(jnp.float32),
        lax.psum_scatter(
            grad_query_value_bias.astype(jnp.bfloat16), "dp", scatter_dimension=0, tiled=True
        ).astype(jnp.float32),
        lax.psum_scatter(
            grad_attend_out.astype(jnp.bfloat16), "dp", scatter_dimension=0, tiled=True
        ).astype(jnp.float32),
        lax.psum_scatter(
            grad_attend_bias.astype(jnp.bfloat16), "dp", scatter_dimension=0, tiled=True
        ).astype(jnp.float32),
        lax.psum_scatter(
            grad_second_gain.astype(jnp.bfloat16), "dp", scatter_dimension=0, tiled=True
        ).astype(jnp.float32),
        lax.psum_scatter(
            grad_second_shift.astype(jnp.bfloat16), "dp", scatter_dimension=0, tiled=True
        ).astype(jnp.float32),
        lax.psum_scatter(
            grad_expand_weight.astype(jnp.bfloat16), "dp", scatter_dimension=0, tiled=True
        ).astype(jnp.float32),
        lax.psum_scatter(
            grad_expand_bias.astype(jnp.bfloat16), "dp", scatter_dimension=0, tiled=True
        ).astype(jnp.float32),
        lax.psum_scatter(
            grad_contract_weight.astype(jnp.bfloat16), "dp", scatter_dimension=0, tiled=True
        ).astype(jnp.float32),
        lax.psum_scatter(
            grad_contract_bias.astype(jnp.bfloat16), "dp", scatter_dimension=0, tiled=True
        ).astype(jnp.float32),
    )
    summed = (
        lax.psum(shares[0].astype(jnp.bfloat16), "blk").astype(jnp.float32),
        lax.psum(shares[1].astype(jnp.bfloat16), "blk").astype(jnp.float32),
        lax.psum(shares[2].astype(jnp.bfloat16), "blk").astype(jnp.float32),
        lax.psum(shares[3].astype(jnp.bfloat16), "blk").astype(jnp.float32),
        lax.psum(shares[4].astype(jnp.bfloat16), "blk").astype(jnp.float32),
        lax.psum(shares[5].astype(jnp.bfloat16), "blk").astype(jnp.float32),
        lax.psum(shares[6].astype(jnp.bfloat16), "blk").astype(jnp.float32),
        lax.psum(shares[7].astype(jnp.bfloat16), "blk").astype(jnp.float32),
        lax.psum(shares[8].astype(jnp.bfloat16), "blk").astype(jnp.float32),
        lax.psum(shares[9].astype(jnp.bfloat16), "blk").astype(jnp.float32),
        lax.psum(shares[10].astype(jnp.bfloat16), "blk").astype(jnp.float32),
        lax.psum(shares[11].astype(jnp.bfloat16), "blk").astype(jnp.float32),
    )
    return (
        kl_rows,
        input_grad,
        summed[0],
        summed[1],
        summed[2],
        summed[3],
        summed[4],
        summed[5],
        summed[6],
        summed[7],
        summed[8],
        summed[9],
        summed[10],
        summed[11],
    )


def nt(left, right):
    return lax.dot_general(
        left, right, (((1,), (1,)), ((), ())), preferred_element_type=jnp.float32
    )


def tn(left, right):
    return lax.dot_general(
        left, right, (((0,), (0,)), ((), ())), preferred_element_type=jnp.float32
    )


def normalise(value):
    centre = value - jnp.mean(value, axis=-1, keepdims=True)
    scale = lax.rsqrt(jnp.mean(centre * centre, axis=-1, keepdims=True) + 1e-05)
    return (centre * scale, scale)


def norm_back(normed, scale, gain, grad):
    weighted = grad * gain
    return scale * (
        weighted
        - jnp.mean(weighted, axis=-1, keepdims=True)
        - normed * jnp.mean(weighted * normed, axis=-1, keepdims=True)
    )


def starts_of(lengths_ref, count):
    places = lax.broadcasted_iota(jnp.int32, (1, count), 1)
    start = jnp.zeros((1, count), jnp.int32)
    end = jnp.int32(0)
    for index in range(lengths_ref.shape[1]):
        end = end + lengths_ref[0, index]
        start = jnp.where(places >= end, jnp.maximum(start, end), start)
    return start


def in_stream_order(target, own_ref, other_ref, blk):
    rows = own_ref.shape[0]
    target[pl.ds(pl.multiple_of(blk * rows, rows), rows), :] = own_ref[...].astype(target.dtype)
    target[pl.ds(pl.multiple_of((1 - blk) * rows, rows), rows), :] = other_ref[...].astype(
        target.dtype
    )


def head_mask(shape, which):
    lanes = lax.broadcasted_iota(jnp.int32, shape, 1)
    return (lanes >= HEAD_DIM) if which else (lanes < HEAD_DIM)


def forward_kernel(*refs):
    place_ref, lengths_ref, own_ref, other_ref = refs[:4]
    vectors = (refs[4:12], refs[12:20])
    final_gain, final_shift = (as_row(ref) for ref in refs[20:22])
    weights_hbm = (refs[22:26], refs[26:30])
    rows_t, rows_s = refs[30:32]
    kept_hbm = refs[32:41]
    wpi, wao, we, wc = weights = refs[41:45]
    kept = refs[45:54]
    normed_v, joined_v, probs_v, mixed_v, after_v, normed_two_v, slope_v, active_v, y_v = kept
    x_v, scaled_v, bias_v, vector_v, wide_v, weight_sem, out_sem, probs_sem = refs[54:]
    count, width = x_v.shape
    block = own_ref.shape[0]
    hidden_width = we.shape[1]
    pair = 2 * HEAD_DIM
    pairs = width // pair

    def load(index, which):
        return pltpu.make_async_copy(weights_hbm[which][index], weights[index], weight_sem.at[index])

    def save(slot, index, *at):
        source, target = kept[index], kept_hbm[index]
        if at:
            source, target = source.at[at], target.at[at]
        return pltpu.make_async_copy(source, target, out_sem.at[slot])

    def save_probs(index):
        heads = pl.ds(2 * index, 2)
        return pltpu.make_async_copy(
            probs_v.at[heads], kept_hbm[2].at[heads], probs_sem.at[index]
        )

    def save_wide(side, part):
        span = pl.ds(part * width, width)
        return save(7 + 4 * side + part, 6 + side, slice(None), span)

    for index in range(4):
        load(index, 0).start()
    in_stream_order(x_v, own_ref, other_ref, place_ref[1])
    scaled_v[...] = normalise(x_v[...])[0]
    for which, group in enumerate(vectors):
        gain, shift, qv_bias, bias_a, gain_two, shift_two, bias_e, bias_c = group
        for row, ref in enumerate((gain, shift, bias_a, gain_two, shift_two, bias_c)):
            vector_v[which, row : row + 1] = as_row(ref)
        both = as_row(qv_bias)
        vector_v[which, 6:7] = both[:, :width]
        vector_v[which, 7:8] = both[:, width:]
        wide_v[which, 0:1] = as_row(bias_e)
    start = starts_of(lengths_ref, count)
    keys_at = lax.broadcasted_iota(jnp.int32, (count, count), 0)
    queries_at = lax.broadcasted_iota(jnp.int32, (count, count), 1)
    bias_v[...] = jnp.where((keys_at <= queries_at) & (keys_at >= start), 0.0, negative)

    def attend(index, _):
        column = pl.ds(pl.multiple_of(index * pair, pair), pair)
        query = joined_v[:, column] * jnp.bfloat16(0.125)
        keys = joined_v[:, pl.ds(pl.multiple_of(width + index * pair, pair), pair)]
        values = joined_v[:, pl.ds(pl.multiple_of(2 * width + index * pair, pair), pair)]
        for piece in range(count // block):
            span = slice(piece * block, (piece + 1) * block)
            reach = (piece + 1) * block
            both = []
            for which in range(2):
                mine = jnp.where(
                    head_mask((block, pair), which), query[span], jnp.bfloat16(0.0)
                )
                scores = nt(keys[:reach], mine) + bias_v[:reach, span]
                expo = jnp.exp(scores - jnp.max(scores, axis=0, keepdims=True))
                probs = expo * (1.0 / jnp.sum(expo, axis=0, keepdims=True))
                probs = probs.astype(jnp.bfloat16)
                probs_v[2 * index + which, :reach, span] = probs
                both.append(tn(probs, values[:reach]))
            mixed_v[span, column] = jnp.where(
                head_mask((block, pair), 0), both[0], both[1]
            ).astype(jnp.bfloat16)
        return 0

    def feed(train, which):
        root = 0.7978845608028654
        total = after_v[...] + vector_v[which, 5:6]
        for part in range(hidden_width // width):
            span = slice(part * width, (part + 1) * width)
            inner = dense(normed_two_v[...], we[:, span]) + wide_v[which, 0:1, span]
            square = inner * inner
            bent = jnp.tanh(root * (inner + 0.044715 * (square * inner)))
            upper = 0.5 * (1.0 + bent)
            active = (inner * upper).astype(jnp.bfloat16)
            if train:
                active_v[:, span] = active
                slope_v[:, span] = (
                    upper
                    + (0.5 * root) * inner * (1.0 - bent * bent) * (1.0 + (3 * 0.044715) * square)
                ).astype(jnp.bfloat16)
                save_wide(0, part).start()
                save_wide(1, part).start()
            total = total + dense(active, wc[span, :])
        normed, _ = normalise(total)
        rows = (normed * final_gain + final_shift).astype(jnp.bfloat16) * jnp.bfloat16(0.5)
        if train:
            y_v[...] = total
            save(6, 8).start()
            rows_s[...] = rows
        else:
            rows_t[...] = rows

    def one(which, _):
        student = which == 1

        def row(index):
            return vector_v[which, index : index + 1]

        normed_v[...] = (scaled_v[...] * row(0) + row(1)).astype(jnp.bfloat16)
        load(0, 0).wait()
        for part in range(3):
            span = slice(part * width, (part + 1) * width)
            value = dense(normed_v[...], wpi[:, span])
            if part == 0:
                value = value + row(6)
            if part == 2:
                value = value + row(7)
            joined_v[:, span] = value.astype(jnp.bfloat16)

        @pl.when(student)
        def _():
            save(0, 0).start()
            save(1, 1).start()

        @pl.when(which == 0)
        def _():
            load(0, 1).start()

        lax.fori_loop(0, pairs, attend, 0, unroll=3)

        @pl.when(student)
        def _():
            for index in range(pairs):
                save_probs(index).start()
            save(2, 3).start()

        load(1, 0).wait()
        after_v[...] = x_v[...] + dense(mixed_v[...], wao[...]) + row(2)
        normed, _ = normalise(after_v[...])
        normed_two_v[...] = (normed * row(3) + row(4)).astype(jnp.bfloat16)
        load(2, 0).wait()
        load(3, 0).wait()

        @pl.when(which == 0)
        def _():
            load(1, 1).start()
            feed(False, 0)
            load(2, 1).start()
            load(3, 1).start()

        @pl.when(student)
        def _():
            save(3, 4).start()
            save(4, 5).start()
            feed(True, 1)

        return 0

    lax.fori_loop(0, 2, one, 0)
    for index in range(pairs):
        save_probs(index).wait()
    for slot, index in enumerate((0, 1, 3, 4, 5)):
        save(slot, index).wait()
    save(6, 8).wait()
    for part in range(hidden_width // width):
        save_wide(0, part).wait()
        save_wide(1, part).wait()


def carrying(kernel, inputs, outputs, carried):
    def body(*refs):
        rest = refs[inputs + carried :]
        kernel(*refs[:inputs], *rest[:outputs], *rest[outputs + carried :])

    return body


def shapes_of(carry):
    return [jax.ShapeDtypeStruct(item.shape, item.dtype) for item in carry]


def aliases(inputs, outputs, carry):
    return {inputs + index: outputs + index for index in range(len(carry))}


def as_row(ref):
    return ref[...].reshape(1, ref.shape[0])


def whole_vmem():
    return pl.BlockSpec(memory_space=pltpu.VMEM)


def in_place():
    return pl.BlockSpec(memory_space=pl.ANY)


def far(*arrays):
    return [pltpu.with_memory_space_constraint(array, pltpu.HBM) for array in arrays]


def near(*arrays):
    return [pltpu.with_memory_space_constraint(array, pltpu.VMEM) for array in arrays]


def scalars():
    return pl.BlockSpec(memory_space=pltpu.SMEM)


def forward(place, lengths, own, other, teacher, student, final):
    rows, width = own.shape
    count = 2 * rows
    weights = [group[index] for group in (teacher, student) for index in (2, 4, 8, 10)]
    vectors = [
        group[index] for group in (teacher, student) for index in (0, 1, 3, 5, 6, 7, 9, 11)
    ]
    hidden_width = weights[2].shape[1]
    low, full = jnp.bfloat16, jnp.float32
    kept = [
        ((count, width), low),
        ((count, 3 * width), low),
        ((HEADS, count, count), low),
        ((count, width), low),
        ((count, width), full),
        ((count, width), low),
        ((count, hidden_width), low),
        ((count, hidden_width), low),
        ((count, width), full),
    ]
    return pl.pallas_call(
        forward_kernel,
        in_specs=[scalars(), scalars()] + [whole_vmem()] * 20 + [in_place()] * 8,
        out_specs=[whole_vmem()] * 2 + [in_place()] * len(kept),
        out_shape=[jax.ShapeDtypeStruct((count, width), low)] * 2
        + [jax.ShapeDtypeStruct(*item) for item in kept],
        scratch_shapes=[pltpu.VMEM(item.shape, low) for item in weights[:4]]
        + [pltpu.VMEM(*item) for item in kept]
        + [
            pltpu.VMEM((count, width), full),
            pltpu.VMEM((count, width), full),
            pltpu.VMEM((count, count), full),
            pltpu.VMEM((2, 8, width), full),
            pltpu.VMEM((2, 8, hidden_width), full),
            pltpu.SemaphoreType.DMA((4,)),
            pltpu.SemaphoreType.DMA((15,)),
            pltpu.SemaphoreType.DMA((HEADS // 2,)),
        ],
        compiler_params=pltpu.CompilerParams(vmem_limit_bytes=56 << 20),
        cost_estimate=pl.CostEstimate(
            flops=16_000_000_000, bytes_accessed=40_000_000, transcendentals=0
        ),
        name="forward",
    )(place, lengths, own, other, *far(*vectors, *final, *weights))


def logits_kernel(student_ref, teacher_ref, table_ref, diff_ref, expo_ref, stats_ref, sums_ref):
    count = student_ref.shape[0]
    span = table_ref.shape[0] // 8
    lanes = lax.broadcasted_iota(jnp.int32, (count, 128), 1)
    packed = jnp.zeros((count, 128), jnp.float32)
    for part in range(8):
        where = slice(part * span, (part + 1) * span)
        table = table_ref[where, :]
        half_s = nt(student_ref[...], table)
        top_s = jnp.max(half_s, axis=1, keepdims=True)
        expo_s = jnp.exp(half_s - top_s)
        mass_s = jnp.sum(expo_s, axis=1, keepdims=True)
        half_t = nt(teacher_ref[...], table)
        top_t = jnp.max(half_t, axis=1, keepdims=True)
        expo_t = jnp.exp(half_t - top_t)
        mass_t = jnp.sum(expo_t, axis=1, keepdims=True)
        cross = jnp.sum(expo_t * (half_t - half_s), axis=1, keepdims=True)
        diff_ref[:, where] = (expo_s * (mass_t / mass_s) - expo_t).astype(jnp.bfloat16)
        expo_ref[:, where] = expo_t.astype(jnp.bfloat16)
        for index, column in enumerate((top_s, mass_s, top_t, mass_t, cross)):
            packed = jnp.where(lanes == 8 * index + part, column, packed)
    stats = packed.T
    stats_ref[0] = stats[:40]
    top_s, mass_s, top_t, mass_t, cross = (stats[8 * i : 8 * i + 8] for i in range(5))

    @pl.when(pl.program_id(0) == 0)
    def _():
        row = lax.broadcasted_iota(jnp.int32, sums_ref.shape, 0)
        sums_ref[...] = jnp.where((row == 0) | (row == 2), negative, 0.0)

    old = sums_ref[...]
    new_s = jnp.maximum(old[0:1], jnp.max(top_s, axis=0, keepdims=True))
    new_t = jnp.maximum(old[2:3], jnp.max(top_t, axis=0, keepdims=True))
    keep_s = jnp.exp(old[0:1] - new_s)
    keep_t = jnp.exp(old[2:3] - new_t)
    scale_s = jnp.exp(top_s - new_s)
    scale_t = jnp.exp(top_t - new_t)
    sums_ref[0:1] = new_s
    sums_ref[1:2] = old[1:2] * keep_s + jnp.sum(mass_s * scale_s, axis=0, keepdims=True)
    sums_ref[2:3] = new_t
    sums_ref[3:4] = old[3:4] * keep_t + jnp.sum(mass_t * scale_t, axis=0, keepdims=True)
    sums_ref[4:5] = old[4:5] * keep_t + jnp.sum(cross * scale_t, axis=0, keepdims=True)


def logits_phase(student, teacher, table):
    count, width = student.shape
    entries = table.shape[0]
    span = TABLE_SPAN
    steps = entries // span
    rows = pl.BlockSpec((count, width), lambda j: (0, 0))
    wide = pl.BlockSpec((count, span), lambda j: (0, j))
    return pl.pallas_call(
        logits_kernel,
        grid=(steps,),
        in_specs=[rows, rows, pl.BlockSpec((span, width), lambda j: (j, 0))],
        out_specs=[
            wide,
            wide,
            pl.BlockSpec((1, 40, count), lambda j: (j, 0, 0)),
            pl.BlockSpec((8, count), lambda j: (0, 0)),
        ],
        out_shape=[
            jax.ShapeDtypeStruct((count, entries), jnp.bfloat16),
            jax.ShapeDtypeStruct((count, entries), jnp.bfloat16),
            jax.ShapeDtypeStruct((steps, 40, count), jnp.float32),
            jax.ShapeDtypeStruct((8, count), jnp.float32),
        ],
        compiler_params=pltpu.CompilerParams(vmem_limit_bytes=24 << 20),
        cost_estimate=pl.CostEstimate(
            flops=4 * count * width * entries, bytes_accessed=60_000_000, transcendentals=0
        ),
        name="logits_phase",
    )(*far(student, teacher, table))


def joined_norms(own, other):
    top_s = jnp.maximum(own[0:1], other[0:1])
    top_t = jnp.maximum(own[2:3], other[2:3])
    own_t, other_t = jnp.exp(own[2:3] - top_t), jnp.exp(other[2:3] - top_t)
    mass_s = own[1:2] * jnp.exp(own[0:1] - top_s) + other[1:2] * jnp.exp(other[0:1] - top_s)
    mass_t = own[3:4] * own_t + other[3:4] * other_t
    cross = own[4:5] * own_t + other[4:5] * other_t
    norm_s = top_s + jnp.log(mass_s)
    norm_t = top_t + jnp.log(mass_t)
    return (norm_s, norm_t, cross / mass_t - norm_t + norm_s)


def chunk_factors(stats_ref, norms, rows):
    top_s, mass_s, top_t, mass_t = (stats_ref[0, 8 * i : 8 * i + 8, rows] for i in range(4))
    first = 0.5 * jnp.exp(top_s - norms[0:1, rows]) * mass_s / mass_t
    second = first - 0.5 * jnp.exp(top_t - norms[1:2, rows])
    pad = jnp.zeros((112, first.shape[1]), jnp.float32)
    return jnp.concatenate([first, second, pad], axis=0).T


def chunk_product(total, diffs, expos, factors, table_ref):
    span = table_ref.shape[0] // 8
    for group in range(2):
        pieces = []
        for part in range(4 * group, 4 * group + 4):
            where = slice(part * span, (part + 1) * span)
            pieces.append(
                jnp.concatenate(
                    [
                        (
                            diff[:, where].astype(jnp.float32) * factor[:, part : part + 1]
                            + expo[:, where].astype(jnp.float32) * factor[:, 8 + part : 9 + part]
                        ).astype(jnp.bfloat16)
                        for diff, expo, factor in zip(diffs, expos, factors)
                    ],
                    axis=0,
                )
            )
        where = slice(4 * group * span, 4 * (group + 1) * span)
        total = total + dense(jnp.concatenate(pieces, axis=1), table_ref[where, :])
    return total


def gradient_kernel(
    joint,
    diff_first,
    diff_second,
    expo_first,
    expo_second,
    table_ref,
    stats_ref,
    own_ref,
    other_ref,
    we_hbm,
    first_out,
    first_low,
    second_out,
    norms_out,
    we_out,
    total_ref,
    load_sem,
):
    step = pl.program_id(0)
    rows = diff_first.shape[0]
    load = pltpu.make_async_copy(we_hbm, we_out, load_sem)
    top, bottom = slice(0, rows), slice(rows, 2 * rows)

    @pl.when(step == 0)
    def _():
        load.start()
        norm_s, norm_t, divergence = joined_norms(own_ref[...], other_ref[...])
        norms_out[0:1] = norm_s
        norms_out[1:2] = norm_t
        norms_out[2:3] = divergence
        total_ref[...] = jnp.zeros_like(total_ref)

    @pl.when(step < joint)
    def _():
        total_ref[...] = chunk_product(
            total_ref[...],
            (diff_first, diff_second),
            (expo_first, expo_second),
            (
                chunk_factors(stats_ref, norms_out, top),
                chunk_factors(stats_ref, norms_out, bottom),
            ),
            table_ref,
        )

    @pl.when(step >= joint)
    def _():
        total_ref[top] = chunk_product(
            total_ref[top],
            (diff_first,),
            (expo_first,),
            (chunk_factors(stats_ref, norms_out, top),),
            table_ref,
        )

    @pl.when(step == pl.num_programs(0) - 1)
    def _():
        first_out[...] = total_ref[top]
        second_out[...] = total_ref[bottom]
        first_low[...] = total_ref[top].astype(jnp.bfloat16)
        load.wait()


def gradient_phase(diff, expo, table, stats, own, other, we):
    count, entries = diff.shape
    rows = count // 2
    width = table.shape[1]
    span = TABLE_SPAN
    steps = entries // span
    joint = steps - SPLIT_STEPS
    top = pl.BlockSpec((rows, span), lambda j: (0, j))
    bottom = pl.BlockSpec((rows, span), lambda j: (1, jnp.minimum(j, joint - 1)))
    sums = pl.BlockSpec((8, count), lambda j: (0, 0))
    fixed = pl.BlockSpec((rows, width), lambda j: (0, 0))
    full = jnp.float32
    return pl.pallas_call(
        functools.partial(gradient_kernel, joint),
        grid=(steps,),
        in_specs=[
            top,
            bottom,
            top,
            bottom,
            pl.BlockSpec((span, width), lambda j: (j, 0)),
            pl.BlockSpec((1, 40, count), lambda j: (j, 0, 0)),
            sums,
            sums,
            in_place(),
        ],
        out_specs=[fixed] * 3 + [sums, whole_vmem()],
        out_shape=[
            jax.ShapeDtypeStruct((rows, width), full),
            jax.ShapeDtypeStruct((rows, width), jnp.bfloat16),
            jax.ShapeDtypeStruct((rows, width), full),
            jax.ShapeDtypeStruct((8, count), full),
            pltpu.VMEM(we.shape, we.dtype),
        ],
        scratch_shapes=[
            pltpu.VMEM((count, width), full),
            pltpu.SemaphoreType.DMA,
        ],
        compiler_params=pltpu.CompilerParams(vmem_limit_bytes=20 << 20),
        cost_estimate=pl.CostEstimate(
            flops=2 * count * width * entries, bytes_accessed=60_000_000, transcendentals=0
        ),
        name="gradient_phase",
    )(diff, diff, *far(expo, expo, table), stats, own, other, *far(we))


def gradient_rest_kernel(
    diff_ref, expo_ref, table_ref, stats_ref, norms_ref, partial_ref, total_ref, low_ref
):
    step = pl.program_id(0)
    rows = diff_ref.shape[0]

    @pl.when(step == 0)
    def _():
        total_ref[...] = partial_ref[...]

    total_ref[...] = chunk_product(
        total_ref[...],
        (diff_ref,),
        (expo_ref,),
        (chunk_factors(stats_ref, norms_ref, slice(rows, 2 * rows)),),
        table_ref,
    )

    @pl.when(step == pl.num_programs(0) - 1)
    def _():
        low_ref[...] = total_ref[...].astype(jnp.bfloat16)


def gradient_rest(diff, expo, table, stats, norms, partial):
    count, entries = diff.shape
    rows, width = partial.shape
    span = TABLE_SPAN
    begin = entries // span - SPLIT_STEPS
    wide = pl.BlockSpec((rows, span), lambda j: (1, begin + j))
    fixed = pl.BlockSpec((rows, width), lambda j: (0, 0))
    return pl.pallas_call(
        gradient_rest_kernel,
        grid=(SPLIT_STEPS,),
        in_specs=[
            wide,
            wide,
            pl.BlockSpec((span, width), lambda j: (begin + j, 0)),
            pl.BlockSpec((1, 40, count), lambda j: (begin + j, 0, 0)),
            pl.BlockSpec((8, count), lambda j: (0, 0)),
            fixed,
        ],
        out_specs=[fixed, fixed],
        out_shape=[
            jax.ShapeDtypeStruct((rows, width), jnp.float32),
            jax.ShapeDtypeStruct((rows, width), jnp.bfloat16),
        ],
        compiler_params=pltpu.CompilerParams(vmem_limit_bytes=18 << 20),
        cost_estimate=pl.CostEstimate(
            flops=12_000_000_000, bytes_accessed=1_000_000, transcendentals=0
        ),
        name="gradient_rest",
    )(diff, *far(expo, table), stats, norms, partial)


def position(device, masks):
    rest = masks[1:]
    place = jnp.int32(0) if not isinstance(device, int) else 0
    for index, mask in enumerate(rest):
        if isinstance(device, int):
            bit = (device // mask) % 2
        else:
            bit = lax.rem(lax.div(device, mask), 2)
        place = place + (bit << (len(rest) - 1 - index))
    return place


def place_shards(me, natural, keep, send, masks, first, shards, rows=slice(None)):
    mine = lax.rem(me, 2)
    place = position(me, masks)
    for pair in range(first // 2, (first + shards) // 2):
        target = lax.bitwise_xor(place, jnp.int32(position(2 * pair, masks)))
        keep[target, rows] = natural[2 * pair + mine, rows]
        send[target, rows] = natural[2 * pair + 1 - mine, rows]


def row_sums(value):
    return jnp.sum(value.astype(jnp.float32), axis=0, keepdims=True)


def back_to_norm(own_ref, other_ref, y_ref, gain):
    normed, scale = normalise(y_ref[...])
    grad = own_ref[...] + other_ref[...].astype(jnp.float32)
    return norm_back(normed, scale, as_row(gain), grad)


def feed_rows(dm, wc, slope, dinner, rows, bias_out, bias_before):
    hidden_width, width = wc.shape
    for part in range(hidden_width // width):
        span = slice(part * width, (part + 1) * width)
        value = nt(dm, wc[span, :]) * slope[rows, span].astype(jnp.float32)
        value = value.astype(jnp.bfloat16)
        dinner[rows, span] = value
        before = 0.0 if bias_before is None else bias_before[:, span]
        bias_out[:, span] = before + row_sums(value)


def branch_rows(dinner, we, after_ref, gain, dy):
    dh2 = nt(dinner[...], we[...])
    normed, scale = normalise(after_ref[...])
    dafter = dy + norm_back(normed, scale, as_row(gain), dh2)
    return dafter, row_sums(dh2 * normed), row_sums(dh2)


def first_kernel(
    own_ref,
    other_ref,
    y_ref,
    after_ref,
    final_gain,
    second_gain,
    wc,
    we,
    wao,
    slope,
    dm_out,
    dinner_out,
    dafter_out,
    dbranch_out,
    dmixed_out,
    contract_bias_out,
    expand_bias_out,
    second_gain_out,
    second_shift_out,
    attend_bias_out,
):
    count = own_ref.shape[0]
    dy = back_to_norm(own_ref, other_ref, y_ref, final_gain)
    dm = dy.astype(jnp.bfloat16)
    dm_out[...] = dm
    contract_bias_out[...] = row_sums(dm)
    feed_rows(dm, wc, slope, dinner_out, slice(0, count), expand_bias_out, None)
    dafter, second_gain_out[...], second_shift_out[...] = branch_rows(
        dinner_out, we, after_ref, second_gain, dy
    )
    dafter_out[...] = dafter
    dbranch = dafter.astype(jnp.bfloat16)
    dbranch_out[...] = dbranch
    attend_bias_out[...] = row_sums(dbranch)
    dmixed_out[...] = nt(dbranch, wao[...]).astype(jnp.bfloat16)


def first_rows(own, other, y, after, final_gain, second_gain, wc, we, wao, slope):
    rows, width = own.shape
    hidden_width = wc.shape[0]
    low, full = jnp.bfloat16, jnp.float32

    def array(size, kind):
        return jax.ShapeDtypeStruct((rows, size), kind)

    def vector(size):
        return jax.ShapeDtypeStruct((1, size), full)

    top = pl.BlockSpec((rows, width), lambda i: (0, 0))
    return pl.pallas_call(
        first_kernel,
        grid=(1,),
        in_specs=[whole_vmem()] * 2 + [top] * 2 + [whole_vmem()] * 6,
        out_specs=[whole_vmem()] * 10,
        out_shape=[
            array(width, low),
            array(hidden_width, low),
            array(width, full),
            array(width, low),
            array(width, low),
            vector(width),
            vector(hidden_width),
            vector(width),
            vector(width),
            vector(width),
        ],
        compiler_params=pltpu.CompilerParams(vmem_limit_bytes=14 << 20),
        cost_estimate=pl.CostEstimate(
            flops=12_000_000_000, bytes_accessed=1_000_000, transcendentals=0
        ),
        name="first_rows",
    )(own, other, *far(y, after, final_gain, second_gain), *near(wc, we, wao, slope))


def feed_kernel(
    place_ref,
    own_ref,
    other_ref,
    y_ref,
    final_gain,
    dm_first,
    normed_two_ref,
    contract_bias_first,
    expand_bias_first,
    wc_hbm,
    slope,
    active,
    dinner_first,
    cw_keep,
    cw_send,
    ew_keep,
    ew_send,
    dy_out,
    dinner_out,
    contract_bias_out,
    expand_bias_out,
    wc,
    dinner_v,
    dm_v,
    cw_natural,
    ew_natural,
    load_sem,
):
    me, blk = place_ref[0], place_ref[1]
    rows = own_ref.shape[0]
    second = slice(rows, 2 * rows)
    hidden_width, width = wc.shape
    parts = hidden_width // width
    part_width = width // 2
    shards = cw_natural.shape[0]
    chunk = width // shards
    loads = [
        pltpu.make_async_copy(
            wc_hbm.at[pl.ds(part * width, width)],
            wc.at[pl.ds(part * width, width)],
            load_sem.at[part],
        )
        for part in range(parts)
    ]
    for load in loads:
        load.start()
    dinner_v[:rows] = dinner_first[...]
    dy = back_to_norm(own_ref, other_ref, y_ref, final_gain)
    dy_out[...] = dy
    dm = dy.astype(jnp.bfloat16)
    dm_v[:rows] = dm_first[...]
    dm_v[second] = dm
    contract_bias_out[...] = contract_bias_first[...] + row_sums(dm)
    dm_half = dm_v[:, pl.ds(pl.multiple_of(blk * part_width, part_width), part_width)]
    group = shards // parts
    for part in range(parts):
        span = slice(part * width, (part + 1) * width)
        value = tn(active[:, span], dm_half).astype(jnp.bfloat16)
        cw_natural[part * group : (part + 1) * group] = value.reshape(
            group, width // group, part_width
        )
        place_shards(me, cw_natural, cw_keep, cw_send, MASKS, part * group, group)
    for load in loads:
        load.wait()
    feed_rows(dm, wc, slope, dinner_v, second, expand_bias_out, expand_bias_first)
    dinner_out[...] = dinner_v[second]
    for part in range(parts // 2):
        offset = pl.multiple_of(blk * (hidden_width // 2), width) + part * width
        value = tn(normed_two_ref[...], dinner_v[:, pl.ds(pl.multiple_of(offset, width), width)])
        value = value.astype(jnp.bfloat16)
        for half in range(2):
            row = (2 * part + half) * chunk
            ew_natural[:, row : row + chunk, :] = value[
                :, half * part_width : (half + 1) * part_width
            ].reshape(shards, chunk, part_width)
        rows_at = slice(2 * part * chunk, (2 * part + 2) * chunk)
        place_shards(me, ew_natural, ew_keep, ew_send, MASKS_B, 0, shards, rows_at)


def feed_back(
    place, own, other, y, final_gain, dm, normed_two, biases, wc, slope, active, dinner, shards
):
    rows, width = own.shape
    count = 2 * rows
    hidden_width = wc.shape[0]
    low, full = jnp.bfloat16, jnp.float32
    height = hidden_width // shards
    half = jax.ShapeDtypeStruct((shards // 2, height, width // 2), low)
    bottom = pl.BlockSpec((rows, width), lambda i: (1, 0))
    return pl.pallas_call(
        feed_kernel,
        grid=(1,),
        in_specs=[scalars()]
        + [whole_vmem()] * 2
        + [bottom]
        + [whole_vmem()] * 5
        + [in_place()]
        + [whole_vmem()] * 3,
        out_specs=[whole_vmem()] * 8,
        out_shape=[half] * 4
        + [
            jax.ShapeDtypeStruct((rows, width), full),
            jax.ShapeDtypeStruct((rows, hidden_width), low),
            jax.ShapeDtypeStruct((1, width), full),
            jax.ShapeDtypeStruct((1, hidden_width), full),
        ],
        scratch_shapes=[
            pltpu.VMEM(wc.shape, low),
            pltpu.VMEM((count, hidden_width), low),
            pltpu.VMEM((count, width), low),
            pltpu.VMEM((shards, height, width // 2), low),
            pltpu.VMEM((shards, height, width // 2), low),
            pltpu.SemaphoreType.DMA((hidden_width // width,)),
        ],
        compiler_params=pltpu.CompilerParams(vmem_limit_bytes=26 << 20),
        cost_estimate=pl.CostEstimate(
            flops=12_000_000_000, bytes_accessed=1_000_000, transcendentals=0
        ),
        name="feed_back",
    )(
        place,
        own,
        other,
        *far(y, final_gain),
        dm,
        *far(normed_two),
        *biases,
        *far(wc),
        *near(slope, active),
        dinner,
    )


def branch_kernel(
    place_ref,
    dy_ref,
    after_ref,
    mixed_ref,
    second_gain,
    dbranch_first,
    second_gain_first,
    second_shift_first,
    attend_bias_first,
    dinner_ref,
    we,
    wao,
    dafter_out,
    dmixed_out,
    attend_out,
    second_gain_out,
    second_shift_out,
    attend_bias_out,
    dbranch_v,
):
    blk = place_ref[1]
    rows, width = after_ref.shape
    part_width = width // 2
    dafter, gain_sum, shift_sum = branch_rows(
        dinner_ref, we, after_ref, second_gain, dy_ref[...]
    )
    dafter_out[...] = dafter
    second_gain_out[...] = second_gain_first[...] + gain_sum
    second_shift_out[...] = second_shift_first[...] + shift_sum
    dbranch = dafter.astype(jnp.bfloat16)
    dbranch_v[:rows] = dbranch_first[...]
    dbranch_v[rows:] = dbranch
    attend_bias_out[...] = attend_bias_first[...] + row_sums(dbranch)
    dmixed_out[...] = nt(dbranch, wao[...]).astype(jnp.bfloat16)
    part = dbranch_v[:, pl.ds(pl.multiple_of(blk * part_width, part_width), part_width)]
    attend_out[...] = tn(mixed_ref[...], part).astype(jnp.bfloat16).reshape(attend_out.shape)


def branch_back(place, dy, after, mixed, second_gain, dbranch, sums, dinner, we, wao, carry, shards):
    rows, width = dy.shape
    low, full = jnp.bfloat16, jnp.float32
    vector = jax.ShapeDtypeStruct((1, width), full)
    bottom = pl.BlockSpec((rows, width), lambda i: (1, 0))
    return pl.pallas_call(
        carrying(branch_kernel, 12, 6, len(carry)),
        grid=(1,),
        in_specs=[scalars(), whole_vmem(), bottom]
        + [whole_vmem()] * 9
        + [in_place()] * len(carry),
        out_specs=[whole_vmem()] * 6 + [in_place()] * len(carry),
        input_output_aliases=aliases(12, 6, carry),
        out_shape=[
            jax.ShapeDtypeStruct((rows, width), full),
            jax.ShapeDtypeStruct((rows, width), low),
            jax.ShapeDtypeStruct((shards, width // shards, width // 2), low),
            vector,
            vector,
            vector,
        ]
        + shapes_of(carry),
        scratch_shapes=[
            pltpu.VMEM((2 * rows, width), low),
        ],
        compiler_params=pltpu.CompilerParams(vmem_limit_bytes=12 << 20),
        cost_estimate=pl.CostEstimate(
            flops=12_000_000_000, bytes_accessed=1_000_000, transcendentals=0
        ),
        name="branch_back",
    )(
        place,
        dy,
        *far(after, mixed, second_gain),
        dbranch,
        *sums,
        dinner,
        *near(we, wao),
        *carry,
    )


def attend_pair(block, query_ref, keys_ref, values_ref, probs_ref, dmixed_refs):
    count, pair = query_ref.shape
    query = query_ref[...] * jnp.bfloat16(0.125)
    zero = jnp.bfloat16(0.0)
    dkeys = jnp.zeros((count, pair), jnp.float32)
    dvalues = jnp.zeros((count, pair), jnp.float32)
    keys = keys_ref[...] * jnp.bfloat16(0.125)
    dqueries = []
    for piece in reversed(range(count // block)):
        span = slice(piece * block, (piece + 1) * block)
        reach = (piece + 1) * block
        dquery = jnp.zeros((block, pair), jnp.float32)
        add_keys = jnp.zeros((reach, pair), jnp.float32)
        add_values = jnp.zeros((reach, pair), jnp.float32)
        for which in range(2):
            mask = head_mask((block, pair), which)
            grad = jnp.where(mask, dmixed_refs[piece][...], zero)
            mine = jnp.where(mask, query[span], zero)
            probs = probs_ref[which, :reach, span]
            dprobs = nt(values_ref[:reach], grad)
            wide = probs.astype(jnp.float32)
            product = wide * dprobs
            balance = jnp.sum(product, axis=0, keepdims=True)
            dscores = (product - wide * balance).astype(jnp.bfloat16)
            add_values = add_values + dense(probs, grad)
            add_keys = add_keys + dense(dscores, mine)
            dquery = dquery + tn(
                dscores, jnp.where(head_mask((reach, pair), which), keys[:reach], zero)
            )
        dqueries.insert(0, dquery.astype(jnp.bfloat16))
        if reach < count:
            pad = jnp.zeros((count - reach, pair), jnp.float32)
            add_keys = jnp.concatenate([add_keys, pad], axis=0)
            add_values = jnp.concatenate([add_values, pad], axis=0)
        dkeys = dkeys + add_keys
        dvalues = dvalues + add_values
    return (
        jnp.concatenate(dqueries, axis=0),
        dkeys.astype(jnp.bfloat16),
        dvalues.astype(jnp.bfloat16),
    )


def attend_kernel(
    block,
    _,
    query_ref,
    keys_ref,
    values_ref,
    probs_ref,
    dmixed_first,
    dmixed_second,
    dq_ref,
    dk_ref,
    dv_ref,
):
    dmixed = (dmixed_first, dmixed_second)
    grads = attend_pair(block, query_ref, keys_ref, values_ref, probs_ref, dmixed)
    for ref, grad in zip((dq_ref, dk_ref, dv_ref), grads):
        ref[...] = grad


def project_kernel(
    block,
    place_ref,
    query_ref,
    keys_ref,
    values_ref,
    probs_ref,
    dmixed_first,
    dmixed_second,
    normed_ref,
    attend_ref,
    dq_ref,
    dk_ref,
    dv_ref,
    keep,
    send,
    natural,
):
    step = pl.program_id(0)
    pair = query_ref.shape[1]
    column = pl.ds(pl.multiple_of(step * pair, pair), pair)
    dmixed = (dmixed_first, dmixed_second)
    grads = attend_pair(block, query_ref, keys_ref, values_ref, probs_ref, dmixed)
    for ref, grad in zip((dq_ref, dk_ref, dv_ref), grads):
        ref[:, column] = grad

    @pl.when(step == pl.num_programs(0) - 1)
    def _():
        me = place_ref[0]
        shards = natural.shape[0]
        width = normed_ref.shape[1]
        part_width = width // 2
        chunk = width // shards
        natural[:, :chunk, :] = attend_ref[...]
        for part, ref in enumerate((dq_ref, dk_ref, dv_ref)):
            value = tn(normed_ref[...], ref[...]).astype(jnp.bfloat16)
            natural[:, (part + 1) * chunk : (part + 2) * chunk, :] = value.reshape(
                shards, chunk, part_width
            )
            rows = slice(0, 2 * chunk) if part == 0 else slice((part + 1) * chunk, (part + 2) * chunk)
            place_shards(me, natural, keep, send, MASKS, 0, shards, rows)


def attend_specs(joined, dmixed, own):
    rows, width = dmixed[0].shape
    count = 2 * rows
    pair = 2 * HEAD_DIM
    pairs = width // pair
    half = pairs // 2

    def first(place_ref):
        blk = place_ref[1]
        return half * (blk if own else 1 - blk)

    def column(height, offset):
        return pl.BlockSpec((height, pair), lambda p, place_ref: (0, offset + first(place_ref) + p))

    return half, [
        column(count, 0),
        column(count, pairs),
        column(count, 2 * pairs),
        pl.BlockSpec((2, count, count), lambda p, place_ref: (first(place_ref) + p, 0, 0)),
        column(rows, 0),
        column(rows, 0),
    ]


def attend_back(place, joined, probs, dmixed, carry, block):
    width = dmixed[0].shape[1]
    count = joined.shape[0]
    half, specs = attend_specs(joined, dmixed, False)
    result = pl.BlockSpec((count, 2 * HEAD_DIM), lambda p, place_ref: (0, p))
    return pl.pallas_call(
        carrying(functools.partial(attend_kernel, block), 7, 3, len(carry)),
        grid_spec=pltpu.PrefetchScalarGridSpec(
            num_scalar_prefetch=1,
            grid=(half,),
            in_specs=specs + [in_place()] * len(carry),
            out_specs=[result] * 3 + [in_place()] * len(carry),
        ),
        out_shape=[jax.ShapeDtypeStruct((count, width // 2), jnp.bfloat16)] * 3
        + shapes_of(carry),
        input_output_aliases=aliases(7, 3, carry),
        compiler_params=pltpu.CompilerParams(vmem_limit_bytes=16 << 20),
        cost_estimate=pl.CostEstimate(
            flops=12_000_000_000, bytes_accessed=1_000_000, transcendentals=0
        ),
        name="attend_back",
    )(place, *far(joined, joined, joined, probs), *dmixed, *carry)


def project_back(place, joined, probs, dmixed, normed, attend, carry, block, shards):
    count, width = normed.shape
    chunk = width // shards
    half, specs = attend_specs(joined, dmixed, True)
    result = pl.BlockSpec((count, width // 2), lambda p, place_ref: (0, 0))
    piece = jax.ShapeDtypeStruct((shards // 2, 4 * chunk, width // 2), jnp.bfloat16)
    specs = specs + [
        pl.BlockSpec(normed.shape, lambda p, place_ref: (0, 0)),
        pl.BlockSpec(attend.shape, lambda p, place_ref: (0, 0, 0)),
    ]
    return pl.pallas_call(
        carrying(functools.partial(project_kernel, block), 9, 5, len(carry)),
        grid_spec=pltpu.PrefetchScalarGridSpec(
            num_scalar_prefetch=1,
            grid=(half,),
            in_specs=specs + [in_place()] * len(carry),
            out_specs=[result] * 3 + [whole_vmem()] * 2 + [in_place()] * len(carry),
            scratch_shapes=[pltpu.VMEM((shards, 4 * chunk, width // 2), jnp.bfloat16)],
        ),
        out_shape=[jax.ShapeDtypeStruct((count, width // 2), jnp.bfloat16)] * 3
        + [piece, piece]
        + shapes_of(carry),
        input_output_aliases=aliases(9, 5, carry),
        compiler_params=pltpu.CompilerParams(vmem_limit_bytes=18 << 20),
        cost_estimate=pl.CostEstimate(
            flops=12_000_000_000, bytes_accessed=1_000_000, transcendentals=0
        ),
        name="project_back",
    )(place, *far(joined, joined, joined, probs), *dmixed, *far(normed), attend, *carry)


def input_kernel(
    place_ref,
    own_ref,
    other_ref,
    dq_own,
    dk_own,
    dv_own,
    dq_other,
    dk_other,
    dv_other,
    dafter_first,
    dafter_second,
    first_gain,
    attend_bias_grad,
    second_gain_grad,
    second_shift_grad,
    expand_bias_grad,
    contract_bias_grad,
    wpi_hbm,
    grad_out,
    keep,
    send,
    wpi,
    joined_v,
    x_v,
    grad_v,
    load_sem,
):
    me, blk = place_ref[0], place_ref[1]
    load = pltpu.make_async_copy(wpi_hbm, wpi, load_sem.at[0])
    load.start()
    count, width = x_v.shape
    part_width = width // 2
    shards = 2 * keep.shape[0]
    in_stream_order(x_v, own_ref, other_ref, blk)
    for side, group in ((blk, (dq_own, dk_own, dv_own)), (1 - blk, (dq_other, dk_other, dv_other))):
        for part, ref in enumerate(group):
            offset = part * width + side * part_width
            joined_v[:, pl.ds(pl.multiple_of(offset, part_width), part_width)] = ref[...]
    normed, scale = normalise(x_v[...])
    load.wait()
    dh1 = nt(joined_v[...], wpi[...])
    sums = jnp.sum(joined_v[...].astype(jnp.float32), axis=0, keepdims=True)
    vectors = [
        jnp.sum(dh1 * normed, axis=0, keepdims=True),
        jnp.sum(dh1, axis=0, keepdims=True),
        jnp.concatenate([sums[:, :width], sums[:, 2 * width :]], axis=1),
        attend_bias_grad[...],
        second_gain_grad[...],
        second_shift_grad[...],
        expand_bias_grad[...],
        contract_bias_grad[...],
    ]
    mine = lax.rem(me, 2)
    place = position(me, MASKS)
    for shard in range(shards):
        rows = []
        for vector in vectors:
            size = vector.shape[1] // shards
            piece = vector[:, shard * size : (shard + 1) * size]
            rows.append(jnp.concatenate([piece, jnp.zeros((1, 256 - size), jnp.float32)], axis=1))
        value = jnp.concatenate(rows, axis=0)
        target = lax.bitwise_xor(place, jnp.int32(position(shard, MASKS)))

        @pl.when(mine == shard % 2)
        def _():
            keep[target] = value

        @pl.when(mine != shard % 2)
        def _():
            send[target] = value

    rows = own_ref.shape[0]
    grad_v[...] = norm_back(normed, scale, as_row(first_gain), dh1)
    grad_v[:rows] += dafter_first[...]
    grad_v[rows:] += dafter_second[...]
    grad_out[...] = grad_v[pl.ds(pl.multiple_of(blk * rows, rows), rows), :]


def input_back(place, own, other, parts, dafter, gain, vectors, wpi, carry, shards):
    rows, width = own.shape
    count = 2 * rows
    low, full = jnp.bfloat16, jnp.float32
    half = jax.ShapeDtypeStruct((shards // 2, len(vectors) + 3, 256), full)
    return pl.pallas_call(
        carrying(input_kernel, 18, 3, len(carry)),
        in_specs=[scalars()] + [whole_vmem()] * 16 + [in_place()] * (1 + len(carry)),
        out_specs=[whole_vmem()] * 3 + [in_place()] * len(carry),
        out_shape=[jax.ShapeDtypeStruct((rows, width), full), half, half] + shapes_of(carry),
        input_output_aliases=aliases(18, 3, carry),
        scratch_shapes=[
            pltpu.VMEM(wpi.shape, low),
            pltpu.VMEM((count, 3 * width), low),
            pltpu.VMEM((count, width), full),
            pltpu.VMEM((count, width), full),
            pltpu.SemaphoreType.DMA((1,)),
        ],
        compiler_params=pltpu.CompilerParams(vmem_limit_bytes=24 << 20),
        cost_estimate=pl.CostEstimate(
            flops=12_000_000_000, bytes_accessed=1_000_000, transcendentals=0
        ),
        name="input_back",
    )(
        place, *far(own, other), *parts, *dafter, *far(gain), *vectors, *far(wpi), *carry
    )


def across(value, mask):
    return lax.ppermute(value, "dp", [(i, i ^ mask) for i in range(lax.axis_size("dp"))])


def halve(keep, received):
    half = keep.shape[0] // 2
    return (keep[:half] + received[:half], keep[half:] + received[half:])


def merge_kernel(layout, *refs):
    inputs, outputs = list(refs[: 2 * len(layout)]), list(refs[2 * len(layout) :])
    for index, mode in enumerate(layout):
        keep, got = inputs[2 * index], inputs[2 * index + 1]
        half = keep.shape[0] // 2
        if mode == "sum":
            outputs.pop(0)[...] = keep[...] + got[...]
        elif mode == "pass":
            outputs.pop(0)[...] = keep[...]
        elif mode == "halve":
            outputs.pop(0)[...] = keep[:half] + got[:half]
            outputs.pop(0)[...] = keep[half:] + got[half:]
        else:
            place = layout[:index].count("stack")
            if place == 0:
                stacked = (outputs.pop(0), outputs.pop(0))
            stacked[0][place : place + half] = keep[:half] + got[:half]
            stacked[1][place : place + half] = keep[half:] + got[half:]


def merge(*groups):
    layout = [mode for mode, _, _ in groups]
    shapes = []
    for index, (mode, keep, _) in enumerate(groups):
        size = keep.shape[0]
        if mode in ("sum", "pass"):
            shapes.append(jax.ShapeDtypeStruct(keep.shape, keep.dtype))
        elif mode == "halve" or "stack" not in layout[:index]:
            rows = size // 2 * (layout.count("stack") if mode == "stack" else 1)
            shapes += [jax.ShapeDtypeStruct((rows, *keep.shape[1:]), keep.dtype)] * 2
    arrays = [array for _, keep, got in groups for array in (keep, got)]
    return pl.pallas_call(
        functools.partial(merge_kernel, layout),
        in_specs=[whole_vmem()] * len(arrays),
        out_specs=[whole_vmem()] * len(shapes),
        out_shape=shapes,
        compiler_params=pltpu.CompilerParams(vmem_limit_bytes=16 << 20),
        cost_estimate=pl.CostEstimate(flops=1_000_000, bytes_accessed=1_000_000, transcendentals=0),
        name="merge",
    )(*arrays)


def feed_finish_kernel(place_ref, own_ref, other_ref, contract_out, expand_out):
    blk = place_ref[1]
    part = own_ref.shape[2]
    chunk = expand_out.shape[0]
    half = expand_out.shape[1] // 2
    for side, ref in ((blk, own_ref), (1 - blk, other_ref)):
        contract_out[:, pl.ds(pl.multiple_of(side * part, part), part)] = ref[0].astype(jnp.float32)
        for index in range(half // part):
            offset = side * half + index * part
            expand_out[:, pl.ds(pl.multiple_of(offset, part), part)] = ref[
                1, index * chunk : (index + 1) * chunk
            ].astype(jnp.float32)


def feed_finish(place, own, other, chunk):
    _, rows, part = own.shape
    full = jnp.float32
    return pl.pallas_call(
        feed_finish_kernel,
        in_specs=[scalars()] + [whole_vmem()] * 2,
        out_specs=[whole_vmem()] * 2,
        out_shape=[
            jax.ShapeDtypeStruct((rows, 2 * part), full),
            jax.ShapeDtypeStruct((chunk, 2 * part * rows // chunk), full),
        ],
        compiler_params=pltpu.CompilerParams(vmem_limit_bytes=16 << 20),
        cost_estimate=pl.CostEstimate(flops=1_000_000, bytes_accessed=1_000_000, transcendentals=0),
        name="feed_finish",
    )(place, own, other)


def finish_kernel(
    place_ref, own_ref, other_ref, keep_ref, got_ref, _, attend_out, project_out, *vector_outs
):
    blk = place_ref[1]
    chunk, width = attend_out.shape
    part = width // 2
    for side, ref in ((blk, own_ref), (1 - blk, other_ref)):
        for index in range(4):
            value = ref[index * chunk : (index + 1) * chunk].astype(jnp.float32)
            if index == 0:
                target, offset = attend_out, side * part
            else:
                target, offset = project_out, (index - 1) * width + side * part
            target[:, pl.ds(pl.multiple_of(offset, part), part)] = value
    total = keep_ref[0] + got_ref[0]
    for index, out in enumerate(vector_outs):
        out[...] = total[index : index + 1, : out.shape[1]]


def finish(place, own, other, keep, got, ready, chunk, sizes):
    width = 2 * own.shape[1]
    full = jnp.float32
    return pl.pallas_call(
        finish_kernel,
        in_specs=[scalars()] + [whole_vmem()] * 4 + [in_place()],
        out_specs=[whole_vmem()] * (2 + len(sizes)),
        out_shape=[
            jax.ShapeDtypeStruct((chunk, width), full),
            jax.ShapeDtypeStruct((chunk, 3 * width), full),
        ]
        + [jax.ShapeDtypeStruct((1, size), full) for size in sizes],
        compiler_params=pltpu.CompilerParams(vmem_limit_bytes=16 << 20),
        cost_estimate=pl.CostEstimate(flops=1_000_000, bytes_accessed=1_000_000, transcendentals=0),
        name="finish",
    )(place, own, other, keep, got, *far(ready))


def swap(value):
    return lax.ppermute(value, "blk", [(0, 1), (1, 0)])


def both_halves(own, other, blk):
    return jnp.where(
        blk == 0,
        jnp.concatenate([own, other], axis=-1),
        jnp.concatenate([other, own], axis=-1),
    ).astype(jnp.float32)


def local_pair(hidden, doc_lengths, *arrays):
    student, teacher = arrays[:12], arrays[12:24]
    final_gain, final_shift, table = arrays[24:]
    rows, width = hidden.shape
    shards = lax.axis_size("dp")
    blk = lax.axis_index("blk")
    place = jnp.stack([lax.axis_index("dp"), blk]).astype(jnp.int32)
    other = swap(hidden)
    rows_t, rows_s, normed, joined, probs, mixed, after, normed_two, slope, active, y = forward(
        place, doc_lengths, hidden, other, teacher, student, (final_gain, final_shift)
    )
    diff, expo, stats, sums = logits_phase(rows_s, rows_t, table)
    gain, shift, wpi, qvb, wao, bao, gain_two, shift_two, we, be, wc, bc = student
    sums_other = swap(sums)
    own_first, low_first, partial, norms, we = gradient_phase(
        diff, expo, table, stats, sums, sums_other, we
    )
    got_first = swap(low_first)
    own_second, low_second = gradient_rest(diff, expo, table, stats, norms, partial)
    got_second = swap(low_second)
    dm, dinner, dafter_first, dbranch, dmixed_first, dbc, dbe, *branch_sums = first_rows(
        own_first, got_first, y, after, final_gain, gain_two, wc, we, wao, slope
    )
    cw_keep, cw_send, ew_keep, ew_send, dy, dinner, dbc, dbe = feed_back(
        place,
        own_second,
        got_second,
        y,
        final_gain,
        dm,
        normed_two,
        (dbc, dbe),
        wc,
        slope,
        active,
        dinner,
        shards,
    )
    cw_got = across(cw_send, MASKS[0])
    ew_got = across(ew_send, MASKS_B[0])
    dafter_second, dmixed_second, attend, dgain_two, dshift_two, dbao, cw_keep, ew_keep = (
        branch_back(
            place,
            dy,
            after,
            mixed,
            gain_two,
            dbranch,
            branch_sums,
            dinner,
            we,
            wao,
            (cw_keep, ew_keep),
            shards,
        )
    )
    dafter, dmixed = (dafter_first, dafter_second), (dmixed_first, dmixed_second)
    cw_keep, cw_send = halve(cw_keep, cw_got)
    cw_got = across(cw_send, MASKS[1])
    ew_keep, ew_send = halve(ew_keep, ew_got)
    ew_got = across(ew_send, MASKS_B[1])
    *own_grads, keep, send, cw_keep, ew_keep = project_back(
        place, joined, probs, dmixed, normed, attend, (cw_keep, ew_keep), rows, shards
    )
    got = across(send, MASKS[0])
    cw_keep, cw_send, ew_keep, ew_send = merge(("halve", cw_keep, cw_got), ("halve", ew_keep, ew_got))
    cw_got = across(cw_send, MASKS[2])
    ew_got = across(ew_send, MASKS_B[2])
    *other_grads, keep, cw_keep, ew_keep = attend_back(
        place, joined, probs, dmixed, (keep, cw_keep, ew_keep), rows
    )
    keep, send, both_keep, both_send = merge(
        ("halve", keep, got), ("stack", cw_keep, cw_got), ("stack", ew_keep, ew_got)
    )
    got = across(send, MASKS[1])
    both_got = across(both_send, MASKS[3])
    input_grad, vector_keep, vector_send, keep, both_keep = input_back(
        place,
        hidden,
        other,
        (*own_grads, *other_grads),
        dafter,
        gain,
        (dbao, dgain_two, dshift_two, dbe, dbc),
        wpi,
        (keep, both_keep),
        shards,
    )
    vector_got = across(vector_send, MASKS[0])
    keep, send, both, vector_keep, vector_send = merge(
        ("halve", keep, got),
        ("sum", both_keep, both_got),
        ("halve", vector_keep, vector_got),
    )
    got, vector_got = across(send, MASKS[2]), across(vector_send, MASKS[1])
    keep, send, both, vector_keep, vector_send = merge(
        ("halve", keep, got),
        ("pass", both, both),
        ("halve", vector_keep, vector_got),
    )
    got, vector_got, both_other = (
        across(send, MASKS[3]),
        across(vector_send, MASKS[2]),
        swap(both),
    )
    last, vector_keep, vector_send = merge(
        ("sum", keep, got), ("halve", vector_keep, vector_got)
    )
    last = last[0]
    last_other = swap(last)
    vector_got = across(vector_send, MASKS[3])
    chunk = width // shards
    grad_cw, grad_ew = feed_finish(place, both, both_other, chunk)
    sizes = (chunk, chunk, 2 * chunk, chunk, chunk, chunk, be.shape[0] // shards, chunk)
    grad_ao, grad_pi, *vectors = finish(
        place, last, last_other, vector_keep, vector_got, grad_cw, chunk, sizes
    )
    dgain, dshift, dqvb, dbao, dgain_two, dshift_two, dbe, dbc = (
        vector.reshape(-1) for vector in vectors
    )
    return (
        lax.dynamic_slice_in_dim(norms[2], blk * rows, rows),
        input_grad,
        dgain,
        dshift,
        grad_pi,
        dqvb,
        grad_ao,
        dbao,
        dgain_two,
        dshift_two,
        grad_ew,
        dbe,
        grad_cw,
        dbc,
    )


def solution(mesh):
    pair = mesh.shape["dp"] == 16 and mesh.shape["blk"] == 2
    return jax.shard_map(
        local_pair if pair else local_general,
        mesh=mesh,
        in_specs=(
            P(("dp", "blk"), None),
            P("dp", None),
            P(),
            P(),
            P(),
            P(),
            P(),
            P(),
            P(),
            P(),
            P(),
            P(),
            P(),
            P(),
            P(),
            P(),
            P(),
            P(),
            P(),
            P(),
            P(),
            P(),
            P(),
            P(),
            P(),
            P(),
            P(),
            P(),
            P("blk", None),
        ),
        out_specs=(
            P(("dp", "blk")),
            P(("dp", "blk"), None),
            P("dp"),
            P("dp"),
            P("dp", None),
            P("dp"),
            P("dp", None),
            P("dp"),
            P("dp"),
            P("dp"),
            P("dp", None),
            P("dp"),
            P("dp", None),
            P("dp"),
        ),
        check_vma=False,
    )
```

```python
import functools

import jax
import jax.numpy as jnp
from jax import lax
from jax.experimental import pallas as pl
from jax.experimental.pallas import tpu as pltpu
from jax.sharding import PartitionSpec as P

HEADS = 12
HEAD_DIM = 64
TABLE_SPAN = 2048
SPLIT_STEPS = 4
MASKS = (1, 2, 4, 8)
MASKS_B = (1, 4, 2, 8)


negative = -1e30


def layer_norm(value, gain, shift):
    centre = value - jnp.mean(value, axis=-1, keepdims=True)
    return (
        centre * lax.rsqrt(jnp.mean(centre * centre, axis=-1, keepdims=True) + 1e-05) * gain + shift
    )


def doc_numbers(lengths, count):
    ends = jnp.cumsum(lengths)
    places = jnp.arange(count, dtype=jnp.int32)
    return jnp.sum((places[:, None] >= ends[None, :]).astype(jnp.int32), axis=1)


def dense(left, right):
    return jnp.dot(left, right, preferred_element_type=jnp.float32)


def split_heads(value):
    return value.reshape(value.shape[0], HEADS, HEAD_DIM)


def input_side(inputs, gain, shift, project_in, qv_bias):
    width = inputs.shape[1]
    normed = layer_norm(inputs, gain, shift).astype(jnp.bfloat16)
    bias = jnp.concatenate([qv_bias[:width], jnp.zeros((width,), jnp.float32), qv_bias[width:]])
    joined = (dense(normed, project_in) + bias).astype(jnp.bfloat16)
    return (normed, joined[:, :width], joined[:, width : 2 * width], joined[:, 2 * width :])


def output_side(
    inputs,
    mixed_low,
    attend_out,
    attend_bias,
    second_gain,
    second_shift,
    expand_weight,
    expand_bias,
    contract_weight,
    contract_bias,
):
    after = inputs + dense(mixed_low, attend_out) + attend_bias
    normed = layer_norm(after, second_gain, second_shift).astype(jnp.bfloat16)
    inner = dense(normed, expand_weight) + expand_bias
    active = jax.nn.gelu(inner, approximate=True).astype(jnp.bfloat16)
    final = after + dense(active, contract_weight) + contract_bias
    return (after, normed, inner, active, final)


def online(state, query, keys, values, allowed):
    top, mass, summed = state
    scores = (
        jnp.einsum(
            "qhd,khd->hqk",
            split_heads(query),
            split_heads(keys),
            preferred_element_type=jnp.float32,
        )
        * 0.125
    )
    scores = jnp.where(allowed[None], scores, negative)
    new_top = jnp.maximum(top, jnp.max(scores, axis=-1))
    factor = jnp.exp(top - new_top)
    weights = jnp.where(allowed[None], jnp.exp(scores - new_top[..., None]), 0.0)
    mass = mass * factor + jnp.sum(weights, axis=-1)
    summed = summed * factor[..., None] + jnp.einsum(
        "hqk,khd->hqd",
        weights.astype(jnp.bfloat16),
        split_heads(values),
        preferred_element_type=jnp.float32,
    )
    return (new_top, mass, summed)


def score_grads(query_heads, grad_heads, log_norm, balance, key_block, value_block, allowed):
    scores = (
        jnp.einsum("qhd,khd->hqk", query_heads, key_block, preferred_element_type=jnp.float32)
        * 0.125
    )
    probs = jnp.where(allowed[None], jnp.exp(scores - log_norm[..., None]), 0.0)
    grad_probs = jnp.einsum(
        "qhd,khd->hqk", grad_heads, value_block, preferred_element_type=jnp.float32
    )
    grad_scores = (probs * (grad_probs - balance[..., None])).astype(jnp.bfloat16)
    return (probs, grad_scores)


def partial_stats(rows_teacher, rows_student, table):
    half_t = jnp.einsum("rd,vd->rv", rows_teacher, table, preferred_element_type=jnp.float32) * 0.5
    half_s = jnp.einsum("rd,vd->rv", rows_student, table, preferred_element_type=jnp.float32) * 0.5
    top_t = jnp.max(half_t, axis=-1)
    expo_t = jnp.exp(half_t - top_t[:, None])
    top_s = jnp.max(half_s, axis=-1)
    return (
        top_t,
        jnp.sum(expo_t, axis=-1),
        jnp.sum(expo_t * (half_t - half_s), axis=-1),
        top_s,
        jnp.sum(jnp.exp(half_s - top_s[:, None]), axis=-1),
    )


def combine(first_stats, second_stats):
    top_t = jnp.maximum(first_stats[0], second_stats[0])
    right_weight = jnp.exp(second_stats[0] - top_t)
    top_s = jnp.maximum(first_stats[3], second_stats[3])
    return (
        top_t,
        second_stats[1] * right_weight,
        second_stats[2] * right_weight,
        top_s,
        second_stats[4] * jnp.exp(second_stats[3] - top_s),
    )


def row_gradient(rows_teacher, rows_student, table, norm_t, norm_s):
    half_t = jnp.einsum("rd,vd->rv", rows_teacher, table, preferred_element_type=jnp.float32) * 0.5
    half_s = jnp.einsum("rd,vd->rv", rows_student, table, preferred_element_type=jnp.float32) * 0.5
    change = ((jnp.exp(half_s - norm_s[:, None]) - jnp.exp(half_t - norm_t[:, None])) * 0.5).astype(
        jnp.bfloat16
    )
    return dense(change, table)


def local_general(
    hidden,
    doc_lengths,
    student_first_gain,
    student_first_shift,
    student_project_in,
    student_query_value_bias,
    student_attend_out,
    student_attend_bias,
    student_second_gain,
    student_second_shift,
    student_expand_weight,
    student_expand_bias,
    student_contract_weight,
    student_contract_bias,
    teacher_first_gain,
    teacher_first_shift,
    teacher_project_in,
    teacher_query_value_bias,
    teacher_attend_out,
    teacher_attend_bias,
    teacher_second_gain,
    teacher_second_shift,
    teacher_expand_weight,
    teacher_expand_bias,
    teacher_contract_weight,
    teacher_contract_bias,
    final_gain,
    final_shift,
    embedding,
):
    rows, width = hidden.shape
    blocks = lax.axis_size("blk")
    stream = rows * blocks
    first = lax.axis_index("blk") * rows
    last_place = first + rows - 1
    docs = doc_numbers(doc_lengths[0], stream)
    own_places = first + jnp.arange(rows, dtype=jnp.int32)
    own_docs = lax.dynamic_slice_in_dim(docs, first, rows)
    inputs = hidden.astype(jnp.float32)
    normed_s, query_s, keys_s, values_s = input_side(
        inputs,
        student_first_gain,
        student_first_shift,
        student_project_in,
        student_query_value_bias,
    )
    normed_t, query_t, keys_t, values_t = input_side(
        inputs,
        teacher_first_gain,
        teacher_first_shift,
        teacher_project_in,
        teacher_query_value_bias,
    )

    def allowed_for(begin):
        key_places = begin + jnp.arange(rows, dtype=jnp.int32)
        key_docs = lax.dynamic_slice_in_dim(docs, begin, rows)
        return (key_places[None, :] <= own_places[:, None]) & (
            key_docs[None, :] == own_docs[:, None]
        )

    start_state = (
        jnp.full((HEADS, rows), negative, jnp.float32),
        jnp.zeros((HEADS, rows), jnp.float32),
        jnp.zeros((HEADS, rows, HEAD_DIM), jnp.float32),
    )
    carry = (start_state, start_state)
    pieces = (
        lax.all_gather(keys_s, "blk", axis=0, tiled=True),
        lax.all_gather(values_s, "blk", axis=0, tiled=True),
        lax.all_gather(keys_t, "blk", axis=0, tiled=True),
        lax.all_gather(values_t, "blk", axis=0, tiled=True),
    )
    count = pieces[0].shape[0]
    stacked = tuple((member.reshape(count // rows, rows, width) for member in pieces))
    begins = rows * jnp.arange(count // rows, dtype=jnp.int32)

    def step(state, item):
        piece_keys_s, piece_values_s, piece_keys_t, piece_values_t, begin = item

        def step_compute(inner_state):
            allowed = allowed_for(begin)
            return (
                online(inner_state[0], query_s, piece_keys_s, piece_values_s, allowed),
                online(inner_state[1], query_t, piece_keys_t, piece_values_t, allowed),
            )

        return (
            lax.cond(begin <= last_place, step_compute, lambda inner_state: inner_state, state),
            None,
        )

    carry, _ = lax.scan(step, carry, stacked + (begins,))
    state_s, state_t = carry
    out_heads_s = state_s[2] / state_s[1][..., None]
    attn_norm = state_s[0] + jnp.log(state_s[1])
    mixed_low_s = out_heads_s.transpose(1, 0, 2).reshape(rows, width).astype(jnp.bfloat16)
    mixed_low_t = (
        (state_t[2] / state_t[1][..., None])
        .transpose(1, 0, 2)
        .reshape(rows, width)
        .astype(jnp.bfloat16)
    )
    after_s, normed_two_s, inner_s, active_s, final_s = output_side(
        inputs,
        mixed_low_s,
        student_attend_out,
        student_attend_bias,
        student_second_gain,
        student_second_shift,
        student_expand_weight,
        student_expand_bias,
        student_contract_weight,
        student_contract_bias,
    )
    after_t, normed_two_t, inner_t, active_t, final_t = output_side(
        inputs,
        mixed_low_t,
        teacher_attend_out,
        teacher_attend_bias,
        teacher_second_gain,
        teacher_second_shift,
        teacher_expand_weight,
        teacher_expand_bias,
        teacher_contract_weight,
        teacher_contract_bias,
    )
    rows_s = layer_norm(final_s, final_gain, final_shift).astype(jnp.bfloat16)
    rows_t = layer_norm(final_t, final_gain, final_shift).astype(jnp.bfloat16)
    identity = (
        jnp.full((rows,), negative, jnp.float32),
        jnp.zeros((rows,), jnp.float32),
        jnp.zeros((rows,), jnp.float32),
        jnp.full((rows,), negative, jnp.float32),
        jnp.zeros((rows,), jnp.float32),
    )
    merged = combine(
        identity,
        partial_stats(rows_t, rows_s, lax.all_gather(embedding, "blk", axis=0, tiled=True)),
    )
    norm_t = merged[0] + jnp.log(merged[1])
    norm_s = merged[3] + jnp.log(merged[4])
    kl_rows = merged[2] / merged[1] - norm_t + norm_s
    grad_final = row_gradient(
        rows_t, rows_s, lax.all_gather(embedding, "blk", axis=0, tiled=True), norm_t, norm_s
    )
    _, final_back = jax.vjp(layer_norm, final_s, final_gain, final_shift)
    grad_y = final_back(grad_final)[0]
    grad_m = grad_y.astype(jnp.bfloat16)
    grad_contract_weight = jnp.einsum(
        "rf,rd->fd", active_s, grad_m, preferred_element_type=jnp.float32
    )
    grad_contract_bias = jnp.sum(grad_m.astype(jnp.float32), axis=0)
    grad_active = jnp.einsum(
        "rd,fd->rf", grad_m, student_contract_weight, preferred_element_type=jnp.float32
    )
    _, gelu_back = jax.vjp(lambda value: jax.nn.gelu(value, approximate=True), inner_s)
    grad_inner = gelu_back(grad_active)[0].astype(jnp.bfloat16)
    grad_expand_weight = jnp.einsum(
        "rd,rf->df", normed_two_s, grad_inner, preferred_element_type=jnp.float32
    )
    grad_expand_bias = jnp.sum(grad_inner.astype(jnp.float32), axis=0)
    grad_normed_two = jnp.einsum(
        "rf,df->rd", grad_inner, student_expand_weight, preferred_element_type=jnp.float32
    )
    _, second_back = jax.vjp(layer_norm, after_s, student_second_gain, student_second_shift)
    grad_after_norm, grad_second_gain, grad_second_shift = second_back(grad_normed_two)
    grad_after = grad_y + grad_after_norm
    grad_branch = grad_after.astype(jnp.bfloat16)
    grad_attend_out = jnp.einsum(
        "rc,rd->cd", mixed_low_s, grad_branch, preferred_element_type=jnp.float32
    )
    grad_attend_bias = jnp.sum(grad_branch.astype(jnp.float32), axis=0)
    grad_mixed = jnp.einsum(
        "rd,cd->rc", grad_branch, student_attend_out, preferred_element_type=jnp.float32
    ).astype(jnp.bfloat16)
    keys_all, values_all = (
        lax.all_gather(keys_s, "blk", axis=0, tiled=True),
        lax.all_gather(values_s, "blk", axis=0, tiled=True),
    )
    grad_heads = split_heads(grad_mixed)
    query_heads = split_heads(query_s)
    balance = jnp.sum(grad_heads.astype(jnp.float32).transpose(1, 0, 2) * out_heads_s, axis=-1)
    begins = rows * jnp.arange(blocks, dtype=jnp.int32)
    zero_query = jnp.zeros((rows, HEADS, HEAD_DIM), jnp.float32)

    def back_step(grad_query, begin):
        key_block = split_heads(lax.dynamic_slice_in_dim(keys_all, begin, rows, 0))
        value_block = split_heads(lax.dynamic_slice_in_dim(values_all, begin, rows, 0))

        def back_compute(total):
            probs, grad_scores = score_grads(
                query_heads,
                grad_heads,
                attn_norm,
                balance,
                key_block,
                value_block,
                allowed_for(begin),
            )
            total = (
                total
                + jnp.einsum(
                    "hqk,khd->qhd", grad_scores, key_block, preferred_element_type=jnp.float32
                )
                * 0.125
            )
            grad_keys = (
                jnp.einsum(
                    "hqk,qhd->khd", grad_scores, query_heads, preferred_element_type=jnp.float32
                )
                * 0.125
            )
            grad_values = jnp.einsum(
                "hqk,qhd->khd",
                probs.astype(jnp.bfloat16),
                grad_heads,
                preferred_element_type=jnp.float32,
            )
            return (
                total,
                jnp.concatenate(
                    [grad_keys.reshape(rows, width), grad_values.reshape(rows, width)], axis=1
                ),
            )

        def skip(total):
            return (total, jnp.zeros((rows, 2 * width), jnp.float32))

        return lax.cond(begin <= last_place, back_compute, skip, grad_query)

    grad_query, key_terms = lax.scan(back_step, zero_query, begins)
    key_value_grad = lax.psum_scatter(
        key_terms.reshape(stream, 2 * width).astype(jnp.bfloat16),
        "blk",
        scatter_dimension=0,
        tiled=True,
    ).astype(jnp.float32)
    grad_keys_low = key_value_grad[:, :width].astype(jnp.bfloat16)
    grad_values_low = key_value_grad[:, width:].astype(jnp.bfloat16)
    grad_query_low = grad_query.reshape(rows, width).astype(jnp.bfloat16)
    grad_joined = jnp.concatenate([grad_query_low, grad_keys_low, grad_values_low], axis=1)
    grad_project_in = jnp.einsum(
        "rd,rc->dc", normed_s, grad_joined, preferred_element_type=jnp.float32
    )
    grad_query_value_bias = jnp.concatenate(
        [
            jnp.sum(grad_query_low.astype(jnp.float32), axis=0),
            jnp.sum(grad_values_low.astype(jnp.float32), axis=0),
        ]
    )
    grad_normed = jnp.einsum(
        "rc,dc->rd", grad_joined, student_project_in, preferred_element_type=jnp.float32
    )
    _, first_back = jax.vjp(layer_norm, inputs, student_first_gain, student_first_shift)
    grad_inputs_norm, grad_first_gain, grad_first_shift = first_back(grad_normed)
    input_grad = grad_after + grad_inputs_norm
    shares = (
        lax.psum_scatter(
            grad_first_gain.astype(jnp.bfloat16), "dp", scatter_dimension=0, tiled=True
        ).astype(jnp.float32),
        lax.psum_scatter(
            grad_first_shift.astype(jnp.bfloat16), "dp", scatter_dimension=0, tiled=True
        ).astype(jnp.float32),
        lax.psum_scatter(
            grad_project_in.astype(jnp.bfloat16), "dp", scatter_dimension=0, tiled=True
        ).astype(jnp.float32),
        lax.psum_scatter(
            grad_query_value_bias.astype(jnp.bfloat16), "dp", scatter_dimension=0, tiled=True
        ).astype(jnp.float32),
        lax.psum_scatter(
            grad_attend_out.astype(jnp.bfloat16), "dp", scatter_dimension=0, tiled=True
        ).astype(jnp.float32),
        lax.psum_scatter(
            grad_attend_bias.astype(jnp.bfloat16), "dp", scatter_dimension=0, tiled=True
        ).astype(jnp.float32),
        lax.psum_scatter(
            grad_second_gain.astype(jnp.bfloat16), "dp", scatter_dimension=0, tiled=True
        ).astype(jnp.float32),
        lax.psum_scatter(
            grad_second_shift.astype(jnp.bfloat16), "dp", scatter_dimension=0, tiled=True
        ).astype(jnp.float32),
        lax.psum_scatter(
            grad_expand_weight.astype(jnp.bfloat16), "dp", scatter_dimension=0, tiled=True
        ).astype(jnp.float32),
        lax.psum_scatter(
            grad_expand_bias.astype(jnp.bfloat16), "dp", scatter_dimension=0, tiled=True
        ).astype(jnp.float32),
        lax.psum_scatter(
            grad_contract_weight.astype(jnp.bfloat16), "dp", scatter_dimension=0, tiled=True
        ).astype(jnp.float32),
        lax.psum_scatter(
            grad_contract_bias.astype(jnp.bfloat16), "dp", scatter_dimension=0, tiled=True
        ).astype(jnp.float32),
    )
    summed = (
        lax.psum(shares[0].astype(jnp.bfloat16), "blk").astype(jnp.float32),
        lax.psum(shares[1].astype(jnp.bfloat16), "blk").astype(jnp.float32),
        lax.psum(shares[2].astype(jnp.bfloat16), "blk").astype(jnp.float32),
        lax.psum(shares[3].astype(jnp.bfloat16), "blk").astype(jnp.float32),
        lax.psum(shares[4].astype(jnp.bfloat16), "blk").astype(jnp.float32),
        lax.psum(shares[5].astype(jnp.bfloat16), "blk").astype(jnp.float32),
        lax.psum(shares[6].astype(jnp.bfloat16), "blk").astype(jnp.float32),
        lax.psum(shares[7].astype(jnp.bfloat16), "blk").astype(jnp.float32),
        lax.psum(shares[8].astype(jnp.bfloat16), "blk").astype(jnp.float32),
        lax.psum(shares[9].astype(jnp.bfloat16), "blk").astype(jnp.float32),
        lax.psum(shares[10].astype(jnp.bfloat16), "blk").astype(jnp.float32),
        lax.psum(shares[11].astype(jnp.bfloat16), "blk").astype(jnp.float32),
    )
    return (
        kl_rows,
        input_grad,
        summed[0],
        summed[1],
        summed[2],
        summed[3],
        summed[4],
        summed[5],
        summed[6],
        summed[7],
        summed[8],
        summed[9],
        summed[10],
        summed[11],
    )


def nt(left, right):
    return lax.dot_general(
        left, right, (((1,), (1,)), ((), ())), preferred_element_type=jnp.float32
    )


def tn(left, right):
    return lax.dot_general(
        left, right, (((0,), (0,)), ((), ())), preferred_element_type=jnp.float32
    )


def normalise(value):
    centre = value - jnp.mean(value, axis=-1, keepdims=True)
    scale = lax.rsqrt(jnp.mean(centre * centre, axis=-1, keepdims=True) + 1e-05)
    return (centre * scale, scale)


def norm_back(normed, scale, gain, grad):
    weighted = grad * gain
    return scale * (
        weighted
        - jnp.mean(weighted, axis=-1, keepdims=True)
        - normed * jnp.mean(weighted * normed, axis=-1, keepdims=True)
    )


def starts_of(lengths_ref, count):
    places = lax.broadcasted_iota(jnp.int32, (1, count), 1)
    start = jnp.zeros((1, count), jnp.int32)
    end = jnp.int32(0)
    for index in range(lengths_ref.shape[1]):
        end = end + lengths_ref[0, index]
        start = jnp.where(places >= end, jnp.maximum(start, end), start)
    return start


def in_stream_order(target, own_ref, other_ref, blk):
    rows = own_ref.shape[0]
    target[pl.ds(pl.multiple_of(blk * rows, rows), rows), :] = own_ref[...].astype(target.dtype)
    target[pl.ds(pl.multiple_of((1 - blk) * rows, rows), rows), :] = other_ref[...].astype(
        target.dtype
    )


def head_mask(shape, which):
    lanes = lax.broadcasted_iota(jnp.int32, shape, 1)
    return (lanes >= HEAD_DIM) if which else (lanes < HEAD_DIM)


def forward_kernel(*refs):
    place_ref, lengths_ref, own_ref, other_ref = refs[:4]
    vectors = (refs[4:12], refs[12:20])
    final_gain, final_shift = (as_row(ref) for ref in refs[20:22])
    weights_hbm = (refs[22:26], refs[26:30])
    rows_t, rows_s = refs[30:32]
    kept_hbm = refs[32:41]
    other_hbm = refs[41]
    wpi, wao, we, wc = weights = refs[42:46]
    kept = refs[46:55]
    normed_v, joined_v, probs_v, mixed_v, after_v, normed_two_v, slope_v, active_v, y_v = kept
    x_v, scaled_v, bias_v, vector_v, wide_v, weight_sem, out_sem, probs_sem = refs[55:]
    keep_other = pltpu.make_async_copy(other_ref, other_hbm, out_sem.at[15])
    keep_other.start()
    count, width = x_v.shape
    block = own_ref.shape[0]
    hidden_width = we.shape[1]
    pair = 2 * HEAD_DIM
    pairs = width // pair

    def load(index, which):
        return pltpu.make_async_copy(weights_hbm[which][index], weights[index], weight_sem.at[index])

    def save(slot, index, *at):
        source, target = kept[index], kept_hbm[index]
        if at:
            source, target = source.at[at], target.at[at]
        return pltpu.make_async_copy(source, target, out_sem.at[slot])

    def save_probs(index):
        heads = pl.ds(2 * index, 2)
        return pltpu.make_async_copy(
            probs_v.at[heads], kept_hbm[2].at[heads], probs_sem.at[index]
        )

    def save_wide(side, part):
        span = pl.ds(part * width, width)
        return save(7 + 4 * side + part, 6 + side, slice(None), span)

    for index in range(4):
        load(index, 0).start()
    in_stream_order(x_v, own_ref, other_ref, place_ref[1])
    scaled_v[...] = normalise(x_v[...])[0]
    for which, group in enumerate(vectors):
        gain, shift, qv_bias, bias_a, gain_two, shift_two, bias_e, bias_c = group
        for row, ref in enumerate((gain, shift, bias_a, gain_two, shift_two, bias_c)):
            vector_v[which, row : row + 1] = as_row(ref)
        both = as_row(qv_bias)
        vector_v[which, 6:7] = both[:, :width]
        vector_v[which, 7:8] = both[:, width:]
        wide_v[which, 0:1] = as_row(bias_e)
    start = starts_of(lengths_ref, count)
    keys_at = lax.broadcasted_iota(jnp.int32, (count, count), 0)
    queries_at = lax.broadcasted_iota(jnp.int32, (count, count), 1)
    bias_v[...] = jnp.where((keys_at <= queries_at) & (keys_at >= start), 0.0, negative)

    def attend(index, _):
        column = pl.ds(pl.multiple_of(index * pair, pair), pair)
        query = joined_v[:, column] * jnp.bfloat16(0.125)
        keys = joined_v[:, pl.ds(pl.multiple_of(width + index * pair, pair), pair)]
        values = joined_v[:, pl.ds(pl.multiple_of(2 * width + index * pair, pair), pair)]
        for piece in range(count // block):
            span = slice(piece * block, (piece + 1) * block)
            reach = (piece + 1) * block
            both = []
            for which in range(2):
                mine = jnp.where(
                    head_mask((block, pair), which), query[span], jnp.bfloat16(0.0)
                )
                scores = nt(keys[:reach], mine) + bias_v[:reach, span]
                expo = jnp.exp(scores - jnp.max(scores, axis=0, keepdims=True))
                probs = expo * (1.0 / jnp.sum(expo, axis=0, keepdims=True))
                probs = probs.astype(jnp.bfloat16)
                probs_v[2 * index + which, :reach, span] = probs
                both.append(tn(probs, values[:reach]))
            mixed_v[span, column] = jnp.where(
                head_mask((block, pair), 0), both[0], both[1]
            ).astype(jnp.bfloat16)
        return 0

    def feed(train, which):
        root = 0.7978845608028654
        total = after_v[...] + vector_v[which, 5:6]
        for part in range(hidden_width // width):
            span = slice(part * width, (part + 1) * width)
            inner = dense(normed_two_v[...], we[:, span]) + wide_v[which, 0:1, span]
            square = inner * inner
            bent = jnp.tanh(root * (inner + 0.044715 * (square * inner)))
            upper = 0.5 * (1.0 + bent)
            active = (inner * upper).astype(jnp.bfloat16)
            if train:
                active_v[:, span] = active
                slope_v[:, span] = (
                    upper
                    + (0.5 * root) * inner * (1.0 - bent * bent) * (1.0 + (3 * 0.044715) * square)
                ).astype(jnp.bfloat16)
                save_wide(0, part).start()
                save_wide(1, part).start()
            total = total + dense(active, wc[span, :])
        normed, _ = normalise(total)
        rows = (normed * final_gain + final_shift).astype(jnp.bfloat16) * jnp.bfloat16(0.5)
        if train:
            y_v[...] = total
            save(6, 8).start()
            rows_s[...] = rows
        else:
            rows_t[...] = rows

    def one(which, _):
        student = which == 1

        def row(index):
            return vector_v[which, index : index + 1]

        normed_v[...] = (scaled_v[...] * row(0) + row(1)).astype(jnp.bfloat16)
        load(0, 0).wait()
        for part in range(3):
            span = slice(part * width, (part + 1) * width)
            value = dense(normed_v[...], wpi[:, span])
            if part == 0:
                value = value + row(6)
            if part == 2:
                value = value + row(7)
            joined_v[:, span] = value.astype(jnp.bfloat16)

        @pl.when(student)
        def _():
            save(0, 0).start()
            save(1, 1).start()

        @pl.when(which == 0)
        def _():
            load(0, 1).start()

        lax.fori_loop(0, pairs, attend, 0, unroll=6)

        @pl.when(student)
        def _():
            for index in range(pairs):
                save_probs(index).start()
            save(2, 3).start()

        load(1, 0).wait()
        after_v[...] = x_v[...] + dense(mixed_v[...], wao[...]) + row(2)
        normed, _ = normalise(after_v[...])
        normed_two_v[...] = (normed * row(3) + row(4)).astype(jnp.bfloat16)
        load(2, 0).wait()
        load(3, 0).wait()

        @pl.when(which == 0)
        def _():
            load(1, 1).start()
            feed(False, 0)
            load(2, 1).start()
            load(3, 1).start()

        @pl.when(student)
        def _():
            save(3, 4).start()
            save(4, 5).start()
            feed(True, 1)

        return 0

    lax.fori_loop(0, 2, one, 0)
    for index in range(pairs):
        save_probs(index).wait()
    for slot, index in enumerate((0, 1, 3, 4, 5)):
        save(slot, index).wait()
    save(6, 8).wait()
    keep_other.wait()
    for part in range(hidden_width // width):
        save_wide(0, part).wait()
        save_wide(1, part).wait()


def carrying(kernel, inputs, outputs, carried):
    def body(*refs):
        rest = refs[inputs + carried :]
        kernel(*refs[:inputs], *rest[:outputs], *rest[outputs + carried :])

    return body


def shapes_of(carry):
    return [jax.ShapeDtypeStruct(item.shape, item.dtype) for item in carry]


def aliases(inputs, outputs, carry):
    return {inputs + index: outputs + index for index in range(len(carry))}


def as_row(ref):
    return ref[...].reshape(1, ref.shape[0])


def whole_vmem():
    return pl.BlockSpec(memory_space=pltpu.VMEM)


def in_place():
    return pl.BlockSpec(memory_space=pl.ANY)


def far(*arrays):
    return [pltpu.with_memory_space_constraint(array, pltpu.HBM) for array in arrays]


def near(*arrays):
    return [pltpu.with_memory_space_constraint(array, pltpu.VMEM) for array in arrays]


def scalars():
    return pl.BlockSpec(memory_space=pltpu.SMEM)


def forward(place, lengths, own, other, teacher, student, final):
    rows, width = own.shape
    count = 2 * rows
    weights = [group[index] for group in (teacher, student) for index in (2, 4, 8, 10)]
    vectors = [
        group[index] for group in (teacher, student) for index in (0, 1, 3, 5, 6, 7, 9, 11)
    ]
    hidden_width = weights[2].shape[1]
    low, full = jnp.bfloat16, jnp.float32
    kept = [
        ((count, width), low),
        ((count, 3 * width), low),
        ((HEADS, count, count), low),
        ((count, width), low),
        ((count, width), full),
        ((count, width), low),
        ((count, hidden_width), low),
        ((count, hidden_width), low),
        ((count, width), full),
    ]
    return pl.pallas_call(
        forward_kernel,
        in_specs=[scalars(), scalars()] + [whole_vmem()] * 20 + [in_place()] * 8,
        out_specs=[whole_vmem()] * 2 + [in_place()] * (len(kept) + 1),
        out_shape=[pltpu.VMEM((count, width), low)] * 2
        + [jax.ShapeDtypeStruct(*item) for item in kept]
        + [jax.ShapeDtypeStruct(other.shape, other.dtype)],
        scratch_shapes=[pltpu.VMEM(item.shape, low) for item in weights[:4]]
        + [pltpu.VMEM(*item) for item in kept]
        + [
            pltpu.VMEM((count, width), full),
            pltpu.VMEM((count, width), full),
            pltpu.VMEM((count, count), full),
            pltpu.VMEM((2, 8, width), full),
            pltpu.VMEM((2, 8, hidden_width), full),
            pltpu.SemaphoreType.DMA((4,)),
            pltpu.SemaphoreType.DMA((16,)),
            pltpu.SemaphoreType.DMA((HEADS // 2,)),
        ],
        compiler_params=pltpu.CompilerParams(vmem_limit_bytes=56 << 20),
        cost_estimate=pl.CostEstimate(
            flops=16_000_000_000, bytes_accessed=40_000_000, transcendentals=0
        ),
        name="forward",
    )(place, lengths, own, other, *far(*vectors, *final, *weights))


def logits_kernel(student_ref, teacher_ref, table_ref, diff_ref, expo_ref, stats_ref, sums_ref):
    count = student_ref.shape[0]
    span = table_ref.shape[0] // 8
    lanes = lax.broadcasted_iota(jnp.int32, (count, 128), 1)
    packed = jnp.zeros((count, 128), jnp.float32)
    for part in range(8):
        where = slice(part * span, (part + 1) * span)
        table = table_ref[where, :]
        half_s = nt(student_ref[...], table)
        top_s = jnp.max(half_s, axis=1, keepdims=True)
        expo_s = jnp.exp(half_s - top_s)
        mass_s = jnp.sum(expo_s, axis=1, keepdims=True)
        half_t = nt(teacher_ref[...], table)
        top_t = jnp.max(half_t, axis=1, keepdims=True)
        expo_t = jnp.exp(half_t - top_t)
        mass_t = jnp.sum(expo_t, axis=1, keepdims=True)
        cross = jnp.sum(expo_t * (half_t - half_s), axis=1, keepdims=True)
        diff_ref[:, where] = (expo_s * (mass_t / mass_s) - expo_t).astype(jnp.bfloat16)
        expo_ref[:, where] = expo_t.astype(jnp.bfloat16)
        for index, column in enumerate((top_s, mass_s, top_t, mass_t, cross)):
            packed = jnp.where(lanes == 8 * index + part, column, packed)
    stats = packed.T
    stats_ref[0] = stats[:40]
    top_s, mass_s, top_t, mass_t, cross = (stats[8 * i : 8 * i + 8] for i in range(5))

    @pl.when(pl.program_id(0) == 0)
    def _():
        row = lax.broadcasted_iota(jnp.int32, sums_ref.shape, 0)
        sums_ref[...] = jnp.where((row == 0) | (row == 2), negative, 0.0)

    old = sums_ref[...]
    new_s = jnp.maximum(old[0:1], jnp.max(top_s, axis=0, keepdims=True))
    new_t = jnp.maximum(old[2:3], jnp.max(top_t, axis=0, keepdims=True))
    keep_s = jnp.exp(old[0:1] - new_s)
    keep_t = jnp.exp(old[2:3] - new_t)
    scale_s = jnp.exp(top_s - new_s)
    scale_t = jnp.exp(top_t - new_t)
    sums_ref[0:1] = new_s
    sums_ref[1:2] = old[1:2] * keep_s + jnp.sum(mass_s * scale_s, axis=0, keepdims=True)
    sums_ref[2:3] = new_t
    sums_ref[3:4] = old[3:4] * keep_t + jnp.sum(mass_t * scale_t, axis=0, keepdims=True)
    sums_ref[4:5] = old[4:5] * keep_t + jnp.sum(cross * scale_t, axis=0, keepdims=True)


def logits_phase(student, teacher, table):
    count, width = student.shape
    entries = table.shape[0]
    span = TABLE_SPAN
    steps = entries // span
    rows = whole_vmem()
    wide = pl.BlockSpec((count, span), lambda j: (0, j))
    return pl.pallas_call(
        logits_kernel,
        grid=(steps,),
        in_specs=[rows, rows, pl.BlockSpec((span, width), lambda j: (j, 0))],
        out_specs=[
            wide,
            wide,
            pl.BlockSpec((1, 40, count), lambda j: (j, 0, 0)),
            pl.BlockSpec((8, count), lambda j: (0, 0)),
        ],
        out_shape=[
            jax.ShapeDtypeStruct((count, entries), jnp.bfloat16),
            jax.ShapeDtypeStruct((count, entries), jnp.bfloat16),
            jax.ShapeDtypeStruct((steps, 40, count), jnp.float32),
            jax.ShapeDtypeStruct((8, count), jnp.float32),
        ],
        compiler_params=pltpu.CompilerParams(vmem_limit_bytes=24 << 20),
        cost_estimate=pl.CostEstimate(
            flops=4 * count * width * entries, bytes_accessed=60_000_000, transcendentals=0
        ),
        name="logits_phase",
    )(*near(student, teacher), *far(table))


def joined_norms(own, other):
    top_s = jnp.maximum(own[0:1], other[0:1])
    top_t = jnp.maximum(own[2:3], other[2:3])
    own_t, other_t = jnp.exp(own[2:3] - top_t), jnp.exp(other[2:3] - top_t)
    mass_s = own[1:2] * jnp.exp(own[0:1] - top_s) + other[1:2] * jnp.exp(other[0:1] - top_s)
    mass_t = own[3:4] * own_t + other[3:4] * other_t
    cross = own[4:5] * own_t + other[4:5] * other_t
    norm_s = top_s + jnp.log(mass_s)
    norm_t = top_t + jnp.log(mass_t)
    return (norm_s, norm_t, cross / mass_t - norm_t + norm_s)


def chunk_factors(stats_ref, norms, rows):
    top_s, mass_s, top_t, mass_t = (stats_ref[0, 8 * i : 8 * i + 8, rows] for i in range(4))
    first = 0.5 * jnp.exp(top_s - norms[0:1, rows]) * mass_s / mass_t
    second = first - 0.5 * jnp.exp(top_t - norms[1:2, rows])
    pad = jnp.zeros((112, first.shape[1]), jnp.float32)
    return jnp.concatenate([first, second, pad], axis=0).T


def chunk_product(total, diffs, expos, factors, table_ref):
    span = table_ref.shape[0] // 8
    for group in range(2):
        pieces = []
        for part in range(4 * group, 4 * group + 4):
            where = slice(part * span, (part + 1) * span)
            pieces.append(
                jnp.concatenate(
                    [
                        (
                            diff[:, where].astype(jnp.float32) * factor[:, part : part + 1]
                            + expo[:, where].astype(jnp.float32) * factor[:, 8 + part : 9 + part]
                        ).astype(jnp.bfloat16)
                        for diff, expo, factor in zip(diffs, expos, factors)
                    ],
                    axis=0,
                )
            )
        where = slice(4 * group * span, 4 * (group + 1) * span)
        total = total + dense(jnp.concatenate(pieces, axis=1), table_ref[where, :])
    return total


def gradient_kernel(
    joint,
    diff_first,
    diff_second,
    expo_first,
    expo_second,
    table_ref,
    stats_ref,
    own_ref,
    other_ref,
    we_hbm,
    first_out,
    first_low,
    second_out,
    norms_out,
    we_out,
    total_ref,
    load_sem,
):
    step = pl.program_id(0)
    rows = diff_first.shape[0]
    load = pltpu.make_async_copy(we_hbm, we_out, load_sem)
    top, bottom = slice(0, rows), slice(rows, 2 * rows)

    @pl.when(step == 0)
    def _():
        load.start()
        norm_s, norm_t, divergence = joined_norms(own_ref[...], other_ref[...])
        norms_out[0:1] = norm_s
        norms_out[1:2] = norm_t
        norms_out[2:3] = divergence
        total_ref[...] = jnp.zeros_like(total_ref)

    @pl.when(step < joint)
    def _():
        total_ref[...] = chunk_product(
            total_ref[...],
            (diff_first, diff_second),
            (expo_first, expo_second),
            (
                chunk_factors(stats_ref, norms_out, top),
                chunk_factors(stats_ref, norms_out, bottom),
            ),
            table_ref,
        )

    @pl.when(step >= joint)
    def _():
        total_ref[top] = chunk_product(
            total_ref[top],
            (diff_first,),
            (expo_first,),
            (chunk_factors(stats_ref, norms_out, top),),
            table_ref,
        )

    @pl.when(step == pl.num_programs(0) - 1)
    def _():
        first_out[...] = total_ref[top]
        second_out[...] = total_ref[bottom]
        first_low[...] = total_ref[top].astype(jnp.bfloat16)
        load.wait()


def gradient_phase(diff, expo, table, stats, own, other, we):
    count, entries = diff.shape
    rows = count // 2
    width = table.shape[1]
    span = TABLE_SPAN
    steps = entries // span
    joint = steps - SPLIT_STEPS
    top = pl.BlockSpec((rows, span), lambda j: (0, j))
    bottom = pl.BlockSpec((rows, span), lambda j: (1, jnp.minimum(j, joint - 1)))
    sums = pl.BlockSpec((8, count), lambda j: (0, 0))
    fixed = pl.BlockSpec((rows, width), lambda j: (0, 0))
    full = jnp.float32
    return pl.pallas_call(
        functools.partial(gradient_kernel, joint),
        grid=(steps,),
        in_specs=[
            top,
            bottom,
            top,
            bottom,
            pl.BlockSpec((span, width), lambda j: (j, 0)),
            pl.BlockSpec((1, 40, count), lambda j: (j, 0, 0)),
            sums,
            sums,
            in_place(),
        ],
        out_specs=[fixed] * 3 + [sums, whole_vmem()],
        out_shape=[
            jax.ShapeDtypeStruct((rows, width), full),
            jax.ShapeDtypeStruct((rows, width), jnp.bfloat16),
            jax.ShapeDtypeStruct((rows, width), full),
            jax.ShapeDtypeStruct((8, count), full),
            pltpu.VMEM(we.shape, we.dtype),
        ],
        scratch_shapes=[
            pltpu.VMEM((count, width), full),
            pltpu.SemaphoreType.DMA,
        ],
        compiler_params=pltpu.CompilerParams(vmem_limit_bytes=20 << 20),
        cost_estimate=pl.CostEstimate(
            flops=2 * count * width * entries, bytes_accessed=60_000_000, transcendentals=0
        ),
        name="gradient_phase",
    )(diff, diff, *far(expo, expo, table), stats, own, other, *far(we))


def gradient_rest_kernel(
    diff_ref, expo_ref, table_ref, stats_ref, norms_ref, partial_ref, total_ref, low_ref
):
    step = pl.program_id(0)
    rows = diff_ref.shape[0]

    @pl.when(step == 0)
    def _():
        total_ref[...] = partial_ref[...]

    total_ref[...] = chunk_product(
        total_ref[...],
        (diff_ref,),
        (expo_ref,),
        (chunk_factors(stats_ref, norms_ref, slice(rows, 2 * rows)),),
        table_ref,
    )

    @pl.when(step == pl.num_programs(0) - 1)
    def _():
        low_ref[...] = total_ref[...].astype(jnp.bfloat16)


def gradient_rest(diff, expo, table, stats, norms, partial):
    count, entries = diff.shape
    rows, width = partial.shape
    span = TABLE_SPAN
    begin = entries // span - SPLIT_STEPS
    wide = pl.BlockSpec((rows, span), lambda j: (1, begin + j))
    fixed = pl.BlockSpec((rows, width), lambda j: (0, 0))
    return pl.pallas_call(
        gradient_rest_kernel,
        grid=(SPLIT_STEPS,),
        in_specs=[
            wide,
            wide,
            pl.BlockSpec((span, width), lambda j: (begin + j, 0)),
            pl.BlockSpec((1, 40, count), lambda j: (begin + j, 0, 0)),
            pl.BlockSpec((8, count), lambda j: (0, 0)),
            fixed,
        ],
        out_specs=[fixed, fixed],
        out_shape=[
            jax.ShapeDtypeStruct((rows, width), jnp.float32),
            jax.ShapeDtypeStruct((rows, width), jnp.bfloat16),
        ],
        compiler_params=pltpu.CompilerParams(vmem_limit_bytes=18 << 20),
        cost_estimate=pl.CostEstimate(
            flops=12_000_000_000, bytes_accessed=1_000_000, transcendentals=0
        ),
        name="gradient_rest",
    )(diff, *far(expo, table), stats, norms, partial)


def position(device, masks):
    rest = masks[1:]
    place = jnp.int32(0) if not isinstance(device, int) else 0
    for index, mask in enumerate(rest):
        if isinstance(device, int):
            bit = (device // mask) % 2
        else:
            bit = lax.rem(lax.div(device, mask), 2)
        place = place + (bit << (len(rest) - 1 - index))
    return place


def place_shards(me, natural, keep, send, masks, first, shards, rows=slice(None)):
    mine = lax.rem(me, 2)
    place = position(me, masks)
    for pair in range(first // 2, (first + shards) // 2):
        target = lax.bitwise_xor(place, jnp.int32(position(2 * pair, masks)))
        keep[target, rows] = natural[2 * pair + mine, rows]
        send[target, rows] = natural[2 * pair + 1 - mine, rows]


def row_sums(value):
    return jnp.sum(value.astype(jnp.float32), axis=0, keepdims=True)


def back_to_norm(own_ref, other_ref, y_ref, gain):
    normed, scale = normalise(y_ref[...])
    grad = own_ref[...] + other_ref[...].astype(jnp.float32)
    return norm_back(normed, scale, as_row(gain), grad)


def feed_rows(dm, wc, slope, dinner, rows, bias_out, bias_before):
    hidden_width, width = wc.shape
    for part in range(hidden_width // width):
        span = slice(part * width, (part + 1) * width)
        value = nt(dm, wc[span, :]) * slope[rows, span].astype(jnp.float32)
        value = value.astype(jnp.bfloat16)
        dinner[rows, span] = value
        before = 0.0 if bias_before is None else bias_before[:, span]
        bias_out[:, span] = before + row_sums(value)


def branch_rows(dinner, we, after_ref, gain, dy):
    dh2 = nt(dinner[...], we[...])
    normed, scale = normalise(after_ref[...])
    dafter = dy + norm_back(normed, scale, as_row(gain), dh2)
    return dafter, row_sums(dh2 * normed), row_sums(dh2)


def first_kernel(
    own_ref,
    other_ref,
    y_ref,
    after_ref,
    final_gain,
    second_gain,
    wc,
    we,
    wao,
    slope,
    dm_out,
    dinner_out,
    dafter_out,
    dbranch_out,
    dmixed_out,
    contract_bias_out,
    expand_bias_out,
    second_gain_out,
    second_shift_out,
    attend_bias_out,
):
    count = own_ref.shape[0]
    dy = back_to_norm(own_ref, other_ref, y_ref, final_gain)
    dm = dy.astype(jnp.bfloat16)
    dm_out[...] = dm
    contract_bias_out[...] = row_sums(dm)
    feed_rows(dm, wc, slope, dinner_out, slice(0, count), expand_bias_out, None)
    dafter, second_gain_out[...], second_shift_out[...] = branch_rows(
        dinner_out, we, after_ref, second_gain, dy
    )
    dafter_out[...] = dafter
    dbranch = dafter.astype(jnp.bfloat16)
    dbranch_out[...] = dbranch
    attend_bias_out[...] = row_sums(dbranch)
    dmixed_out[...] = nt(dbranch, wao[...]).astype(jnp.bfloat16)


def first_rows(own, other, y, after, final_gain, second_gain, wc, we, wao, slope):
    rows, width = own.shape
    hidden_width = wc.shape[0]
    low, full = jnp.bfloat16, jnp.float32

    def array(size, kind):
        return jax.ShapeDtypeStruct((rows, size), kind)

    def vector(size):
        return jax.ShapeDtypeStruct((1, size), full)

    top = pl.BlockSpec((rows, width), lambda i: (0, 0))
    return pl.pallas_call(
        first_kernel,
        grid=(1,),
        in_specs=[whole_vmem()] * 2 + [top] * 2 + [whole_vmem()] * 6,
        out_specs=[whole_vmem()] * 10,
        out_shape=[
            array(width, low),
            array(hidden_width, low),
            array(width, full),
            array(width, low),
            array(width, low),
            vector(width),
            vector(hidden_width),
            vector(width),
            vector(width),
            vector(width),
        ],
        compiler_params=pltpu.CompilerParams(vmem_limit_bytes=14 << 20),
        cost_estimate=pl.CostEstimate(
            flops=12_000_000_000, bytes_accessed=1_000_000, transcendentals=0
        ),
        name="first_rows",
    )(own, other, *far(y, after, final_gain, second_gain), *near(wc, we, wao, slope))


def feed_kernel(
    place_ref,
    own_ref,
    other_ref,
    y_ref,
    final_gain,
    dm_first,
    normed_two_ref,
    contract_bias_first,
    expand_bias_first,
    wc_hbm,
    slope,
    active,
    dinner_first,
    cw_keep,
    cw_send,
    ew_keep,
    ew_send,
    dy_out,
    dinner_out,
    contract_bias_out,
    expand_bias_out,
    wc,
    dinner_v,
    dm_v,
    cw_natural,
    ew_natural,
    load_sem,
):
    me, blk = place_ref[0], place_ref[1]
    rows = own_ref.shape[0]
    second = slice(rows, 2 * rows)
    hidden_width, width = wc.shape
    parts = hidden_width // width
    part_width = width // 2
    shards = cw_natural.shape[0]
    chunk = width // shards
    loads = [
        pltpu.make_async_copy(
            wc_hbm.at[pl.ds(part * width, width)],
            wc.at[pl.ds(part * width, width)],
            load_sem.at[part],
        )
        for part in range(parts)
    ]
    for load in loads:
        load.start()
    dinner_v[:rows] = dinner_first[...]
    dy = back_to_norm(own_ref, other_ref, y_ref, final_gain)
    dy_out[...] = dy
    dm = dy.astype(jnp.bfloat16)
    dm_v[:rows] = dm_first[...]
    dm_v[second] = dm
    contract_bias_out[...] = contract_bias_first[...] + row_sums(dm)
    dm_half = dm_v[:, pl.ds(pl.multiple_of(blk * part_width, part_width), part_width)]
    group = shards // parts
    for part in range(parts):
        span = slice(part * width, (part + 1) * width)
        value = tn(active[:, span], dm_half).astype(jnp.bfloat16)
        cw_natural[part * group : (part + 1) * group] = value.reshape(
            group, width // group, part_width
        )
        place_shards(me, cw_natural, cw_keep, cw_send, MASKS, part * group, group)
    for load in loads:
        load.wait()
    feed_rows(dm, wc, slope, dinner_v, second, expand_bias_out, expand_bias_first)
    dinner_out[...] = dinner_v[second]
    for part in range(parts // 2):
        offset = pl.multiple_of(blk * (hidden_width // 2), width) + part * width
        value = tn(normed_two_ref[...], dinner_v[:, pl.ds(pl.multiple_of(offset, width), width)])
        value = value.astype(jnp.bfloat16)
        for half in range(2):
            row = (2 * part + half) * chunk
            ew_natural[:, row : row + chunk, :] = value[
                :, half * part_width : (half + 1) * part_width
            ].reshape(shards, chunk, part_width)
        rows_at = slice(2 * part * chunk, (2 * part + 2) * chunk)
        place_shards(me, ew_natural, ew_keep, ew_send, MASKS_B, 0, shards, rows_at)


def feed_back(
    place, own, other, y, final_gain, dm, normed_two, biases, wc, slope, active, dinner, shards
):
    rows, width = own.shape
    count = 2 * rows
    hidden_width = wc.shape[0]
    low, full = jnp.bfloat16, jnp.float32
    height = hidden_width // shards
    half = jax.ShapeDtypeStruct((shards // 2, height, width // 2), low)
    bottom = pl.BlockSpec((rows, width), lambda i: (1, 0))
    return pl.pallas_call(
        feed_kernel,
        grid=(1,),
        in_specs=[scalars()]
        + [whole_vmem()] * 2
        + [bottom]
        + [whole_vmem()] * 5
        + [in_place()]
        + [whole_vmem()] * 3,
        out_specs=[whole_vmem()] * 8,
        out_shape=[half] * 4
        + [
            jax.ShapeDtypeStruct((rows, width), full),
            jax.ShapeDtypeStruct((rows, hidden_width), low),
            jax.ShapeDtypeStruct((1, width), full),
            jax.ShapeDtypeStruct((1, hidden_width), full),
        ],
        scratch_shapes=[
            pltpu.VMEM(wc.shape, low),
            pltpu.VMEM((count, hidden_width), low),
            pltpu.VMEM((count, width), low),
            pltpu.VMEM((shards, height, width // 2), low),
            pltpu.VMEM((shards, height, width // 2), low),
            pltpu.SemaphoreType.DMA((hidden_width // width,)),
        ],
        compiler_params=pltpu.CompilerParams(vmem_limit_bytes=26 << 20),
        cost_estimate=pl.CostEstimate(
            flops=12_000_000_000, bytes_accessed=1_000_000, transcendentals=0
        ),
        name="feed_back",
    )(
        place,
        own,
        other,
        *far(y, final_gain),
        dm,
        *far(normed_two),
        *biases,
        *far(wc),
        *near(slope, active),
        dinner,
    )


def branch_kernel(
    place_ref,
    dy_ref,
    after_ref,
    mixed_ref,
    second_gain,
    dbranch_first,
    second_gain_first,
    second_shift_first,
    attend_bias_first,
    dinner_ref,
    we,
    wao,
    dafter_out,
    dmixed_out,
    attend_out,
    second_gain_out,
    second_shift_out,
    attend_bias_out,
    dbranch_v,
):
    blk = place_ref[1]
    rows, width = after_ref.shape
    part_width = width // 2
    dafter, gain_sum, shift_sum = branch_rows(
        dinner_ref, we, after_ref, second_gain, dy_ref[...]
    )
    dafter_out[...] = dafter
    second_gain_out[...] = second_gain_first[...] + gain_sum
    second_shift_out[...] = second_shift_first[...] + shift_sum
    dbranch = dafter.astype(jnp.bfloat16)
    dbranch_v[:rows] = dbranch_first[...]
    dbranch_v[rows:] = dbranch
    attend_bias_out[...] = attend_bias_first[...] + row_sums(dbranch)
    dmixed_out[...] = nt(dbranch, wao[...]).astype(jnp.bfloat16)
    part = dbranch_v[:, pl.ds(pl.multiple_of(blk * part_width, part_width), part_width)]
    attend_out[...] = tn(mixed_ref[...], part).astype(jnp.bfloat16).reshape(attend_out.shape)


def branch_back(place, dy, after, mixed, second_gain, dbranch, sums, dinner, we, wao, carry, shards):
    rows, width = dy.shape
    low, full = jnp.bfloat16, jnp.float32
    vector = jax.ShapeDtypeStruct((1, width), full)
    bottom = pl.BlockSpec((rows, width), lambda i: (1, 0))
    return pl.pallas_call(
        carrying(branch_kernel, 12, 6, len(carry)),
        grid=(1,),
        in_specs=[scalars(), whole_vmem(), bottom]
        + [whole_vmem()] * 9
        + [in_place()] * len(carry),
        out_specs=[whole_vmem()] * 6 + [in_place()] * len(carry),
        input_output_aliases=aliases(12, 6, carry),
        out_shape=[
            jax.ShapeDtypeStruct((rows, width), full),
            jax.ShapeDtypeStruct((rows, width), low),
            jax.ShapeDtypeStruct((shards, width // shards, width // 2), low),
            vector,
            vector,
            vector,
        ]
        + shapes_of(carry),
        scratch_shapes=[
            pltpu.VMEM((2 * rows, width), low),
        ],
        compiler_params=pltpu.CompilerParams(vmem_limit_bytes=12 << 20),
        cost_estimate=pl.CostEstimate(
            flops=12_000_000_000, bytes_accessed=1_000_000, transcendentals=0
        ),
        name="branch_back",
    )(
        place,
        dy,
        *far(after, mixed, second_gain),
        dbranch,
        *sums,
        dinner,
        *near(we, wao),
        *carry,
    )


def attend_pair(block, query_ref, keys_ref, values_ref, probs_ref, dmixed_refs):
    count, pair = query_ref.shape
    query = query_ref[...] * jnp.bfloat16(0.125)
    zero = jnp.bfloat16(0.0)
    dkeys = jnp.zeros((count, pair), jnp.float32)
    dvalues = jnp.zeros((count, pair), jnp.float32)
    keys = keys_ref[...] * jnp.bfloat16(0.125)
    dqueries = []
    for piece in reversed(range(count // block)):
        span = slice(piece * block, (piece + 1) * block)
        reach = (piece + 1) * block
        dquery = jnp.zeros((block, pair), jnp.float32)
        add_keys = jnp.zeros((reach, pair), jnp.float32)
        add_values = jnp.zeros((reach, pair), jnp.float32)
        for which in range(2):
            mask = head_mask((block, pair), which)
            grad = jnp.where(mask, dmixed_refs[piece][...], zero)
            mine = jnp.where(mask, query[span], zero)
            probs = probs_ref[which, :reach, span]
            dprobs = nt(values_ref[:reach], grad)
            wide = probs.astype(jnp.float32)
            product = wide * dprobs
            balance = jnp.sum(product, axis=0, keepdims=True)
            dscores = (product - wide * balance).astype(jnp.bfloat16)
            add_values = add_values + dense(probs, grad)
            add_keys = add_keys + dense(dscores, mine)
            dquery = dquery + tn(
                dscores, jnp.where(head_mask((reach, pair), which), keys[:reach], zero)
            )
        dqueries.insert(0, dquery.astype(jnp.bfloat16))
        if reach < count:
            pad = jnp.zeros((count - reach, pair), jnp.float32)
            add_keys = jnp.concatenate([add_keys, pad], axis=0)
            add_values = jnp.concatenate([add_values, pad], axis=0)
        dkeys = dkeys + add_keys
        dvalues = dvalues + add_values
    return (
        jnp.concatenate(dqueries, axis=0),
        dkeys.astype(jnp.bfloat16),
        dvalues.astype(jnp.bfloat16),
    )


def attend_kernel(
    block,
    _,
    query_ref,
    keys_ref,
    values_ref,
    probs_ref,
    dmixed_first,
    dmixed_second,
    dq_ref,
    dk_ref,
    dv_ref,
):
    dmixed = (dmixed_first, dmixed_second)
    grads = attend_pair(block, query_ref, keys_ref, values_ref, probs_ref, dmixed)
    for ref, grad in zip((dq_ref, dk_ref, dv_ref), grads):
        ref[...] = grad


def project_kernel(
    block,
    place_ref,
    query_ref,
    keys_ref,
    values_ref,
    probs_ref,
    dmixed_first,
    dmixed_second,
    normed_ref,
    attend_ref,
    dq_ref,
    dk_ref,
    dv_ref,
    keep,
    send,
    natural,
):
    step = pl.program_id(0)
    pair = query_ref.shape[1]
    column = pl.ds(pl.multiple_of(step * pair, pair), pair)
    dmixed = (dmixed_first, dmixed_second)
    grads = attend_pair(block, query_ref, keys_ref, values_ref, probs_ref, dmixed)
    for ref, grad in zip((dq_ref, dk_ref, dv_ref), grads):
        ref[:, column] = grad

    @pl.when(step == pl.num_programs(0) - 1)
    def _():
        me = place_ref[0]
        shards = natural.shape[0]
        width = normed_ref.shape[1]
        part_width = width // 2
        chunk = width // shards
        natural[:, :chunk, :] = attend_ref[...]
        for part, ref in enumerate((dq_ref, dk_ref, dv_ref)):
            value = tn(normed_ref[...], ref[...]).astype(jnp.bfloat16)
            natural[:, (part + 1) * chunk : (part + 2) * chunk, :] = value.reshape(
                shards, chunk, part_width
            )
            rows = slice(0, 2 * chunk) if part == 0 else slice((part + 1) * chunk, (part + 2) * chunk)
            place_shards(me, natural, keep, send, MASKS, 0, shards, rows)


def attend_specs(joined, dmixed, own):
    rows, width = dmixed[0].shape
    count = 2 * rows
    pair = 2 * HEAD_DIM
    pairs = width // pair
    half = pairs // 2

    def first(place_ref):
        blk = place_ref[1]
        return half * (blk if own else 1 - blk)

    def column(height, offset):
        return pl.BlockSpec((height, pair), lambda p, place_ref: (0, offset + first(place_ref) + p))

    return half, [
        column(count, 0),
        column(count, pairs),
        column(count, 2 * pairs),
        pl.BlockSpec((2, count, count), lambda p, place_ref: (first(place_ref) + p, 0, 0)),
        column(rows, 0),
        column(rows, 0),
    ]


def attend_back(place, joined, probs, dmixed, carry, block):
    width = dmixed[0].shape[1]
    count = joined.shape[0]
    half, specs = attend_specs(joined, dmixed, False)
    result = pl.BlockSpec((count, 2 * HEAD_DIM), lambda p, place_ref: (0, p))
    return pl.pallas_call(
        carrying(functools.partial(attend_kernel, block), 7, 3, len(carry)),
        grid_spec=pltpu.PrefetchScalarGridSpec(
            num_scalar_prefetch=1,
            grid=(half,),
            in_specs=specs + [in_place()] * len(carry),
            out_specs=[result] * 3 + [in_place()] * len(carry),
        ),
        out_shape=[jax.ShapeDtypeStruct((count, width // 2), jnp.bfloat16)] * 3
        + shapes_of(carry),
        input_output_aliases=aliases(7, 3, carry),
        compiler_params=pltpu.CompilerParams(vmem_limit_bytes=16 << 20),
        cost_estimate=pl.CostEstimate(
            flops=12_000_000_000, bytes_accessed=1_000_000, transcendentals=0
        ),
        name="attend_back",
    )(place, *far(joined, joined, joined, probs), *dmixed, *carry)


def project_back(place, joined, probs, dmixed, normed, attend, carry, block, shards):
    count, width = normed.shape
    chunk = width // shards
    half, specs = attend_specs(joined, dmixed, True)
    result = pl.BlockSpec((count, width // 2), lambda p, place_ref: (0, 0))
    piece = jax.ShapeDtypeStruct((shards // 2, 4 * chunk, width // 2), jnp.bfloat16)
    specs = specs + [
        pl.BlockSpec(normed.shape, lambda p, place_ref: (0, 0)),
        pl.BlockSpec(attend.shape, lambda p, place_ref: (0, 0, 0)),
    ]
    return pl.pallas_call(
        carrying(functools.partial(project_kernel, block), 9, 5, len(carry)),
        grid_spec=pltpu.PrefetchScalarGridSpec(
            num_scalar_prefetch=1,
            grid=(half,),
            in_specs=specs + [in_place()] * len(carry),
            out_specs=[result] * 3 + [whole_vmem()] * 2 + [in_place()] * len(carry),
            scratch_shapes=[pltpu.VMEM((shards, 4 * chunk, width // 2), jnp.bfloat16)],
        ),
        out_shape=[jax.ShapeDtypeStruct((count, width // 2), jnp.bfloat16)] * 3
        + [piece, piece]
        + shapes_of(carry),
        input_output_aliases=aliases(9, 5, carry),
        compiler_params=pltpu.CompilerParams(vmem_limit_bytes=18 << 20),
        cost_estimate=pl.CostEstimate(
            flops=12_000_000_000, bytes_accessed=1_000_000, transcendentals=0
        ),
        name="project_back",
    )(place, *far(joined, joined, joined, probs), *dmixed, *far(normed), attend, *carry)


def input_kernel(
    place_ref,
    own_ref,
    other_ref,
    dq_own,
    dk_own,
    dv_own,
    dq_other,
    dk_other,
    dv_other,
    dafter_first,
    dafter_second,
    first_gain,
    attend_bias_grad,
    second_gain_grad,
    second_shift_grad,
    expand_bias_grad,
    contract_bias_grad,
    wpi_hbm,
    grad_out,
    keep,
    send,
    wpi,
    joined_v,
    x_v,
    grad_v,
    load_sem,
):
    me, blk = place_ref[0], place_ref[1]
    load = pltpu.make_async_copy(wpi_hbm, wpi, load_sem.at[0])
    load.start()
    count, width = x_v.shape
    part_width = width // 2
    shards = 2 * keep.shape[0]
    in_stream_order(x_v, own_ref, other_ref, blk)
    for side, group in ((blk, (dq_own, dk_own, dv_own)), (1 - blk, (dq_other, dk_other, dv_other))):
        for part, ref in enumerate(group):
            offset = part * width + side * part_width
            joined_v[:, pl.ds(pl.multiple_of(offset, part_width), part_width)] = ref[...]
    normed, scale = normalise(x_v[...])
    load.wait()
    dh1 = nt(joined_v[...], wpi[...])
    sums = jnp.sum(joined_v[...].astype(jnp.float32), axis=0, keepdims=True)
    vectors = [
        jnp.sum(dh1 * normed, axis=0, keepdims=True),
        jnp.sum(dh1, axis=0, keepdims=True),
        jnp.concatenate([sums[:, :width], sums[:, 2 * width :]], axis=1),
        attend_bias_grad[...],
        second_gain_grad[...],
        second_shift_grad[...],
        expand_bias_grad[...],
        contract_bias_grad[...],
    ]
    mine = lax.rem(me, 2)
    place = position(me, MASKS)
    for shard in range(shards):
        rows = []
        for vector in vectors:
            size = vector.shape[1] // shards
            piece = vector[:, shard * size : (shard + 1) * size]
            rows.append(jnp.concatenate([piece, jnp.zeros((1, 256 - size), jnp.float32)], axis=1))
        value = jnp.concatenate(rows, axis=0)
        target = lax.bitwise_xor(place, jnp.int32(position(shard, MASKS)))

        @pl.when(mine == shard % 2)
        def _():
            keep[target] = value

        @pl.when(mine != shard % 2)
        def _():
            send[target] = value

    rows = own_ref.shape[0]
    grad_v[...] = norm_back(normed, scale, as_row(first_gain), dh1)
    grad_v[:rows] += dafter_first[...]
    grad_v[rows:] += dafter_second[...]
    grad_out[...] = grad_v[pl.ds(pl.multiple_of(blk * rows, rows), rows), :]


def input_back(place, own, other, parts, dafter, gain, vectors, wpi, carry, shards):
    rows, width = own.shape
    count = 2 * rows
    low, full = jnp.bfloat16, jnp.float32
    half = jax.ShapeDtypeStruct((shards // 2, len(vectors) + 3, 256), full)
    return pl.pallas_call(
        carrying(input_kernel, 18, 3, len(carry)),
        in_specs=[scalars()] + [whole_vmem()] * 16 + [in_place()] * (1 + len(carry)),
        out_specs=[whole_vmem()] * 3 + [in_place()] * len(carry),
        out_shape=[jax.ShapeDtypeStruct((rows, width), full), half, half] + shapes_of(carry),
        input_output_aliases=aliases(18, 3, carry),
        scratch_shapes=[
            pltpu.VMEM(wpi.shape, low),
            pltpu.VMEM((count, 3 * width), low),
            pltpu.VMEM((count, width), full),
            pltpu.VMEM((count, width), full),
            pltpu.SemaphoreType.DMA((1,)),
        ],
        compiler_params=pltpu.CompilerParams(vmem_limit_bytes=24 << 20),
        cost_estimate=pl.CostEstimate(
            flops=12_000_000_000, bytes_accessed=1_000_000, transcendentals=0
        ),
        name="input_back",
    )(
        place, *far(own, other), *parts, *dafter, *far(gain), *vectors, *far(wpi), *carry
    )


def across(value, mask):
    return lax.ppermute(value, "dp", [(i, i ^ mask) for i in range(lax.axis_size("dp"))])


def halve(keep, received):
    half = keep.shape[0] // 2
    return (keep[:half] + received[:half], keep[half:] + received[half:])


def merge_kernel(layout, *refs):
    inputs, outputs = list(refs[: 2 * len(layout)]), list(refs[2 * len(layout) :])
    for index, mode in enumerate(layout):
        keep, got = inputs[2 * index], inputs[2 * index + 1]
        half = keep.shape[0] // 2
        if mode == "sum":
            outputs.pop(0)[...] = keep[...] + got[...]
        elif mode == "pass":
            outputs.pop(0)[...] = keep[...]
        elif mode == "halve":
            outputs.pop(0)[...] = keep[:half] + got[:half]
            outputs.pop(0)[...] = keep[half:] + got[half:]
        else:
            place = layout[:index].count("stack")
            if place == 0:
                stacked = (outputs.pop(0), outputs.pop(0))
            stacked[0][place : place + half] = keep[:half] + got[:half]
            stacked[1][place : place + half] = keep[half:] + got[half:]


def merge(*groups):
    layout = [mode for mode, _, _ in groups]
    shapes = []
    for index, (mode, keep, _) in enumerate(groups):
        size = keep.shape[0]
        if mode in ("sum", "pass"):
            shapes.append(jax.ShapeDtypeStruct(keep.shape, keep.dtype))
        elif mode == "halve" or "stack" not in layout[:index]:
            rows = size // 2 * (layout.count("stack") if mode == "stack" else 1)
            shapes += [jax.ShapeDtypeStruct((rows, *keep.shape[1:]), keep.dtype)] * 2
    arrays = [array for _, keep, got in groups for array in (keep, got)]
    return pl.pallas_call(
        functools.partial(merge_kernel, layout),
        in_specs=[whole_vmem()] * len(arrays),
        out_specs=[whole_vmem()] * len(shapes),
        out_shape=shapes,
        compiler_params=pltpu.CompilerParams(vmem_limit_bytes=16 << 20),
        cost_estimate=pl.CostEstimate(flops=1_000_000, bytes_accessed=1_000_000, transcendentals=0),
        name="merge",
    )(*arrays)


def feed_finish_kernel(place_ref, own_ref, other_ref, contract_out, expand_out):
    blk = place_ref[1]
    part = own_ref.shape[2]
    chunk = expand_out.shape[0]
    half = expand_out.shape[1] // 2
    for side, ref in ((blk, own_ref), (1 - blk, other_ref)):
        contract_out[:, pl.ds(pl.multiple_of(side * part, part), part)] = ref[0].astype(jnp.float32)
        for index in range(half // part):
            offset = side * half + index * part
            expand_out[:, pl.ds(pl.multiple_of(offset, part), part)] = ref[
                1, index * chunk : (index + 1) * chunk
            ].astype(jnp.float32)


def feed_finish(place, own, other, chunk):
    _, rows, part = own.shape
    full = jnp.float32
    return pl.pallas_call(
        feed_finish_kernel,
        in_specs=[scalars()] + [whole_vmem()] * 2,
        out_specs=[whole_vmem()] * 2,
        out_shape=[
            jax.ShapeDtypeStruct((rows, 2 * part), full),
            jax.ShapeDtypeStruct((chunk, 2 * part * rows // chunk), full),
        ],
        compiler_params=pltpu.CompilerParams(vmem_limit_bytes=16 << 20),
        cost_estimate=pl.CostEstimate(flops=1_000_000, bytes_accessed=1_000_000, transcendentals=0),
        name="feed_finish",
    )(place, own, other)


def finish_kernel(
    place_ref, own_ref, other_ref, keep_ref, got_ref, _, attend_out, project_out, *vector_outs
):
    blk = place_ref[1]
    chunk, width = attend_out.shape
    part = width // 2
    for side, ref in ((blk, own_ref), (1 - blk, other_ref)):
        for index in range(4):
            value = ref[index * chunk : (index + 1) * chunk].astype(jnp.float32)
            if index == 0:
                target, offset = attend_out, side * part
            else:
                target, offset = project_out, (index - 1) * width + side * part
            target[:, pl.ds(pl.multiple_of(offset, part), part)] = value
    total = keep_ref[0] + got_ref[0]
    for index, out in enumerate(vector_outs):
        out[...] = total[index : index + 1, : out.shape[1]]


def finish(place, own, other, keep, got, ready, chunk, sizes):
    width = 2 * own.shape[1]
    full = jnp.float32
    return pl.pallas_call(
        finish_kernel,
        in_specs=[scalars()] + [whole_vmem()] * 4 + [in_place()],
        out_specs=[whole_vmem()] * (2 + len(sizes)),
        out_shape=[
            jax.ShapeDtypeStruct((chunk, width), full),
            jax.ShapeDtypeStruct((chunk, 3 * width), full),
        ]
        + [jax.ShapeDtypeStruct((1, size), full) for size in sizes],
        compiler_params=pltpu.CompilerParams(vmem_limit_bytes=16 << 20),
        cost_estimate=pl.CostEstimate(flops=1_000_000, bytes_accessed=1_000_000, transcendentals=0),
        name="finish",
    )(place, own, other, keep, got, *far(ready))


def swap(value):
    return lax.ppermute(value, "blk", [(0, 1), (1, 0)])


def both_halves(own, other, blk):
    return jnp.where(
        blk == 0,
        jnp.concatenate([own, other], axis=-1),
        jnp.concatenate([other, own], axis=-1),
    ).astype(jnp.float32)


def local_pair(hidden, doc_lengths, *arrays):
    student, teacher = arrays[:12], arrays[12:24]
    final_gain, final_shift, table = arrays[24:]
    rows, width = hidden.shape
    shards = lax.axis_size("dp")
    blk = lax.axis_index("blk")
    place = jnp.stack([lax.axis_index("dp"), blk]).astype(jnp.int32)
    other = swap(hidden)
    rows_t, rows_s, *kept, other = forward(
        place, doc_lengths, hidden, other, teacher, student, (final_gain, final_shift)
    )
    normed, joined, probs, mixed, after, normed_two, slope, active, y = kept
    diff, expo, stats, sums = logits_phase(rows_s, rows_t, table)
    gain, shift, wpi, qvb, wao, bao, gain_two, shift_two, we, be, wc, bc = student
    sums_other = swap(sums)
    own_first, low_first, partial, norms, we = gradient_phase(
        diff, expo, table, stats, sums, sums_other, we
    )
    got_first = swap(low_first)
    own_second, low_second = gradient_rest(diff, expo, table, stats, norms, partial)
    got_second = swap(low_second)
    dm, dinner, dafter_first, dbranch, dmixed_first, dbc, dbe, *branch_sums = first_rows(
        own_first, got_first, y, after, final_gain, gain_two, wc, we, wao, slope
    )
    cw_keep, cw_send, ew_keep, ew_send, dy, dinner, dbc, dbe = feed_back(
        place,
        own_second,
        got_second,
        y,
        final_gain,
        dm,
        normed_two,
        (dbc, dbe),
        wc,
        slope,
        active,
        dinner,
        shards,
    )
    cw_got = across(cw_send, MASKS[0])
    ew_got = across(ew_send, MASKS_B[0])
    dafter_second, dmixed_second, attend, dgain_two, dshift_two, dbao, cw_keep, ew_keep = (
        branch_back(
            place,
            dy,
            after,
            mixed,
            gain_two,
            dbranch,
            branch_sums,
            dinner,
            we,
            wao,
            (cw_keep, ew_keep),
            shards,
        )
    )
    dafter, dmixed = (dafter_first, dafter_second), (dmixed_first, dmixed_second)
    cw_keep, cw_send = halve(cw_keep, cw_got)
    cw_got = across(cw_send, MASKS[1])
    ew_keep, ew_send = halve(ew_keep, ew_got)
    ew_got = across(ew_send, MASKS_B[1])
    *own_grads, keep, send, cw_keep, ew_keep = project_back(
        place, joined, probs, dmixed, normed, attend, (cw_keep, ew_keep), rows, shards
    )
    got = across(send, MASKS[0])
    cw_keep, cw_send, ew_keep, ew_send = merge(("halve", cw_keep, cw_got), ("halve", ew_keep, ew_got))
    cw_got = across(cw_send, MASKS[2])
    ew_got = across(ew_send, MASKS_B[2])
    *other_grads, keep, cw_keep, ew_keep = attend_back(
        place, joined, probs, dmixed, (keep, cw_keep, ew_keep), rows
    )
    keep, send, both_keep, both_send = merge(
        ("halve", keep, got), ("stack", cw_keep, cw_got), ("stack", ew_keep, ew_got)
    )
    got = across(send, MASKS[1])
    both_got = across(both_send, MASKS[3])
    input_grad, vector_keep, vector_send, keep, both_keep = input_back(
        place,
        hidden,
        other,
        (*own_grads, *other_grads),
        dafter,
        gain,
        (dbao, dgain_two, dshift_two, dbe, dbc),
        wpi,
        (keep, both_keep),
        shards,
    )
    vector_got = across(vector_send, MASKS[0])
    keep, send, both, vector_keep, vector_send = merge(
        ("halve", keep, got),
        ("sum", both_keep, both_got),
        ("halve", vector_keep, vector_got),
    )
    got, vector_got = across(send, MASKS[2]), across(vector_send, MASKS[1])
    keep, send, both, vector_keep, vector_send = merge(
        ("halve", keep, got),
        ("pass", both, both),
        ("halve", vector_keep, vector_got),
    )
    got, vector_got, both_other = (
        across(send, MASKS[3]),
        across(vector_send, MASKS[2]),
        swap(both),
    )
    last, vector_keep, vector_send = merge(
        ("sum", keep, got), ("halve", vector_keep, vector_got)
    )
    last = last[0]
    last_other = swap(last)
    vector_got = across(vector_send, MASKS[3])
    chunk = width // shards
    grad_cw, grad_ew = feed_finish(place, both, both_other, chunk)
    sizes = (chunk, chunk, 2 * chunk, chunk, chunk, chunk, be.shape[0] // shards, chunk)
    grad_ao, grad_pi, *vectors = finish(
        place, last, last_other, vector_keep, vector_got, grad_cw, chunk, sizes
    )
    dgain, dshift, dqvb, dbao, dgain_two, dshift_two, dbe, dbc = (
        vector.reshape(-1) for vector in vectors
    )
    return (
        lax.dynamic_slice_in_dim(norms[2], blk * rows, rows),
        input_grad,
        dgain,
        dshift,
        grad_pi,
        dqvb,
        grad_ao,
        dbao,
        dgain_two,
        dshift_two,
        grad_ew,
        dbe,
        grad_cw,
        dbc,
    )


def solution(mesh):
    pair = mesh.shape["dp"] == 16 and mesh.shape["blk"] == 2
    return jax.shard_map(
        local_pair if pair else local_general,
        mesh=mesh,
        in_specs=(
            P(("dp", "blk"), None),
            P("dp", None),
            P(),
            P(),
            P(),
            P(),
            P(),
            P(),
            P(),
            P(),
            P(),
            P(),
            P(),
            P(),
            P(),
            P(),
            P(),
            P(),
            P(),
            P(),
            P(),
            P(),
            P(),
            P(),
            P(),
            P(),
            P(),
            P(),
            P("blk", None),
        ),
        out_specs=(
            P(("dp", "blk")),
            P(("dp", "blk"), None),
            P("dp"),
            P("dp"),
            P("dp", None),
            P("dp"),
            P("dp", None),
            P("dp"),
            P("dp"),
            P("dp"),
            P("dp", None),
            P("dp"),
            P("dp", None),
            P("dp"),
        ),
        check_vma=False,
    )
```

```python
import functools

import jax
import jax.numpy as jnp
from jax import lax
from jax.experimental import pallas as pl
from jax.experimental.pallas import tpu as pltpu
from jax.sharding import PartitionSpec as P

HEADS = 12
HEAD_DIM = 64
TABLE_SPAN = 2048
SPLIT_STEPS = 4
MASKS = (1, 2, 4, 8)
MASKS_B = (1, 4, 2, 8)


negative = -1e30


def layer_norm(value, gain, shift):
    centre = value - jnp.mean(value, axis=-1, keepdims=True)
    return (
        centre * lax.rsqrt(jnp.mean(centre * centre, axis=-1, keepdims=True) + 1e-05) * gain + shift
    )


def doc_numbers(lengths, count):
    ends = jnp.cumsum(lengths)
    places = jnp.arange(count, dtype=jnp.int32)
    return jnp.sum((places[:, None] >= ends[None, :]).astype(jnp.int32), axis=1)


def dense(left, right):
    return jnp.dot(left, right, preferred_element_type=jnp.float32)


def split_heads(value):
    return value.reshape(value.shape[0], HEADS, HEAD_DIM)


def input_side(inputs, gain, shift, project_in, qv_bias):
    width = inputs.shape[1]
    normed = layer_norm(inputs, gain, shift).astype(jnp.bfloat16)
    bias = jnp.concatenate([qv_bias[:width], jnp.zeros((width,), jnp.float32), qv_bias[width:]])
    joined = (dense(normed, project_in) + bias).astype(jnp.bfloat16)
    return (normed, joined[:, :width], joined[:, width : 2 * width], joined[:, 2 * width :])


def output_side(
    inputs,
    mixed_low,
    attend_out,
    attend_bias,
    second_gain,
    second_shift,
    expand_weight,
    expand_bias,
    contract_weight,
    contract_bias,
):
    after = inputs + dense(mixed_low, attend_out) + attend_bias
    normed = layer_norm(after, second_gain, second_shift).astype(jnp.bfloat16)
    inner = dense(normed, expand_weight) + expand_bias
    active = jax.nn.gelu(inner, approximate=True).astype(jnp.bfloat16)
    final = after + dense(active, contract_weight) + contract_bias
    return (after, normed, inner, active, final)


def online(state, query, keys, values, allowed):
    top, mass, summed = state
    scores = (
        jnp.einsum(
            "qhd,khd->hqk",
            split_heads(query),
            split_heads(keys),
            preferred_element_type=jnp.float32,
        )
        * 0.125
    )
    scores = jnp.where(allowed[None], scores, negative)
    new_top = jnp.maximum(top, jnp.max(scores, axis=-1))
    factor = jnp.exp(top - new_top)
    weights = jnp.where(allowed[None], jnp.exp(scores - new_top[..., None]), 0.0)
    mass = mass * factor + jnp.sum(weights, axis=-1)
    summed = summed * factor[..., None] + jnp.einsum(
        "hqk,khd->hqd",
        weights.astype(jnp.bfloat16),
        split_heads(values),
        preferred_element_type=jnp.float32,
    )
    return (new_top, mass, summed)


def score_grads(query_heads, grad_heads, log_norm, balance, key_block, value_block, allowed):
    scores = (
        jnp.einsum("qhd,khd->hqk", query_heads, key_block, preferred_element_type=jnp.float32)
        * 0.125
    )
    probs = jnp.where(allowed[None], jnp.exp(scores - log_norm[..., None]), 0.0)
    grad_probs = jnp.einsum(
        "qhd,khd->hqk", grad_heads, value_block, preferred_element_type=jnp.float32
    )
    grad_scores = (probs * (grad_probs - balance[..., None])).astype(jnp.bfloat16)
    return (probs, grad_scores)


def partial_stats(rows_teacher, rows_student, table):
    half_t = jnp.einsum("rd,vd->rv", rows_teacher, table, preferred_element_type=jnp.float32) * 0.5
    half_s = jnp.einsum("rd,vd->rv", rows_student, table, preferred_element_type=jnp.float32) * 0.5
    top_t = jnp.max(half_t, axis=-1)
    expo_t = jnp.exp(half_t - top_t[:, None])
    top_s = jnp.max(half_s, axis=-1)
    return (
        top_t,
        jnp.sum(expo_t, axis=-1),
        jnp.sum(expo_t * (half_t - half_s), axis=-1),
        top_s,
        jnp.sum(jnp.exp(half_s - top_s[:, None]), axis=-1),
    )


def combine(first_stats, second_stats):
    top_t = jnp.maximum(first_stats[0], second_stats[0])
    right_weight = jnp.exp(second_stats[0] - top_t)
    top_s = jnp.maximum(first_stats[3], second_stats[3])
    return (
        top_t,
        second_stats[1] * right_weight,
        second_stats[2] * right_weight,
        top_s,
        second_stats[4] * jnp.exp(second_stats[3] - top_s),
    )


def row_gradient(rows_teacher, rows_student, table, norm_t, norm_s):
    half_t = jnp.einsum("rd,vd->rv", rows_teacher, table, preferred_element_type=jnp.float32) * 0.5
    half_s = jnp.einsum("rd,vd->rv", rows_student, table, preferred_element_type=jnp.float32) * 0.5
    change = ((jnp.exp(half_s - norm_s[:, None]) - jnp.exp(half_t - norm_t[:, None])) * 0.5).astype(
        jnp.bfloat16
    )
    return dense(change, table)


def local_general(
    hidden,
    doc_lengths,
    student_first_gain,
    student_first_shift,
    student_project_in,
    student_query_value_bias,
    student_attend_out,
    student_attend_bias,
    student_second_gain,
    student_second_shift,
    student_expand_weight,
    student_expand_bias,
    student_contract_weight,
    student_contract_bias,
    teacher_first_gain,
    teacher_first_shift,
    teacher_project_in,
    teacher_query_value_bias,
    teacher_attend_out,
    teacher_attend_bias,
    teacher_second_gain,
    teacher_second_shift,
    teacher_expand_weight,
    teacher_expand_bias,
    teacher_contract_weight,
    teacher_contract_bias,
    final_gain,
    final_shift,
    embedding,
):
    rows, width = hidden.shape
    blocks = lax.axis_size("blk")
    stream = rows * blocks
    first = lax.axis_index("blk") * rows
    last_place = first + rows - 1
    docs = doc_numbers(doc_lengths[0], stream)
    own_places = first + jnp.arange(rows, dtype=jnp.int32)
    own_docs = lax.dynamic_slice_in_dim(docs, first, rows)
    inputs = hidden.astype(jnp.float32)
    normed_s, query_s, keys_s, values_s = input_side(
        inputs,
        student_first_gain,
        student_first_shift,
        student_project_in,
        student_query_value_bias,
    )
    normed_t, query_t, keys_t, values_t = input_side(
        inputs,
        teacher_first_gain,
        teacher_first_shift,
        teacher_project_in,
        teacher_query_value_bias,
    )

    def allowed_for(begin):
        key_places = begin + jnp.arange(rows, dtype=jnp.int32)
        key_docs = lax.dynamic_slice_in_dim(docs, begin, rows)
        return (key_places[None, :] <= own_places[:, None]) & (
            key_docs[None, :] == own_docs[:, None]
        )

    start_state = (
        jnp.full((HEADS, rows), negative, jnp.float32),
        jnp.zeros((HEADS, rows), jnp.float32),
        jnp.zeros((HEADS, rows, HEAD_DIM), jnp.float32),
    )
    carry = (start_state, start_state)
    pieces = (
        lax.all_gather(keys_s, "blk", axis=0, tiled=True),
        lax.all_gather(values_s, "blk", axis=0, tiled=True),
        lax.all_gather(keys_t, "blk", axis=0, tiled=True),
        lax.all_gather(values_t, "blk", axis=0, tiled=True),
    )
    count = pieces[0].shape[0]
    stacked = tuple((member.reshape(count // rows, rows, width) for member in pieces))
    begins = rows * jnp.arange(count // rows, dtype=jnp.int32)

    def step(state, item):
        piece_keys_s, piece_values_s, piece_keys_t, piece_values_t, begin = item

        def step_compute(inner_state):
            allowed = allowed_for(begin)
            return (
                online(inner_state[0], query_s, piece_keys_s, piece_values_s, allowed),
                online(inner_state[1], query_t, piece_keys_t, piece_values_t, allowed),
            )

        return (
            lax.cond(begin <= last_place, step_compute, lambda inner_state: inner_state, state),
            None,
        )

    carry, _ = lax.scan(step, carry, stacked + (begins,))
    state_s, state_t = carry
    out_heads_s = state_s[2] / state_s[1][..., None]
    attn_norm = state_s[0] + jnp.log(state_s[1])
    mixed_low_s = out_heads_s.transpose(1, 0, 2).reshape(rows, width).astype(jnp.bfloat16)
    mixed_low_t = (
        (state_t[2] / state_t[1][..., None])
        .transpose(1, 0, 2)
        .reshape(rows, width)
        .astype(jnp.bfloat16)
    )
    after_s, normed_two_s, inner_s, active_s, final_s = output_side(
        inputs,
        mixed_low_s,
        student_attend_out,
        student_attend_bias,
        student_second_gain,
        student_second_shift,
        student_expand_weight,
        student_expand_bias,
        student_contract_weight,
        student_contract_bias,
    )
    after_t, normed_two_t, inner_t, active_t, final_t = output_side(
        inputs,
        mixed_low_t,
        teacher_attend_out,
        teacher_attend_bias,
        teacher_second_gain,
        teacher_second_shift,
        teacher_expand_weight,
        teacher_expand_bias,
        teacher_contract_weight,
        teacher_contract_bias,
    )
    rows_s = layer_norm(final_s, final_gain, final_shift).astype(jnp.bfloat16)
    rows_t = layer_norm(final_t, final_gain, final_shift).astype(jnp.bfloat16)
    identity = (
        jnp.full((rows,), negative, jnp.float32),
        jnp.zeros((rows,), jnp.float32),
        jnp.zeros((rows,), jnp.float32),
        jnp.full((rows,), negative, jnp.float32),
        jnp.zeros((rows,), jnp.float32),
    )
    merged = combine(
        identity,
        partial_stats(rows_t, rows_s, lax.all_gather(embedding, "blk", axis=0, tiled=True)),
    )
    norm_t = merged[0] + jnp.log(merged[1])
    norm_s = merged[3] + jnp.log(merged[4])
    kl_rows = merged[2] / merged[1] - norm_t + norm_s
    grad_final = row_gradient(
        rows_t, rows_s, lax.all_gather(embedding, "blk", axis=0, tiled=True), norm_t, norm_s
    )
    _, final_back = jax.vjp(layer_norm, final_s, final_gain, final_shift)
    grad_y = final_back(grad_final)[0]
    grad_m = grad_y.astype(jnp.bfloat16)
    grad_contract_weight = jnp.einsum(
        "rf,rd->fd", active_s, grad_m, preferred_element_type=jnp.float32
    )
    grad_contract_bias = jnp.sum(grad_m.astype(jnp.float32), axis=0)
    grad_active = jnp.einsum(
        "rd,fd->rf", grad_m, student_contract_weight, preferred_element_type=jnp.float32
    )
    _, gelu_back = jax.vjp(lambda value: jax.nn.gelu(value, approximate=True), inner_s)
    grad_inner = gelu_back(grad_active)[0].astype(jnp.bfloat16)
    grad_expand_weight = jnp.einsum(
        "rd,rf->df", normed_two_s, grad_inner, preferred_element_type=jnp.float32
    )
    grad_expand_bias = jnp.sum(grad_inner.astype(jnp.float32), axis=0)
    grad_normed_two = jnp.einsum(
        "rf,df->rd", grad_inner, student_expand_weight, preferred_element_type=jnp.float32
    )
    _, second_back = jax.vjp(layer_norm, after_s, student_second_gain, student_second_shift)
    grad_after_norm, grad_second_gain, grad_second_shift = second_back(grad_normed_two)
    grad_after = grad_y + grad_after_norm
    grad_branch = grad_after.astype(jnp.bfloat16)
    grad_attend_out = jnp.einsum(
        "rc,rd->cd", mixed_low_s, grad_branch, preferred_element_type=jnp.float32
    )
    grad_attend_bias = jnp.sum(grad_branch.astype(jnp.float32), axis=0)
    grad_mixed = jnp.einsum(
        "rd,cd->rc", grad_branch, student_attend_out, preferred_element_type=jnp.float32
    ).astype(jnp.bfloat16)
    keys_all, values_all = (
        lax.all_gather(keys_s, "blk", axis=0, tiled=True),
        lax.all_gather(values_s, "blk", axis=0, tiled=True),
    )
    grad_heads = split_heads(grad_mixed)
    query_heads = split_heads(query_s)
    balance = jnp.sum(grad_heads.astype(jnp.float32).transpose(1, 0, 2) * out_heads_s, axis=-1)
    begins = rows * jnp.arange(blocks, dtype=jnp.int32)
    zero_query = jnp.zeros((rows, HEADS, HEAD_DIM), jnp.float32)

    def back_step(grad_query, begin):
        key_block = split_heads(lax.dynamic_slice_in_dim(keys_all, begin, rows, 0))
        value_block = split_heads(lax.dynamic_slice_in_dim(values_all, begin, rows, 0))

        def back_compute(total):
            probs, grad_scores = score_grads(
                query_heads,
                grad_heads,
                attn_norm,
                balance,
                key_block,
                value_block,
                allowed_for(begin),
            )
            total = (
                total
                + jnp.einsum(
                    "hqk,khd->qhd", grad_scores, key_block, preferred_element_type=jnp.float32
                )
                * 0.125
            )
            grad_keys = (
                jnp.einsum(
                    "hqk,qhd->khd", grad_scores, query_heads, preferred_element_type=jnp.float32
                )
                * 0.125
            )
            grad_values = jnp.einsum(
                "hqk,qhd->khd",
                probs.astype(jnp.bfloat16),
                grad_heads,
                preferred_element_type=jnp.float32,
            )
            return (
                total,
                jnp.concatenate(
                    [grad_keys.reshape(rows, width), grad_values.reshape(rows, width)], axis=1
                ),
            )

        def skip(total):
            return (total, jnp.zeros((rows, 2 * width), jnp.float32))

        return lax.cond(begin <= last_place, back_compute, skip, grad_query)

    grad_query, key_terms = lax.scan(back_step, zero_query, begins)
    key_value_grad = lax.psum_scatter(
        key_terms.reshape(stream, 2 * width).astype(jnp.bfloat16),
        "blk",
        scatter_dimension=0,
        tiled=True,
    ).astype(jnp.float32)
    grad_keys_low = key_value_grad[:, :width].astype(jnp.bfloat16)
    grad_values_low = key_value_grad[:, width:].astype(jnp.bfloat16)
    grad_query_low = grad_query.reshape(rows, width).astype(jnp.bfloat16)
    grad_joined = jnp.concatenate([grad_query_low, grad_keys_low, grad_values_low], axis=1)
    grad_project_in = jnp.einsum(
        "rd,rc->dc", normed_s, grad_joined, preferred_element_type=jnp.float32
    )
    grad_query_value_bias = jnp.concatenate(
        [
            jnp.sum(grad_query_low.astype(jnp.float32), axis=0),
            jnp.sum(grad_values_low.astype(jnp.float32), axis=0),
        ]
    )
    grad_normed = jnp.einsum(
        "rc,dc->rd", grad_joined, student_project_in, preferred_element_type=jnp.float32
    )
    _, first_back = jax.vjp(layer_norm, inputs, student_first_gain, student_first_shift)
    grad_inputs_norm, grad_first_gain, grad_first_shift = first_back(grad_normed)
    input_grad = grad_after + grad_inputs_norm
    shares = (
        lax.psum_scatter(
            grad_first_gain.astype(jnp.bfloat16), "dp", scatter_dimension=0, tiled=True
        ).astype(jnp.float32),
        lax.psum_scatter(
            grad_first_shift.astype(jnp.bfloat16), "dp", scatter_dimension=0, tiled=True
        ).astype(jnp.float32),
        lax.psum_scatter(
            grad_project_in.astype(jnp.bfloat16), "dp", scatter_dimension=0, tiled=True
        ).astype(jnp.float32),
        lax.psum_scatter(
            grad_query_value_bias.astype(jnp.bfloat16), "dp", scatter_dimension=0, tiled=True
        ).astype(jnp.float32),
        lax.psum_scatter(
            grad_attend_out.astype(jnp.bfloat16), "dp", scatter_dimension=0, tiled=True
        ).astype(jnp.float32),
        lax.psum_scatter(
            grad_attend_bias.astype(jnp.bfloat16), "dp", scatter_dimension=0, tiled=True
        ).astype(jnp.float32),
        lax.psum_scatter(
            grad_second_gain.astype(jnp.bfloat16), "dp", scatter_dimension=0, tiled=True
        ).astype(jnp.float32),
        lax.psum_scatter(
            grad_second_shift.astype(jnp.bfloat16), "dp", scatter_dimension=0, tiled=True
        ).astype(jnp.float32),
        lax.psum_scatter(
            grad_expand_weight.astype(jnp.bfloat16), "dp", scatter_dimension=0, tiled=True
        ).astype(jnp.float32),
        lax.psum_scatter(
            grad_expand_bias.astype(jnp.bfloat16), "dp", scatter_dimension=0, tiled=True
        ).astype(jnp.float32),
        lax.psum_scatter(
            grad_contract_weight.astype(jnp.bfloat16), "dp", scatter_dimension=0, tiled=True
        ).astype(jnp.float32),
        lax.psum_scatter(
            grad_contract_bias.astype(jnp.bfloat16), "dp", scatter_dimension=0, tiled=True
        ).astype(jnp.float32),
    )
    summed = (
        lax.psum(shares[0].astype(jnp.bfloat16), "blk").astype(jnp.float32),
        lax.psum(shares[1].astype(jnp.bfloat16), "blk").astype(jnp.float32),
        lax.psum(shares[2].astype(jnp.bfloat16), "blk").astype(jnp.float32),
        lax.psum(shares[3].astype(jnp.bfloat16), "blk").astype(jnp.float32),
        lax.psum(shares[4].astype(jnp.bfloat16), "blk").astype(jnp.float32),
        lax.psum(shares[5].astype(jnp.bfloat16), "blk").astype(jnp.float32),
        lax.psum(shares[6].astype(jnp.bfloat16), "blk").astype(jnp.float32),
        lax.psum(shares[7].astype(jnp.bfloat16), "blk").astype(jnp.float32),
        lax.psum(shares[8].astype(jnp.bfloat16), "blk").astype(jnp.float32),
        lax.psum(shares[9].astype(jnp.bfloat16), "blk").astype(jnp.float32),
        lax.psum(shares[10].astype(jnp.bfloat16), "blk").astype(jnp.float32),
        lax.psum(shares[11].astype(jnp.bfloat16), "blk").astype(jnp.float32),
    )
    return (
        kl_rows,
        input_grad,
        summed[0],
        summed[1],
        summed[2],
        summed[3],
        summed[4],
        summed[5],
        summed[6],
        summed[7],
        summed[8],
        summed[9],
        summed[10],
        summed[11],
    )


def nt(left, right):
    return lax.dot_general(
        left, right, (((1,), (1,)), ((), ())), preferred_element_type=jnp.float32
    )


def tn(left, right):
    return lax.dot_general(
        left, right, (((0,), (0,)), ((), ())), preferred_element_type=jnp.float32
    )


def normalise(value):
    centre = value - jnp.mean(value, axis=-1, keepdims=True)
    scale = lax.rsqrt(jnp.mean(centre * centre, axis=-1, keepdims=True) + 1e-05)
    return (centre * scale, scale)


def norm_back(normed, scale, gain, grad):
    weighted = grad * gain
    return scale * (
        weighted
        - jnp.mean(weighted, axis=-1, keepdims=True)
        - normed * jnp.mean(weighted * normed, axis=-1, keepdims=True)
    )


def starts_of(lengths_ref, count):
    places = lax.broadcasted_iota(jnp.int32, (1, count), 1)
    start = jnp.zeros((1, count), jnp.int32)
    end = jnp.int32(0)
    for index in range(lengths_ref.shape[1]):
        end = end + lengths_ref[0, index]
        start = jnp.where(places >= end, jnp.maximum(start, end), start)
    return start


def in_stream_order(target, own_ref, other_ref, blk):
    rows = own_ref.shape[0]
    target[pl.ds(pl.multiple_of(blk * rows, rows), rows), :] = own_ref[...].astype(target.dtype)
    target[pl.ds(pl.multiple_of((1 - blk) * rows, rows), rows), :] = other_ref[...].astype(
        target.dtype
    )


def head_mask(shape, which):
    lanes = lax.broadcasted_iota(jnp.int32, shape, 1)
    return (lanes >= HEAD_DIM) if which else (lanes < HEAD_DIM)


def forward_kernel(train, *refs):
    (
        place_ref,
        lengths_ref,
        own_ref,
        other_ref,
    ) = refs[:4]
    (
        first_gain,
        first_shift,
        qv_bias,
        attend_bias,
        second_gain,
        second_shift,
        expand_bias,
        contract_bias,
        final_gain,
        final_shift,
    ) = (as_row(ref) for ref in refs[4:14])
    weights_hbm = refs[14:18]
    rest = refs[18:]
    if train:
        rows_out, kept_hbm, rest = rest[0], rest[1:10], rest[10:]
    else:
        rows_out, kept_hbm, rest = rest[0], (), rest[1:]
    wpi, wao, we, wc = rest[:4]
    normed_v, joined_v, probs_v, mixed_v, after_v, normed_two_v, slope_v, active_v, y_v = rest[4:13]
    x_v, bias_v, weight_sem, out_sem, probs_sem = rest[13:]
    kept = (normed_v, joined_v, probs_v, mixed_v, after_v, normed_two_v, slope_v, active_v, y_v)
    loads = [
        pltpu.make_async_copy(source, target, weight_sem.at[index])
        for index, (source, target) in enumerate(zip(weights_hbm, (wpi, wao, we, wc)))
    ]
    stores = []

    def save(index, *at):
        if train:
            source, target = kept[index], kept_hbm[index]
            if at:
                source, target = source.at[at], target.at[at]
            store = pltpu.make_async_copy(source, target, out_sem.at[len(stores)])
            store.start()
            stores.append(store)

    for load in loads:
        load.start()
    blk = place_ref[1]
    in_stream_order(x_v, own_ref, other_ref, blk)
    count, width = x_v.shape
    block = own_ref.shape[0]
    normed, _ = normalise(x_v[...])
    normed_v[...] = (normed * first_gain + first_shift).astype(jnp.bfloat16)
    save(0)
    start = starts_of(lengths_ref, count)
    keys_at = lax.broadcasted_iota(jnp.int32, (count, count), 0)
    queries_at = lax.broadcasted_iota(jnp.int32, (count, count), 1)
    bias_v[...] = jnp.where((keys_at <= queries_at) & (keys_at >= start), 0.0, negative)
    loads[0].wait()
    for part in range(3):
        span = slice(part * width, (part + 1) * width)
        value = dense(normed_v[...], wpi[:, span])
        if part == 0:
            value = value + qv_bias[:, :width]
        if part == 2:
            value = value + qv_bias[:, width:]
        joined_v[:, span] = value.astype(jnp.bfloat16)
    save(1)
    pair = 2 * HEAD_DIM
    pairs = width // pair

    def attend(index, _):
        column = pl.ds(pl.multiple_of(index * pair, pair), pair)
        query = joined_v[:, column] * jnp.bfloat16(0.125)
        keys = joined_v[:, pl.ds(pl.multiple_of(width + index * pair, pair), pair)]
        values = joined_v[:, pl.ds(pl.multiple_of(2 * width + index * pair, pair), pair)]
        for piece in range(count // block):
            span = slice(piece * block, (piece + 1) * block)
            reach = (piece + 1) * block
            both = []
            for which in range(2):
                mine = jnp.where(
                    head_mask((block, pair), which), query[span], jnp.bfloat16(0.0)
                )
                scores = nt(keys[:reach], mine) + bias_v[:reach, span]
                expo = jnp.exp(scores - jnp.max(scores, axis=0, keepdims=True))
                probs = expo * (1.0 / jnp.sum(expo, axis=0, keepdims=True))
                probs = probs.astype(jnp.bfloat16)
                if train:
                    probs_v[2 * index + which, :reach, span] = probs
                both.append(tn(probs, values[:reach]))
            mixed_v[span, column] = jnp.where(
                head_mask((block, pair), 0), both[0], both[1]
            ).astype(jnp.bfloat16)
        if train:
            heads = pl.ds(2 * index, 2)
            pltpu.make_async_copy(
                probs_v.at[heads], kept_hbm[2].at[heads], probs_sem.at[index]
            ).start()
        return 0

    lax.fori_loop(0, pairs, attend, 0, unroll=3)
    if train:
        for index in range(pairs):
            heads = pl.ds(2 * index, 2)
            stores.append(
                pltpu.make_async_copy(
                    probs_v.at[heads], kept_hbm[2].at[heads], probs_sem.at[index]
                )
            )
    save(3)
    loads[1].wait()
    after_v[...] = x_v[...] + dense(mixed_v[...], wao[...]) + attend_bias
    save(4)
    normed, _ = normalise(after_v[...])
    normed_two_v[...] = (normed * second_gain + second_shift).astype(jnp.bfloat16)
    save(5)
    loads[2].wait()
    loads[3].wait()
    hidden_width = we.shape[1]
    total = after_v[...] + contract_bias
    root = 0.7978845608028654
    for part in range(hidden_width // width):
        span = slice(part * width, (part + 1) * width)
        inner = dense(normed_two_v[...], we[:, span]) + expand_bias[:, span]
        square = inner * inner
        bent = jnp.tanh(root * (inner + 0.044715 * (square * inner)))
        upper = 0.5 * (1.0 + bent)
        active = (inner * upper).astype(jnp.bfloat16)
        if train:
            active_v[:, span] = active
            slope_v[:, span] = (
                upper
                + (0.5 * root) * inner * (1.0 - bent * bent) * (1.0 + (3 * 0.044715) * square)
            ).astype(jnp.bfloat16)
            save(6, slice(None), pl.ds(part * width, width))
            save(7, slice(None), pl.ds(part * width, width))
        total = total + dense(active, wc[span, :])
    if train:
        y_v[...] = total
    save(8)
    normed, _ = normalise(total)
    rows_out[...] = (normed * final_gain + final_shift).astype(jnp.bfloat16) * jnp.bfloat16(0.5)
    if train:
        for store in stores:
            store.wait()


def carrying(kernel, inputs, outputs, carried):
    def body(*refs):
        rest = refs[inputs + carried :]
        kernel(*refs[:inputs], *rest[:outputs], *rest[outputs + carried :])

    return body


def shapes_of(carry):
    return [jax.ShapeDtypeStruct(item.shape, item.dtype) for item in carry]


def aliases(inputs, outputs, carry):
    return {inputs + index: outputs + index for index in range(len(carry))}


def as_row(ref):
    return ref[...].reshape(1, ref.shape[0])


def whole_vmem():
    return pl.BlockSpec(memory_space=pltpu.VMEM)


def in_place():
    return pl.BlockSpec(memory_space=pl.ANY)


def far(*arrays):
    return [pltpu.with_memory_space_constraint(array, pltpu.HBM) for array in arrays]


def near(*arrays):
    return [pltpu.with_memory_space_constraint(array, pltpu.VMEM) for array in arrays]


def scalars():
    return pl.BlockSpec(memory_space=pltpu.SMEM)


def forward(train, place, lengths, own, other, vectors, weights):
    rows, width = own.shape
    count = 2 * rows
    hidden_width = weights[2].shape[1]
    low, full = jnp.bfloat16, jnp.float32
    kept = [
        ((count, width), low),
        ((count, 3 * width), low),
        ((HEADS, count, count), low),
        ((count, width), low),
        ((count, width), full),
        ((count, width), low),
        ((count, hidden_width), low),
        ((count, hidden_width), low),
        ((count, width), full),
    ]
    small = ((8, 128), low)
    scratch = [kept[0], kept[1], kept[2] if train else ((1, 8, 128), low), kept[3], kept[4], kept[5]]
    scratch += [kept[6], kept[7], kept[8]] if train else [small, small, ((8, 128), full)]
    out_shape = [pltpu.VMEM((count, width), low)]
    out_specs = [whole_vmem()]
    if train:
        out_shape += [jax.ShapeDtypeStruct(*item) for item in kept]
        out_specs += [in_place()] * len(kept)
    return pl.pallas_call(
        functools.partial(forward_kernel, train),
        in_specs=[scalars(), scalars()] + [whole_vmem()] * 12 + [in_place()] * 4,
        out_specs=out_specs,
        out_shape=out_shape,
        scratch_shapes=[pltpu.VMEM(item.shape, low) for item in weights]
        + [pltpu.VMEM(*item) for item in scratch]
        + [
            pltpu.VMEM((count, width), full),
            pltpu.VMEM((count, count), full),
            pltpu.SemaphoreType.DMA((4,)),
            pltpu.SemaphoreType.DMA((32,)),
            pltpu.SemaphoreType.DMA((HEADS // 2,)),
        ],
        compiler_params=pltpu.CompilerParams(vmem_limit_bytes=(54 if train else 44) << 20),
        cost_estimate=pl.CostEstimate(
            flops=8_000_000_000, bytes_accessed=20_000_000, transcendentals=0
        ),
        name="forward_student" if train else "forward_teacher",
    )(place, lengths, own, other, *far(*vectors, *weights))


def logits_kernel(student_ref, teacher_ref, table_ref, diff_ref, expo_ref, stats_ref, sums_ref):
    count = student_ref.shape[0]
    span = table_ref.shape[0] // 8
    lanes = lax.broadcasted_iota(jnp.int32, (count, 128), 1)
    packed = jnp.zeros((count, 128), jnp.float32)
    for part in range(8):
        where = slice(part * span, (part + 1) * span)
        table = table_ref[where, :]
        half_s = nt(student_ref[...], table)
        top_s = jnp.max(half_s, axis=1, keepdims=True)
        expo_s = jnp.exp(half_s - top_s)
        mass_s = jnp.sum(expo_s, axis=1, keepdims=True)
        half_t = nt(teacher_ref[...], table)
        top_t = jnp.max(half_t, axis=1, keepdims=True)
        expo_t = jnp.exp(half_t - top_t)
        mass_t = jnp.sum(expo_t, axis=1, keepdims=True)
        cross = jnp.sum(expo_t * (half_t - half_s), axis=1, keepdims=True)
        diff_ref[:, where] = (expo_s * (mass_t / mass_s) - expo_t).astype(jnp.bfloat16)
        expo_ref[:, where] = expo_t.astype(jnp.bfloat16)
        for index, column in enumerate((top_s, mass_s, top_t, mass_t, cross)):
            packed = jnp.where(lanes == 8 * index + part, column, packed)
    stats = packed.T
    stats_ref[0] = stats[:40]
    top_s, mass_s, top_t, mass_t, cross = (stats[8 * i : 8 * i + 8] for i in range(5))

    @pl.when(pl.program_id(0) == 0)
    def _():
        row = lax.broadcasted_iota(jnp.int32, sums_ref.shape, 0)
        sums_ref[...] = jnp.where((row == 0) | (row == 2), negative, 0.0)

    old = sums_ref[...]
    new_s = jnp.maximum(old[0:1], jnp.max(top_s, axis=0, keepdims=True))
    new_t = jnp.maximum(old[2:3], jnp.max(top_t, axis=0, keepdims=True))
    keep_s = jnp.exp(old[0:1] - new_s)
    keep_t = jnp.exp(old[2:3] - new_t)
    scale_s = jnp.exp(top_s - new_s)
    scale_t = jnp.exp(top_t - new_t)
    sums_ref[0:1] = new_s
    sums_ref[1:2] = old[1:2] * keep_s + jnp.sum(mass_s * scale_s, axis=0, keepdims=True)
    sums_ref[2:3] = new_t
    sums_ref[3:4] = old[3:4] * keep_t + jnp.sum(mass_t * scale_t, axis=0, keepdims=True)
    sums_ref[4:5] = old[4:5] * keep_t + jnp.sum(cross * scale_t, axis=0, keepdims=True)


def logits_phase(student, teacher, table):
    count, width = student.shape
    entries = table.shape[0]
    span = TABLE_SPAN
    steps = entries // span
    rows = whole_vmem()
    wide = pl.BlockSpec((count, span), lambda j: (0, j))
    return pl.pallas_call(
        logits_kernel,
        grid=(steps,),
        in_specs=[rows, rows, pl.BlockSpec((span, width), lambda j: (j, 0))],
        out_specs=[
            wide,
            wide,
            pl.BlockSpec((1, 40, count), lambda j: (j, 0, 0)),
            pl.BlockSpec((8, count), lambda j: (0, 0)),
        ],
        out_shape=[
            jax.ShapeDtypeStruct((count, entries), jnp.bfloat16),
            jax.ShapeDtypeStruct((count, entries), jnp.bfloat16),
            jax.ShapeDtypeStruct((steps, 40, count), jnp.float32),
            jax.ShapeDtypeStruct((8, count), jnp.float32),
        ],
        compiler_params=pltpu.CompilerParams(vmem_limit_bytes=24 << 20),
        cost_estimate=pl.CostEstimate(
            flops=4 * count * width * entries, bytes_accessed=60_000_000, transcendentals=0
        ),
        name="logits_phase",
    )(*near(student, teacher), *far(table))


def joined_norms(own, other):
    top_s = jnp.maximum(own[0:1], other[0:1])
    top_t = jnp.maximum(own[2:3], other[2:3])
    own_t, other_t = jnp.exp(own[2:3] - top_t), jnp.exp(other[2:3] - top_t)
    mass_s = own[1:2] * jnp.exp(own[0:1] - top_s) + other[1:2] * jnp.exp(other[0:1] - top_s)
    mass_t = own[3:4] * own_t + other[3:4] * other_t
    cross = own[4:5] * own_t + other[4:5] * other_t
    norm_s = top_s + jnp.log(mass_s)
    norm_t = top_t + jnp.log(mass_t)
    return (norm_s, norm_t, cross / mass_t - norm_t + norm_s)


def chunk_factors(stats_ref, norms, rows):
    top_s, mass_s, top_t, mass_t = (stats_ref[0, 8 * i : 8 * i + 8, rows] for i in range(4))
    first = 0.5 * jnp.exp(top_s - norms[0:1, rows]) * mass_s / mass_t
    second = first - 0.5 * jnp.exp(top_t - norms[1:2, rows])
    pad = jnp.zeros((112, first.shape[1]), jnp.float32)
    return jnp.concatenate([first, second, pad], axis=0).T


def chunk_product(total, diffs, expos, factors, table_ref):
    span = table_ref.shape[0] // 8
    for group in range(2):
        pieces = []
        for part in range(4 * group, 4 * group + 4):
            where = slice(part * span, (part + 1) * span)
            pieces.append(
                jnp.concatenate(
                    [
                        (
                            diff[:, where].astype(jnp.float32) * factor[:, part : part + 1]
                            + expo[:, where].astype(jnp.float32) * factor[:, 8 + part : 9 + part]
                        ).astype(jnp.bfloat16)
                        for diff, expo, factor in zip(diffs, expos, factors)
                    ],
                    axis=0,
                )
            )
        where = slice(4 * group * span, 4 * (group + 1) * span)
        total = total + dense(jnp.concatenate(pieces, axis=1), table_ref[where, :])
    return total


def gradient_kernel(
    joint,
    diff_first,
    diff_second,
    expo_first,
    expo_second,
    table_ref,
    stats_ref,
    own_ref,
    other_ref,
    we_hbm,
    first_out,
    first_low,
    second_out,
    norms_out,
    we_out,
    total_ref,
    load_sem,
):
    step = pl.program_id(0)
    rows = diff_first.shape[0]
    load = pltpu.make_async_copy(we_hbm, we_out, load_sem)
    top, bottom = slice(0, rows), slice(rows, 2 * rows)

    @pl.when(step == 0)
    def _():
        load.start()
        norm_s, norm_t, divergence = joined_norms(own_ref[...], other_ref[...])
        norms_out[0:1] = norm_s
        norms_out[1:2] = norm_t
        norms_out[2:3] = divergence
        total_ref[...] = jnp.zeros_like(total_ref)

    @pl.when(step < joint)
    def _():
        total_ref[...] = chunk_product(
            total_ref[...],
            (diff_first, diff_second),
            (expo_first, expo_second),
            (
                chunk_factors(stats_ref, norms_out, top),
                chunk_factors(stats_ref, norms_out, bottom),
            ),
            table_ref,
        )

    @pl.when(step >= joint)
    def _():
        total_ref[top] = chunk_product(
            total_ref[top],
            (diff_first,),
            (expo_first,),
            (chunk_factors(stats_ref, norms_out, top),),
            table_ref,
        )

    @pl.when(step == pl.num_programs(0) - 1)
    def _():
        first_out[...] = total_ref[top]
        second_out[...] = total_ref[bottom]
        first_low[...] = total_ref[top].astype(jnp.bfloat16)
        load.wait()


def gradient_phase(diff, expo, table, stats, own, other, we):
    count, entries = diff.shape
    rows = count // 2
    width = table.shape[1]
    span = TABLE_SPAN
    steps = entries // span
    joint = steps - SPLIT_STEPS
    top = pl.BlockSpec((rows, span), lambda j: (0, j))
    bottom = pl.BlockSpec((rows, span), lambda j: (1, jnp.minimum(j, joint - 1)))
    sums = pl.BlockSpec((8, count), lambda j: (0, 0))
    fixed = pl.BlockSpec((rows, width), lambda j: (0, 0))
    full = jnp.float32
    return pl.pallas_call(
        functools.partial(gradient_kernel, joint),
        grid=(steps,),
        in_specs=[
            top,
            bottom,
            top,
            bottom,
            pl.BlockSpec((span, width), lambda j: (j, 0)),
            pl.BlockSpec((1, 40, count), lambda j: (j, 0, 0)),
            sums,
            sums,
            in_place(),
        ],
        out_specs=[fixed] * 3 + [sums, whole_vmem()],
        out_shape=[
            jax.ShapeDtypeStruct((rows, width), full),
            jax.ShapeDtypeStruct((rows, width), jnp.bfloat16),
            jax.ShapeDtypeStruct((rows, width), full),
            jax.ShapeDtypeStruct((8, count), full),
            pltpu.VMEM(we.shape, we.dtype),
        ],
        scratch_shapes=[
            pltpu.VMEM((count, width), full),
            pltpu.SemaphoreType.DMA,
        ],
        compiler_params=pltpu.CompilerParams(vmem_limit_bytes=20 << 20),
        cost_estimate=pl.CostEstimate(
            flops=2 * count * width * entries, bytes_accessed=60_000_000, transcendentals=0
        ),
        name="gradient_phase",
    )(diff, diff, *far(expo, expo, table), stats, own, other, *far(we))


def gradient_rest_kernel(
    diff_ref, expo_ref, table_ref, stats_ref, norms_ref, partial_ref, total_ref, low_ref
):
    step = pl.program_id(0)
    rows = diff_ref.shape[0]

    @pl.when(step == 0)
    def _():
        total_ref[...] = partial_ref[...]

    total_ref[...] = chunk_product(
        total_ref[...],
        (diff_ref,),
        (expo_ref,),
        (chunk_factors(stats_ref, norms_ref, slice(rows, 2 * rows)),),
        table_ref,
    )

    @pl.when(step == pl.num_programs(0) - 1)
    def _():
        low_ref[...] = total_ref[...].astype(jnp.bfloat16)


def gradient_rest(diff, expo, table, stats, norms, partial):
    count, entries = diff.shape
    rows, width = partial.shape
    span = TABLE_SPAN
    begin = entries // span - SPLIT_STEPS
    wide = pl.BlockSpec((rows, span), lambda j: (1, begin + j))
    fixed = pl.BlockSpec((rows, width), lambda j: (0, 0))
    return pl.pallas_call(
        gradient_rest_kernel,
        grid=(SPLIT_STEPS,),
        in_specs=[
            wide,
            wide,
            pl.BlockSpec((span, width), lambda j: (begin + j, 0)),
            pl.BlockSpec((1, 40, count), lambda j: (begin + j, 0, 0)),
            pl.BlockSpec((8, count), lambda j: (0, 0)),
            fixed,
        ],
        out_specs=[fixed, fixed],
        out_shape=[
            jax.ShapeDtypeStruct((rows, width), jnp.float32),
            jax.ShapeDtypeStruct((rows, width), jnp.bfloat16),
        ],
        compiler_params=pltpu.CompilerParams(vmem_limit_bytes=18 << 20),
        cost_estimate=pl.CostEstimate(
            flops=12_000_000_000, bytes_accessed=1_000_000, transcendentals=0
        ),
        name="gradient_rest",
    )(diff, *far(expo, table), stats, norms, partial)


def position(device, masks):
    rest = masks[1:]
    place = jnp.int32(0) if not isinstance(device, int) else 0
    for index, mask in enumerate(rest):
        if isinstance(device, int):
            bit = (device // mask) % 2
        else:
            bit = lax.rem(lax.div(device, mask), 2)
        place = place + (bit << (len(rest) - 1 - index))
    return place


def place_shards(me, natural, keep, send, masks, first, shards, rows=slice(None)):
    mine = lax.rem(me, 2)
    place = position(me, masks)
    for pair in range(first // 2, (first + shards) // 2):
        target = lax.bitwise_xor(place, jnp.int32(position(2 * pair, masks)))
        keep[target, rows] = natural[2 * pair + mine, rows]
        send[target, rows] = natural[2 * pair + 1 - mine, rows]


def row_sums(value):
    return jnp.sum(value.astype(jnp.float32), axis=0, keepdims=True)


def back_to_norm(own_ref, other_ref, y_ref, gain):
    normed, scale = normalise(y_ref[...])
    grad = own_ref[...] + other_ref[...].astype(jnp.float32)
    return norm_back(normed, scale, as_row(gain), grad)


def feed_rows(dm, wc, slope, dinner, rows, bias_out, bias_before):
    hidden_width, width = wc.shape
    for part in range(hidden_width // width):
        span = slice(part * width, (part + 1) * width)
        value = nt(dm, wc[span, :]) * slope[rows, span].astype(jnp.float32)
        value = value.astype(jnp.bfloat16)
        dinner[rows, span] = value
        before = 0.0 if bias_before is None else bias_before[:, span]
        bias_out[:, span] = before + row_sums(value)


def branch_rows(dinner, we, after_ref, gain, dy):
    dh2 = nt(dinner[...], we[...])
    normed, scale = normalise(after_ref[...])
    dafter = dy + norm_back(normed, scale, as_row(gain), dh2)
    return dafter, row_sums(dh2 * normed), row_sums(dh2)


def first_kernel(
    own_ref,
    other_ref,
    y_ref,
    after_ref,
    final_gain,
    second_gain,
    wc,
    we,
    wao,
    slope,
    dm_out,
    dinner_out,
    dafter_out,
    dbranch_out,
    dmixed_out,
    contract_bias_out,
    expand_bias_out,
    second_gain_out,
    second_shift_out,
    attend_bias_out,
):
    count = own_ref.shape[0]
    dy = back_to_norm(own_ref, other_ref, y_ref, final_gain)
    dm = dy.astype(jnp.bfloat16)
    dm_out[...] = dm
    contract_bias_out[...] = row_sums(dm)
    feed_rows(dm, wc, slope, dinner_out, slice(0, count), expand_bias_out, None)
    dafter, second_gain_out[...], second_shift_out[...] = branch_rows(
        dinner_out, we, after_ref, second_gain, dy
    )
    dafter_out[...] = dafter
    dbranch = dafter.astype(jnp.bfloat16)
    dbranch_out[...] = dbranch
    attend_bias_out[...] = row_sums(dbranch)
    dmixed_out[...] = nt(dbranch, wao[...]).astype(jnp.bfloat16)


def first_rows(own, other, y, after, final_gain, second_gain, wc, we, wao, slope):
    rows, width = own.shape
    hidden_width = wc.shape[0]
    low, full = jnp.bfloat16, jnp.float32

    def array(size, kind):
        return jax.ShapeDtypeStruct((rows, size), kind)

    def vector(size):
        return jax.ShapeDtypeStruct((1, size), full)

    top = pl.BlockSpec((rows, width), lambda i: (0, 0))
    return pl.pallas_call(
        first_kernel,
        grid=(1,),
        in_specs=[whole_vmem()] * 2 + [top] * 2 + [whole_vmem()] * 6,
        out_specs=[whole_vmem()] * 10,
        out_shape=[
            array(width, low),
            array(hidden_width, low),
            array(width, full),
            array(width, low),
            array(width, low),
            vector(width),
            vector(hidden_width),
            vector(width),
            vector(width),
            vector(width),
        ],
        compiler_params=pltpu.CompilerParams(vmem_limit_bytes=14 << 20),
        cost_estimate=pl.CostEstimate(
            flops=12_000_000_000, bytes_accessed=1_000_000, transcendentals=0
        ),
        name="first_rows",
    )(own, other, *far(y, after, final_gain, second_gain), *near(wc, we, wao, slope))


def feed_kernel(
    place_ref,
    own_ref,
    other_ref,
    y_ref,
    final_gain,
    dm_first,
    normed_two_ref,
    contract_bias_first,
    expand_bias_first,
    wc_hbm,
    slope,
    active,
    dinner_first,
    cw_keep,
    cw_send,
    ew_keep,
    ew_send,
    dy_out,
    dinner_out,
    contract_bias_out,
    expand_bias_out,
    wc,
    dinner_v,
    dm_v,
    cw_natural,
    ew_natural,
    load_sem,
):
    me, blk = place_ref[0], place_ref[1]
    rows = own_ref.shape[0]
    second = slice(rows, 2 * rows)
    hidden_width, width = wc.shape
    parts = hidden_width // width
    part_width = width // 2
    shards = cw_natural.shape[0]
    chunk = width // shards
    loads = [
        pltpu.make_async_copy(
            wc_hbm.at[pl.ds(part * width, width)],
            wc.at[pl.ds(part * width, width)],
            load_sem.at[part],
        )
        for part in range(parts)
    ]
    for load in loads:
        load.start()
    dinner_v[:rows] = dinner_first[...]
    dy = back_to_norm(own_ref, other_ref, y_ref, final_gain)
    dy_out[...] = dy
    dm = dy.astype(jnp.bfloat16)
    dm_v[:rows] = dm_first[...]
    dm_v[second] = dm
    contract_bias_out[...] = contract_bias_first[...] + row_sums(dm)
    dm_half = dm_v[:, pl.ds(pl.multiple_of(blk * part_width, part_width), part_width)]
    group = shards // parts
    for part in range(parts):
        span = slice(part * width, (part + 1) * width)
        value = tn(active[:, span], dm_half).astype(jnp.bfloat16)
        cw_natural[part * group : (part + 1) * group] = value.reshape(
            group, width // group, part_width
        )
        place_shards(me, cw_natural, cw_keep, cw_send, MASKS, part * group, group)
    for load in loads:
        load.wait()
    feed_rows(dm, wc, slope, dinner_v, second, expand_bias_out, expand_bias_first)
    dinner_out[...] = dinner_v[second]
    for part in range(parts // 2):
        offset = pl.multiple_of(blk * (hidden_width // 2), width) + part * width
        value = tn(normed_two_ref[...], dinner_v[:, pl.ds(pl.multiple_of(offset, width), width)])
        value = value.astype(jnp.bfloat16)
        for half in range(2):
            row = (2 * part + half) * chunk
            ew_natural[:, row : row + chunk, :] = value[
                :, half * part_width : (half + 1) * part_width
            ].reshape(shards, chunk, part_width)
        rows_at = slice(2 * part * chunk, (2 * part + 2) * chunk)
        place_shards(me, ew_natural, ew_keep, ew_send, MASKS_B, 0, shards, rows_at)


def feed_back(
    place, own, other, y, final_gain, dm, normed_two, biases, wc, slope, active, dinner, shards
):
    rows, width = own.shape
    count = 2 * rows
    hidden_width = wc.shape[0]
    low, full = jnp.bfloat16, jnp.float32
    height = hidden_width // shards
    half = jax.ShapeDtypeStruct((shards // 2, height, width // 2), low)
    bottom = pl.BlockSpec((rows, width), lambda i: (1, 0))
    return pl.pallas_call(
        feed_kernel,
        grid=(1,),
        in_specs=[scalars()]
        + [whole_vmem()] * 2
        + [bottom]
        + [whole_vmem()] * 5
        + [in_place()]
        + [whole_vmem()] * 3,
        out_specs=[whole_vmem()] * 8,
        out_shape=[half] * 4
        + [
            jax.ShapeDtypeStruct((rows, width), full),
            jax.ShapeDtypeStruct((rows, hidden_width), low),
            jax.ShapeDtypeStruct((1, width), full),
            jax.ShapeDtypeStruct((1, hidden_width), full),
        ],
        scratch_shapes=[
            pltpu.VMEM(wc.shape, low),
            pltpu.VMEM((count, hidden_width), low),
            pltpu.VMEM((count, width), low),
            pltpu.VMEM((shards, height, width // 2), low),
            pltpu.VMEM((shards, height, width // 2), low),
            pltpu.SemaphoreType.DMA((hidden_width // width,)),
        ],
        compiler_params=pltpu.CompilerParams(vmem_limit_bytes=26 << 20),
        cost_estimate=pl.CostEstimate(
            flops=12_000_000_000, bytes_accessed=1_000_000, transcendentals=0
        ),
        name="feed_back",
    )(
        place,
        own,
        other,
        *far(y, final_gain),
        dm,
        *far(normed_two),
        *biases,
        *far(wc),
        *near(slope, active),
        dinner,
    )


def branch_kernel(
    place_ref,
    dy_ref,
    after_ref,
    mixed_ref,
    second_gain,
    dbranch_first,
    second_gain_first,
    second_shift_first,
    attend_bias_first,
    dinner_ref,
    we,
    wao,
    dafter_out,
    dmixed_out,
    attend_out,
    second_gain_out,
    second_shift_out,
    attend_bias_out,
    dbranch_v,
):
    blk = place_ref[1]
    rows, width = after_ref.shape
    part_width = width // 2
    dafter, gain_sum, shift_sum = branch_rows(
        dinner_ref, we, after_ref, second_gain, dy_ref[...]
    )
    dafter_out[...] = dafter
    second_gain_out[...] = second_gain_first[...] + gain_sum
    second_shift_out[...] = second_shift_first[...] + shift_sum
    dbranch = dafter.astype(jnp.bfloat16)
    dbranch_v[:rows] = dbranch_first[...]
    dbranch_v[rows:] = dbranch
    attend_bias_out[...] = attend_bias_first[...] + row_sums(dbranch)
    dmixed_out[...] = nt(dbranch, wao[...]).astype(jnp.bfloat16)
    part = dbranch_v[:, pl.ds(pl.multiple_of(blk * part_width, part_width), part_width)]
    attend_out[...] = tn(mixed_ref[...], part).astype(jnp.bfloat16).reshape(attend_out.shape)


def branch_back(place, dy, after, mixed, second_gain, dbranch, sums, dinner, we, wao, carry, shards):
    rows, width = dy.shape
    low, full = jnp.bfloat16, jnp.float32
    vector = jax.ShapeDtypeStruct((1, width), full)
    bottom = pl.BlockSpec((rows, width), lambda i: (1, 0))
    return pl.pallas_call(
        carrying(branch_kernel, 12, 6, len(carry)),
        grid=(1,),
        in_specs=[scalars(), whole_vmem(), bottom]
        + [whole_vmem()] * 9
        + [in_place()] * len(carry),
        out_specs=[whole_vmem()] * 6 + [in_place()] * len(carry),
        input_output_aliases=aliases(12, 6, carry),
        out_shape=[
            jax.ShapeDtypeStruct((rows, width), full),
            jax.ShapeDtypeStruct((rows, width), low),
            jax.ShapeDtypeStruct((shards, width // shards, width // 2), low),
            vector,
            vector,
            vector,
        ]
        + shapes_of(carry),
        scratch_shapes=[
            pltpu.VMEM((2 * rows, width), low),
        ],
        compiler_params=pltpu.CompilerParams(vmem_limit_bytes=12 << 20),
        cost_estimate=pl.CostEstimate(
            flops=12_000_000_000, bytes_accessed=1_000_000, transcendentals=0
        ),
        name="branch_back",
    )(
        place,
        dy,
        *far(after, mixed, second_gain),
        dbranch,
        *sums,
        dinner,
        *near(we, wao),
        *carry,
    )


def attend_pair(block, query_ref, keys_ref, values_ref, probs_ref, dmixed_refs):
    count, pair = query_ref.shape
    query = query_ref[...] * jnp.bfloat16(0.125)
    zero = jnp.bfloat16(0.0)
    dkeys = jnp.zeros((count, pair), jnp.float32)
    dvalues = jnp.zeros((count, pair), jnp.float32)
    keys = keys_ref[...] * jnp.bfloat16(0.125)
    dqueries = []
    for piece in reversed(range(count // block)):
        span = slice(piece * block, (piece + 1) * block)
        reach = (piece + 1) * block
        dquery = jnp.zeros((block, pair), jnp.float32)
        add_keys = jnp.zeros((reach, pair), jnp.float32)
        add_values = jnp.zeros((reach, pair), jnp.float32)
        for which in range(2):
            mask = head_mask((block, pair), which)
            grad = jnp.where(mask, dmixed_refs[piece][...], zero)
            mine = jnp.where(mask, query[span], zero)
            probs = probs_ref[which, :reach, span]
            dprobs = nt(values_ref[:reach], grad)
            wide = probs.astype(jnp.float32)
            product = wide * dprobs
            balance = jnp.sum(product, axis=0, keepdims=True)
            dscores = (product - wide * balance).astype(jnp.bfloat16)
            add_values = add_values + dense(probs, grad)
            add_keys = add_keys + dense(dscores, mine)
            dquery = dquery + tn(
                dscores, jnp.where(head_mask((reach, pair), which), keys[:reach], zero)
            )
        dqueries.insert(0, dquery.astype(jnp.bfloat16))
        if reach < count:
            pad = jnp.zeros((count - reach, pair), jnp.float32)
            add_keys = jnp.concatenate([add_keys, pad], axis=0)
            add_values = jnp.concatenate([add_values, pad], axis=0)
        dkeys = dkeys + add_keys
        dvalues = dvalues + add_values
    return (
        jnp.concatenate(dqueries, axis=0),
        dkeys.astype(jnp.bfloat16),
        dvalues.astype(jnp.bfloat16),
    )


def attend_kernel(
    block,
    _,
    query_ref,
    keys_ref,
    values_ref,
    probs_ref,
    dmixed_first,
    dmixed_second,
    dq_ref,
    dk_ref,
    dv_ref,
):
    dmixed = (dmixed_first, dmixed_second)
    grads = attend_pair(block, query_ref, keys_ref, values_ref, probs_ref, dmixed)
    for ref, grad in zip((dq_ref, dk_ref, dv_ref), grads):
        ref[...] = grad


def project_kernel(
    block,
    place_ref,
    query_ref,
    keys_ref,
    values_ref,
    probs_ref,
    dmixed_first,
    dmixed_second,
    normed_ref,
    attend_ref,
    dq_ref,
    dk_ref,
    dv_ref,
    keep,
    send,
    natural,
):
    step = pl.program_id(0)
    pair = query_ref.shape[1]
    column = pl.ds(pl.multiple_of(step * pair, pair), pair)
    dmixed = (dmixed_first, dmixed_second)
    grads = attend_pair(block, query_ref, keys_ref, values_ref, probs_ref, dmixed)
    for ref, grad in zip((dq_ref, dk_ref, dv_ref), grads):
        ref[:, column] = grad

    @pl.when(step == pl.num_programs(0) - 1)
    def _():
        me = place_ref[0]
        shards = natural.shape[0]
        width = normed_ref.shape[1]
        part_width = width // 2
        chunk = width // shards
        natural[:, :chunk, :] = attend_ref[...]
        for part, ref in enumerate((dq_ref, dk_ref, dv_ref)):
            value = tn(normed_ref[...], ref[...]).astype(jnp.bfloat16)
            natural[:, (part + 1) * chunk : (part + 2) * chunk, :] = value.reshape(
                shards, chunk, part_width
            )
            rows = slice(0, 2 * chunk) if part == 0 else slice((part + 1) * chunk, (part + 2) * chunk)
            place_shards(me, natural, keep, send, MASKS, 0, shards, rows)


def attend_specs(joined, dmixed, own):
    rows, width = dmixed[0].shape
    count = 2 * rows
    pair = 2 * HEAD_DIM
    pairs = width // pair
    half = pairs // 2

    def first(place_ref):
        blk = place_ref[1]
        return half * (blk if own else 1 - blk)

    def column(height, offset):
        return pl.BlockSpec((height, pair), lambda p, place_ref: (0, offset + first(place_ref) + p))

    return half, [
        column(count, 0),
        column(count, pairs),
        column(count, 2 * pairs),
        pl.BlockSpec((2, count, count), lambda p, place_ref: (first(place_ref) + p, 0, 0)),
        column(rows, 0),
        column(rows, 0),
    ]


def attend_back(place, joined, probs, dmixed, carry, block):
    width = dmixed[0].shape[1]
    count = joined.shape[0]
    half, specs = attend_specs(joined, dmixed, False)
    result = pl.BlockSpec((count, 2 * HEAD_DIM), lambda p, place_ref: (0, p))
    return pl.pallas_call(
        carrying(functools.partial(attend_kernel, block), 7, 3, len(carry)),
        grid_spec=pltpu.PrefetchScalarGridSpec(
            num_scalar_prefetch=1,
            grid=(half,),
            in_specs=specs + [in_place()] * len(carry),
            out_specs=[result] * 3 + [in_place()] * len(carry),
        ),
        out_shape=[jax.ShapeDtypeStruct((count, width // 2), jnp.bfloat16)] * 3
        + shapes_of(carry),
        input_output_aliases=aliases(7, 3, carry),
        compiler_params=pltpu.CompilerParams(vmem_limit_bytes=16 << 20),
        cost_estimate=pl.CostEstimate(
            flops=12_000_000_000, bytes_accessed=1_000_000, transcendentals=0
        ),
        name="attend_back",
    )(place, *far(joined, joined, joined, probs), *dmixed, *carry)


def project_back(place, joined, probs, dmixed, normed, attend, carry, block, shards):
    count, width = normed.shape
    chunk = width // shards
    half, specs = attend_specs(joined, dmixed, True)
    result = pl.BlockSpec((count, width // 2), lambda p, place_ref: (0, 0))
    piece = jax.ShapeDtypeStruct((shards // 2, 4 * chunk, width // 2), jnp.bfloat16)
    specs = specs + [
        pl.BlockSpec(normed.shape, lambda p, place_ref: (0, 0)),
        pl.BlockSpec(attend.shape, lambda p, place_ref: (0, 0, 0)),
    ]
    return pl.pallas_call(
        carrying(functools.partial(project_kernel, block), 9, 5, len(carry)),
        grid_spec=pltpu.PrefetchScalarGridSpec(
            num_scalar_prefetch=1,
            grid=(half,),
            in_specs=specs + [in_place()] * len(carry),
            out_specs=[result] * 3 + [whole_vmem()] * 2 + [in_place()] * len(carry),
            scratch_shapes=[pltpu.VMEM((shards, 4 * chunk, width // 2), jnp.bfloat16)],
        ),
        out_shape=[jax.ShapeDtypeStruct((count, width // 2), jnp.bfloat16)] * 3
        + [piece, piece]
        + shapes_of(carry),
        input_output_aliases=aliases(9, 5, carry),
        compiler_params=pltpu.CompilerParams(vmem_limit_bytes=18 << 20),
        cost_estimate=pl.CostEstimate(
            flops=12_000_000_000, bytes_accessed=1_000_000, transcendentals=0
        ),
        name="project_back",
    )(place, *far(joined, joined, joined, probs), *dmixed, *far(normed), attend, *carry)


def input_kernel(
    place_ref,
    own_ref,
    other_ref,
    dq_own,
    dk_own,
    dv_own,
    dq_other,
    dk_other,
    dv_other,
    dafter_first,
    dafter_second,
    first_gain,
    attend_bias_grad,
    second_gain_grad,
    second_shift_grad,
    expand_bias_grad,
    contract_bias_grad,
    wpi_hbm,
    grad_out,
    keep,
    send,
    wpi,
    joined_v,
    x_v,
    grad_v,
    load_sem,
):
    me, blk = place_ref[0], place_ref[1]
    load = pltpu.make_async_copy(wpi_hbm, wpi, load_sem.at[0])
    load.start()
    count, width = x_v.shape
    part_width = width // 2
    shards = 2 * keep.shape[0]
    in_stream_order(x_v, own_ref, other_ref, blk)
    for side, group in ((blk, (dq_own, dk_own, dv_own)), (1 - blk, (dq_other, dk_other, dv_other))):
        for part, ref in enumerate(group):
            offset = part * width + side * part_width
            joined_v[:, pl.ds(pl.multiple_of(offset, part_width), part_width)] = ref[...]
    normed, scale = normalise(x_v[...])
    load.wait()
    dh1 = nt(joined_v[...], wpi[...])
    sums = jnp.sum(joined_v[...].astype(jnp.float32), axis=0, keepdims=True)
    vectors = [
        jnp.sum(dh1 * normed, axis=0, keepdims=True),
        jnp.sum(dh1, axis=0, keepdims=True),
        jnp.concatenate([sums[:, :width], sums[:, 2 * width :]], axis=1),
        attend_bias_grad[...],
        second_gain_grad[...],
        second_shift_grad[...],
        expand_bias_grad[...],
        contract_bias_grad[...],
    ]
    mine = lax.rem(me, 2)
    place = position(me, MASKS)
    for shard in range(shards):
        rows = []
        for vector in vectors:
            size = vector.shape[1] // shards
            piece = vector[:, shard * size : (shard + 1) * size]
            rows.append(jnp.concatenate([piece, jnp.zeros((1, 256 - size), jnp.float32)], axis=1))
        value = jnp.concatenate(rows, axis=0)
        target = lax.bitwise_xor(place, jnp.int32(position(shard, MASKS)))

        @pl.when(mine == shard % 2)
        def _():
            keep[target] = value

        @pl.when(mine != shard % 2)
        def _():
            send[target] = value

    rows = own_ref.shape[0]
    grad_v[...] = norm_back(normed, scale, as_row(first_gain), dh1)
    grad_v[:rows] += dafter_first[...]
    grad_v[rows:] += dafter_second[...]
    grad_out[...] = grad_v[pl.ds(pl.multiple_of(blk * rows, rows), rows), :]


def input_back(place, own, other, parts, dafter, gain, vectors, wpi, carry, shards):
    rows, width = own.shape
    count = 2 * rows
    low, full = jnp.bfloat16, jnp.float32
    half = jax.ShapeDtypeStruct((shards // 2, len(vectors) + 3, 256), full)
    return pl.pallas_call(
        carrying(input_kernel, 18, 3, len(carry)),
        in_specs=[scalars()] + [whole_vmem()] * 16 + [in_place()] * (1 + len(carry)),
        out_specs=[whole_vmem()] * 3 + [in_place()] * len(carry),
        out_shape=[jax.ShapeDtypeStruct((rows, width), full), half, half] + shapes_of(carry),
        input_output_aliases=aliases(18, 3, carry),
        scratch_shapes=[
            pltpu.VMEM(wpi.shape, low),
            pltpu.VMEM((count, 3 * width), low),
            pltpu.VMEM((count, width), full),
            pltpu.VMEM((count, width), full),
            pltpu.SemaphoreType.DMA((1,)),
        ],
        compiler_params=pltpu.CompilerParams(vmem_limit_bytes=24 << 20),
        cost_estimate=pl.CostEstimate(
            flops=12_000_000_000, bytes_accessed=1_000_000, transcendentals=0
        ),
        name="input_back",
    )(
        place, *far(own, other), *parts, *dafter, *far(gain), *vectors, *far(wpi), *carry
    )


def across(value, mask):
    return lax.ppermute(value, "dp", [(i, i ^ mask) for i in range(lax.axis_size("dp"))])


def halve(keep, received):
    half = keep.shape[0] // 2
    return (keep[:half] + received[:half], keep[half:] + received[half:])


def merge_kernel(layout, *refs):
    inputs, outputs = list(refs[: 2 * len(layout)]), list(refs[2 * len(layout) :])
    for index, mode in enumerate(layout):
        keep, got = inputs[2 * index], inputs[2 * index + 1]
        half = keep.shape[0] // 2
        if mode == "sum":
            outputs.pop(0)[...] = keep[...] + got[...]
        elif mode == "pass":
            outputs.pop(0)[...] = keep[...]
        elif mode == "halve":
            outputs.pop(0)[...] = keep[:half] + got[:half]
            outputs.pop(0)[...] = keep[half:] + got[half:]
        else:
            place = layout[:index].count("stack")
            if place == 0:
                stacked = (outputs.pop(0), outputs.pop(0))
            stacked[0][place : place + half] = keep[:half] + got[:half]
            stacked[1][place : place + half] = keep[half:] + got[half:]


def merge(*groups):
    layout = [mode for mode, _, _ in groups]
    shapes = []
    for index, (mode, keep, _) in enumerate(groups):
        size = keep.shape[0]
        if mode in ("sum", "pass"):
            shapes.append(jax.ShapeDtypeStruct(keep.shape, keep.dtype))
        elif mode == "halve" or "stack" not in layout[:index]:
            rows = size // 2 * (layout.count("stack") if mode == "stack" else 1)
            shapes += [jax.ShapeDtypeStruct((rows, *keep.shape[1:]), keep.dtype)] * 2
    arrays = [array for _, keep, got in groups for array in (keep, got)]
    return pl.pallas_call(
        functools.partial(merge_kernel, layout),
        in_specs=[whole_vmem()] * len(arrays),
        out_specs=[whole_vmem()] * len(shapes),
        out_shape=shapes,
        compiler_params=pltpu.CompilerParams(vmem_limit_bytes=16 << 20),
        cost_estimate=pl.CostEstimate(flops=1_000_000, bytes_accessed=1_000_000, transcendentals=0),
        name="merge",
    )(*arrays)


def feed_finish_kernel(place_ref, own_ref, other_ref, contract_out, expand_out):
    blk = place_ref[1]
    part = own_ref.shape[2]
    chunk = expand_out.shape[0]
    half = expand_out.shape[1] // 2
    for side, ref in ((blk, own_ref), (1 - blk, other_ref)):
        contract_out[:, pl.ds(pl.multiple_of(side * part, part), part)] = ref[0].astype(jnp.float32)
        for index in range(half // part):
            offset = side * half + index * part
            expand_out[:, pl.ds(pl.multiple_of(offset, part), part)] = ref[
                1, index * chunk : (index + 1) * chunk
            ].astype(jnp.float32)


def feed_finish(place, own, other, chunk):
    _, rows, part = own.shape
    full = jnp.float32
    return pl.pallas_call(
        feed_finish_kernel,
        in_specs=[scalars()] + [whole_vmem()] * 2,
        out_specs=[whole_vmem()] * 2,
        out_shape=[
            jax.ShapeDtypeStruct((rows, 2 * part), full),
            jax.ShapeDtypeStruct((chunk, 2 * part * rows // chunk), full),
        ],
        compiler_params=pltpu.CompilerParams(vmem_limit_bytes=16 << 20),
        cost_estimate=pl.CostEstimate(flops=1_000_000, bytes_accessed=1_000_000, transcendentals=0),
        name="feed_finish",
    )(place, own, other)


def finish_kernel(
    place_ref, own_ref, other_ref, keep_ref, got_ref, _, attend_out, project_out, *vector_outs
):
    blk = place_ref[1]
    chunk, width = attend_out.shape
    part = width // 2
    for side, ref in ((blk, own_ref), (1 - blk, other_ref)):
        for index in range(4):
            value = ref[index * chunk : (index + 1) * chunk].astype(jnp.float32)
            if index == 0:
                target, offset = attend_out, side * part
            else:
                target, offset = project_out, (index - 1) * width + side * part
            target[:, pl.ds(pl.multiple_of(offset, part), part)] = value
    total = keep_ref[0] + got_ref[0]
    for index, out in enumerate(vector_outs):
        out[...] = total[index : index + 1, : out.shape[1]]


def finish(place, own, other, keep, got, ready, chunk, sizes):
    width = 2 * own.shape[1]
    full = jnp.float32
    return pl.pallas_call(
        finish_kernel,
        in_specs=[scalars()] + [whole_vmem()] * 4 + [in_place()],
        out_specs=[whole_vmem()] * (2 + len(sizes)),
        out_shape=[
            jax.ShapeDtypeStruct((chunk, width), full),
            jax.ShapeDtypeStruct((chunk, 3 * width), full),
        ]
        + [jax.ShapeDtypeStruct((1, size), full) for size in sizes],
        compiler_params=pltpu.CompilerParams(vmem_limit_bytes=16 << 20),
        cost_estimate=pl.CostEstimate(flops=1_000_000, bytes_accessed=1_000_000, transcendentals=0),
        name="finish",
    )(place, own, other, keep, got, *far(ready))


def swap(value):
    return lax.ppermute(value, "blk", [(0, 1), (1, 0)])


def both_halves(own, other, blk):
    return jnp.where(
        blk == 0,
        jnp.concatenate([own, other], axis=-1),
        jnp.concatenate([other, own], axis=-1),
    ).astype(jnp.float32)


def local_pair(hidden, doc_lengths, *arrays):
    student, teacher = arrays[:12], arrays[12:24]
    final_gain, final_shift, table = arrays[24:]
    rows, width = hidden.shape
    shards = lax.axis_size("dp")
    blk = lax.axis_index("blk")
    place = jnp.stack([lax.axis_index("dp"), blk]).astype(jnp.int32)
    other = swap(hidden)
    def block(train, params):
        gain, shift, wpi, qvb, wao, bao, gain_two, shift_two, we, be, wc, bc = params
        vectors = (gain, shift, qvb, bao, gain_two, shift_two, be, bc, final_gain, final_shift)
        return forward(
            train,
            place,
            doc_lengths,
            hidden,
            other,
            vectors,
            (wpi, wao, we, wc),
        )

    (rows_t,) = block(False, teacher)
    rows_s, normed, joined, probs, mixed, after, normed_two, slope, active, y = block(True, student)
    diff, expo, stats, sums = logits_phase(rows_s, rows_t, table)
    gain, shift, wpi, qvb, wao, bao, gain_two, shift_two, we, be, wc, bc = student
    sums_other = swap(sums)
    own_first, low_first, partial, norms, we = gradient_phase(
        diff, expo, table, stats, sums, sums_other, we
    )
    got_first = swap(low_first)
    own_second, low_second = gradient_rest(diff, expo, table, stats, norms, partial)
    got_second = swap(low_second)
    dm, dinner, dafter_first, dbranch, dmixed_first, dbc, dbe, *branch_sums = first_rows(
        own_first, got_first, y, after, final_gain, gain_two, wc, we, wao, slope
    )
    cw_keep, cw_send, ew_keep, ew_send, dy, dinner, dbc, dbe = feed_back(
        place,
        own_second,
        got_second,
        y,
        final_gain,
        dm,
        normed_two,
        (dbc, dbe),
        wc,
        slope,
        active,
        dinner,
        shards,
    )
    cw_got = across(cw_send, MASKS[0])
    ew_got = across(ew_send, MASKS_B[0])
    dafter_second, dmixed_second, attend, dgain_two, dshift_two, dbao, cw_keep, ew_keep = (
        branch_back(
            place,
            dy,
            after,
            mixed,
            gain_two,
            dbranch,
            branch_sums,
            dinner,
            we,
            wao,
            (cw_keep, ew_keep),
            shards,
        )
    )
    dafter, dmixed = (dafter_first, dafter_second), (dmixed_first, dmixed_second)
    cw_keep, cw_send = halve(cw_keep, cw_got)
    cw_got = across(cw_send, MASKS[1])
    ew_keep, ew_send = halve(ew_keep, ew_got)
    ew_got = across(ew_send, MASKS_B[1])
    *own_grads, keep, send, cw_keep, ew_keep = project_back(
        place, joined, probs, dmixed, normed, attend, (cw_keep, ew_keep), rows, shards
    )
    got = across(send, MASKS[0])
    cw_keep, cw_send, ew_keep, ew_send = merge(("halve", cw_keep, cw_got), ("halve", ew_keep, ew_got))
    cw_got = across(cw_send, MASKS[2])
    ew_got = across(ew_send, MASKS_B[2])
    *other_grads, keep, cw_keep, ew_keep = attend_back(
        place, joined, probs, dmixed, (keep, cw_keep, ew_keep), rows
    )
    keep, send, both_keep, both_send = merge(
        ("halve", keep, got), ("stack", cw_keep, cw_got), ("stack", ew_keep, ew_got)
    )
    got = across(send, MASKS[1])
    both_got = across(both_send, MASKS[3])
    input_grad, vector_keep, vector_send, keep, both_keep = input_back(
        place,
        hidden,
        other,
        (*own_grads, *other_grads),
        dafter,
        gain,
        (dbao, dgain_two, dshift_two, dbe, dbc),
        wpi,
        (keep, both_keep),
        shards,
    )
    vector_got = across(vector_send, MASKS[0])
    keep, send, both, vector_keep, vector_send = merge(
        ("halve", keep, got),
        ("sum", both_keep, both_got),
        ("halve", vector_keep, vector_got),
    )
    got, vector_got = across(send, MASKS[2]), across(vector_send, MASKS[1])
    keep, send, both, vector_keep, vector_send = merge(
        ("halve", keep, got),
        ("pass", both, both),
        ("halve", vector_keep, vector_got),
    )
    got, vector_got, both_other = (
        across(send, MASKS[3]),
        across(vector_send, MASKS[2]),
        swap(both),
    )
    last, vector_keep, vector_send = merge(
        ("sum", keep, got), ("halve", vector_keep, vector_got)
    )
    last = last[0]
    last_other = swap(last)
    vector_got = across(vector_send, MASKS[3])
    chunk = width // shards
    grad_cw, grad_ew = feed_finish(place, both, both_other, chunk)
    sizes = (chunk, chunk, 2 * chunk, chunk, chunk, chunk, be.shape[0] // shards, chunk)
    grad_ao, grad_pi, *vectors = finish(
        place, last, last_other, vector_keep, vector_got, grad_cw, chunk, sizes
    )
    dgain, dshift, dqvb, dbao, dgain_two, dshift_two, dbe, dbc = (
        vector.reshape(-1) for vector in vectors
    )
    return (
        lax.dynamic_slice_in_dim(norms[2], blk * rows, rows),
        input_grad,
        dgain,
        dshift,
        grad_pi,
        dqvb,
        grad_ao,
        dbao,
        dgain_two,
        dshift_two,
        grad_ew,
        dbe,
        grad_cw,
        dbc,
    )


def solution(mesh):
    pair = mesh.shape["dp"] == 16 and mesh.shape["blk"] == 2
    return jax.shard_map(
        local_pair if pair else local_general,
        mesh=mesh,
        in_specs=(
            P(("dp", "blk"), None),
            P("dp", None),
            P(),
            P(),
            P(),
            P(),
            P(),
            P(),
            P(),
            P(),
            P(),
            P(),
            P(),
            P(),
            P(),
            P(),
            P(),
            P(),
            P(),
            P(),
            P(),
            P(),
            P(),
            P(),
            P(),
            P(),
            P(),
            P(),
            P("blk", None),
        ),
        out_specs=(
            P(("dp", "blk")),
            P(("dp", "blk"), None),
            P("dp"),
            P("dp"),
            P("dp", None),
            P("dp"),
            P("dp", None),
            P("dp"),
            P("dp"),
            P("dp"),
            P("dp", None),
            P("dp"),
            P("dp", None),
            P("dp"),
        ),
        check_vma=False,
    )
```
